32 devices in a mesh: dp: 2 (over y), station: 16 (over z, x, core).
Axes of the slice: x: 2, y: 2, z: 4, core: 2. Of those that a mesh axis runs over, the one named last changes fastest.
Arguments:
- query_states: bfloat16 [2, 16, 128, 768], P('dp', 'station'), may hold values from -6 to 6
- key_states: bfloat16 [2, 16, 128, 768], P('dp', 'station'), may hold values from -6 to 6
- value_states: bfloat16 [2, 16, 128, 768], P('dp', 'station'), may hold values from -15 to 15
- grad_output: bfloat16 [2, 16, 128, 768], P('dp', 'station'), may hold values from -6 to 6
- out_weight: bfloat16 [768, 768], replicated, may hold values from -0.21875 to 0.21875
- partner_ids: int32 [16, 6], replicated, may hold values from 0 to 15, as said below
- partner_count: int32 [16], replicated, may hold values from 1 to 6, as said below
Outputs:
- layer_output: bfloat16 [2, 16, 128, 768], P('dp', 'station')
- grad_query: bfloat16 [2, 16, 128, 768], P('dp', 'station')
- grad_key: bfloat16 [2, 16, 128, 768], P('dp', 'station')
- grad_value: bfloat16 [2, 16, 128, 768], P('dp', 'station')
- grad_weight: float32 [768, 768], P('dp')
The draws below stay inside these ranges and needn't reach their ends.
Inputs may be any that keep to these rules, and one draw needn't show every extreme that they name: `partner_ids`: row s lists 6 different stations other than s, all held by devices within 3 places of the device of s along the station axis, taken as a loop (station s lies on device s); only the first partner_count[s] entries are partners. `partner_count`: some station has exactly 6 partners.
All inputs are finite; a program needn't handle non-finite values.
Results may differ from the reference program's by a relative error of at most 0.025.
Values may be sent and summed in bfloat16 or wider, within the bound.
No kernel may reach another device: no remote copies, remote signals or barrier semaphores. Data moves between devices by JAX's collectives and lax.ppermute only.
A program may use at most 64 MiB of HBM per device.

```python
import math
import jax
import jax.numpy as jnp
from jax import lax

D = 768
HEADS = 12
SPAN = 128
PMAX = 6
HOPS = 3
STA_DEV = 1
STATIONS = 16
WINDOWS = 2


def draw_query_states(key, part):
    shape = (WINDOWS, STATIONS, SPAN, D)
    result = jnp.clip(jax.random.normal(jax.random.fold_in(key, 1), shape, jnp.float32), -6.0, 6.0)
    return result.astype(jnp.bfloat16)


def draw_key_states(key, part):
    shape = (WINDOWS, STATIONS, SPAN, D)
    result = jnp.clip(jax.random.normal(jax.random.fold_in(key, 2), shape, jnp.float32), -6.0, 6.0)
    return result.astype(jnp.bfloat16)


def draw_partner_count(key, part):
    order = jax.random.permutation(jax.random.fold_in(key, 3), STATIONS)
    base_count = jax.random.randint(jax.random.fold_in(key, 4), (STATIONS,), 1, 3)
    return jnp.where(order < max(1, STATIONS // 16), PMAX, base_count).astype(jnp.int32)


def draw_partner_ids(key, part):
    others = (2 * HOPS + 1) * STA_DEV - 1
    ranking = jax.random.randint(jax.random.fold_in(key, 6), (STATIONS, others), 0, 1 << 18) * 64 + jnp.arange(others, dtype=jnp.int32)[None, :]
    unused, picks = lax.top_k(ranking, PMAX)
    station_ids = jnp.arange(STATIONS, dtype=jnp.int32)[:, None]
    self_pos = HOPS * STA_DEV + station_ids % STA_DEV
    window_pos = picks + (picks >= self_pos).astype(jnp.int32)
    global_ids = jnp.mod(station_ids // STA_DEV * STA_DEV - HOPS * STA_DEV + window_pos, STATIONS)
    return global_ids.astype(jnp.int32)


def level_of(key, extent, split, least, top_value):
    gain, own = 1.0, jax.random.fold_in(key, 6)
    for dim, blocks in split:
        draws = jnp.exp(jax.random.uniform(jax.random.fold_in(own, dim), (blocks,), jnp.float32, least / len(split), top_value / len(split)))
        gain = gain * jnp.repeat(draws, extent[dim] // blocks).reshape([-1 if axis == dim else 1 for axis in range(len(extent))])
    return gain


def scatter_about(key, extent, width, limit, pieces=(), kind=jnp.bfloat16):
    array = width * jax.random.normal(key, extent, jnp.float32)
    if pieces:
        array = array * level_of(key, extent, pieces, -0.22, 0.18)
    return jnp.clip(array, -limit, limit).astype(kind)


def setup_inputs(seed: int = 0) -> dict:
    keys = jax.random.split(jax.random.key(seed), 8)
    return {
        "query_states": draw_query_states(jax.random.fold_in(keys[7], 71), 0),
        "key_states": draw_key_states(jax.random.fold_in(keys[7], 71), 0),
        "value_states": scatter_about(keys[2], (WINDOWS, STATIONS, SPAN, D), 2.5, 15.0, ((0, 2), (1, 16))),
        "grad_output": scatter_about(keys[3], (WINDOWS, STATIONS, SPAN, D), 1.0, 6.0, ((0, 2), (1, 16))),
        "out_weight": scatter_about(keys[4], (D, D), D ** -0.5, 0.21875),
        "partner_ids": draw_partner_ids(jax.random.fold_in(keys[7], 71), 0),
        "partner_count": draw_partner_count(jax.random.fold_in(keys[7], 71), 0),
    }


neg_big = -1e+30

def reference(query_states, key_states, value_states, grad_output, out_weight, partner_ids, partner_count):
    window_count, station_count, span_rows, model_width = query_states.shape
    head_count = HEADS
    head_width = model_width // head_count
    score_scale = 1.0 / math.sqrt(head_width)
    slot_count = PMAX + 1
    row_count = window_count * station_count * span_rows
    flat_grad = grad_output.reshape(row_count, model_width)
    grad_mixed = jnp.dot(flat_grad, out_weight.T, preferred_element_type=jnp.float32).astype(jnp.bfloat16)
    grad_mixed = grad_mixed.reshape(query_states.shape)

    def visit(carry, number):
        key_acc, value_acc = carry
        window_no = number // station_count
        station_no = number % station_count
        slot_station = jnp.concatenate([station_no[None].astype(jnp.int32), partner_ids[station_no].astype(jnp.int32)])
        slot_live = (jnp.arange(slot_count, dtype=jnp.int32) <= partner_count[station_no]).astype(jnp.float32)
        allowed = jnp.repeat(slot_live, span_rows)
        key_rows = key_states[window_no][slot_station].astype(jnp.float32).reshape(slot_count * span_rows, head_count, head_width)
        value_rows = value_states[window_no][slot_station].astype(jnp.float32).reshape(slot_count * span_rows, head_count, head_width)
        query_rows = query_states[window_no, station_no].astype(jnp.float32).reshape(span_rows, head_count, head_width)
        grad_rows = grad_mixed[window_no, station_no].astype(jnp.float32).reshape(span_rows, head_count, head_width)
        scores = jnp.einsum('qhd,khd->hqk', query_rows, key_rows) * score_scale
        masked = jnp.where(allowed[None, None, :] > 0, scores, neg_big)
        row_max = lax.optimization_barrier(jnp.max(masked, -1))
        weights_raw = jnp.exp(masked - row_max[..., None])
        row_sum = lax.optimization_barrier(jnp.sum(weights_raw, -1))
        attn_probs = weights_raw / row_sum[..., None]
        probs_half = lax.optimization_barrier(attn_probs.astype(jnp.bfloat16)).astype(jnp.float32)
        mixed_rows = jnp.einsum('hqk,khd->qhd', probs_half, value_rows).astype(jnp.bfloat16)
        mixed_back = lax.optimization_barrier(mixed_rows).astype(jnp.float32)
        row_delta = lax.optimization_barrier(jnp.sum(grad_rows * mixed_back, -1)).T
        grad_probs = jnp.einsum('qhd,khd->hqk', grad_rows, value_rows)
        grad_scores = (attn_probs * (grad_probs - row_delta[..., None])).astype(jnp.bfloat16)
        scores_back = lax.optimization_barrier(grad_scores).astype(jnp.float32)
        query_grad = (score_scale * jnp.einsum('hqk,khd->qhd', scores_back, key_rows)).astype(jnp.bfloat16)
        key_part = score_scale * jnp.einsum('hqk,qhd->khd', scores_back, query_rows)
        value_part = jnp.einsum('hqk,qhd->khd', probs_half, grad_rows)
        key_acc = key_acc.at[window_no, slot_station].add(key_part.reshape(slot_count, span_rows, model_width))
        value_acc = value_acc.at[window_no, slot_station].add(value_part.reshape(slot_count, span_rows, model_width))
        return ((key_acc, value_acc), (mixed_rows.reshape(span_rows, model_width), query_grad.reshape(span_rows, model_width)))
    zeros = jnp.zeros(key_states.shape, jnp.float32)
    numbers = jnp.arange(window_count * station_count, dtype=jnp.int32)
    (key_acc, value_acc), (mixed_all, query_all) = lax.scan(visit, (zeros, zeros), numbers)
    mixed_flat = mixed_all.reshape(row_count, model_width)
    layer_output = jnp.dot(mixed_flat, out_weight, preferred_element_type=jnp.float32).astype(jnp.bfloat16)
    grad_weight = jnp.dot(mixed_flat.T, flat_grad, preferred_element_type=jnp.float32) / math.sqrt(row_count)
    return (layer_output.reshape(query_states.shape), query_all.reshape(query_states.shape), key_acc.astype(jnp.bfloat16), value_acc.astype(jnp.bfloat16), grad_weight)
```

```python
import functools
import math

import jax
import jax.numpy as jnp
from jax import lax
from jax.experimental import pallas as pl
from jax.experimental.pallas import tpu as pltpu
from jax.sharding import PartitionSpec as P

HEADS = 12
PMAX = 6
GROUP = 4

neg_big = -1e30


def attend(
    my_ref, ids_ref, count_ref, q_ref, g_ref, k_ref, v_ref, a_ref, b_ref, c_ref, s_ref, sa_ref, sb_ref,
    mixed_ref, dq_ref, own_ref, sib_ref, oa_ref, ob_ref, oc_ref,
    keys, values, q_wide, g_wide, probs, probs_half, grads, grads_half,
    *, station_count,
):
    span, width = q_ref.shape
    head_width = width // HEADS
    lanes = GROUP * head_width
    slots = PMAX + 1
    me = my_ref[0]
    side = 2 * lax.rem(me, 2) - 1
    offsets = (0, side, 2 * side, 3 * side, -side, -2 * side, -3 * side)
    live = []
    for offset in offsets:
        station = lax.rem(me + offset + station_count, station_count)
        hit = jnp.int32(1) if not live else jnp.int32(0)
        for j in range(PMAX):
            here = jnp.logical_and(ids_ref[me, j] == station, j < count_ref[me])
            hit = jnp.maximum(hit, here.astype(jnp.int32))
        live.append(hit)
    keys[0:span] = k_ref[...]
    values[0:span] = v_ref[...]
    for j, ref in enumerate((a_ref, b_ref, c_ref, s_ref, sa_ref, sb_ref)):
        keys[(j + 1) * span : (j + 2) * span] = ref[0]
        values[(j + 1) * span : (j + 2) * span] = ref[1]
    head_of = lax.broadcasted_iota(jnp.int32, (span, lanes), 1) // head_width
    nt = (((1,), (1,)), ((), ()))
    tn = (((0,), (0,)), ((), ()))
    nn = (((1,), (0,)), ((), ()))
    f32 = jnp.float32

    def dot(x, y, dims):
        return lax.dot_general(x, y, dims, preferred_element_type=f32)

    def pick(wide):
        blocks = [
            wide[h * head_width : (h + 1) * head_width, h * span : (h + 1) * span] for h in range(GROUP)
        ]
        return jnp.concatenate(blocks, 0).T

    for group in range(HEADS // GROUP):
        at = slice(group * lanes, (group + 1) * lanes)
        q_now = q_ref[:, at] * jnp.bfloat16(1.0 / math.sqrt(head_width))
        g_now = g_ref[:, at]
        zero = jnp.zeros_like(q_now)
        for h in range(GROUP):
            q_wide[h * span : (h + 1) * span] = jnp.where(head_of == h, q_now, zero)
            g_wide[h * span : (h + 1) * span] = jnp.where(head_of == h, g_now, zero)
        top = None
        for j in range(slots):
            rows = slice(j * span, (j + 1) * span)
            scores = dot(keys[rows, at], q_wide[...], nt)
            scores = jnp.where(live[j] > 0, scores, neg_big)
            probs[rows] = scores
            here = jnp.max(scores, 0, keepdims=True)
            top = here if top is None else jnp.maximum(top, here)
        total = jnp.zeros_like(top)
        for j in range(slots):
            rows = slice(j * span, (j + 1) * span)
            raw = jnp.exp(probs[rows] - top)
            probs[rows] = raw
            total = total + jnp.sum(raw, 0, keepdims=True)
        inverse = 1.0 / total
        delta = jnp.zeros_like(top)
        for j in range(slots):
            rows = slice(j * span, (j + 1) * span)
            prob = probs[rows] * inverse
            probs[rows] = prob
            probs_half[rows] = prob.astype(jnp.bfloat16)
            back = dot(values[rows, at], g_wide[...], nt)
            grads[rows] = back
            delta = delta + jnp.sum(back * prob, 0, keepdims=True)
        for j in range(slots):
            rows = slice(j * span, (j + 1) * span)
            grads_half[rows] = (probs[rows] * (grads[rows] - delta)).astype(jnp.bfloat16)
        mixed_ref[:, at] = pick(dot(values[:, at], probs_half[...], tn)).astype(jnp.bfloat16)
        query_grad = pick(dot(keys[:, at], grads_half[...], tn))
        dq_ref[:, at] = (query_grad * (1.0 / math.sqrt(head_width))).astype(jnp.bfloat16)
        for part, left, right in ((0, grads_half, q_wide), (1, probs_half, g_wide)):
            for j in range(slots):
                rows = slice(j * span, (j + 1) * span)
                piece = dot(left[rows], right[...], nn)
                if j == 0:
                    own_ref[part, :, at] = piece
                elif j <= 3:
                    (oa_ref, ob_ref, oc_ref)[j - 1][part, :, at] = piece.astype(jnp.bfloat16)
                else:
                    sib_ref[j - 4, part, :, at] = piece.astype(jnp.bfloat16)


def local(
    query_states, key_states, value_states, grad_output, out_weight, partner_ids, partner_count
):
    span, width = query_states.shape[2:]
    bf16, f32 = jnp.bfloat16, jnp.float32
    stations = lax.axis_size("station")
    windows = lax.axis_size("dp")
    me = lax.axis_index("station")
    side = [1 if s % 2 else -1 for s in range(stations)]

    def routes(steps):
        return [((s + steps * side[s]) % stations, s) for s in range(stations)]

    def back(pairs):
        return [(d, s) for s, d in pairs]

    def swap(value, stride):
        return lax.ppermute(value, "station", [(s ^ stride, s) for s in range(stations)])

    def flat(x):
        return x.reshape(span, width)

    q, k, v, g = flat(query_states), flat(key_states), flat(value_states), flat(grad_output)
    own = jnp.stack([k, v], 0)
    near = lax.ppermute(own, "station", routes(1))
    middle = lax.ppermute(own, "station", routes(2))
    far = lax.ppermute(own, "station", routes(3))
    sib = swap(own, 1)
    sib_near = swap(near, 1)
    sib_middle = swap(middle, 1)
    if windows == 2:
        g_peer = lax.ppermute(g, "dp", [(0, 1), (1, 0)])
    grad_mixed = lax.dot_general(
        g, out_weight, (((1,), (1,)), ((), ())), preferred_element_type=f32
    ).astype(bf16)

    slots = PMAX + 1
    lanes = width // HEADS * GROUP
    pair = jax.ShapeDtypeStruct((2, span, width), bf16)
    flat_shape = jax.ShapeDtypeStruct((span, width), bf16)
    smem = pl.BlockSpec(memory_space=pltpu.SMEM)
    vmem = pl.BlockSpec(memory_space=pltpu.VMEM)
    mixed, grad_query, own_grad, sib_grad, near_grad, middle_grad, far_grad = pl.pallas_call(
        functools.partial(attend, station_count=stations),
        in_specs=[smem] * 3 + [vmem] * 10,
        out_specs=[vmem] * 7,
        out_shape=[
            flat_shape,
            flat_shape,
            jax.ShapeDtypeStruct((2, span, width), f32),
            jax.ShapeDtypeStruct((3, 2, span, width), bf16),
            pair,
            pair,
            pair,
        ],
        scratch_shapes=[
            pltpu.VMEM((slots * span, width), bf16),
            pltpu.VMEM((slots * span, width), bf16),
            pltpu.VMEM((GROUP * span, lanes), bf16),
            pltpu.VMEM((GROUP * span, lanes), bf16),
            pltpu.VMEM((slots * span, GROUP * span), f32),
            pltpu.VMEM((slots * span, GROUP * span), bf16),
            pltpu.VMEM((slots * span, GROUP * span), f32),
            pltpu.VMEM((slots * span, GROUP * span), bf16),
        ],
        compiler_params=pltpu.CompilerParams(vmem_limit_bytes=40 * 1024 * 1024),
        cost_estimate=pl.CostEstimate(
            flops=2 * 5 * slots * span * span * width * 4,
            bytes_accessed=30 * span * width * 2,
            transcendentals=HEADS * slots * span * span,
        ),
        name="attend",
    )(
        me.reshape(1).astype(jnp.int32), partner_ids, partner_count,
        q, grad_mixed, k, v, near, middle, far, sib, sib_near, sib_middle,
    )

    far_home = lax.ppermute(far_grad, "station", back(routes(3)))
    from_sib = swap(sib_grad, 1)
    near_sum = (near_grad.astype(f32) + from_sib[1].astype(f32)).astype(bf16)
    middle_sum = (middle_grad.astype(f32) + from_sib[2].astype(f32)).astype(bf16)
    near_home = lax.ppermute(near_sum, "station", back(routes(1)))
    middle_home = lax.ppermute(middle_sum, "station", back(routes(2)))

    layer_output = jnp.dot(mixed, out_weight, preferred_element_type=f32).astype(bf16)

    dims = (((0,), (0,)), ((), ()))
    rows = width // windows
    if windows == 2:
        w_no = lax.axis_index("dp")
        mine = lax.dynamic_slice_in_dim(mixed, w_no * rows, rows, 1)
        other = lax.dynamic_slice_in_dim(mixed, (1 - w_no) * rows, rows, 1)
        peer = lax.ppermute(other, "dp", [(0, 1), (1, 0)])
        part = lax.dot_general(
            jnp.concatenate([mine, peer], 0), jnp.concatenate([g, g_peer], 0), dims,
            preferred_element_type=f32,
        )
    else:
        whole = lax.dot_general(mixed, g, dims, preferred_element_type=f32).astype(bf16)
        part = lax.psum_scatter(whole, "dp", scatter_dimension=0, tiled=True).astype(f32)
    stride = 1
    halved = []
    while stride < stations:
        if rows % 32 == 0 and rows >= 96:
            rows //= 2
            bit = (me // stride) % 2
            keep = lax.dynamic_slice_in_dim(part, bit * rows, rows, 0)
            send = lax.dynamic_slice_in_dim(part, (1 - bit) * rows, rows, 0).astype(bf16)
            part = keep + swap(send, stride).astype(f32)
            halved.append((stride, bit))
        else:
            half = part.astype(bf16)
            part = half.astype(f32) + swap(half, stride).astype(f32)
        stride *= 2
    result = part.astype(bf16)
    for stride, bit in reversed(halved):
        got = swap(result, stride)
        result = jnp.where(
            bit == 0, jnp.concatenate([result, got], 0), jnp.concatenate([got, result], 0)
        )
    token_count = span * windows * stations
    grad_weight = result.astype(f32) / math.sqrt(token_count)

    home = (
        own_grad + from_sib[0].astype(f32) + far_home.astype(f32) + near_home.astype(f32)
        + middle_home.astype(f32)
    ).astype(bf16)
    shape = query_states.shape
    return (
        layer_output.reshape(shape),
        grad_query.reshape(shape),
        home[0].reshape(shape),
        home[1].reshape(shape),
        grad_weight,
    )


def solution(mesh):
    split = P("dp", "station", None, None)
    return jax.shard_map(
        local,
        mesh=mesh,
        in_specs=(split, split, split, split, P(), P(), P()),
        out_specs=(split, split, split, split, P("dp", None)),
        check_vma=False,
    )
```

```python
import functools
import math

import jax
import jax.numpy as jnp
from jax import lax
from jax.experimental import pallas as pl
from jax.experimental.pallas import tpu as pltpu
from jax.sharding import PartitionSpec as P

HEADS = 12
PMAX = 6
GROUP = 4
SLOTS = PMAX + 1
MIB = 1024 * 1024

neg_big = -1e30
bf16, f32 = jnp.bfloat16, jnp.float32
SMEM = pl.BlockSpec(memory_space=pltpu.SMEM)
VMEM = pl.BlockSpec(memory_space=pltpu.VMEM)
ANY = pl.BlockSpec(memory_space=pl.ANY)
NN = (((1,), (0,)), ((), ()))
NT = (((1,), (1,)), ((), ()))
TN = (((0,), (0,)), ((), ()))


def dot(x, y, dims):
    return lax.dot_general(x, y, dims, preferred_element_type=f32)


def shape_of(*dims, dtype=bf16):
    return jax.ShapeDtypeStruct(dims, dtype)


def call(kernel, ins, outs, args, scratch=(), limit=8, flops=1000, name=None):
    moved = sum(x.size * x.dtype.itemsize for x in outs)
    return pl.pallas_call(
        kernel,
        in_specs=ins,
        out_specs=[VMEM] * len(outs),
        out_shape=outs,
        scratch_shapes=list(scratch),
        compiler_params=pltpu.CompilerParams(vmem_limit_bytes=limit * MIB),
        cost_estimate=pl.CostEstimate(flops=flops, bytes_accessed=2 * moved, transcendentals=0),
        name=name,
    )(*args)


def fetch(pairs, sems):
    copies = [pltpu.make_async_copy(a, b, sems.at[n]) for n, (a, b) in enumerate(pairs)]
    for copy in copies:
        copy.start()
    return copies


def pack_kernel(k_ref, v_ref, out_ref, sems):
    for copy in fetch([(k_ref, out_ref.at[0]), (v_ref, out_ref.at[1])], sems):
        copy.wait()


def widen(x, wide_ref, head_of):
    span = x.shape[0]
    zero = jnp.zeros_like(x)
    for h in range(GROUP):
        wide_ref[h * span : (h + 1) * span] = jnp.where(head_of == h, x, zero)


def pick(wide, span, head_width):
    blocks = [
        wide[h * head_width : (h + 1) * head_width, h * span : (h + 1) * span] for h in range(GROUP)
    ]
    return jnp.concatenate(blocks, 0)


def forward_kernel(
    at_ref, ids_ref, count_ref, q_ref, own_ref, near_ref, middle_ref, far_ref, sib_ref, sib_near_ref,
    sib_middle_ref, g_win_ref, g_sib_ref, g_both_ref,
    mixed_ref, mine_ref, to_win_ref, to_sib_ref, to_both_ref, probs_ref, keys, values,
    q_all, q_wide, raw, sems,
    *, station_count,
):
    span, width = q_all.shape
    head_width = width // HEADS
    lanes = GROUP * head_width
    parts = (own_ref, near_ref, middle_ref, far_ref, sib_ref, sib_near_ref, sib_middle_ref)
    pairs = [(q_ref, q_all)]
    for j, ref in enumerate(parts):
        pairs.append((ref.at[0], keys.at[j * span : (j + 1) * span]))
    for j, ref in enumerate(parts):
        pairs.append((ref.at[1], values.at[j * span : (j + 1) * span]))
    copies = fetch(pairs, sems)
    me = at_ref[0]
    side = 2 * lax.rem(me, 2) - 1
    live = [None]
    for offset in (side, 2 * side, 3 * side, -side, -2 * side, -3 * side):
        station = lax.rem(me + offset + station_count, station_count)
        hit = jnp.int32(0)
        for j in range(PMAX):
            here = jnp.logical_and(ids_ref[me, j] == station, j < count_ref[me])
            hit = jnp.maximum(hit, here.astype(jnp.int32))
        live.append(hit)
    head_of = lax.broadcasted_iota(jnp.int32, (span, lanes), 1) // head_width
    copies[0].wait()
    for group in range(HEADS // GROUP):
        cols = slice(group * lanes, (group + 1) * lanes)
        widen(q_all[:, cols] * bf16(1.0 / math.sqrt(head_width)), q_wide, head_of)
        top = None
        for j in range(SLOTS):
            rows = slice(j * span, (j + 1) * span)
            if group == 0:
                copies[1 + j].wait()
            scores = dot(keys[rows, cols], q_wide[...], NT)
            if j:
                scores = jnp.where(live[j] > 0, scores, neg_big)
            raw[rows] = scores
            here = jnp.max(scores, 0, keepdims=True)
            top = here if top is None else jnp.maximum(top, here)
        total = jnp.zeros_like(top)
        for j in range(SLOTS):
            rows = slice(j * span, (j + 1) * span)
            weight = jnp.exp(raw[rows] - top)
            raw[rows] = weight
            total = total + jnp.sum(weight, 0, keepdims=True)
        inverse = 1.0 / total
        for j in range(SLOTS):
            rows = slice(j * span, (j + 1) * span)
            probs_ref[group, rows] = (raw[rows] * inverse).astype(bf16)
            if group == 0:
                copies[1 + SLOTS + j].wait()
        wide = dot(values[:, cols], probs_ref[group], TN)
        mixed_ref[cols] = pick(wide, span, head_width).astype(bf16)
    quarter = mine_ref.shape[0]
    core, window = lax.rem(me, 2), at_ref[1]
    for ref, w, c in (
        (mine_ref, window, core),
        (to_win_ref, 1 - window, core),
        (to_sib_ref, window, 1 - core),
        (to_both_ref, 1 - window, 1 - core),
    ):
        start = pl.multiple_of(lax.rem(2 * w + c, width // quarter) * quarter, quarter)
        ref[...] = mixed_ref[pl.ds(start, quarter)]


def backward_kernel(
    q_ref, g_ref, keys, values, probs_ref,
    dq_ref, own_ref, near_ref, middle_ref, far_ref, sib_ref,
    q_all, g_all, q_wide, g_wide, grads, grads_half, sems,
):
    span, width = q_all.shape
    head_width = width // HEADS
    lanes = GROUP * head_width
    scale = 1.0 / math.sqrt(head_width)
    for copy in fetch([(q_ref, q_all), (g_ref, g_all)], sems):
        copy.wait()
    head_of = lax.broadcasted_iota(jnp.int32, (span, lanes), 1) // head_width
    for group in range(HEADS // GROUP):
        cols = slice(group * lanes, (group + 1) * lanes)
        widen(q_all[:, cols] * bf16(scale), q_wide, head_of)
        widen(g_all[:, cols], g_wide, head_of)
        delta = None
        for j in range(SLOTS):
            rows = slice(j * span, (j + 1) * span)
            back = dot(values[rows, cols], g_wide[...], NT)
            grads[rows] = back
            here = jnp.sum(back * probs_ref[group, rows].astype(f32), 0, keepdims=True)
            delta = here if delta is None else delta + here
        for j in range(SLOTS):
            rows = slice(j * span, (j + 1) * span)
            grad = probs_ref[group, rows].astype(f32) * (grads[rows] - delta)
            grads_half[rows] = grad.astype(bf16)
        wide = dot(keys[:, cols], grads_half[...], TN)
        dq_ref[:, cols] = (pick(wide, span, head_width).T * scale).astype(bf16)
        for part, left, right in ((0, grads_half, q_wide), (1, probs_ref.at[group], g_wide)):
            for j in range(SLOTS):
                rows = slice(j * span, (j + 1) * span)
                piece = dot(left[rows], right[...], NN)
                if j == 0:
                    own_ref[part, :, cols] = piece
                elif j <= 3:
                    (near_ref, middle_ref, far_ref)[j - 1][part, :, cols] = piece.astype(bf16)
                else:
                    sib_ref[j - 4, part, :, cols] = piece.astype(bf16)


def sums_kernel(own_ref, near_ref, middle_ref, got_ref, own_out, near_out, middle_out, got, sems):
    copies = fetch([(got_ref.at[j], got.at[j]) for j in range(3)], sems)
    copies[1].wait()
    near_out[...] = (near_ref[...].astype(f32) + got[1].astype(f32)).astype(bf16)
    copies[2].wait()
    middle_out[...] = (middle_ref[...].astype(f32) + got[2].astype(f32)).astype(bf16)
    copies[0].wait()
    own_out[...] = own_ref[...] + got[0].astype(f32)


def home_kernel(own_ref, near_ref, middle_ref, far_ref, dk_ref, dv_ref, got, sems):
    refs = (near_ref, middle_ref, far_ref)
    copies = fetch([(ref, got.at[j]) for j, ref in enumerate(refs)], sems)
    for copy in copies:
        copy.wait()
    for part, out in ((0, dk_ref), (1, dv_ref)):
        total = own_ref[part]
        for j in range(3):
            total = total + got[j, part].astype(f32)
        out[...] = total.astype(bf16)


def weight_kernel(
    stride, at_ref, mine_ref, win_ref, sib_ref, both_ref, g_ref, g_win_ref, g_sib_ref, g_both_ref,
    after_ref, send_ref, keep_ref, left, right, sems,
):
    span = mine_ref.shape[1]
    half = send_ref.shape[0]
    pairs = []
    for j, (a, b) in enumerate(
        ((mine_ref, g_ref), (win_ref, g_win_ref), (sib_ref, g_sib_ref), (both_ref, g_both_ref))
    ):
        pairs.append((a, left.at[:, j * span : (j + 1) * span]))
        pairs.append((b, right.at[j * span : (j + 1) * span]))
    for copy in fetch(pairs, sems):
        copy.wait()
    bit = lax.rem(at_ref[0] // stride, 2)
    send = pl.ds(pl.multiple_of((1 - bit) * half, half), half)
    keep = pl.ds(pl.multiple_of(bit * half, half), half)
    send_ref[...] = dot(left[send], right[...], NN).astype(bf16)
    keep_ref[...] = dot(left[keep], right[...], NN)


def split_kernel(stride, at_ref, part_ref, got_ref, after_ref, send_ref, keep_ref, got, sems):
    half = send_ref.shape[0]
    for copy in fetch([(got_ref, got)], sems):
        copy.wait()
    bit = lax.rem(at_ref[0] // stride, 2)
    send = pl.ds(pl.multiple_of((1 - bit) * half, half), half)
    keep = pl.ds(pl.multiple_of(bit * half, half), half)
    send_ref[...] = (part_ref[send] + got[send].astype(f32)).astype(bf16)
    keep_ref[...] = part_ref[keep] + got[keep].astype(f32)


def round_kernel(part_ref, got_ref, after_ref, out_ref, got, sems):
    for copy in fetch([(got_ref, got)], sems):
        copy.wait()
    out_ref[...] = (part_ref[...].astype(f32) + got[...].astype(f32)).astype(bf16)


def join_kernel(stride, scale, at_ref, mine_ref, got_ref, after_a, after_b, after_c, out_ref, got, sems):
    half = mine_ref.shape[0]
    copies = fetch([(got_ref, got)], sems)
    bit = lax.rem(at_ref[0] // stride, 2)

    def put(place, value):
        if scale is not None:
            value = value.astype(f32) * scale
        out_ref[pl.ds(pl.multiple_of(place * half, half), half)] = value

    put(bit, mine_ref[...])
    copies[0].wait()
    put(1 - bit, got[...])


def local(
    query_states, key_states, value_states, grad_output, out_weight, partner_ids, partner_count
):
    span, width = query_states.shape[2:]
    stations = lax.axis_size("station")
    windows = lax.axis_size("dp")
    me = lax.axis_index("station").astype(jnp.int32)
    window = lax.axis_index("dp").astype(jnp.int32)
    at = jnp.stack([me, window])
    side = [1 if s % 2 else -1 for s in range(stations)]

    def routes(steps):
        return [((s + steps * side[s]) % stations, s) for s in range(stations)]

    def back(pairs):
        return [(d, s) for s, d in pairs]

    def swap(value, stride):
        return lax.ppermute(value, "station", [(s ^ stride, s) for s in range(stations)])

    def other_window(value):
        return lax.ppermute(value, "dp", [(0, 1), (1, 0)])

    def other_both(value):
        count = 2 * stations
        pairs = [(s, (s + stations) % count ^ 1) for s in range(count)]
        return lax.ppermute(value, ("dp", "station"), pairs)

    def flat(x):
        return x.reshape(span, width)

    q, k, v, g = flat(query_states), flat(key_states), flat(value_states), flat(grad_output)
    dma = pltpu.SemaphoreType.DMA
    (own,) = call(
        pack_kernel, [ANY, ANY], [shape_of(2, span, width)], (k, v), [dma((2,))], name="pack"
    )
    near = lax.ppermute(own, "station", routes(1))
    middle = lax.ppermute(own, "station", routes(2))
    far = lax.ppermute(own, "station", routes(3))
    sib = swap(own, 1)
    sib_near = swap(near, 1)
    sib_middle = swap(middle, 1)
    grad_mixed = dot(g, out_weight, NT).astype(bf16)

    if windows == 2:
        g_late, near = lax.optimization_barrier((g, near))
        peers = (other_window(g_late), swap(g_late, 1), other_both(g_late))
    else:
        peers = (g, g, g)

    lanes = width // HEADS * GROUP
    groups = HEADS // GROUP
    quarter = width // 4
    attend_flops = 2 * SLOTS * span * span * width * 8
    small = shape_of(quarter, span)
    mixed, mine, to_win, to_sib, to_both, probs, keys, values = call(
        functools.partial(forward_kernel, station_count=stations),
        [SMEM] * 3 + [ANY] * 11,
        [
            shape_of(width, span), small, small, small, small,
            shape_of(groups, SLOTS * span, GROUP * span),
            shape_of(SLOTS * span, width),
            shape_of(SLOTS * span, width),
        ],
        (at, partner_ids, partner_count, q, own, near, middle, far, sib, sib_near, sib_middle)
        + peers,
        [
            pltpu.VMEM((span, width), bf16),
            pltpu.VMEM((GROUP * span, lanes), bf16),
            pltpu.VMEM((SLOTS * span, GROUP * span), f32),
            dma((1 + 2 * SLOTS,)),
        ],
        limit=24, flops=attend_flops, name="forward",
    )
    pair = shape_of(2, span, width)
    grad_query, own_grad, near_grad, middle_grad, far_grad, sib_grad = call(
        backward_kernel,
        [ANY, ANY, VMEM, VMEM, VMEM],
        [
            shape_of(span, width), shape_of(2, span, width, dtype=f32), pair, pair, pair,
            shape_of(3, 2, span, width),
        ],
        (q, grad_mixed, keys, values, probs),
        [
            pltpu.VMEM((span, width), bf16),
            pltpu.VMEM((span, width), bf16),
            pltpu.VMEM((GROUP * span, lanes), bf16),
            pltpu.VMEM((GROUP * span, lanes), bf16),
            pltpu.VMEM((SLOTS * span, GROUP * span), f32),
            pltpu.VMEM((SLOTS * span, GROUP * span), bf16),
            dma((2,)),
        ],
        limit=24, flops=2 * attend_flops, name="backward",
    )

    if windows == 2:
        quarters = (other_window(to_win), swap(to_sib, 1), other_both(to_both))
        far_grad, sib_grad, own_grad, *quarters = lax.optimization_barrier(
            (far_grad, sib_grad, own_grad, *quarters)
        )

    far_home = lax.ppermute(far_grad, "station", back(routes(3)))
    from_sib = swap(sib_grad, 1)
    own_sum, near_sum, middle_sum = call(
        sums_kernel,
        [VMEM, VMEM, VMEM, ANY],
        [shape_of(2, span, width, dtype=f32), pair, pair],
        (own_grad, near_grad, middle_grad, from_sib),
        [pltpu.VMEM((3, 2, span, width), bf16), dma((3,))],
        name="sums",
    )
    near_home = lax.ppermute(near_sum, "station", back(routes(1)))
    middle_home = lax.ppermute(middle_sum, "station", back(routes(2)))

    if windows == 2:
        stride, rows = 2, quarter // 2
        send, part = call(
            functools.partial(weight_kernel, stride),
            [SMEM] + [ANY] * 9,
            [shape_of(rows, width), shape_of(rows, width, dtype=f32)],
            (
                at, mine, *quarters,
                g, *peers, own_grad,
            ),
            [pltpu.VMEM((quarter, 4 * span), bf16), pltpu.VMEM((4 * span, width), bf16), dma((8,))],
            flops=2 * quarter * 4 * span * width, name="weight",
        )
    else:
        stride = 1
        whole = lax.dot_general(mixed, g, NN, preferred_element_type=f32).astype(bf16)
        whole = lax.psum_scatter(whole, "dp", scatter_dimension=0, tiled=True).astype(f32)
        rows = whole.shape[0] // 2
        bit = me % 2
        part = lax.dynamic_slice_in_dim(whole, bit * rows, rows, 0)
        send = lax.dynamic_slice_in_dim(whole, (1 - bit) * rows, rows, 0).astype(bf16)
    first = stride
    got = swap(send, stride)
    halved = [stride]
    stride *= 2
    after = near_sum
    while rows >= 96 and stride < stations:
        rows //= 2
        send, part = call(
            functools.partial(split_kernel, stride),
            [SMEM, VMEM, ANY, ANY],
            [shape_of(rows, width), shape_of(rows, width, dtype=f32)],
            (at, part, got, after),
            [pltpu.VMEM((2 * rows, width), bf16), dma((1,))],
            name="split",
        )
        got = swap(send, stride)
        halved.append(stride)
        stride *= 2

    def add_round(part, got):
        (total,) = call(
            round_kernel,
            [VMEM, ANY, ANY],
            [shape_of(rows, width)],
            (part, got, after),
            [pltpu.VMEM((rows, width), bf16), dma((1,))],
            name="add",
        )
        return total

    total = add_round(part, got)
    while stride < stations:
        total = add_round(total, swap(total, stride))
        stride *= 2
    if first == 2:
        halved.insert(0, 1)
    scale = 1.0 / math.sqrt(span * windows * stations)
    for stride in reversed(halved):
        last = stride == 1
        got = swap(total, stride)
        half = total.shape[0]
        (total,) = call(
            functools.partial(join_kernel, stride, scale if last else None),
            [SMEM, VMEM, ANY, ANY, ANY, ANY],
            [shape_of(2 * half, width, dtype=f32 if last else bf16)],
            (at, total, got, *((near_home, middle_home, far_home) if stride == 2 else (after,) * 3)),
            [pltpu.VMEM((half, width), bf16), dma((1,))],
            name="join",
        )

    layer_output = lax.dot_general(mixed, out_weight, TN, preferred_element_type=f32).astype(bf16)
    grad_key, grad_value = call(
        home_kernel,
        [VMEM, ANY, ANY, ANY],
        [shape_of(span, width)] * 2,
        (own_sum, near_home, middle_home, far_home),
        [pltpu.VMEM((3, 2, span, width), bf16), dma((3,))],
        name="home",
    )
    shape = query_states.shape
    return (
        layer_output.reshape(shape),
        grad_query.reshape(shape),
        grad_key.reshape(shape),
        grad_value.reshape(shape),
        total,
    )


def solution(mesh):
    split = P("dp", "station", None, None)
    return jax.shard_map(
        local,
        mesh=mesh,
        in_specs=(split, split, split, split, P(), P(), P()),
        out_specs=(split, split, split, split, P("dp", None)),
        check_vma=False,
    )
```

```python
import functools
import math

import jax
import jax.numpy as jnp
from jax import lax
from jax.experimental import pallas as pl
from jax.experimental.pallas import tpu as pltpu
from jax.sharding import PartitionSpec as P

HEADS = 12
PMAX = 6
GROUP = 4
SLOTS = PMAX + 1
MIB = 1024 * 1024

neg_big = -1e30
bf16, f32 = jnp.bfloat16, jnp.float32
SMEM = pl.BlockSpec(memory_space=pltpu.SMEM)
VMEM = pl.BlockSpec(memory_space=pltpu.VMEM)
ANY = pl.BlockSpec(memory_space=pl.ANY)
NN = (((1,), (0,)), ((), ()))
NT = (((1,), (1,)), ((), ()))
TN = (((0,), (0,)), ((), ()))


def dot(x, y, dims):
    return lax.dot_general(x, y, dims, preferred_element_type=f32)


def shape_of(*dims, dtype=bf16):
    return jax.ShapeDtypeStruct(dims, dtype)


def skip_refs(kernel, first, count, *refs):
    kernel(*refs[:first], *refs[first + count :])


def call(kernel, ins, outs, args, scratch=(), limit=8, name=None, after=()):
    ins, args = [*ins, *[ANY] * len(after)], (*args, *after)
    if after:
        kernel = functools.partial(skip_refs, kernel, len(args) - len(after), len(after))
    return pl.pallas_call(
        kernel,
        in_specs=ins,
        out_specs=[VMEM] * len(outs),
        out_shape=outs,
        scratch_shapes=list(scratch),
        compiler_params=pltpu.CompilerParams(vmem_limit_bytes=limit * MIB),
        cost_estimate=pl.CostEstimate(flops=1, bytes_accessed=1, transcendentals=0),
        name=name,
    )(*args)


def pack_kernel(k_ref, v_ref, out_ref, sems):
    copies = [
        pltpu.make_async_copy(ref, out_ref.at[n], sems.at[n]) for n, ref in enumerate((k_ref, v_ref))
    ]
    for copy in copies:
        copy.start()
    for copy in copies:
        copy.wait()


def query_kernel(q_ref, g_ref, weight_ref, out_ref):
    out_ref[0] = q_ref[...]
    out_ref[1] = dot(g_ref[...], weight_ref[...], NT).astype(bf16)


def widen(x, wide_ref):
    span, lanes = x.shape
    head_of = lax.broadcasted_iota(jnp.int32, (span, lanes), 1) // (lanes // GROUP)
    zero = jnp.zeros_like(x)
    for h in range(GROUP):
        wide_ref[h * span : (h + 1) * span] = jnp.where(head_of == h, x, zero)


def pick(wide, span, head_width):
    blocks = [
        wide[h * head_width : (h + 1) * head_width, h * span : (h + 1) * span] for h in range(GROUP)
    ]
    return jnp.concatenate(blocks, 0)


def offsets_of(me):
    side = 2 * lax.rem(me, 2) - 1
    return (0, side, 2 * side, 3 * side, -side, -2 * side, -3 * side)


def listed(ids_ref, count_ref, reader, block):
    hit = jnp.int32(0)
    for j in range(PMAX):
        here = jnp.logical_and(ids_ref[reader, j] == block, j < count_ref[reader])
        hit = jnp.maximum(hit, here.astype(jnp.int32))
    return hit


def forward_kernel(
    ids_ref, count_ref, query_ref, own_ref, near_ref, middle_ref, far_ref, sib_ref, sib_near_ref,
    sib_middle_ref,
    mixed_ref, mine_ref, to_win_ref, stats_ref, probs_ref, keys, values,
    q_wide, raw,
    *, station_count,
):
    span, width = query_ref.shape[1:]
    head_width = width // HEADS
    lanes = GROUP * head_width
    me = lax.axis_index("station")
    window = lax.axis_index("dp")
    parts = (own_ref, near_ref, middle_ref, far_ref, sib_ref, sib_near_ref, sib_middle_ref)
    live = []
    for j, offset in enumerate(offsets_of(me)):
        station = lax.rem(me + offset + station_count, station_count)
        live.append(listed(ids_ref, count_ref, me, station) if j else None)
        keys[j * span : (j + 1) * span] = parts[j][0]
        values[j * span : (j + 1) * span] = parts[j][1]
    for group in range(HEADS // GROUP):
        cols = slice(group * lanes, (group + 1) * lanes)
        widen(query_ref[0, :, cols] * bf16(1.0 / math.sqrt(head_width)), q_wide)
        top = None
        for j in range(SLOTS):
            rows = slice(j * span, (j + 1) * span)
            scores = dot(keys[rows, cols], q_wide[...], NT)
            if j:
                scores = jnp.where(live[j] > 0, scores, neg_big)
            raw[rows] = scores
            here = jnp.max(scores, 0, keepdims=True)
            top = here if top is None else jnp.maximum(top, here)
        total = jnp.zeros_like(top)
        for j in range(SLOTS):
            rows = slice(j * span, (j + 1) * span)
            weight = jnp.exp(raw[rows] - top)
            raw[rows] = weight
            total = total + jnp.sum(weight, 0, keepdims=True)
        inverse = 1.0 / total
        for j in range(SLOTS):
            rows = slice(j * span, (j + 1) * span)
            probs_ref[group, rows] = (raw[rows] * inverse).astype(bf16)
        mixed = pick(dot(values[:, cols], probs_ref[group], TN), span, head_width).astype(bf16)
        mixed_ref[cols] = mixed
        product = query_ref[1, :, cols].astype(f32).T * mixed.astype(f32)
        log_sum = top + jnp.log(total)
        for h in range(GROUP):
            head = group * GROUP + h
            stats_ref[head : head + 1] = log_sum[:, h * span : (h + 1) * span]
            stats_ref[HEADS + head : HEADS + head + 1] = jnp.sum(
                product[h * head_width : (h + 1) * head_width], 0, keepdims=True
            )
    half = mine_ref.shape[0]
    for ref, w in ((mine_ref, window), (to_win_ref, 1 - window)):
        start = pl.multiple_of(lax.rem(w, 2) * half, half)
        ref[...] = mixed_ref[pl.ds(start, half)]


def query_grad_kernel(query_ref, stats_ref, keys, values, probs_ref, dq_ref, g_wide, grads_half):
    span, width = query_ref.shape[1:]
    head_width = width // HEADS
    lanes = GROUP * head_width
    scale = 1.0 / math.sqrt(head_width)
    for group in range(HEADS // GROUP):
        cols = slice(group * lanes, (group + 1) * lanes)
        widen(query_ref[1, :, cols], g_wide)
        first = HEADS + group * GROUP
        delta = jnp.concatenate([stats_ref[first + h : first + h + 1] for h in range(GROUP)], 1)
        for j in range(SLOTS):
            rows = slice(j * span, (j + 1) * span)
            back = dot(values[rows, cols], g_wide[...], NT)
            grads_half[rows] = (probs_ref[group, rows].astype(f32) * (back - delta)).astype(bf16)
        wide = dot(keys[:, cols], grads_half[...], TN)
        dq_ref[:, cols] = (pick(wide, span, head_width).T * scale).astype(bf16)


def key_grad_kernel(
    ids_ref, count_ref, stats_ref, kv_ref, own_ref, near_ref, middle_ref, far_ref, sib_ref,
    sib_near_ref, sib_middle_ref,
    dk_ref, dv_ref,
    queries, grads, k_wide, v_wide, stats, probs_half, grads_half,
    *, station_count,
):
    span, width = kv_ref.shape[1:]
    head_width = width // HEADS
    lanes = GROUP * head_width
    scale = 1.0 / math.sqrt(head_width)
    me = lax.axis_index("station")
    parts = (own_ref, near_ref, middle_ref, far_ref, sib_ref, sib_near_ref, sib_middle_ref)
    live = []
    for j, offset in enumerate(offsets_of(me)):
        station = lax.rem(me + offset + station_count, station_count)
        live.append(listed(ids_ref, count_ref, station, me) if j else None)
        queries[j * span : (j + 1) * span] = parts[j][0]
        grads[j * span : (j + 1) * span] = parts[j][1]
        stats[j] = stats_ref[station].T
    for group in range(HEADS // GROUP):
        cols = slice(group * lanes, (group + 1) * lanes)
        widen(kv_ref[0, :, cols] * bf16(scale), k_wide)
        widen(kv_ref[1, :, cols], v_wide)
        for j in range(SLOTS):
            rows = slice(j * span, (j + 1) * span)
            scores = dot(queries[rows, cols], k_wide[...], NT)
            back = dot(grads[rows, cols], v_wide[...], NT)
            for h in range(GROUP):
                head = group * GROUP + h
                at = slice(h * span, (h + 1) * span)
                prob = jnp.exp(scores[:, at] - stats[j, :, head : head + 1])
                if j:
                    prob = jnp.where(live[j] > 0, prob, 0.0)
                probs_half[rows, at] = prob.astype(bf16)
                delta = stats[j, :, HEADS + head : HEADS + head + 1]
                grads_half[rows, at] = (prob * (back[:, at] - delta)).astype(bf16)
        wide = dot(queries[:, cols], grads_half[...], TN)
        dk_ref[:, cols] = (pick(wide, span, head_width).T * scale).astype(bf16)
        wide = dot(grads[:, cols], probs_half[...], TN)
        dv_ref[:, cols] = pick(wide, span, head_width).T.astype(bf16)


def sides(stride, half):
    bit = lax.rem(lax.axis_index("station") // stride, 2)
    send = pl.ds(pl.multiple_of((1 - bit) * half, half), half)
    keep = pl.ds(pl.multiple_of(bit * half, half), half)
    return send, keep


def weight_kernel(stride, mine_ref, win_ref, g_ref, g_win_ref, send_ref, keep_ref, left, right):
    span = mine_ref.shape[1]
    send, keep = sides(stride, send_ref.shape[0])
    left[:, :span] = mine_ref[...]
    left[:, span:] = win_ref[...]
    right[:span] = g_ref[...]
    right[span:] = g_win_ref[...]
    send_ref[...] = dot(left[send], right[...], NN).astype(bf16)
    keep_ref[...] = dot(left[keep], right[...], NN)


def split_kernel(stride, part_ref, got_ref, send_ref, keep_ref):
    send, keep = sides(stride, send_ref.shape[0])
    send_ref[...] = (part_ref[send] + got_ref[send].astype(f32)).astype(bf16)
    keep_ref[...] = part_ref[keep] + got_ref[keep].astype(f32)


def round_kernel(part_ref, got_ref, out_ref):
    out_ref[...] = (part_ref[...].astype(f32) + got_ref[...].astype(f32)).astype(bf16)


def join_kernel(stride, scale, mine_ref, got_ref, out_ref):
    other, here = sides(stride, mine_ref.shape[0])
    for place, ref in ((here, mine_ref), (other, got_ref)):
        value = ref[...]
        if scale is not None:
            value = value.astype(f32) * scale
        out_ref[place] = value


def local(
    query_states, key_states, value_states, grad_output, out_weight, partner_ids, partner_count
):
    span, width = query_states.shape[2:]
    stations = lax.axis_size("station")
    windows = lax.axis_size("dp")
    me = lax.axis_index("station").astype(jnp.int32)
    side = [1 if s % 2 else -1 for s in range(stations)]

    def routes(steps):
        return [((s + steps * side[s]) % stations, s) for s in range(stations)]

    def swap(value, stride):
        return lax.ppermute(value, "station", [(s ^ stride, s) for s in range(stations)])

    def other_window(value):
        return lax.ppermute(value, "dp", [(0, 1), (1, 0)])

    def flat(x):
        return x.reshape(span, width)

    q, k, v, g = flat(query_states), flat(key_states), flat(value_states), flat(grad_output)
    dma = pltpu.SemaphoreType.DMA
    pair = shape_of(2, span, width)
    (kv,) = call(pack_kernel, [ANY, ANY], [pair], (k, v), [dma((2,))], limit=56, name="pack")

    def spread(value):
        near, middle, far = (lax.ppermute(value, "station", routes(n)) for n in (1, 2, 3))
        return value, near, middle, far, swap(value, 1), swap(near, 1), swap(middle, 1)

    kv_all = spread(kv)
    g_win = other_window(g) if windows == 2 else g
    (qg,) = call(query_kernel, [VMEM] * 3, [pair], (q, g, out_weight), name="queries")
    qg_all = spread(qg)

    lanes = width // HEADS * GROUP
    groups = HEADS // GROUP
    half = width // 2
    half_shape = shape_of(half, span)
    mixed, mine, to_win, stats, probs, keys, values = call(
        functools.partial(forward_kernel, station_count=stations),
        [SMEM] * 2 + [VMEM] * 8,
        [
            shape_of(width, span), half_shape, half_shape,
            shape_of(2 * HEADS, span, dtype=f32),
            shape_of(groups, SLOTS * span, GROUP * span),
            shape_of(SLOTS * span, width),
            shape_of(SLOTS * span, width),
        ],
        (partner_ids, partner_count, qg, *kv_all),
        [pltpu.VMEM((GROUP * span, lanes), bf16), pltpu.VMEM((SLOTS * span, GROUP * span), f32)],
        limit=20, name="forward",
    )
    all_stats = lax.all_gather(stats, "station", axis=0)
    (grad_query,) = call(
        query_grad_kernel,
        [VMEM] * 5,
        [shape_of(span, width)],
        (qg, stats, keys, values, probs),
        [pltpu.VMEM((GROUP * span, lanes), bf16), pltpu.VMEM((SLOTS * span, GROUP * span), bf16)],
        limit=20, name="query_grad",
    )

    grad_key, grad_value = call(
        functools.partial(key_grad_kernel, station_count=stations),
        [SMEM] * 2 + [VMEM] * 9,
        [shape_of(span, width)] * 2,
        (partner_ids, partner_count, all_stats, kv, *qg_all),
        [
            pltpu.VMEM((SLOTS * span, width), bf16),
            pltpu.VMEM((SLOTS * span, width), bf16),
            pltpu.VMEM((GROUP * span, lanes), bf16),
            pltpu.VMEM((GROUP * span, lanes), bf16),
            pltpu.VMEM((SLOTS, span, 2 * HEADS), f32),
            pltpu.VMEM((SLOTS * span, GROUP * span), bf16),
            pltpu.VMEM((SLOTS * span, GROUP * span), bf16),
        ],
        limit=20, name="key_grad",
    )

    if windows == 2:
        rows = half // 2
        send, part = call(
            functools.partial(weight_kernel, 1),
            [VMEM] * 4,
            [shape_of(rows, width), shape_of(rows, width, dtype=f32)],
            (mine, other_window(to_win), g, g_win),
            [pltpu.VMEM((half, 2 * span), bf16), pltpu.VMEM((2 * span, width), bf16)],
            name="weight", after=(grad_query, *qg_all[1:3]),
        )
    else:
        whole = lax.dot_general(mixed, g, NN, preferred_element_type=f32).astype(bf16)
        whole = lax.psum_scatter(whole, "dp", scatter_dimension=0, tiled=True).astype(f32)
        rows = whole.shape[0] // 2
        bit = me % 2
        part = lax.dynamic_slice_in_dim(whole, bit * rows, rows, 0)
        send = lax.dynamic_slice_in_dim(whole, (1 - bit) * rows, rows, 0).astype(bf16)
    got = swap(send, 1)
    halved = [1]
    stride = 2
    while rows >= 96 and stride < stations:
        rows //= 2
        send, part = call(
            functools.partial(split_kernel, stride),
            [VMEM, VMEM],
            [shape_of(rows, width), shape_of(rows, width, dtype=f32)],
            (part, got),
            name="split", after=qg_all[3:4] if stride == 4 else (),
        )
        got = swap(send, stride)
        halved.append(stride)
        stride *= 2

    def add_round(part, got, after=()):
        out = [shape_of(rows, width)]
        return call(round_kernel, [VMEM, VMEM], out, (part, got), name="add", after=after)[0]

    total = add_round(part, got, (all_stats,))
    while stride < stations:
        total = add_round(total, swap(total, stride))
        stride *= 2
    scale = 1.0 / math.sqrt(span * windows * stations)
    for stride in reversed(halved):
        last = stride == 1
        (total,) = call(
            functools.partial(join_kernel, stride, scale if last else None),
            [VMEM, VMEM],
            [shape_of(2 * total.shape[0], width, dtype=f32 if last else bf16)],
            (total, swap(total, stride)),
            name="join", after=(grad_key,) if stride == 2 else (),
        )

    layer_output = lax.dot_general(mixed, out_weight, TN, preferred_element_type=f32).astype(bf16)
    shape = query_states.shape
    return (
        layer_output.reshape(shape),
        grad_query.reshape(shape),
        grad_key.reshape(shape),
        grad_value.reshape(shape),
        total,
    )


def solution(mesh):
    split = P("dp", "station", None, None)
    return jax.shard_map(
        local,
        mesh=mesh,
        in_specs=(split, split, split, split, P(), P(), P()),
        out_specs=(split, split, split, split, P("dp", None)),
        check_vma=False,
    )
```

```python
import functools
import math

import jax
import jax.numpy as jnp
from jax import lax
from jax.experimental import pallas as pl
from jax.experimental.pallas import tpu as pltpu
from jax.sharding import PartitionSpec as P

HEADS = 12
PMAX = 6
GROUP = 4
SLOTS = PMAX + 1
MIB = 1024 * 1024

neg_big = -1e30
bf16, f32 = jnp.bfloat16, jnp.float32
SMEM = pl.BlockSpec(memory_space=pltpu.SMEM)
VMEM = pl.BlockSpec(memory_space=pltpu.VMEM)
ANY = pl.BlockSpec(memory_space=pl.ANY)
NN = (((1,), (0,)), ((), ()))
NT = (((1,), (1,)), ((), ()))
TN = (((0,), (0,)), ((), ()))


def dot(x, y, dims):
    return lax.dot_general(x, y, dims, preferred_element_type=f32)


def shape_of(*dims, dtype=bf16):
    return jax.ShapeDtypeStruct(dims, dtype)


def skip_refs(kernel, first, count, *refs):
    kernel(*refs[:first], *refs[first + count :])


def call(kernel, ins, outs, args, scratch=(), limit=8, name=None, after=(), place=None, alias={}):
    ins, args = [*ins, *[ANY] * len(after)], (*args, *after)
    if after:
        kernel = functools.partial(skip_refs, kernel, len(args) - len(after), len(after))
    return pl.pallas_call(
        kernel,
        in_specs=ins,
        out_specs=place or [VMEM] * len(outs),
        input_output_aliases=alias,
        out_shape=outs,
        scratch_shapes=list(scratch),
        compiler_params=pltpu.CompilerParams(vmem_limit_bytes=limit * MIB),
        cost_estimate=pl.CostEstimate(flops=1, bytes_accessed=1, transcendentals=0),
        name=name,
    )(*args)


def pack_kernel(k_ref, v_ref, out_ref, sems):
    copies = [
        pltpu.make_async_copy(ref, out_ref.at[n], sems.at[n]) for n, ref in enumerate((k_ref, v_ref))
    ]
    for copy in copies:
        copy.start()
    for copy in copies:
        copy.wait()


def query_kernel(q_ref, g_ref, weight_ref, out_ref, copy_ref):
    copy_ref[...] = g_ref[...]
    out_ref[0] = q_ref[...]
    out_ref[1] = dot(g_ref[...], weight_ref[...], NT).astype(bf16)


def widen(x, wide_ref):
    span, lanes = x.shape
    head_of = lax.broadcasted_iota(jnp.int32, (span, lanes), 1) // (lanes // GROUP)
    zero = jnp.zeros_like(x)
    for h in range(GROUP):
        wide_ref[h * span : (h + 1) * span] = jnp.where(head_of == h, x, zero)


def pick(wide, span, head_width):
    blocks = [
        wide[h * head_width : (h + 1) * head_width, h * span : (h + 1) * span] for h in range(GROUP)
    ]
    return jnp.concatenate(blocks, 0)


def offsets_of(me):
    side = 2 * lax.rem(me, 2) - 1
    return (0, side, 2 * side, 3 * side, -side, -2 * side, -3 * side)


def listed(ids_ref, count_ref, reader, block):
    hit = jnp.int32(0)
    for j in range(PMAX):
        here = jnp.logical_and(ids_ref[reader, j] == block, j < count_ref[reader])
        hit = jnp.maximum(hit, here.astype(jnp.int32))
    return hit


def forward_kernel(
    ids_ref, count_ref, query_ref, own_ref, near_ref, middle_ref, far_ref, sib_ref, sib_near_ref,
    sib_middle_ref,
    mixed_ref, mine_ref, to_win_ref, stats_ref, dead_ref, probs_ref, keys, values,
    q_wide, raw,
    *, station_count,
):
    span, width = query_ref.shape[1:]
    head_width = width // HEADS
    lanes = GROUP * head_width
    me = lax.axis_index("station")
    window = lax.axis_index("dp")
    parts = (own_ref, near_ref, middle_ref, far_ref, sib_ref, sib_near_ref, sib_middle_ref)
    live = []
    for j, offset in enumerate(offsets_of(me)):
        station = lax.rem(me + offset + station_count, station_count)
        live.append(listed(ids_ref, count_ref, me, station) if j else None)
        reads = listed(ids_ref, count_ref, station, me) if j else jnp.int32(1)
        dead_ref[j : j + 1] = jnp.where(reads > 0, 0.0, -neg_big) * jnp.ones((1, span), f32)
        keys[j * span : (j + 1) * span] = parts[j][0]
        values[j * span : (j + 1) * span] = parts[j][1]
    for group in range(HEADS // GROUP):
        cols = slice(group * lanes, (group + 1) * lanes)
        widen(query_ref[0, :, cols] * bf16(1.0 / math.sqrt(head_width)), q_wide)
        top = None
        for j in range(SLOTS):
            rows = slice(j * span, (j + 1) * span)
            scores = dot(keys[rows, cols], q_wide[...], NT)
            if j:
                scores = jnp.where(live[j] > 0, scores, neg_big)
            raw[rows] = scores
            here = jnp.max(scores, 0, keepdims=True)
            top = here if top is None else jnp.maximum(top, here)
        total = jnp.zeros_like(top)
        for j in range(SLOTS):
            rows = slice(j * span, (j + 1) * span)
            weight = jnp.exp(raw[rows] - top)
            raw[rows] = weight
            total = total + jnp.sum(weight, 0, keepdims=True)
        inverse = 1.0 / total
        for j in range(SLOTS):
            rows = slice(j * span, (j + 1) * span)
            probs_ref[group, rows] = (raw[rows] * inverse).astype(bf16)
        mixed = pick(dot(values[:, cols], probs_ref[group], TN), span, head_width).astype(bf16)
        mixed_ref[cols] = mixed
        product = query_ref[1, :, cols].astype(f32).T * mixed.astype(f32)
        log_sum = top + jnp.log(total)
        for h in range(GROUP):
            head = group * GROUP + h
            stats_ref[head : head + 1] = log_sum[:, h * span : (h + 1) * span]
            stats_ref[HEADS + head : HEADS + head + 1] = jnp.sum(
                product[h * head_width : (h + 1) * head_width], 0, keepdims=True
            )
    half = mine_ref.shape[0]
    for ref, w in ((mine_ref, window), (to_win_ref, 1 - window)):
        start = pl.multiple_of(lax.rem(w, 2) * half, half)
        ref[...] = mixed_ref[pl.ds(start, half)]


def query_grad_kernel(
    query_ref, stats_ref, keys, values, probs_ref, dq_ref, token_ref, g_wide, grads_half
):
    token_ref[...] = jnp.zeros_like(token_ref)
    span, width = query_ref.shape[1:]
    head_width = width // HEADS
    lanes = GROUP * head_width
    scale = 1.0 / math.sqrt(head_width)
    for group in range(HEADS // GROUP):
        cols = slice(group * lanes, (group + 1) * lanes)
        widen(query_ref[1, :, cols], g_wide)
        first = HEADS + group * GROUP
        delta = jnp.concatenate([stats_ref[first + h : first + h + 1] for h in range(GROUP)], 1)
        for j in range(SLOTS):
            rows = slice(j * span, (j + 1) * span)
            back = dot(values[rows, cols], g_wide[...], NT)
            grads_half[rows] = (probs_ref[group, rows].astype(f32) * (back - delta)).astype(bf16)
        wide = dot(keys[:, cols], grads_half[...], TN)
        dq_ref[:, cols] = (pick(wide, span, head_width).T * scale).astype(bf16)


def key_grad_kernel(group, kv_ref, dead_ref, *refs):
    queries_in, stats_in, refs = refs[:SLOTS], refs[SLOTS : 2 * SLOTS], refs[2 * SLOTS :]
    if group:
        refs = refs[2:]
    dk_ref, dv_ref, token_ref, queries, grads, k_wide, v_wide, stats, probs_half, grads_half, out, sems = refs
    span, width = kv_ref.shape[1:]
    head_width = width // HEADS
    lanes = GROUP * head_width
    scale = 1.0 / math.sqrt(head_width)
    cols = slice(group * lanes, (group + 1) * lanes)
    widen(kv_ref[0, :, cols] * bf16(scale), k_wide)
    widen(kv_ref[1, :, cols], v_wide)
    for j in range(SLOTS):
        rows = slice(j * span, (j + 1) * span)
        queries[rows] = queries_in[j][0, :, cols]
        grads[rows] = queries_in[j][1, :, cols]
        stats[j, :HEADS] = stats_in[j][:HEADS] + dead_ref[j : j + 1]
        stats[j, HEADS:] = stats_in[j][HEADS:]
        columns = stats[j].T
        scores = dot(queries[rows], k_wide[...], NT)
        back = dot(grads[rows], v_wide[...], NT)
        for h in range(GROUP):
            head = group * GROUP + h
            at = slice(h * span, (h + 1) * span)
            prob = jnp.exp(scores[:, at] - columns[:, head : head + 1])
            probs_half[rows, at] = prob.astype(bf16)
            delta = columns[:, HEADS + head : HEADS + head + 1]
            grads_half[rows, at] = (prob * (back[:, at] - delta)).astype(bf16)
    wide = dot(queries[...], grads_half[...], TN)
    out[0] = (pick(wide, span, head_width).T * scale).astype(bf16)
    wide = dot(grads[...], probs_half[...], TN)
    out[1] = pick(wide, span, head_width).T.astype(bf16)
    copies = [
        pltpu.make_async_copy(out.at[n], ref.at[:, cols], sems.at[n])
        for n, ref in enumerate((dk_ref, dv_ref))
    ]
    for copy in copies:
        copy.start()
    token_ref[...] = jnp.zeros_like(token_ref)
    for copy in copies:
        copy.wait()


def sides(stride, half):
    bit = lax.rem(lax.axis_index("station") // stride, 2)
    send = pl.ds(pl.multiple_of((1 - bit) * half, half), half)
    keep = pl.ds(pl.multiple_of(bit * half, half), half)
    return send, keep


def weight_kernel(stride, mine_ref, win_ref, g_ref, g_win_ref, send_ref, keep_ref, left, right):
    span = mine_ref.shape[1]
    send, keep = sides(stride, send_ref.shape[0])
    left[:, :span] = mine_ref[...]
    left[:, span:] = win_ref[...]
    right[:span] = g_ref[...]
    right[span:] = g_win_ref[...]
    send_ref[...] = dot(left[send], right[...], NN).astype(bf16)
    keep_ref[...] = dot(left[keep], right[...], NN)


def split_kernel(stride, part_ref, got_ref, send_ref, keep_ref):
    send, keep = sides(stride, send_ref.shape[0])
    send_ref[...] = (part_ref[send] + got_ref[send].astype(f32)).astype(bf16)
    keep_ref[...] = part_ref[keep] + got_ref[keep].astype(f32)


def round_kernel(part_ref, got_ref, out_ref):
    out_ref[...] = (part_ref[...].astype(f32) + got_ref[...].astype(f32)).astype(bf16)


def join_kernel(stride, scale, mine_ref, got_ref, out_ref):
    other, here = sides(stride, mine_ref.shape[0])
    for place, ref in ((here, mine_ref), (other, got_ref)):
        value = ref[...]
        if scale is not None:
            value = value.astype(f32) * scale
        out_ref[place] = value


def local(
    query_states, key_states, value_states, grad_output, out_weight, partner_ids, partner_count
):
    span, width = query_states.shape[2:]
    stations = lax.axis_size("station")
    windows = lax.axis_size("dp")
    me = lax.axis_index("station").astype(jnp.int32)
    side = [1 if s % 2 else -1 for s in range(stations)]

    def routes(steps):
        return [((s + steps * side[s]) % stations, s) for s in range(stations)]

    def swap(value, stride):
        return lax.ppermute(value, "station", [(s ^ stride, s) for s in range(stations)])

    def other_window(value):
        return lax.ppermute(value, "dp", [(0, 1), (1, 0)])

    def flat(x):
        return x.reshape(span, width)

    q, k, v, g = flat(query_states), flat(key_states), flat(value_states), flat(grad_output)
    dma = pltpu.SemaphoreType.DMA
    pair = shape_of(2, span, width)
    (kv,) = call(pack_kernel, [ANY, ANY], [pair], (k, v), [dma((2,))], limit=56, name="pack")

    def to_reach(value):
        return [lax.ppermute(value, "station", routes(n)) for n in (1, 2, 3)]

    def spread(value):
        near, middle, far = to_reach(value)
        return value, near, middle, far, swap(value, 1), swap(near, 1), swap(middle, 1)

    near, middle, far = to_reach(kv)
    sib = swap(kv, 1)
    g_win = other_window(g) if windows == 2 else g
    qg, g_near = call(
        query_kernel, [VMEM] * 3, [pair, shape_of(span, width)], (q, g, out_weight), name="queries"
    )
    near, qg_later = lax.optimization_barrier((near, qg))
    kv_all = kv, near, middle, far, sib, swap(near, 1), swap(middle, 1)
    qg_all = spread(qg_later)

    lanes = width // HEADS * GROUP
    groups = HEADS // GROUP
    half = width // 2
    half_shape = shape_of(half, span)
    token_shape = shape_of(8, 128, dtype=f32)
    mixed, mine, to_win, stats, dead, probs, keys, values = call(
        functools.partial(forward_kernel, station_count=stations),
        [SMEM] * 2 + [VMEM] * 8,
        [
            shape_of(width, span), half_shape, half_shape,
            shape_of(2 * HEADS, span, dtype=f32),
            shape_of(SLOTS, span, dtype=f32),
            shape_of(groups, SLOTS * span, GROUP * span),
            shape_of(SLOTS * span, width),
            shape_of(SLOTS * span, width),
        ],
        (partner_ids, partner_count, qg, *kv_all),
        [pltpu.VMEM((GROUP * span, lanes), bf16), pltpu.VMEM((SLOTS * span, GROUP * span), f32)],
        limit=20, name="forward",
    )
    stats_in = spread(stats)
    grad_query, query_token = call(
        query_grad_kernel,
        [VMEM] * 5,
        [shape_of(span, width), token_shape],
        (qg, stats, keys, values, probs),
        [pltpu.VMEM((GROUP * span, lanes), bf16), pltpu.VMEM((SLOTS * span, GROUP * span), bf16)],
        limit=20, name="query_grad",
    )

    grads_out, key_grads = (), []
    for group in range(groups):
        *grads_out, token = call(
            functools.partial(key_grad_kernel, group),
            [VMEM] * (2 + 2 * SLOTS) + [ANY] * len(grads_out),
            [shape_of(span, width)] * 2 + [token_shape],
            (kv, dead, *qg_all, *stats_in, *grads_out),
            [
                pltpu.VMEM((SLOTS * span, lanes), bf16),
                pltpu.VMEM((SLOTS * span, lanes), bf16),
                pltpu.VMEM((GROUP * span, lanes), bf16),
                pltpu.VMEM((GROUP * span, lanes), bf16),
                pltpu.VMEM((SLOTS, 2 * HEADS, span), f32),
                pltpu.VMEM((SLOTS * span, GROUP * span), bf16),
                pltpu.VMEM((SLOTS * span, GROUP * span), bf16),
                pltpu.VMEM((2, span, lanes), bf16),
                dma((2,)),
            ],
            limit=20, name="key_grad", place=[ANY, ANY, VMEM],
            alias={2 + 2 * SLOTS + n: n for n in range(len(grads_out))},
        )
        key_grads.append(token)
    grad_key, grad_value = grads_out

    layer_output = lax.dot_general(mixed, out_weight, TN, preferred_element_type=f32).astype(bf16)

    if windows == 2:
        rows = half // 2
        send, part = call(
            functools.partial(weight_kernel, 1),
            [VMEM] * 4,
            [shape_of(rows, width), shape_of(rows, width, dtype=f32)],
            (mine, other_window(to_win), g_near, g_win),
            [pltpu.VMEM((half, 2 * span), bf16), pltpu.VMEM((2 * span, width), bf16)],
            name="weight", after=(query_token, *qg_all[1:3]),
        )
    else:
        whole = lax.dot_general(mixed, g, NN, preferred_element_type=f32).astype(bf16)
        whole = lax.psum_scatter(whole, "dp", scatter_dimension=0, tiled=True).astype(f32)
        rows = whole.shape[0] // 2
        bit = me % 2
        part = lax.dynamic_slice_in_dim(whole, bit * rows, rows, 0)
        send = lax.dynamic_slice_in_dim(whole, (1 - bit) * rows, rows, 0).astype(bf16)
    got = swap(send, 1)
    halved = [1]
    stride = 2
    while rows >= 96 and stride < stations:
        rows //= 2
        send, part = call(
            functools.partial(split_kernel, stride),
            [VMEM, VMEM],
            [shape_of(rows, width), shape_of(rows, width, dtype=f32)],
            (part, got),
            name="split", after={2: stats_in[1::3], 4: (stats_in[2], qg_all[3])}.get(stride, ()),
        )
        got = swap(send, stride)
        halved.append(stride)
        stride *= 2

    def add_round(part, got, after=()):
        out = [shape_of(rows, width)]
        return call(round_kernel, [VMEM, VMEM], out, (part, got), name="add", after=after)[0]

    total = add_round(part, got, stats_in[3:6:2])
    while stride < stations:
        total = add_round(total, swap(total, stride), key_grads[:1])
        stride *= 2
    scale = 1.0 / math.sqrt(span * windows * stations)
    for stride in reversed(halved):
        last = stride == 1
        (total,) = call(
            functools.partial(join_kernel, stride, scale if last else None),
            [VMEM, VMEM],
            [shape_of(2 * total.shape[0], width, dtype=f32 if last else bf16)],
            (total, swap(total, stride)),
            name="join", after={4: key_grads[1:2], 2: key_grads[2:], 1: [layer_output]}.get(stride, ()),
        )

    shape = query_states.shape
    return (
        layer_output.reshape(shape),
        grad_query.reshape(shape),
        grad_key.reshape(shape),
        grad_value.reshape(shape),
        total,
    )


def solution(mesh):
    split = P("dp", "station", None, None)
    return jax.shard_map(
        local,
        mesh=mesh,
        in_specs=(split, split, split, split, P(), P(), P()),
        out_specs=(split, split, split, split, P("dp", None)),
        check_vma=False,
    )
```

```python
import functools
import math

import jax
import jax.numpy as jnp
from jax import lax
from jax.experimental import pallas as pl
from jax.experimental.pallas import tpu as pltpu
from jax.sharding import PartitionSpec as P

HEADS = 12
PMAX = 6
HOPS = 3
LAYER = 4
LOCAL = HEADS // LAYER
BLOCKS = LAYER + 2 * HOPS
SLOTS = 2 * HOPS + 1
MIB = 1024 * 1024

neg_big = -1e30
bf16, f32 = jnp.bfloat16, jnp.float32
SMEM = pl.BlockSpec(memory_space=pltpu.SMEM)
VMEM = pl.BlockSpec(memory_space=pltpu.VMEM)
ANY = pl.BlockSpec(memory_space=pl.ANY)
HBM = pl.BlockSpec(memory_space=pltpu.HBM)
NN = (((1,), (0,)), ((), ()))
NT = (((1,), (1,)), ((), ()))
TN = (((0,), (0,)), ((), ()))


def dot(x, y, dims):
    return lax.dot_general(x, y, dims, preferred_element_type=f32)


def shape_of(*dims, dtype=bf16):
    return jax.ShapeDtypeStruct(dims, dtype)


TOKEN = shape_of(8, 128, dtype=f32)


def skip_refs(kernel, first, count, *refs):
    kernel(*refs[:first], *refs[first + count :])


def call(kernel, ins, outs, args, scratch=(), limit=8, name=None, after=()):
    ins, args = [*ins, *[ANY] * len(after)], (*args, *after)
    if after:
        kernel = functools.partial(skip_refs, kernel, len(args) - len(after), len(after))
    return pl.pallas_call(
        kernel,
        in_specs=ins,
        out_specs=[VMEM] * len(outs),
        out_shape=outs,
        scratch_shapes=list(scratch),
        compiler_params=pltpu.CompilerParams(vmem_limit_bytes=limit * MIB),
        cost_estimate=pl.CostEstimate(flops=1, bytes_accessed=1, transcendentals=0),
        name=name,
    )(*args)


def place(peer, size):
    position = jnp.bitwise_xor(lax.rem(lax.axis_index("station"), LAYER), peer)
    return pl.ds(pl.multiple_of(position * size, size), size)


def block(j, span):
    return slice(j * span, (j + 1) * span)


def readers(j):
    return max(0, j - 2 * HOPS), min(LAYER - 1, j)


def pack_kernel(k_ref, v_ref, q_ref, *refs):
    outs, (natural, flipped, sems) = refs[:LAYER], refs[LAYER:]
    rows = outs[0].shape[1]
    copies = [
        pltpu.make_async_copy(ref, natural.at[n], sems.at[n])
        for n, ref in enumerate((k_ref, v_ref, q_ref))
    ]
    for copy in copies:
        copy.start()
    scale = 1.0 / math.sqrt(flipped.shape[1] // HEADS)
    for n, copy in enumerate(copies):
        copy.wait()
        value = natural[n].T
        flipped[n] = value * bf16(scale) if n == 2 else value
    for peer, out in enumerate(outs):
        out[...] = flipped[:, place(peer, rows)]


def gather_kernel(*refs):
    ins, (up_ref, down_ref, pair_ref, query_ref) = refs[:LAYER], refs[LAYER:]
    span = ins[0].shape[2]
    for peer, ref in enumerate(ins):
        at = place(peer, span)
        pair_ref[0, :, at] = ref[0]
        pair_ref[1, :, at] = ref[1]
        query_ref[:, at] = ref[2]
    up_ref[...] = pair_ref[:, :, span:]
    down_ref[...] = pair_ref[:, :, : HOPS * span]


def project_kernel(
    station_count, ids_ref, count_ref, *refs
):
    ins, refs = refs[:LAYER], refs[LAYER:]
    weight_ref, query_ref, all_ref, grad_ref, up_ref, down_ref, bias_ref, dead_ref = refs
    span = ins[0].shape[0]
    rows = query_ref.shape[0]
    for peer, ref in enumerate(ins):
        all_ref[place(peer, span)] = ref[...]
    grad_ref[...] = dot(weight_ref[place(0, rows)], all_ref[...], NT).astype(bf16)
    for n, ref in enumerate((query_ref, grad_ref)):
        up_ref[n] = ref[:, span:]
        down_ref[n] = ref[:, : HOPS * span]
    first = lax.axis_index("station") // LAYER * LAYER
    ones = jnp.ones((1, span), f32)

    def listed(reader, other):
        hit = jnp.int32(0)
        for j in range(PMAX):
            here = jnp.logical_and(ids_ref[reader, j] == other, j < count_ref[reader])
            hit = jnp.maximum(hit, here.astype(jnp.int32))
        return hit > 0

    for j in range(BLOCKS):
        outer = lax.rem(first + (j - HOPS) + station_count, station_count)
        low, high = readers(j)
        for i in range(low, high + 1):
            inner = first + i
            slot = j - i
            if slot == HOPS:
                bias_ref[j : j + 1, block(i, span)] = 0.0 * ones
                dead_ref[i : i + 1, block(slot, span)] = 0.0 * ones
            else:
                reads = jnp.where(listed(inner, outer), 0.0, neg_big)
                bias_ref[j : j + 1, block(i, span)] = reads * ones
                read_by = jnp.where(listed(outer, inner), 0.0, -neg_big)
                dead_ref[i : i + 1, block(slot, span)] = read_by * ones


def clear(ref, span):
    for j in range(BLOCKS):
        low, high = readers(j)
        for i in range(LAYER):
            if not low <= i <= high:
                ref[block(j, span), block(i, span)] = jnp.zeros((span, span), bf16)


def forward_kernel(
    pair_ref, low_ref, high_ref, query_ref, grad_ref, bias_ref,
    mixed_ref, stats_ref, stats_up, stats_down, probs_ref, window_ref,
    raw,
):
    rows = query_ref.shape[0]
    span = query_ref.shape[1] // LAYER
    head_width = rows // LOCAL
    reach = HOPS * span
    window_ref[:, :, :reach] = low_ref[...]
    window_ref[:, :, reach : reach + LAYER * span] = pair_ref[...]
    window_ref[:, :, reach + LAYER * span :] = high_ref[...]
    for head in range(LOCAL):
        clear(probs_ref.at[head], span)
        at = block(head, head_width)
        query = query_ref[at]
        tops = [None] * LAYER
        for j in range(BLOCKS):
            low, high = readers(j)
            cols = slice(low * span, (high + 1) * span)
            scores = dot(window_ref[0, at, block(j, span)], query[:, cols], TN)
            scores = scores + bias_ref[j : j + 1, cols]
            raw[block(j, span), cols] = scores
            here = jnp.max(scores, 0, keepdims=True)
            for i in range(low, high + 1):
                mine = here[:, block(i - low, span)]
                tops[i] = mine if tops[i] is None else jnp.maximum(tops[i], mine)
        top = jnp.concatenate(tops, 1)
        totals = [jnp.zeros((1, span), f32)] * LAYER
        for j in range(BLOCKS):
            low, high = readers(j)
            cols = slice(low * span, (high + 1) * span)
            weight = jnp.exp(raw[block(j, span), cols] - top[:, cols])
            raw[block(j, span), cols] = weight
            here = jnp.sum(weight, 0, keepdims=True)
            for i in range(low, high + 1):
                totals[i] = totals[i] + here[:, block(i - low, span)]
        total = jnp.concatenate(totals, 1)
        inverse = 1.0 / total
        for j in range(BLOCKS):
            low, high = readers(j)
            cols = slice(low * span, (high + 1) * span)
            probs_ref[head, block(j, span), cols] = (
                raw[block(j, span), cols] * inverse[:, cols]
            ).astype(bf16)
        mixed = dot(window_ref[1, at], probs_ref[head], NN).astype(bf16)
        mixed_ref[at] = mixed
        product = grad_ref[at].astype(f32) * mixed.astype(f32)
        stats_ref[head : head + 1] = top + jnp.log(total)
        stats_ref[LOCAL + head : LOCAL + head + 1] = jnp.sum(product, 0, keepdims=True)
    stats_ref[2 * LOCAL :] = jnp.zeros((8 - 2 * LOCAL, LAYER * span), f32)
    stats_up[...] = stats_ref[:, span:]
    stats_down[...] = stats_ref[:, :reach]


def query_grad_kernel(window_ref, probs_ref, grad_ref, stats_ref, mixed_ref, *refs):
    outs, (token_ref, grads, flipped) = refs[:LAYER], refs[LAYER:]
    rows = grad_ref.shape[0]
    span = grad_ref.shape[1] // LAYER
    head_width = rows // LOCAL
    scale = 1.0 / math.sqrt(head_width)
    clear(grads, span)
    for head in range(LOCAL):
        at = block(head, head_width)
        grad = grad_ref[at]
        delta = stats_ref[LOCAL + head : LOCAL + head + 1]
        for j in range(BLOCKS):
            low, high = readers(j)
            cols = slice(low * span, (high + 1) * span)
            back = dot(window_ref[1, at, block(j, span)], grad[:, cols], TN)
            prob = probs_ref[head, block(j, span), cols].astype(f32)
            grads[block(j, span), cols] = (prob * (back - delta[:, cols])).astype(bf16)
        flipped[at] = (dot(window_ref[0, at], grads[...], NN) * scale).astype(bf16)
    for peer, out in enumerate(outs):
        out[0] = mixed_ref[:, place(peer, span)]
        out[1] = flipped[:, place(peer, span)]
    token_ref[...] = jnp.zeros_like(token_ref)


def key_grad_kernel(
    head, pair_ref, query_ref, grad_ref, low_ref, high_ref, stats_ref, stats_low, stats_high,
    dead_ref, *refs
):
    before, refs = refs[:head], refs[head:]
    out_ref, refs = refs[0], refs[1:]
    span = query_ref.shape[1] // LAYER
    head_width = query_ref.shape[0] // LOCAL
    at = block(head, head_width)

    def window(low, own, high):
        return jnp.concatenate([low, own, high], 1)

    query = window(low_ref[0, at], query_ref[at], high_ref[0, at])
    grad = window(low_ref[1, at], grad_ref[at], high_ref[1, at])
    row = slice(head, head + 1)
    log_sum = window(stats_low[row], stats_ref[row], stats_high[row])
    row = slice(LOCAL + head, LOCAL + head + 1)
    delta = window(stats_low[row], stats_ref[row], stats_high[row])
    for i in range(LAYER):
        cols = slice(i * span, (i + SLOTS) * span)
        own = block(i, span)
        scores = dot(pair_ref[0, at, own], query[:, cols], TN)
        prob = jnp.exp(scores - (log_sum[:, cols] + dead_ref[i : i + 1]))
        back = dot(pair_ref[1, at, own], grad[:, cols], TN)
        grads = (prob * (back - delta[:, cols])).astype(bf16)
        out_ref[0, :, own] = dot(query[:, cols], grads, NT).astype(bf16)
        out_ref[1, :, own] = dot(grad[:, cols], prob.astype(bf16), NT).astype(bf16)
    if head == LOCAL - 1:
        for peer, ref in enumerate(refs[:LAYER]):
            for h, source in enumerate((*before, out_ref)):
                ref[:, block(h, head_width)] = source[:, :, place(peer, span)]
    refs[-1][...] = jnp.zeros_like(refs[-1])


def output_kernel(*refs):
    ins, (weight_ref, out_ref, dq_ref, token_ref, flipped) = refs[:LAYER], refs[LAYER:]
    for peer, ref in enumerate(ins):
        flipped[:, place(peer, ref.shape[1])] = ref[...]
    out_ref[...] = dot(flipped[0], weight_ref[...], TN).astype(bf16)
    dq_ref[...] = flipped[1].T
    token_ref[...] = jnp.zeros_like(token_ref)


def key_output_kernel(*refs):
    ins, (dk_ref, dv_ref, flipped) = refs[:LAYER], refs[LAYER:]
    for peer, ref in enumerate(ins):
        flipped[:, place(peer, ref.shape[1])] = ref[...]
    dk_ref[...] = flipped[0].T
    dv_ref[...] = flipped[1].T


def halves(bit, half):
    send = pl.ds(pl.multiple_of((1 - bit) * half, half), half)
    keep = pl.ds(pl.multiple_of(bit * half, half), half)
    return send, keep


def bit_of(stride):
    return lax.rem(lax.axis_index("station") // stride, 2)


def weight_kernel(mixed_ref, all_ref, send_ref, keep_ref):
    send, keep = halves(lax.rem(lax.axis_index("dp"), 2), send_ref.shape[0])
    send_ref[...] = dot(mixed_ref[send], all_ref[...], NN).astype(bf16)
    keep_ref[...] = dot(mixed_ref[keep], all_ref[...], NN)


def split_kernel(stride, part_ref, got_ref, send_ref, keep_ref):
    send, keep = halves(bit_of(stride), send_ref.shape[0])
    send_ref[...] = (part_ref[send] + got_ref[send].astype(f32)).astype(bf16)
    keep_ref[...] = part_ref[keep] + got_ref[keep].astype(f32)


def round_kernel(part_ref, got_ref, out_ref):
    out_ref[...] = (part_ref[...].astype(f32) + got_ref[...].astype(f32)).astype(bf16)


def join_kernel(stride, scale, mine_ref, got_ref, out_ref):
    other, here = halves(bit_of(stride), mine_ref.shape[0])
    for at, ref in ((here, mine_ref), (other, got_ref)):
        value = ref[...]
        if scale is not None:
            value = value.astype(f32) * scale
        out_ref[at] = value


def cross_kernel(mine_ref, first_ref, second_ref, out_ref):
    window = lax.rem(lax.axis_index("dp"), 2)
    other, here = halves(window, mine_ref.shape[0])
    at_home = bit_of(2) == window
    mine, first, second = mine_ref[...], first_ref[...], second_ref[...]
    out_ref[here] = jnp.where(at_home, mine, first)
    out_ref[other] = jnp.where(at_home, first, second)


def local(
    query_states, key_states, value_states, grad_output, out_weight, partner_ids, partner_count
):
    span, width = query_states.shape[2:]
    stations = lax.axis_size("station")
    windows = lax.axis_size("dp")
    rows = width // LAYER
    dma = pltpu.SemaphoreType.DMA

    def swap(value, stride):
        return lax.ppermute(value, "station", [(s ^ stride, s) for s in range(stations)])

    def in_layer(values):
        return [swap(values[n], n + 1) for n in range(LAYER - 1)]

    def along(up, down):
        low = lax.ppermute(up, "station", [(s, (s + LAYER) % stations) for s in range(stations)])
        high = lax.ppermute(down, "station", [(s, (s - LAYER) % stations) for s in range(stations)])
        return low, high

    def other_window(value):
        return lax.ppermute(value, "dp", [(0, 1), (1, 0)])

    def flat(x):
        return x.reshape(span, width)

    q, k, v, g = flat(query_states), flat(key_states), flat(value_states), flat(grad_output)
    reach_shape = shape_of(2, rows, HOPS * span)
    layer_shape = shape_of(rows, LAYER * span)
    mine, *parts = call(
        pack_kernel, [HBM] * 3, [shape_of(3, rows, span)] * LAYER, (k, v, q),
        [pltpu.VMEM((3, span, width), bf16), pltpu.VMEM((3, width, span), bf16), dma((3,))],
        limit=58, name="pack",
    )
    parts = in_layer(parts)
    up, down, pair, query = call(
        gather_kernel, [VMEM] * LAYER,
        [reach_shape, reach_shape, shape_of(2, rows, LAYER * span), layer_shape],
        (mine, *parts), name="gather",
    )
    g_later, up, down = lax.optimization_barrier((g, up, down))
    kv_low, kv_high = along(up, down)
    g_parts = in_layer([g_later] * 3)
    all_grad, grad, up, down, bias, dead = call(
        functools.partial(project_kernel, stations),
        [SMEM] * 2 + [VMEM] * (LAYER + 2),
        [
            shape_of(LAYER * span, width), layer_shape, reach_shape, reach_shape,
            shape_of(16, LAYER * span, dtype=f32), shape_of(8, SLOTS * span, dtype=f32),
        ],
        (partner_ids, partner_count, g, *g_parts, out_weight, query),
        limit=16, name="project",
    )
    qg_low, qg_high = along(up, down)
    stats_shape = shape_of(8, HOPS * span, dtype=f32)
    mixed, stats, up, down, probs, window = call(
        forward_kernel, [VMEM] * 6,
        [
            layer_shape, shape_of(8, LAYER * span, dtype=f32), stats_shape, stats_shape,
            shape_of(LOCAL, BLOCKS * span, LAYER * span), shape_of(2, rows, BLOCKS * span),
        ],
        (pair, kv_low, kv_high, query, grad, bias),
        [pltpu.VMEM((BLOCKS * span, LAYER * span), f32)],
        limit=20, name="forward",
    )
    stats_low, stats_high = along(up, down)

    send, part = call(
        weight_kernel, [VMEM] * 2,
        [shape_of(rows // 2, width), shape_of(rows // 2, width, dtype=f32)],
        (mixed, all_grad), name="weight",
    )

    part_shape = shape_of(2, rows, span)
    mine, *parts, query_token = call(
        query_grad_kernel, [VMEM] * 5, [part_shape] * LAYER + [TOKEN],
        (window, probs, grad, stats, mixed),
        [pltpu.VMEM((BLOCKS * span, LAYER * span), bf16), pltpu.VMEM((rows, LAYER * span), bf16)],
        limit=20, name="query_grad",
    )
    parts = in_layer(parts)
    layer_output, grad_query, output_token = call(
        output_kernel, [VMEM] * (LAYER + 1), [shape_of(span, width)] * 2 + [TOKEN],
        (mine, *parts, out_weight), [pltpu.VMEM((2, width, span), bf16)], name="output",
    )

    before, key_tokens = [], []
    for head in range(LOCAL):
        last = head == LOCAL - 1
        out, *parts, token = call(
            functools.partial(key_grad_kernel, head),
            [VMEM] * (9 + len(before)),
            [shape_of(2, rows // LOCAL, LAYER * span)] + [part_shape] * (LAYER * last) + [TOKEN],
            (pair, query, grad, qg_low, qg_high, stats, stats_low, stats_high, dead, *before),
            limit=20, name="key_grad",
        )
        before.append(out)
        key_tokens.append(token)
    mine, *parts = parts
    grad_key, grad_value = call(
        key_output_kernel, [VMEM] * LAYER, [shape_of(span, width)] * 2,
        (mine, *in_layer(parts)), [pltpu.VMEM((2, width, span), bf16)], name="key_output",
    )

    scale = 1.0 / math.sqrt(span * windows * stations)
    if windows == 2:
        count = rows // 4
        got = other_window(send)
        send, part = call(
            functools.partial(split_kernel, LAYER), [VMEM] * 2,
            [shape_of(count, width), shape_of(count, width, dtype=f32)],
            (part, got), name="split", after=(query_token, qg_low, qg_high),
        )

        def add_round(part, got, after=()):
            out = [shape_of(count, width)]
            return call(round_kernel, [VMEM] * 2, out, (part, got), name="add", after=after)[0]

        total = add_round(part, swap(send, LAYER), key_tokens[:1])
        stride = 2 * LAYER
        while stride < stations:
            total = add_round(total, swap(total, stride), key_tokens[1:2])
            stride *= 2
        (total,) = call(
            functools.partial(join_kernel, LAYER, None), [VMEM] * 2, [shape_of(2 * count, width)],
            (total, swap(total, LAYER)), name="join", after=key_tokens[2:],
        )
        first, second = [], []
        for w in range(2):
            for s in range(stations):
                if s // 2 % 2 == w:
                    first.append((w * stations + s, w * stations + (s ^ 2)))
                else:
                    first.append((w * stations + s, (1 - w) * stations + s))
                    second.append((w * stations + s, (1 - w) * stations + (s ^ 2)))
        axes = ("dp", "station")
        (total,) = call(
            cross_kernel, [VMEM] * 3, [shape_of(4 * count, width)],
            (total, lax.ppermute(total, axes, first), lax.ppermute(total, axes, second)),
            name="cross", after=(output_token,),
        )
        (grad_weight,) = call(
            functools.partial(join_kernel, 1, scale), [VMEM] * 2,
            [shape_of(8 * count, width, dtype=f32)], (total, swap(total, 1)), name="last",
        )
    else:
        start = lax.axis_index("station") % LAYER * rows
        mine = dot(mixed, all_grad, NN).astype(bf16)
        whole = lax.dynamic_update_slice_in_dim(jnp.zeros((width, width), bf16), mine, start, 0)
        whole = lax.psum_scatter(whole, "dp", scatter_dimension=0, tiled=True)
        grad_weight = lax.psum(whole.astype(f32), "station") * scale
    shape = query_states.shape
    return (
        layer_output.reshape(shape),
        grad_query.reshape(shape),
        grad_key.reshape(shape),
        grad_value.reshape(shape),
        grad_weight,
    )


def solution(mesh):
    split = P("dp", "station", None, None)
    return jax.shard_map(
        local,
        mesh=mesh,
        in_specs=(split, split, split, split, P(), P(), P()),
        out_specs=(split, split, split, split, P("dp", None)),
        check_vma=False,
    )
```

```python
import functools
import math

import jax
import jax.numpy as jnp
from jax import lax
from jax.experimental import pallas as pl
from jax.experimental.pallas import tpu as pltpu
from jax.sharding import PartitionSpec as P

HEADS = 12
PMAX = 6
HOPS = 3
LAYER = 4
LOCAL = HEADS // LAYER
BLOCKS = LAYER + 2 * HOPS
SLOTS = 2 * HOPS + 1
MIB = 1024 * 1024

neg_big = -1e30
bf16, f32 = jnp.bfloat16, jnp.float32
SMEM = pl.BlockSpec(memory_space=pltpu.SMEM)
VMEM = pl.BlockSpec(memory_space=pltpu.VMEM)
ANY = pl.BlockSpec(memory_space=pl.ANY)
HBM = pl.BlockSpec(memory_space=pltpu.HBM)
NN = (((1,), (0,)), ((), ()))
NT = (((1,), (1,)), ((), ()))
TN = (((0,), (0,)), ((), ()))


def dot(x, y, dims):
    return lax.dot_general(x, y, dims, preferred_element_type=f32)


def shape_of(*dims, dtype=bf16):
    return jax.ShapeDtypeStruct(dims, dtype)


TOKEN = shape_of(8, 128, dtype=f32)


def skip_refs(kernel, first, count, *refs):
    kernel(*refs[:first], *refs[first + count :])


def call(kernel, ins, outs, args, scratch=(), limit=8, name=None, after=()):
    ins, args = [*ins, *[ANY] * len(after)], (*args, *after)
    if after:
        kernel = functools.partial(skip_refs, kernel, len(args) - len(after), len(after))
    return pl.pallas_call(
        kernel,
        in_specs=ins,
        out_specs=[VMEM] * len(outs),
        out_shape=outs,
        scratch_shapes=list(scratch),
        compiler_params=pltpu.CompilerParams(vmem_limit_bytes=limit * MIB),
        cost_estimate=pl.CostEstimate(flops=1, bytes_accessed=1, transcendentals=0),
        name=name,
    )(*args)


def place(peer, size):
    position = jnp.bitwise_xor(lax.rem(lax.axis_index("station"), LAYER), peer)
    return pl.ds(pl.multiple_of(position * size, size), size)


def block(j, span):
    return slice(j * span, (j + 1) * span)


def readers(j):
    return max(0, j - 2 * HOPS), min(LAYER - 1, j)


def pack_kernel(k_ref, v_ref, *refs):
    outs, (natural, flipped, sems) = refs[:LAYER], refs[LAYER:]
    rows = outs[0].shape[1]
    copies = [
        pltpu.make_async_copy(ref, natural.at[n], sems.at[n]) for n, ref in enumerate((k_ref, v_ref))
    ]
    for copy in copies:
        copy.start()
    for n, copy in enumerate(copies):
        copy.wait()
        flipped[n] = natural[n].T
    for peer, out in enumerate(outs):
        out[...] = flipped[:, place(peer, rows)]


def project_kernel(q_ref, g_ref, weight_ref, *refs):
    outs, (copy_ref, flipped) = refs[:LAYER], refs[LAYER:]
    rows = outs[0].shape[1]
    copy_ref[...] = g_ref[...]
    flipped[0] = q_ref[...].T * bf16(1.0 / math.sqrt(flipped.shape[1] // HEADS))
    flipped[1] = dot(weight_ref[...], g_ref[...], NT).astype(bf16)
    for peer, out in enumerate(outs):
        out[...] = flipped[:, place(peer, rows)]


def pair_kernel(first_ref, second_ref, out_ref):
    out_ref[0] = first_ref[...]
    out_ref[1] = second_ref[...]


def gather_kernel(*refs):
    ins, (up_ref, down_ref, pair_ref) = refs[:LAYER], refs[LAYER:]
    span = ins[0].shape[2]
    for peer, ref in enumerate(ins):
        pair_ref[:, :, place(peer, span)] = ref[...]
    up_ref[...] = pair_ref[:, :, span:]
    down_ref[...] = pair_ref[:, :, : HOPS * span]


def live_kernel(station_count, ids_ref, count_ref, bias_ref, dead_ref):
    span = bias_ref.shape[1] // LAYER
    first = lax.axis_index("station") // LAYER * LAYER
    ones = jnp.ones((1, span), f32)

    def listed(reader, other):
        hit = jnp.int32(0)
        for j in range(PMAX):
            here = jnp.logical_and(ids_ref[reader, j] == other, j < count_ref[reader])
            hit = jnp.maximum(hit, here.astype(jnp.int32))
        return hit > 0

    for j in range(BLOCKS):
        outer = lax.rem(first + (j - HOPS) + station_count, station_count)
        low, high = readers(j)
        for i in range(low, high + 1):
            inner = first + i
            slot = j - i
            if slot == HOPS:
                bias_ref[j : j + 1, block(i, span)] = 0.0 * ones
                dead_ref[i : i + 1, block(slot, span)] = 0.0 * ones
            else:
                reads = jnp.where(listed(inner, outer), 0.0, neg_big)
                bias_ref[j : j + 1, block(i, span)] = reads * ones
                read_by = jnp.where(listed(outer, inner), 0.0, -neg_big)
                dead_ref[i : i + 1, block(slot, span)] = read_by * ones


def clear(ref, span):
    for j in range(BLOCKS):
        low, high = readers(j)
        for i in range(LAYER):
            if not low <= i <= high:
                ref[block(j, span), block(i, span)] = jnp.zeros((span, span), bf16)


def forward_kernel(
    pair_ref, low_ref, high_ref, query_ref, bias_ref,
    mixed_ref, stats_ref, stats_up, stats_down, probs_ref, window_ref,
    raw,
):
    rows = query_ref.shape[1]
    span = query_ref.shape[2] // LAYER
    head_width = rows // LOCAL
    reach = HOPS * span
    window_ref[:, :, :reach] = low_ref[...]
    window_ref[:, :, reach : reach + LAYER * span] = pair_ref[...]
    window_ref[:, :, reach + LAYER * span :] = high_ref[...]
    for head in range(LOCAL):
        clear(probs_ref.at[head], span)
        at = block(head, head_width)
        query = query_ref[0, at]
        tops = [None] * LAYER
        for j in range(BLOCKS):
            low, high = readers(j)
            cols = slice(low * span, (high + 1) * span)
            scores = dot(window_ref[0, at, block(j, span)], query[:, cols], TN)
            scores = scores + bias_ref[j : j + 1, cols]
            raw[block(j, span), cols] = scores
            here = jnp.max(scores, 0, keepdims=True)
            for i in range(low, high + 1):
                mine = here[:, block(i - low, span)]
                tops[i] = mine if tops[i] is None else jnp.maximum(tops[i], mine)
        top = jnp.concatenate(tops, 1)
        totals = [jnp.zeros((1, span), f32)] * LAYER
        for j in range(BLOCKS):
            low, high = readers(j)
            cols = slice(low * span, (high + 1) * span)
            weight = jnp.exp(raw[block(j, span), cols] - top[:, cols])
            raw[block(j, span), cols] = weight
            here = jnp.sum(weight, 0, keepdims=True)
            for i in range(low, high + 1):
                totals[i] = totals[i] + here[:, block(i - low, span)]
        total = jnp.concatenate(totals, 1)
        inverse = 1.0 / total
        for j in range(BLOCKS):
            low, high = readers(j)
            cols = slice(low * span, (high + 1) * span)
            probs_ref[head, block(j, span), cols] = (
                raw[block(j, span), cols] * inverse[:, cols]
            ).astype(bf16)
        mixed = dot(window_ref[1, at], probs_ref[head], NN).astype(bf16)
        mixed_ref[at] = mixed
        product = query_ref[1, at].astype(f32) * mixed.astype(f32)
        stats_ref[head : head + 1] = top + jnp.log(total)
        stats_ref[LOCAL + head : LOCAL + head + 1] = jnp.sum(product, 0, keepdims=True)
    stats_ref[2 * LOCAL :] = jnp.zeros((8 - 2 * LOCAL, LAYER * span), f32)
    stats_up[...] = stats_ref[:, span:]
    stats_down[...] = stats_ref[:, :reach]


def query_grad_kernel(window_ref, probs_ref, query_ref, stats_ref, mixed_ref, *refs):
    outs, (token_ref, grads, flipped) = refs[:LAYER], refs[LAYER:]
    rows = query_ref.shape[1]
    span = query_ref.shape[2] // LAYER
    head_width = rows // LOCAL
    scale = 1.0 / math.sqrt(head_width)
    clear(grads, span)
    for head in range(LOCAL):
        at = block(head, head_width)
        grad = query_ref[1, at]
        delta = stats_ref[LOCAL + head : LOCAL + head + 1]
        for j in range(BLOCKS):
            low, high = readers(j)
            cols = slice(low * span, (high + 1) * span)
            back = dot(window_ref[1, at, block(j, span)], grad[:, cols], TN)
            prob = probs_ref[head, block(j, span), cols].astype(f32)
            grads[block(j, span), cols] = (prob * (back - delta[:, cols])).astype(bf16)
        flipped[at] = (dot(window_ref[0, at], grads[...], NN) * scale).astype(bf16)
    for peer, out in enumerate(outs):
        out[0] = mixed_ref[:, place(peer, span)]
        out[1] = flipped[:, place(peer, span)]
    token_ref[...] = jnp.zeros_like(token_ref)


def key_grad_kernel(
    head, pair_ref, query_ref, low_ref, high_ref, stats_ref, stats_low, stats_high,
    dead_ref, *refs
):
    before, refs = refs[:head], refs[head:]
    out_ref, refs = refs[0], refs[1:]
    span = query_ref.shape[2] // LAYER
    head_width = query_ref.shape[1] // LOCAL
    at = block(head, head_width)

    def window(low, own, high):
        return jnp.concatenate([low, own, high], 1)

    query = window(low_ref[0, at], query_ref[0, at], high_ref[0, at])
    grad = window(low_ref[1, at], query_ref[1, at], high_ref[1, at])
    row = slice(head, head + 1)
    log_sum = window(stats_low[row], stats_ref[row], stats_high[row])
    row = slice(LOCAL + head, LOCAL + head + 1)
    delta = window(stats_low[row], stats_ref[row], stats_high[row])
    for i in range(LAYER):
        cols = slice(i * span, (i + SLOTS) * span)
        own = block(i, span)
        scores = dot(pair_ref[0, at, own], query[:, cols], TN)
        prob = jnp.exp(scores - (log_sum[:, cols] + dead_ref[i : i + 1]))
        back = dot(pair_ref[1, at, own], grad[:, cols], TN)
        grads = (prob * (back - delta[:, cols])).astype(bf16)
        out_ref[0, :, own] = dot(query[:, cols], grads, NT).astype(bf16)
        out_ref[1, :, own] = dot(grad[:, cols], prob.astype(bf16), NT).astype(bf16)
    if head == LOCAL - 1:
        for peer, ref in enumerate(refs[:LAYER]):
            for h, source in enumerate((*before, out_ref)):
                ref[:, block(h, head_width)] = source[:, :, place(peer, span)]
    refs[-1][...] = jnp.zeros_like(refs[-1])


def output_kernel(*refs):
    ins, (weight_ref, out_ref, dq_ref, token_ref, flipped) = refs[:LAYER], refs[LAYER:]
    for peer, ref in enumerate(ins):
        flipped[:, place(peer, ref.shape[1])] = ref[...]
    out_ref[...] = dot(flipped[0], weight_ref[...], TN).astype(bf16)
    dq_ref[...] = flipped[1].T
    token_ref[...] = jnp.zeros_like(token_ref)


def key_output_kernel(*refs):
    ins, (dk_ref, dv_ref, token_ref, flipped) = refs[:LAYER], refs[LAYER:]
    for peer, ref in enumerate(ins):
        flipped[:, place(peer, ref.shape[1])] = ref[...]
    dk_ref[...] = flipped[0].T
    dv_ref[...] = flipped[1].T
    token_ref[...] = jnp.zeros_like(token_ref)


def halves(bit, half):
    send = pl.ds(pl.multiple_of((1 - bit) * half, half), half)
    keep = pl.ds(pl.multiple_of(bit * half, half), half)
    return send, keep


def bit_of(stride):
    return lax.rem(lax.axis_index("station") // stride, 2)


def weight_kernel(mixed_ref, mine_ref, sib_ref, send_ref, keep_ref, right):
    for n in range(2):
        right[place(2 * n, mine_ref.shape[1])] = mine_ref[n]
        right[place(2 * n + 1, mine_ref.shape[1])] = sib_ref[n]
    send, keep = halves(lax.rem(lax.axis_index("dp"), 2), send_ref.shape[0])
    send_ref[...] = dot(mixed_ref[send], right[...], NN).astype(bf16)
    keep_ref[...] = dot(mixed_ref[keep], right[...], NN)


def split_kernel(stride, part_ref, got_ref, send_ref, keep_ref):
    send, keep = halves(bit_of(stride), send_ref.shape[0])
    send_ref[...] = (part_ref[send] + got_ref[send].astype(f32)).astype(bf16)
    keep_ref[...] = part_ref[keep] + got_ref[keep].astype(f32)


def round_kernel(part_ref, got_ref, out_ref):
    out_ref[...] = (part_ref[...].astype(f32) + got_ref[...].astype(f32)).astype(bf16)


def join_kernel(stride, scale, mine_ref, got_ref, out_ref):
    other, here = halves(bit_of(stride), mine_ref.shape[0])
    for at, ref in ((here, mine_ref), (other, got_ref)):
        value = ref[...]
        if scale is not None:
            value = value.astype(f32) * scale
        out_ref[at] = value


def cross_kernel(mine_ref, first_ref, second_ref, out_ref):
    window = lax.rem(lax.axis_index("dp"), 2)
    other, here = halves(window, mine_ref.shape[0])
    at_home = bit_of(2) == window
    mine, first, second = mine_ref[...], first_ref[...], second_ref[...]
    out_ref[here] = jnp.where(at_home, mine, first)
    out_ref[other] = jnp.where(at_home, first, second)


def local(
    query_states, key_states, value_states, grad_output, out_weight, partner_ids, partner_count
):
    span, width = query_states.shape[2:]
    stations = lax.axis_size("station")
    windows = lax.axis_size("dp")
    rows = width // LAYER
    dma = pltpu.SemaphoreType.DMA

    def swap(value, stride):
        return lax.ppermute(value, "station", [(s ^ stride, s) for s in range(stations)])

    def in_layer(values):
        return [swap(values[n], n + 1) for n in range(LAYER - 1)]

    def along(up, down):
        low = lax.ppermute(up, "station", [(s, (s + LAYER) % stations) for s in range(stations)])
        high = lax.ppermute(down, "station", [(s, (s - LAYER) % stations) for s in range(stations)])
        return low, high

    def other_window(value):
        return lax.ppermute(value, "dp", [(0, 1), (1, 0)])

    def flat(x):
        return x.reshape(span, width)

    q, k, v, g = flat(query_states), flat(key_states), flat(value_states), flat(grad_output)
    flat_shape = shape_of(span, width)
    part_shape = shape_of(2, rows, span)
    reach_shape = shape_of(2, rows, HOPS * span)
    layer_shape = shape_of(2, rows, LAYER * span)

    def gather(parts, after=()):
        return call(
            gather_kernel, [VMEM] * LAYER, [reach_shape, reach_shape, layer_shape], parts,
            name="gather", after=after,
        )

    mine, *parts = call(
        pack_kernel, [HBM] * 2, [part_shape] * LAYER, (k, v),
        [pltpu.VMEM((2, span, width), bf16), pltpu.VMEM((2, width, span), bf16), dma((2,))],
        limit=58, name="pack",
    )
    up, down, pair = gather((mine, *in_layer(parts)))
    mine, *parts, g_copy = call(
        project_kernel, [VMEM] * 3, [part_shape] * LAYER + [flat_shape],
        (q, g, out_weight), [pltpu.VMEM((2, width, span), bf16)], name="project",
    )
    up, g_copy, *parts = lax.optimization_barrier((up, g_copy, *parts))
    kv_low, kv_high = along(up, down)
    up, down, query = gather((mine, *in_layer(parts)))
    qg_low, qg_high = along(up, down)
    bias, dead = call(
        functools.partial(live_kernel, stations), [SMEM] * 2,
        [
            shape_of(16, LAYER * span, dtype=f32), shape_of(8, SLOTS * span, dtype=f32),
        ],
        (partner_ids, partner_count), name="live",
    )
    (g_pair,) = call(
        pair_kernel, [VMEM] * 2, [shape_of(2, span, width)], (g_copy, swap(g_copy, 2)), name="pair",
        after=(kv_low, kv_high, query, bias),
    )
    g_pairs = g_pair, swap(g_pair, 1)
    stats_shape = shape_of(8, HOPS * span, dtype=f32)
    mixed, stats, up, down, probs, window = call(
        forward_kernel, [VMEM] * 5,
        [
            shape_of(rows, LAYER * span), shape_of(8, LAYER * span, dtype=f32),
            stats_shape, stats_shape,
            shape_of(LOCAL, BLOCKS * span, LAYER * span), shape_of(2, rows, BLOCKS * span),
        ],
        (pair, kv_low, kv_high, query, bias),
        [pltpu.VMEM((BLOCKS * span, LAYER * span), f32)],
        limit=20, name="forward",
    )
    stats_low, stats_high = along(up, down)

    send, part = call(
        weight_kernel, [VMEM] * 3,
        [shape_of(rows // 2, width), shape_of(rows // 2, width, dtype=f32)],
        (mixed, *g_pairs), [pltpu.VMEM((LAYER * span, width), bf16)], name="weight",
    )

    mine, *parts, query_token = call(
        query_grad_kernel, [VMEM] * 5, [part_shape] * LAYER + [TOKEN],
        (window, probs, query, stats, mixed),
        [pltpu.VMEM((BLOCKS * span, LAYER * span), bf16), pltpu.VMEM((rows, LAYER * span), bf16)],
        limit=20, name="query_grad",
    )
    query_parts = in_layer(parts)
    layer_output, grad_query, output_token = call(
        output_kernel, [VMEM] * (LAYER + 1), [flat_shape] * 2 + [TOKEN],
        (mine, *query_parts, out_weight), [pltpu.VMEM((2, width, span), bf16)], name="output",
    )

    before, key_tokens = [], []
    for head in range(LOCAL):
        last = head == LOCAL - 1
        out, *parts, token = call(
            functools.partial(key_grad_kernel, head),
            [VMEM] * (8 + len(before)),
            [shape_of(2, rows // LOCAL, LAYER * span)] + [part_shape] * (LAYER * last) + [TOKEN],
            (pair, query, qg_low, qg_high, stats, stats_low, stats_high, dead, *before),
            limit=20, name="key_grad",
        )
        before.append(out)
        key_tokens.append(token)
    mine, *parts = parts
    key_parts = in_layer(parts)
    grad_key, grad_value, key_output_token = call(
        key_output_kernel, [VMEM] * LAYER, [flat_shape] * 2 + [TOKEN],
        (mine, *key_parts), [pltpu.VMEM((2, width, span), bf16)], name="key_output",
    )

    scale = 1.0 / math.sqrt(span * windows * stations)
    if windows == 2:
        count = rows // 4
        got = other_window(send)
        send, part = call(
            functools.partial(split_kernel, LAYER), [VMEM] * 2,
            [shape_of(count, width), shape_of(count, width, dtype=f32)],
            (part, got), name="split", after=(query_token, qg_low, qg_high, stats_low, stats_high),
        )

        def add_round(part, got, after=()):
            out = [shape_of(count, width)]
            return call(round_kernel, [VMEM] * 2, out, (part, got), name="add", after=after)[0]

        total = add_round(part, swap(send, LAYER), key_tokens[:1] + query_parts)
        stride = 2 * LAYER
        while stride < stations:
            total = add_round(total, swap(total, stride), key_tokens[1:])
            stride *= 2
        (total,) = call(
            functools.partial(join_kernel, LAYER, None), [VMEM] * 2, [shape_of(2 * count, width)],
            (total, swap(total, LAYER)), name="join", after=key_parts,
        )
        first, second = [], []
        for w in range(2):
            for s in range(stations):
                if s // 2 % 2 == w:
                    first.append((w * stations + s, w * stations + (s ^ 2)))
                else:
                    first.append((w * stations + s, (1 - w) * stations + s))
                    second.append((w * stations + s, (1 - w) * stations + (s ^ 2)))
        axes = ("dp", "station")
        (total,) = call(
            cross_kernel, [VMEM] * 3, [shape_of(4 * count, width)],
            (total, lax.ppermute(total, axes, first), lax.ppermute(total, axes, second)),
            name="cross", after=(output_token,),
        )
        (grad_weight,) = call(
            functools.partial(join_kernel, 1, scale), [VMEM] * 2,
            [shape_of(8 * count, width, dtype=f32)], (total, swap(total, 1)), name="last",
        )
    else:
        start = lax.axis_index("station") % LAYER * rows
        all_grad = jnp.zeros((LAYER * span, width), bf16)
        for peer in range(LAYER):
            value = g_pairs[peer % 2][peer // 2]
            spot = lax.axis_index("station") % LAYER ^ peer
            all_grad = lax.dynamic_update_slice_in_dim(all_grad, value, spot * span, 0)
        mine = dot(mixed, all_grad, NN).astype(bf16)
        whole = lax.dynamic_update_slice_in_dim(jnp.zeros((width, width), bf16), mine, start, 0)
        whole = lax.psum_scatter(whole, "dp", scatter_dimension=0, tiled=True)
        grad_weight = lax.psum(whole.astype(f32), "station") * scale
    shape = query_states.shape
    return (
        layer_output.reshape(shape),
        grad_query.reshape(shape),
        grad_key.reshape(shape),
        grad_value.reshape(shape),
        grad_weight,
    )


def solution(mesh):
    split = P("dp", "station", None, None)
    return jax.shard_map(
        local,
        mesh=mesh,
        in_specs=(split, split, split, split, P(), P(), P()),
        out_specs=(split, split, split, split, P("dp", None)),
        check_vma=False,
    )
```

```python
import functools
import math

import jax
import jax.numpy as jnp
from jax import lax
from jax.experimental import pallas as pl
from jax.experimental.pallas import tpu as pltpu
from jax.sharding import PartitionSpec as P

HEADS = 12
PMAX = 6
HOPS = 3
LAYER = 4
LOCAL = HEADS // LAYER
BLOCKS = LAYER + 2 * HOPS
SLOTS = 2 * HOPS + 1
MIB = 1024 * 1024

neg_big = -1e30
bf16, f32 = jnp.bfloat16, jnp.float32
SMEM = pl.BlockSpec(memory_space=pltpu.SMEM)
VMEM = pl.BlockSpec(memory_space=pltpu.VMEM)
ANY = pl.BlockSpec(memory_space=pl.ANY)
HBM = pl.BlockSpec(memory_space=pltpu.HBM)
NN = (((1,), (0,)), ((), ()))
NT = (((1,), (1,)), ((), ()))
TN = (((0,), (0,)), ((), ()))


def dot(x, y, dims):
    return lax.dot_general(x, y, dims, preferred_element_type=f32)


def shape_of(*dims, dtype=bf16):
    return jax.ShapeDtypeStruct(dims, dtype)


TOKEN = shape_of(8, 128, dtype=f32)


def skip_refs(kernel, first, count, *refs):
    kernel(*refs[:first], *refs[first + count :])


def call(kernel, ins, outs, args, scratch=(), limit=8, name=None, after=()):
    ins, args = [*ins, *[ANY] * len(after)], (*args, *after)
    if after:
        kernel = functools.partial(skip_refs, kernel, len(args) - len(after), len(after))
    return pl.pallas_call(
        kernel,
        in_specs=ins,
        out_specs=[VMEM] * len(outs),
        out_shape=outs,
        scratch_shapes=list(scratch),
        compiler_params=pltpu.CompilerParams(vmem_limit_bytes=limit * MIB),
        cost_estimate=pl.CostEstimate(flops=1, bytes_accessed=1, transcendentals=0),
        name=name,
    )(*args)


def place(peer, size):
    position = jnp.bitwise_xor(lax.rem(lax.axis_index("station"), LAYER), peer)
    return pl.ds(pl.multiple_of(position * size, size), size)


def block(j, span):
    return slice(j * span, (j + 1) * span)


def readers(j):
    return max(0, j - 2 * HOPS), min(LAYER - 1, j)


def pack_kernel(k_ref, v_ref, *refs):
    outs, (natural, flipped, sems) = refs[:LAYER], refs[LAYER:]
    rows = outs[0].shape[1]
    copies = [
        pltpu.make_async_copy(ref, natural.at[n], sems.at[n]) for n, ref in enumerate((k_ref, v_ref))
    ]
    for copy in copies:
        copy.start()
    for n, copy in enumerate(copies):
        copy.wait()
        flipped[n] = natural[n].T
    for peer, out in enumerate(outs):
        out[...] = flipped[:, place(peer, rows)]


def project_kernel(q_ref, g_ref, weight_ref, *refs):
    outs, (copy_ref, flipped) = refs[:LAYER], refs[LAYER:]
    rows = outs[0].shape[1]
    copy_ref[...] = g_ref[...]
    flipped[0] = q_ref[...].T * bf16(1.0 / math.sqrt(flipped.shape[1] // HEADS))
    flipped[1] = dot(weight_ref[...], g_ref[...], NT).astype(bf16)
    for peer, out in enumerate(outs):
        out[...] = flipped[:, place(peer, rows)]


def pair_kernel(first_ref, second_ref, out_ref):
    out_ref[0] = first_ref[...]
    out_ref[1] = second_ref[...]


def relay_kernel(sib_ref, across_ref, out_ref):
    out_ref[0] = sib_ref[...]
    out_ref[1] = across_ref[1]


def gather_kernel(*refs):
    ins, (up_ref, down_ref, pair_ref) = refs[:LAYER], refs[LAYER:]
    span = ins[0].shape[2]
    for peer, ref in enumerate(ins):
        pair_ref[:, :, place(peer, span)] = ref[...]
    up_ref[...] = pair_ref[:, :, span:]
    down_ref[...] = pair_ref[:, :, : HOPS * span]


def live_kernel(station_count, ids_ref, count_ref, bias_ref, dead_ref):
    span = bias_ref.shape[1] // LAYER
    first = lax.axis_index("station") // LAYER * LAYER
    ones = jnp.ones((1, span), f32)

    def listed(reader, other):
        hit = jnp.int32(0)
        for j in range(PMAX):
            here = jnp.logical_and(ids_ref[reader, j] == other, j < count_ref[reader])
            hit = jnp.maximum(hit, here.astype(jnp.int32))
        return hit > 0

    for j in range(BLOCKS):
        outer = lax.rem(first + (j - HOPS) + station_count, station_count)
        low, high = readers(j)
        for i in range(low, high + 1):
            inner = first + i
            slot = j - i
            if slot == HOPS:
                bias_ref[j : j + 1, block(i, span)] = 0.0 * ones
            else:
                reads = jnp.where(listed(inner, outer), 0.0, neg_big)
                bias_ref[j : j + 1, block(i, span)] = reads * ones
            if not HOPS <= j < HOPS + LAYER:
                read_by = jnp.where(listed(outer, inner), 0.0, -neg_big)
                spot = slot if j < HOPS else slot - LAYER
                dead_ref[i : i + 1, block(spot, span)] = read_by * ones


def clear(ref, span):
    for j in range(BLOCKS):
        low, high = readers(j)
        for i in range(LAYER):
            if not low <= i <= high:
                ref[block(j, span), block(i, span)] = jnp.zeros((span, span), bf16)


def forward_kernel(
    pair_ref, low_ref, high_ref, query_ref, bias_ref,
    mixed_ref, stats_ref, stats_up, stats_down, probs_ref, window_ref,
    raw,
):
    rows = query_ref.shape[1]
    span = query_ref.shape[2] // LAYER
    head_width = rows // LOCAL
    reach = HOPS * span
    window_ref[:, :, :reach] = low_ref[...]
    window_ref[:, :, reach : reach + LAYER * span] = pair_ref[...]
    window_ref[:, :, reach + LAYER * span :] = high_ref[...]
    for head in range(LOCAL):
        clear(probs_ref.at[head], span)
        at = block(head, head_width)
        query = query_ref[0, at]
        tops = [None] * LAYER
        for j in range(BLOCKS):
            low, high = readers(j)
            cols = slice(low * span, (high + 1) * span)
            scores = dot(window_ref[0, at, block(j, span)], query[:, cols], TN)
            scores = scores + bias_ref[j : j + 1, cols]
            raw[block(j, span), cols] = scores
            here = jnp.max(scores, 0, keepdims=True)
            for i in range(low, high + 1):
                mine = here[:, block(i - low, span)]
                tops[i] = mine if tops[i] is None else jnp.maximum(tops[i], mine)
        top = jnp.concatenate(tops, 1)
        totals = [jnp.zeros((1, span), f32)] * LAYER
        for j in range(BLOCKS):
            low, high = readers(j)
            cols = slice(low * span, (high + 1) * span)
            weight = jnp.exp(raw[block(j, span), cols] - top[:, cols])
            raw[block(j, span), cols] = weight
            here = jnp.sum(weight, 0, keepdims=True)
            for i in range(low, high + 1):
                totals[i] = totals[i] + here[:, block(i - low, span)]
        total = jnp.concatenate(totals, 1)
        inverse = 1.0 / total
        for j in range(BLOCKS):
            low, high = readers(j)
            cols = slice(low * span, (high + 1) * span)
            probs_ref[head, block(j, span), cols] = (
                raw[block(j, span), cols] * inverse[:, cols]
            ).astype(bf16)
        mixed = dot(window_ref[1, at], probs_ref[head], NN).astype(bf16)
        mixed_ref[at] = mixed
        product = query_ref[1, at].astype(f32) * mixed.astype(f32)
        stats_ref[head : head + 1] = top + jnp.log(total)
        stats_ref[LOCAL + head : LOCAL + head + 1] = jnp.sum(product, 0, keepdims=True)
    stats_ref[2 * LOCAL :] = jnp.zeros((8 - 2 * LOCAL, LAYER * span), f32)
    stats_up[...] = stats_ref[:, span:]
    stats_down[...] = stats_ref[:, :reach]


def query_grad_kernel(
    window_ref, probs_ref, query_ref, stats_ref, mixed_ref, mine_ref, sib_ref, across_ref, own_ref,
    token_ref, grads, flipped
):
    rows = query_ref.shape[1]
    span = query_ref.shape[2] // LAYER
    head_width = rows // LOCAL
    scale = 1.0 / math.sqrt(head_width)
    inside = slice(HOPS * span, (HOPS + LAYER) * span)
    clear(grads, span)
    for head in range(LOCAL):
        at = block(head, head_width)
        grad = query_ref[1, at]
        delta = stats_ref[LOCAL + head : LOCAL + head + 1]
        for j in range(BLOCKS):
            low, high = readers(j)
            cols = slice(low * span, (high + 1) * span)
            back = dot(window_ref[1, at, block(j, span)], grad[:, cols], TN)
            prob = probs_ref[head, block(j, span), cols].astype(f32)
            grads[block(j, span), cols] = (prob * (back - delta[:, cols])).astype(bf16)
        flipped[at] = (dot(window_ref[0, at], grads[...], NN) * scale).astype(bf16)
        own_ref[0, at] = dot(query_ref[0, at], grads[inside], NT)
        own_ref[1, at] = dot(grad, probs_ref[head, inside], NT)
    for peer, out in enumerate((mine_ref, sib_ref, across_ref.at[0], across_ref.at[1])):
        out[0] = mixed_ref[:, place(peer, span)]
        out[1] = flipped[:, place(peer, span)]
    token_ref[...] = jnp.zeros_like(token_ref)


def key_grad_kernel(
    pair_ref, low_ref, high_ref, stats_low, stats_high, dead_ref, own_ref, *refs
):
    outs, (token_ref, flipped) = refs[:LAYER], refs[LAYER:]
    rows = pair_ref.shape[1]
    span = pair_ref.shape[2] // LAYER
    head_width = rows // LOCAL
    for head in range(LOCAL):
        at = block(head, head_width)
        log_row = slice(head, head + 1)
        delta_row = slice(LOCAL + head, LOCAL + head + 1)
        for i in range(LAYER):
            own = block(i, span)

            def outside(low, high):
                sides = [low[:, i * span :]] if i < HOPS else []
                return jnp.concatenate(sides + ([high[:, : i * span]] if i else []), 1)

            query = outside(low_ref[0, at], high_ref[0, at])
            grad = outside(low_ref[1, at], high_ref[1, at])
            log_sum = outside(stats_low[log_row], stats_high[log_row]) + dead_ref[i : i + 1]
            delta = outside(stats_low[delta_row], stats_high[delta_row])
            prob = jnp.exp(dot(pair_ref[0, at, own], query, TN) - log_sum)
            back = dot(pair_ref[1, at, own], grad, TN)
            grads = (prob * (back - delta)).astype(bf16)
            keys = own_ref[0, at, own] + dot(query, grads, NT)
            values = own_ref[1, at, own] + dot(grad, prob.astype(bf16), NT)
            flipped[0, at, own] = keys.astype(bf16)
            flipped[1, at, own] = values.astype(bf16)
    for peer, out in enumerate(outs):
        out[...] = flipped[:, :, place(peer, span)]
    token_ref[...] = jnp.zeros_like(token_ref)


def output_kernel(
    mine_ref, across_ref, sib_ref, weight_ref, out_ref, dq_ref, token_ref, flipped
):
    ins = mine_ref, sib_ref.at[0], across_ref.at[0], sib_ref.at[1]
    for peer, ref in enumerate(ins):
        flipped[:, place(peer, ref.shape[1])] = ref[...]
    out_ref[...] = dot(flipped[0], weight_ref[...], TN).astype(bf16)
    dq_ref[...] = flipped[1].T
    token_ref[...] = jnp.zeros_like(token_ref)


def key_output_kernel(*refs):
    ins, (dk_ref, dv_ref, token_ref, flipped) = refs[:LAYER], refs[LAYER:]
    for peer, ref in enumerate(ins):
        flipped[:, place(peer, ref.shape[1])] = ref[...]
    dk_ref[...] = flipped[0].T
    dv_ref[...] = flipped[1].T
    token_ref[...] = jnp.zeros_like(token_ref)


def halves(bit, half):
    send = pl.ds(pl.multiple_of((1 - bit) * half, half), half)
    keep = pl.ds(pl.multiple_of(bit * half, half), half)
    return send, keep


def bit_of(stride):
    return lax.rem(lax.axis_index("station") // stride, 2)


def weight_kernel(mixed_ref, mine_ref, sib_ref, send_ref, keep_ref, right):
    for n in range(2):
        right[place(2 * n, mine_ref.shape[1])] = mine_ref[n]
        right[place(2 * n + 1, mine_ref.shape[1])] = sib_ref[n]
    send, keep = halves(lax.rem(lax.axis_index("dp"), 2), send_ref.shape[0])
    send_ref[...] = dot(mixed_ref[send], right[...], NN).astype(bf16)
    keep_ref[...] = dot(mixed_ref[keep], right[...], NN)


def split_kernel(stride, part_ref, got_ref, send_ref, keep_ref):
    send, keep = halves(bit_of(stride), send_ref.shape[0])
    send_ref[...] = (part_ref[send] + got_ref[send].astype(f32)).astype(bf16)
    keep_ref[...] = part_ref[keep] + got_ref[keep].astype(f32)


def round_kernel(part_ref, got_ref, out_ref):
    out_ref[...] = (part_ref[...].astype(f32) + got_ref[...].astype(f32)).astype(bf16)


def join_kernel(stride, scale, mine_ref, got_ref, out_ref):
    other, here = halves(bit_of(stride), mine_ref.shape[0])
    for at, ref in ((here, mine_ref), (other, got_ref)):
        value = ref[...]
        if scale is not None:
            value = value.astype(f32) * scale
        out_ref[at] = value


def cross_kernel(mine_ref, first_ref, second_ref, out_ref):
    window = lax.rem(lax.axis_index("dp"), 2)
    other, here = halves(window, mine_ref.shape[0])
    at_home = bit_of(2) == window
    mine, first, second = mine_ref[...], first_ref[...], second_ref[...]
    out_ref[here] = jnp.where(at_home, mine, first)
    out_ref[other] = jnp.where(at_home, first, second)


def local(
    query_states, key_states, value_states, grad_output, out_weight, partner_ids, partner_count
):
    span, width = query_states.shape[2:]
    stations = lax.axis_size("station")
    windows = lax.axis_size("dp")
    rows = width // LAYER
    dma = pltpu.SemaphoreType.DMA

    def swap(value, stride):
        return lax.ppermute(value, "station", [(s ^ stride, s) for s in range(stations)])

    def in_layer(values):
        return [swap(values[n], n + 1) for n in range(LAYER - 1)]

    def along(up, down):
        low = lax.ppermute(up, "station", [(s, (s + LAYER) % stations) for s in range(stations)])
        high = lax.ppermute(down, "station", [(s, (s - LAYER) % stations) for s in range(stations)])
        return low, high

    def other_window(value):
        return lax.ppermute(value, "dp", [(0, 1), (1, 0)])

    def flat(x):
        return x.reshape(span, width)

    q, k, v, g = flat(query_states), flat(key_states), flat(value_states), flat(grad_output)
    flat_shape = shape_of(span, width)
    part_shape = shape_of(2, rows, span)
    reach_shape = shape_of(2, rows, HOPS * span)
    layer_shape = shape_of(2, rows, LAYER * span)

    def gather(parts, after=()):
        return call(
            gather_kernel, [VMEM] * LAYER, [reach_shape, reach_shape, layer_shape], parts,
            name="gather", after=after,
        )

    g_across = swap(g, 2)
    mine, *parts = call(
        pack_kernel, [HBM] * 2, [part_shape] * LAYER, (k, v),
        [pltpu.VMEM((2, span, width), bf16), pltpu.VMEM((2, width, span), bf16), dma((2,))],
        limit=58, name="pack",
    )
    up, down, pair = gather((mine, *in_layer(parts)), (g_across,))
    mine, *parts, g_copy = call(
        project_kernel, [VMEM] * 3, [part_shape] * LAYER + [flat_shape],
        (q, g, out_weight), [pltpu.VMEM((2, width, span), bf16)], name="project",
    )
    up, *parts = lax.optimization_barrier((up, *parts))
    kv_low, kv_high = along(up, down)
    (g_pair,) = call(
        pair_kernel, [VMEM] * 2, [shape_of(2, span, width)], (g_copy, g_across), name="pair",
    )
    g_pairs = g_pair, swap(g_pair, 1)
    bias, dead = call(
        functools.partial(live_kernel, stations), [SMEM] * 2,
        [shape_of(16, LAYER * span, dtype=f32), shape_of(8, HOPS * span, dtype=f32)],
        (partner_ids, partner_count), name="live",
    )
    up, down, query = gather((mine, *in_layer(parts)), (bias, g_pairs[1]))
    qg_low, qg_high = along(up, down)
    stats_shape = shape_of(8, HOPS * span, dtype=f32)
    mixed, stats, up, down, probs, window = call(
        forward_kernel, [VMEM] * 5,
        [
            shape_of(rows, LAYER * span), shape_of(8, LAYER * span, dtype=f32),
            stats_shape, stats_shape,
            shape_of(LOCAL, BLOCKS * span, LAYER * span), shape_of(2, rows, BLOCKS * span),
        ],
        (pair, kv_low, kv_high, query, bias),
        [pltpu.VMEM((BLOCKS * span, LAYER * span), f32)],
        limit=20, name="forward",
    )
    stats_low, stats_high = along(up, down)

    send, part = call(
        weight_kernel, [VMEM] * 3,
        [shape_of(rows // 2, width), shape_of(rows // 2, width, dtype=f32)],
        (mixed, *g_pairs), [pltpu.VMEM((LAYER * span, width), bf16)], name="weight",
    )

    mine, to_sib, to_across, own_grad, query_token = call(
        query_grad_kernel, [VMEM] * 5,
        [part_shape, part_shape, shape_of(2, 2, rows, span), shape_of(2, rows, LAYER * span, dtype=f32)]
        + [TOKEN],
        (window, probs, query, stats, mixed),
        [pltpu.VMEM((BLOCKS * span, LAYER * span), bf16), pltpu.VMEM((rows, LAYER * span), bf16)],
        limit=20, name="query_grad", after=(send,),
    )
    across = swap(to_across, 2)
    (relay,) = call(
        relay_kernel, [VMEM] * 2, [shape_of(2, 2, rows, span)], (to_sib, across), name="relay"
    )
    relayed = swap(relay, 1)
    layer_output, grad_query, output_token = call(
        output_kernel, [VMEM] * 4, [flat_shape] * 2 + [TOKEN],
        (mine, across, relayed, out_weight), [pltpu.VMEM((2, width, span), bf16)], name="output",
    )

    mine, *parts, key_token = call(
        key_grad_kernel, [VMEM] * 7, [part_shape] * LAYER + [TOKEN],
        (pair, qg_low, qg_high, stats_low, stats_high, dead, own_grad),
        [pltpu.VMEM((2, rows, LAYER * span), bf16)], limit=20, name="key_grad",
    )
    key_parts = in_layer(parts)
    grad_key, grad_value, key_output_token = call(
        key_output_kernel, [VMEM] * LAYER, [flat_shape] * 2 + [TOKEN],
        (mine, *key_parts), [pltpu.VMEM((2, width, span), bf16)], name="key_output",
    )

    scale = 1.0 / math.sqrt(span * windows * stations)
    if windows == 2:
        count = rows // 4
        got = other_window(send)
        send, part = call(
            functools.partial(split_kernel, LAYER), [VMEM] * 2,
            [shape_of(count, width), shape_of(count, width, dtype=f32)],
            (part, got), name="split", after=(query_token, qg_low, qg_high),
        )

        def add_round(part, got, after=()):
            out = [shape_of(count, width)]
            return call(round_kernel, [VMEM] * 2, out, (part, got), name="add", after=after)[0]

        total = add_round(part, swap(send, LAYER), (stats_low, stats_high))
        stride = 2 * LAYER
        while stride < stations:
            total = add_round(total, swap(total, stride), (key_token, across))
            stride *= 2
        (total,) = call(
            functools.partial(join_kernel, LAYER, None), [VMEM] * 2, [shape_of(2 * count, width)],
            (total, swap(total, LAYER)), name="join", after=key_parts,
        )
        first, second = [], []
        for w in range(2):
            for s in range(stations):
                if s // 2 % 2 == w:
                    first.append((w * stations + s, w * stations + (s ^ 2)))
                else:
                    first.append((w * stations + s, (1 - w) * stations + s))
                    second.append((w * stations + s, (1 - w) * stations + (s ^ 2)))
        axes = ("dp", "station")
        (total,) = call(
            cross_kernel, [VMEM] * 3, [shape_of(4 * count, width)],
            (total, lax.ppermute(total, axes, first), lax.ppermute(total, axes, second)),
            name="cross", after=(output_token, key_output_token),
        )
        (grad_weight,) = call(
            functools.partial(join_kernel, 1, scale), [VMEM] * 2,
            [shape_of(8 * count, width, dtype=f32)], (total, swap(total, 1)), name="last",
        )
    else:
        start = lax.axis_index("station") % LAYER * rows
        all_grad = jnp.zeros((LAYER * span, width), bf16)
        for peer in range(LAYER):
            value = g_pairs[peer % 2][peer // 2]
            spot = lax.axis_index("station") % LAYER ^ peer
            all_grad = lax.dynamic_update_slice_in_dim(all_grad, value, spot * span, 0)
        mine = dot(mixed, all_grad, NN).astype(bf16)
        whole = lax.dynamic_update_slice_in_dim(jnp.zeros((width, width), bf16), mine, start, 0)
        whole = lax.psum_scatter(whole, "dp", scatter_dimension=0, tiled=True)
        grad_weight = lax.psum(whole.astype(f32), "station") * scale
    shape = query_states.shape
    return (
        layer_output.reshape(shape),
        grad_query.reshape(shape),
        grad_key.reshape(shape),
        grad_value.reshape(shape),
        grad_weight,
    )


def solution(mesh):
    split = P("dp", "station", None, None)
    return jax.shard_map(
        local,
        mesh=mesh,
        in_specs=(split, split, split, split, P(), P(), P()),
        out_specs=(split, split, split, split, P("dp", None)),
        check_vma=False,
    )
```

```python
import functools
import math

import jax
import jax.numpy as jnp
from jax import lax
from jax.experimental import pallas as pl
from jax.experimental.pallas import tpu as pltpu
from jax.sharding import PartitionSpec as P

HEADS = 12
PMAX = 6
HOPS = 3
LAYER = 4
LOCAL = HEADS // LAYER
BLOCKS = LAYER + 2 * HOPS
SLOTS = 2 * HOPS + 1
MIB = 1024 * 1024

neg_big = -1e30
bf16, f32 = jnp.bfloat16, jnp.float32
SMEM = pl.BlockSpec(memory_space=pltpu.SMEM)
VMEM = pl.BlockSpec(memory_space=pltpu.VMEM)
ANY = pl.BlockSpec(memory_space=pl.ANY)
HBM = pl.BlockSpec(memory_space=pltpu.HBM)
NN = (((1,), (0,)), ((), ()))
NT = (((1,), (1,)), ((), ()))
TN = (((0,), (0,)), ((), ()))


def dot(x, y, dims):
    return lax.dot_general(x, y, dims, preferred_element_type=f32)


def shape_of(*dims, dtype=bf16):
    return jax.ShapeDtypeStruct(dims, dtype)


TOKEN = shape_of(8, 128, dtype=f32)


def skip_refs(kernel, first, count, *refs):
    kernel(*refs[:first], *refs[first + count :])


def call(kernel, ins, outs, args, scratch=(), limit=8, name=None, after=()):
    ins, args = [*ins, *[ANY] * len(after)], (*args, *after)
    if after:
        kernel = functools.partial(skip_refs, kernel, len(args) - len(after), len(after))
    return pl.pallas_call(
        kernel,
        in_specs=ins,
        out_specs=[VMEM] * len(outs),
        out_shape=outs,
        scratch_shapes=list(scratch),
        compiler_params=pltpu.CompilerParams(vmem_limit_bytes=limit * MIB),
        cost_estimate=pl.CostEstimate(flops=1, bytes_accessed=1, transcendentals=0),
        name=name,
    )(*args)


def place(peer, size):
    position = jnp.bitwise_xor(lax.rem(lax.axis_index("station"), LAYER), peer)
    return pl.ds(pl.multiple_of(position * size, size), size)


def block(j, span):
    return slice(j * span, (j + 1) * span)


def readers(j):
    return max(0, j - 2 * HOPS), min(LAYER - 1, j)


def pack_kernel(k_ref, v_ref, *refs):
    outs, (natural, flipped, sems) = refs[:LAYER], refs[LAYER:]
    rows = outs[0].shape[1]
    copies = [
        pltpu.make_async_copy(ref, natural.at[n], sems.at[n]) for n, ref in enumerate((k_ref, v_ref))
    ]
    for copy in copies:
        copy.start()
    for n, copy in enumerate(copies):
        copy.wait()
        flipped[n] = natural[n].T
    for peer, out in enumerate(outs):
        out[...] = flipped[:, place(peer, rows)]


def project_kernel(q_ref, g_ref, weight_ref, *refs):
    outs, (copy_ref, flipped) = refs[:LAYER], refs[LAYER:]
    rows = outs[0].shape[1]
    copy_ref[...] = g_ref[...]
    flipped[0] = q_ref[...].T * bf16(1.0 / math.sqrt(flipped.shape[1] // HEADS))
    flipped[1] = dot(weight_ref[...], g_ref[...], NT).astype(bf16)
    for peer, out in enumerate(outs):
        out[...] = flipped[:, place(peer, rows)]


def pair_kernel(first_ref, second_ref, out_ref):
    out_ref[0] = first_ref[...]
    out_ref[1] = second_ref[...]


def relay_kernel(sib_ref, across_ref, out_ref):
    out_ref[0] = sib_ref[...]
    out_ref[1] = across_ref[1]


def gather_kernel(*refs):
    ins, (up_ref, down_ref, pair_ref) = refs[:LAYER], refs[LAYER:]
    span = ins[0].shape[2]
    for peer, ref in enumerate(ins):
        pair_ref[:, :, place(peer, span)] = ref[...]
    up_ref[...] = pair_ref[:, :, span:]
    down_ref[...] = pair_ref[:, :, : HOPS * span]


def live_kernel(station_count, ids_ref, count_ref, bias_ref, dead_ref):
    span = bias_ref.shape[1] // LAYER
    first = lax.axis_index("station") // LAYER * LAYER
    ones = jnp.ones((1, span), f32)

    def listed(reader, other):
        hit = jnp.int32(0)
        for j in range(PMAX):
            here = jnp.logical_and(ids_ref[reader, j] == other, j < count_ref[reader])
            hit = jnp.maximum(hit, here.astype(jnp.int32))
        return hit > 0

    for j in range(BLOCKS):
        outer = lax.rem(first + (j - HOPS) + station_count, station_count)
        low, high = readers(j)
        for i in range(low, high + 1):
            inner = first + i
            slot = j - i
            if slot == HOPS:
                bias_ref[j : j + 1, block(i, span)] = 0.0 * ones
            else:
                reads = jnp.where(listed(inner, outer), 0.0, neg_big)
                bias_ref[j : j + 1, block(i, span)] = reads * ones
            if not HOPS <= j < HOPS + LAYER:
                read_by = jnp.where(listed(outer, inner), 0.0, -neg_big)
                spot = slot if j < HOPS else slot - LAYER
                dead_ref[i : i + 1, block(spot, span)] = read_by * ones


def clear(ref, span):
    for j in range(BLOCKS):
        low, high = readers(j)
        for i in range(LAYER):
            if not low <= i <= high:
                ref[block(j, span), block(i, span)] = jnp.zeros((span, span), bf16)


def forward_kernel(
    pair_ref, low_ref, high_ref, query_ref, bias_ref,
    mixed_ref, stats_ref, stats_up, stats_down, probs_ref, window_ref,
    raw,
):
    rows = query_ref.shape[1]
    span = query_ref.shape[2] // LAYER
    head_width = rows // LOCAL
    reach = HOPS * span
    window_ref[:, :, :reach] = low_ref[...]
    window_ref[:, :, reach : reach + LAYER * span] = pair_ref[...]
    window_ref[:, :, reach + LAYER * span :] = high_ref[...]
    for head in range(LOCAL):
        clear(probs_ref.at[head], span)
        at = block(head, head_width)
        query = query_ref[0, at]
        tops = [None] * LAYER
        for j in range(BLOCKS):
            low, high = readers(j)
            cols = slice(low * span, (high + 1) * span)
            scores = dot(window_ref[0, at, block(j, span)], query[:, cols], TN)
            scores = scores + bias_ref[j : j + 1, cols]
            raw[block(j, span), cols] = scores
            here = jnp.max(scores, 0, keepdims=True)
            for i in range(low, high + 1):
                mine = here[:, block(i - low, span)]
                tops[i] = mine if tops[i] is None else jnp.maximum(tops[i], mine)
        top = jnp.concatenate(tops, 1)
        totals = [jnp.zeros((1, span), f32)] * LAYER
        for j in range(BLOCKS):
            low, high = readers(j)
            cols = slice(low * span, (high + 1) * span)
            weight = jnp.exp(raw[block(j, span), cols] - top[:, cols])
            raw[block(j, span), cols] = weight
            here = jnp.sum(weight, 0, keepdims=True)
            for i in range(low, high + 1):
                totals[i] = totals[i] + here[:, block(i - low, span)]
        total = jnp.concatenate(totals, 1)
        inverse = 1.0 / total
        for j in range(BLOCKS):
            low, high = readers(j)
            cols = slice(low * span, (high + 1) * span)
            probs_ref[head, block(j, span), cols] = (
                raw[block(j, span), cols] * inverse[:, cols]
            ).astype(bf16)
        mixed = dot(window_ref[1, at], probs_ref[head], NN).astype(bf16)
        mixed_ref[at] = mixed
        product = query_ref[1, at].astype(f32) * mixed.astype(f32)
        stats_ref[head : head + 1] = top + jnp.log(total)
        stats_ref[LOCAL + head : LOCAL + head + 1] = jnp.sum(product, 0, keepdims=True)
    stats_ref[2 * LOCAL :] = jnp.zeros((8 - 2 * LOCAL, LAYER * span), f32)
    stats_up[...] = stats_ref[:, span:]
    stats_down[...] = stats_ref[:, :reach]


def query_grad_kernel(
    window_ref, probs_ref, query_ref, stats_ref, mixed_ref, mine_ref, sib_ref, across_ref, own_ref,
    token_ref, grads, flipped
):
    rows = query_ref.shape[1]
    span = query_ref.shape[2] // LAYER
    head_width = rows // LOCAL
    scale = 1.0 / math.sqrt(head_width)
    inside = slice(HOPS * span, (HOPS + LAYER) * span)
    clear(grads, span)
    for head in range(LOCAL):
        at = block(head, head_width)
        grad = query_ref[1, at]
        delta = stats_ref[LOCAL + head : LOCAL + head + 1]
        for j in range(BLOCKS):
            low, high = readers(j)
            cols = slice(low * span, (high + 1) * span)
            back = dot(window_ref[1, at, block(j, span)], grad[:, cols], TN)
            prob = probs_ref[head, block(j, span), cols].astype(f32)
            grads[block(j, span), cols] = (prob * (back - delta[:, cols])).astype(bf16)
        flipped[at] = (dot(window_ref[0, at], grads[...], NN) * scale).astype(bf16)
        own_ref[0, at] = dot(query_ref[0, at], grads[inside], NT)
        own_ref[1, at] = dot(grad, probs_ref[head, inside], NT)
    for peer, out in enumerate((mine_ref, sib_ref, across_ref.at[0], across_ref.at[1])):
        out[0] = mixed_ref[:, place(peer, span)]
        out[1] = flipped[:, place(peer, span)]
    token_ref[...] = jnp.zeros_like(token_ref)


def key_grad_kernel(
    pair_ref, low_ref, high_ref, stats_low, stats_high, dead_ref, own_ref, *refs
):
    outs, (token_ref, flipped) = refs[:LAYER], refs[LAYER:]
    rows = pair_ref.shape[1]
    span = pair_ref.shape[2] // LAYER
    head_width = rows // LOCAL
    for head in range(LOCAL):
        at = block(head, head_width)
        log_row = slice(head, head + 1)
        delta_row = slice(LOCAL + head, LOCAL + head + 1)
        for i in range(LAYER):
            own = block(i, span)

            def outside(low, high):
                sides = [low[:, i * span :]] if i < HOPS else []
                return jnp.concatenate(sides + ([high[:, : i * span]] if i else []), 1)

            query = outside(low_ref[0, at], high_ref[0, at])
            grad = outside(low_ref[1, at], high_ref[1, at])
            log_sum = outside(stats_low[log_row], stats_high[log_row]) + dead_ref[i : i + 1]
            delta = outside(stats_low[delta_row], stats_high[delta_row])
            prob = jnp.exp(dot(pair_ref[0, at, own], query, TN) - log_sum)
            back = dot(pair_ref[1, at, own], grad, TN)
            grads = (prob * (back - delta)).astype(bf16)
            keys = own_ref[0, at, own] + dot(query, grads, NT)
            values = own_ref[1, at, own] + dot(grad, prob.astype(bf16), NT)
            flipped[0, at, own] = keys.astype(bf16)
            flipped[1, at, own] = values.astype(bf16)
    for peer, out in enumerate(outs):
        out[...] = flipped[:, :, place(peer, span)]
    token_ref[...] = jnp.zeros_like(token_ref)


def output_kernel(
    mine_ref, across_ref, sib_ref, weight_ref, out_ref, dq_ref, token_ref, flipped
):
    ins = mine_ref, sib_ref.at[0], across_ref.at[0], sib_ref.at[1]
    for peer, ref in enumerate(ins):
        flipped[:, place(peer, ref.shape[1])] = ref[...]
    out_ref[...] = dot(flipped[0], weight_ref[...], TN).astype(bf16)
    dq_ref[...] = flipped[1].T
    token_ref[...] = jnp.zeros_like(token_ref)


def key_output_kernel(*refs):
    ins, (dk_ref, dv_ref, token_ref, flipped) = refs[:LAYER], refs[LAYER:]
    for peer, ref in enumerate(ins):
        flipped[:, place(peer, ref.shape[1])] = ref[...]
    dk_ref[...] = flipped[0].T
    dv_ref[...] = flipped[1].T
    token_ref[...] = jnp.zeros_like(token_ref)


def halves(bit, half):
    send = pl.ds(pl.multiple_of((1 - bit) * half, half), half)
    keep = pl.ds(pl.multiple_of(bit * half, half), half)
    return send, keep


def bit_of(stride):
    return lax.rem(lax.axis_index("station") // stride, 2)


def weight_kernel(mixed_ref, mine_ref, sib_ref, send_ref, keep_ref, right):
    for n in range(2):
        right[place(2 * n, mine_ref.shape[1])] = mine_ref[n]
        right[place(2 * n + 1, mine_ref.shape[1])] = sib_ref[n]
    send, keep = halves(lax.rem(lax.axis_index("dp"), 2), send_ref.shape[0])
    send_ref[...] = dot(mixed_ref[send], right[...], NN).astype(bf16)
    keep_ref[...] = dot(mixed_ref[keep], right[...], NN)


def split_kernel(stride, part_ref, got_ref, send_ref, keep_ref):
    send, keep = halves(bit_of(stride), send_ref.shape[0])
    send_ref[...] = (part_ref[send] + got_ref[send].astype(f32)).astype(bf16)
    keep_ref[...] = part_ref[keep] + got_ref[keep].astype(f32)


def round_kernel(part_ref, got_ref, out_ref):
    out_ref[...] = (part_ref[...].astype(f32) + got_ref[...].astype(f32)).astype(bf16)


def join_kernel(stride, scale, mine_ref, got_ref, out_ref):
    other, here = halves(bit_of(stride), mine_ref.shape[0])
    for at, ref in ((here, mine_ref), (other, got_ref)):
        value = ref[...]
        if scale is not None:
            value = value.astype(f32) * scale
        out_ref[at] = value


def cross_kernel(mine_ref, second_ref, first_ref, out_ref):
    window = lax.rem(lax.axis_index("dp"), 2)
    other, here = halves(window, mine_ref.shape[0])
    at_home = bit_of(2) == window
    mine, first, second = mine_ref[...], first_ref[...], second_ref[...]
    out_ref[here] = jnp.where(at_home, mine, first)
    out_ref[other] = jnp.where(at_home, first, second)


def local(
    query_states, key_states, value_states, grad_output, out_weight, partner_ids, partner_count
):
    span, width = query_states.shape[2:]
    stations = lax.axis_size("station")
    windows = lax.axis_size("dp")
    rows = width // LAYER
    dma = pltpu.SemaphoreType.DMA

    def swap(value, stride):
        return lax.ppermute(value, "station", [(s ^ stride, s) for s in range(stations)])

    def in_layer(values):
        return [swap(values[n], n + 1) for n in range(LAYER - 1)]

    def along(up, down):
        low = lax.ppermute(up, "station", [(s, (s + LAYER) % stations) for s in range(stations)])
        high = lax.ppermute(down, "station", [(s, (s - LAYER) % stations) for s in range(stations)])
        return low, high

    def other_window(value):
        return lax.ppermute(value, "dp", [(0, 1), (1, 0)])

    def flat(x):
        return x.reshape(span, width)

    q, k, v, g = flat(query_states), flat(key_states), flat(value_states), flat(grad_output)
    flat_shape = shape_of(span, width)
    part_shape = shape_of(2, rows, span)
    reach_shape = shape_of(2, rows, HOPS * span)
    layer_shape = shape_of(2, rows, LAYER * span)

    def gather(parts, after=()):
        return call(
            gather_kernel, [VMEM] * LAYER, [reach_shape, reach_shape, layer_shape], parts,
            name="gather", after=after,
        )

    g_across = swap(g, 2)
    mine, *parts = call(
        pack_kernel, [HBM] * 2, [part_shape] * LAYER, (k, v),
        [pltpu.VMEM((2, span, width), bf16), pltpu.VMEM((2, width, span), bf16), dma((2,))],
        limit=58, name="pack",
    )
    q, *parts = lax.optimization_barrier((q, *parts))
    parts = in_layer(parts)
    up, down, pair = gather((mine, *parts), (g_across,))
    mine, *query_parts, g_copy = call(
        project_kernel, [VMEM] * 3, [part_shape] * LAYER + [flat_shape],
        (q, g, out_weight), [pltpu.VMEM((2, width, span), bf16)], name="project",
    )
    up, *query_parts = lax.optimization_barrier((up, *query_parts))
    kv_low, kv_high = along(up, down)
    (g_pair,) = call(
        pair_kernel, [VMEM] * 2, [shape_of(2, span, width)], (g_copy, g_across), name="pair",
        after=parts,
    )
    g_pairs = g_pair, swap(g_pair, 1)
    bias, dead = call(
        functools.partial(live_kernel, stations), [SMEM] * 2,
        [shape_of(16, LAYER * span, dtype=f32), shape_of(8, HOPS * span, dtype=f32)],
        (partner_ids, partner_count), name="live",
    )
    up, down, query = gather((mine, *in_layer(query_parts)), (bias, g_pairs[1]))
    qg_low, qg_high = along(up, down)
    stats_shape = shape_of(8, HOPS * span, dtype=f32)
    mixed, stats, up, down, probs, window = call(
        forward_kernel, [VMEM] * 5,
        [
            shape_of(rows, LAYER * span), shape_of(8, LAYER * span, dtype=f32),
            stats_shape, stats_shape,
            shape_of(LOCAL, BLOCKS * span, LAYER * span), shape_of(2, rows, BLOCKS * span),
        ],
        (pair, kv_low, kv_high, query, bias),
        [pltpu.VMEM((BLOCKS * span, LAYER * span), f32)],
        limit=20, name="forward",
    )
    stats_low, stats_high = along(up, down)

    send, part = call(
        weight_kernel, [VMEM] * 3,
        [shape_of(rows // 2, width), shape_of(rows // 2, width, dtype=f32)],
        (mixed, *g_pairs), [pltpu.VMEM((LAYER * span, width), bf16)], name="weight",
    )

    mine, to_sib, to_across, own_grad, query_token = call(
        query_grad_kernel, [VMEM] * 5,
        [part_shape, part_shape, shape_of(2, 2, rows, span), shape_of(2, rows, LAYER * span, dtype=f32)]
        + [TOKEN],
        (window, probs, query, stats, mixed),
        [pltpu.VMEM((BLOCKS * span, LAYER * span), bf16), pltpu.VMEM((rows, LAYER * span), bf16)],
        limit=20, name="query_grad", after=(send,),
    )
    across = swap(to_across, 2)
    (relay,) = call(
        relay_kernel, [VMEM] * 2, [shape_of(2, 2, rows, span)], (to_sib, across), name="relay"
    )
    relayed = swap(relay, 1)
    layer_output, grad_query, output_token = call(
        output_kernel, [VMEM] * 4, [flat_shape] * 2 + [TOKEN],
        (mine, across, relayed, out_weight), [pltpu.VMEM((2, width, span), bf16)], name="output",
    )

    mine, *parts, key_token = call(
        key_grad_kernel, [VMEM] * 7, [part_shape] * LAYER + [TOKEN],
        (pair, qg_low, qg_high, stats_low, stats_high, dead, own_grad),
        [pltpu.VMEM((2, rows, LAYER * span), bf16)], limit=20, name="key_grad",
    )
    key_parts = in_layer(parts)
    grad_key, grad_value, key_output_token = call(
        key_output_kernel, [VMEM] * LAYER, [flat_shape] * 2 + [TOKEN],
        (mine, *key_parts), [pltpu.VMEM((2, width, span), bf16)], name="key_output",
    )

    scale = 1.0 / math.sqrt(span * windows * stations)
    if windows == 2:
        count = rows // 4
        got = other_window(send)
        send, part = call(
            functools.partial(split_kernel, LAYER), [VMEM] * 2,
            [shape_of(count, width), shape_of(count, width, dtype=f32)],
            (part, got), name="split", after=(query_token, qg_low, qg_high, stats_low, stats_high),
        )

        def add_round(part, got, after=()):
            out = [shape_of(count, width)]
            return call(round_kernel, [VMEM] * 2, out, (part, got), name="add", after=after)[0]

        total = add_round(part, swap(send, LAYER), (key_token,))
        stride = 2 * LAYER
        while stride < stations:
            total = add_round(total, swap(total, stride), (across,))
            stride *= 2
        (total,) = call(
            functools.partial(join_kernel, LAYER, None), [VMEM] * 2, [shape_of(2 * count, width)],
            (total, swap(total, LAYER)), name="join", after=key_parts,
        )
        first, second = [], []
        for w in range(2):
            for s in range(stations):
                if s // 2 % 2 == w:
                    first.append((w * stations + s, w * stations + (s ^ 2)))
                else:
                    first.append((w * stations + s, (1 - w) * stations + s))
                    second.append((w * stations + s, (1 - w) * stations + (s ^ 2)))
        axes = ("dp", "station")
        (total,) = call(
            cross_kernel, [VMEM] * 3, [shape_of(4 * count, width)],
            (total, lax.ppermute(total, axes, second), lax.ppermute(total, axes, first)),
            name="cross", after=(output_token, key_output_token),
        )
        (grad_weight,) = call(
            functools.partial(join_kernel, 1, scale), [VMEM] * 2,
            [shape_of(8 * count, width, dtype=f32)], (total, swap(total, 1)), name="last",
        )
    else:
        start = lax.axis_index("station") % LAYER * rows
        all_grad = jnp.zeros((LAYER * span, width), bf16)
        for peer in range(LAYER):
            value = g_pairs[peer % 2][peer // 2]
            spot = lax.axis_index("station") % LAYER ^ peer
            all_grad = lax.dynamic_update_slice_in_dim(all_grad, value, spot * span, 0)
        mine = dot(mixed, all_grad, NN).astype(bf16)
        whole = lax.dynamic_update_slice_in_dim(jnp.zeros((width, width), bf16), mine, start, 0)
        whole = lax.psum_scatter(whole, "dp", scatter_dimension=0, tiled=True)
        grad_weight = lax.psum(whole.astype(f32), "station") * scale
    shape = query_states.shape
    return (
        layer_output.reshape(shape),
        grad_query.reshape(shape),
        grad_key.reshape(shape),
        grad_value.reshape(shape),
        grad_weight,
    )


def solution(mesh):
    split = P("dp", "station", None, None)
    return jax.shard_map(
        local,
        mesh=mesh,
        in_specs=(split, split, split, split, P(), P(), P()),
        out_specs=(split, split, split, split, P("dp", None)),
        check_vma=False,
    )
```

```python
import functools
import math

import jax
import jax.numpy as jnp
from jax import lax
from jax.experimental import pallas as pl
from jax.experimental.pallas import tpu as pltpu
from jax.sharding import PartitionSpec as P

HEADS = 12
PMAX = 6
HOPS = 3
LAYER = 4
LOCAL = HEADS // LAYER
BLOCKS = LAYER + 2 * HOPS
SLOTS = 2 * HOPS + 1
MIB = 1024 * 1024

neg_big = -1e30
bf16, f32 = jnp.bfloat16, jnp.float32
SMEM = pl.BlockSpec(memory_space=pltpu.SMEM)
VMEM = pl.BlockSpec(memory_space=pltpu.VMEM)
ANY = pl.BlockSpec(memory_space=pl.ANY)
HBM = pl.BlockSpec(memory_space=pltpu.HBM)
NN = (((1,), (0,)), ((), ()))
NT = (((1,), (1,)), ((), ()))
TN = (((0,), (0,)), ((), ()))


def dot(x, y, dims):
    return lax.dot_general(x, y, dims, preferred_element_type=f32)


def shape_of(*dims, dtype=bf16):
    return jax.ShapeDtypeStruct(dims, dtype)


TOKEN = shape_of(8, 128, dtype=f32)


def skip_refs(kernel, first, count, *refs):
    kernel(*refs[:first], *refs[first + count :])


def call(kernel, ins, outs, args, scratch=(), limit=8, name=None, after=()):
    ins, args = [*ins, *[ANY] * len(after)], (*args, *after)
    if after:
        kernel = functools.partial(skip_refs, kernel, len(args) - len(after), len(after))
    return pl.pallas_call(
        kernel,
        in_specs=ins,
        out_specs=[VMEM] * len(outs),
        out_shape=outs,
        scratch_shapes=list(scratch),
        compiler_params=pltpu.CompilerParams(vmem_limit_bytes=limit * MIB),
        cost_estimate=pl.CostEstimate(flops=1, bytes_accessed=1, transcendentals=0),
        name=name,
    )(*args)


def place(peer, size):
    position = jnp.bitwise_xor(lax.rem(lax.axis_index("station"), LAYER), peer)
    return pl.ds(pl.multiple_of(position * size, size), size)


def block(j, span):
    return slice(j * span, (j + 1) * span)


def readers(j):
    return max(0, j - 2 * HOPS), min(LAYER - 1, j)


def pack_kernel(k_ref, v_ref, *refs):
    outs, (natural, flipped, sems) = refs[:LAYER], refs[LAYER:]
    rows = outs[0].shape[1]
    copies = [
        pltpu.make_async_copy(ref, natural.at[n], sems.at[n]) for n, ref in enumerate((k_ref, v_ref))
    ]
    for copy in copies:
        copy.start()
    for n, copy in enumerate(copies):
        copy.wait()
        flipped[n] = natural[n].T
    for peer, out in enumerate(outs):
        out[...] = flipped[:, place(peer, rows)]


def project_kernel(q_ref, g_ref, weight_ref, *refs):
    outs, (copy_ref, flipped) = refs[:LAYER], refs[LAYER:]
    rows = outs[0].shape[1]
    copy_ref[...] = g_ref[...]
    flipped[0] = q_ref[...].T * bf16(1.0 / math.sqrt(flipped.shape[1] // HEADS))
    flipped[1] = dot(weight_ref[...], g_ref[...], NT).astype(bf16)
    for peer, out in enumerate(outs):
        out[...] = flipped[:, place(peer, rows)]


def pair_kernel(first_ref, second_ref, out_ref):
    out_ref[0] = first_ref[...]
    out_ref[1] = second_ref[...]


def relay_kernel(sib_ref, across_ref, out_ref):
    out_ref[0] = sib_ref[...]
    out_ref[1] = across_ref[1]


def gather_kernel(*refs):
    ins, (up_ref, down_ref, pair_ref) = refs[:LAYER], refs[LAYER:]
    span = ins[0].shape[2]
    for peer, ref in enumerate(ins):
        pair_ref[:, :, place(peer, span)] = ref[...]
    up_ref[...] = pair_ref[:, :, span:]
    down_ref[...] = pair_ref[:, :, : HOPS * span]


def live_kernel(station_count, ids_ref, count_ref, bias_ref, dead_ref):
    span = bias_ref.shape[1] // LAYER
    first = lax.axis_index("station") // LAYER * LAYER
    ones = jnp.ones((1, span), f32)

    def listed(reader, other):
        hit = jnp.int32(0)
        for j in range(PMAX):
            here = jnp.logical_and(ids_ref[reader, j] == other, j < count_ref[reader])
            hit = jnp.maximum(hit, here.astype(jnp.int32))
        return hit > 0

    for j in range(BLOCKS):
        outer = lax.rem(first + (j - HOPS) + station_count, station_count)
        low, high = readers(j)
        for i in range(low, high + 1):
            inner = first + i
            slot = j - i
            if slot == HOPS:
                bias_ref[j : j + 1, block(i, span)] = 0.0 * ones
            else:
                reads = jnp.where(listed(inner, outer), 0.0, neg_big)
                bias_ref[j : j + 1, block(i, span)] = reads * ones
            if not HOPS <= j < HOPS + LAYER:
                read_by = jnp.where(listed(outer, inner), 0.0, -neg_big)
                spot = slot if j < HOPS else slot - LAYER
                dead_ref[i : i + 1, block(spot, span)] = read_by * ones


def clear(ref, span):
    for j in range(BLOCKS):
        low, high = readers(j)
        for i in range(LAYER):
            if not low <= i <= high:
                ref[block(j, span), block(i, span)] = jnp.zeros((span, span), bf16)


def forward_kernel(
    pair_ref, low_ref, high_ref, query_ref, bias_ref,
    mixed_ref, stats_ref, stats_up, stats_down, probs_ref, window_ref,
    raw,
):
    rows = query_ref.shape[1]
    span = query_ref.shape[2] // LAYER
    head_width = rows // LOCAL
    reach = HOPS * span
    window_ref[:, :, :reach] = low_ref[...]
    window_ref[:, :, reach : reach + LAYER * span] = pair_ref[...]
    window_ref[:, :, reach + LAYER * span :] = high_ref[...]
    for head in range(LOCAL):
        clear(probs_ref.at[head], span)
        at = block(head, head_width)
        query = query_ref[0, at]
        tops = [None] * LAYER
        for j in range(BLOCKS):
            low, high = readers(j)
            cols = slice(low * span, (high + 1) * span)
            scores = dot(window_ref[0, at, block(j, span)], query[:, cols], TN)
            scores = scores + bias_ref[j : j + 1, cols]
            raw[block(j, span), cols] = scores
            here = jnp.max(scores, 0, keepdims=True)
            for i in range(low, high + 1):
                mine = here[:, block(i - low, span)]
                tops[i] = mine if tops[i] is None else jnp.maximum(tops[i], mine)
        top = jnp.concatenate(tops, 1)
        totals = [jnp.zeros((1, span), f32)] * LAYER
        for j in range(BLOCKS):
            low, high = readers(j)
            cols = slice(low * span, (high + 1) * span)
            weight = jnp.exp(raw[block(j, span), cols] - top[:, cols])
            raw[block(j, span), cols] = weight
            here = jnp.sum(weight, 0, keepdims=True)
            for i in range(low, high + 1):
                totals[i] = totals[i] + here[:, block(i - low, span)]
        total = jnp.concatenate(totals, 1)
        inverse = 1.0 / total
        for j in range(BLOCKS):
            low, high = readers(j)
            cols = slice(low * span, (high + 1) * span)
            probs_ref[head, block(j, span), cols] = (
                raw[block(j, span), cols] * inverse[:, cols]
            ).astype(bf16)
        mixed = dot(window_ref[1, at], probs_ref[head], NN).astype(bf16)
        mixed_ref[at] = mixed
        product = query_ref[1, at].astype(f32) * mixed.astype(f32)
        stats_ref[head : head + 1] = top + jnp.log(total)
        stats_ref[LOCAL + head : LOCAL + head + 1] = jnp.sum(product, 0, keepdims=True)
    stats_ref[2 * LOCAL :] = jnp.zeros((8 - 2 * LOCAL, LAYER * span), f32)
    stats_up[...] = stats_ref[:, span:]
    stats_down[...] = stats_ref[:, :reach]


def query_grad_kernel(
    window_ref, probs_ref, query_ref, stats_ref, mixed_ref, mine_ref, sib_ref, across_ref, own_ref,
    token_ref, grads, flipped
):
    rows = query_ref.shape[1]
    span = query_ref.shape[2] // LAYER
    head_width = rows // LOCAL
    scale = 1.0 / math.sqrt(head_width)
    inside = slice(HOPS * span, (HOPS + LAYER) * span)
    clear(grads, span)
    for head in range(LOCAL):
        at = block(head, head_width)
        grad = query_ref[1, at]
        delta = stats_ref[LOCAL + head : LOCAL + head + 1]
        for j in range(BLOCKS):
            low, high = readers(j)
            cols = slice(low * span, (high + 1) * span)
            back = dot(window_ref[1, at, block(j, span)], grad[:, cols], TN)
            prob = probs_ref[head, block(j, span), cols].astype(f32)
            grads[block(j, span), cols] = (prob * (back - delta[:, cols])).astype(bf16)
        flipped[at] = (dot(window_ref[0, at], grads[...], NN) * scale).astype(bf16)
        own_ref[0, at] = dot(query_ref[0, at], grads[inside], NT)
        own_ref[1, at] = dot(grad, probs_ref[head, inside], NT)
    for peer, out in enumerate((mine_ref, sib_ref, across_ref.at[0], across_ref.at[1])):
        out[0] = mixed_ref[:, place(peer, span)]
        out[1] = flipped[:, place(peer, span)]
    token_ref[...] = jnp.zeros_like(token_ref)


def key_grad_kernel(
    pair_ref, low_ref, high_ref, stats_low, stats_high, dead_ref, own_ref, *refs
):
    outs, (token_ref, flipped) = refs[:LAYER], refs[LAYER:]
    rows = pair_ref.shape[1]
    span = pair_ref.shape[2] // LAYER
    head_width = rows // LOCAL
    for head in range(LOCAL):
        at = block(head, head_width)
        log_row = slice(head, head + 1)
        delta_row = slice(LOCAL + head, LOCAL + head + 1)
        for i in range(LAYER):
            own = block(i, span)

            def outside(low, high):
                sides = [low[:, i * span :]] if i < HOPS else []
                return jnp.concatenate(sides + ([high[:, : i * span]] if i else []), 1)

            query = outside(low_ref[0, at], high_ref[0, at])
            grad = outside(low_ref[1, at], high_ref[1, at])
            log_sum = outside(stats_low[log_row], stats_high[log_row]) + dead_ref[i : i + 1]
            delta = outside(stats_low[delta_row], stats_high[delta_row])
            prob = jnp.exp(dot(pair_ref[0, at, own], query, TN) - log_sum)
            back = dot(pair_ref[1, at, own], grad, TN)
            grads = (prob * (back - delta)).astype(bf16)
            keys = own_ref[0, at, own] + dot(query, grads, NT)
            values = own_ref[1, at, own] + dot(grad, prob.astype(bf16), NT)
            flipped[0, at, own] = keys.astype(bf16)
            flipped[1, at, own] = values.astype(bf16)
    for peer, out in enumerate(outs):
        out[...] = flipped[:, :, place(peer, span)]
    token_ref[...] = jnp.zeros_like(token_ref)


def output_kernel(
    mine_ref, across_ref, sib_ref, weight_ref, out_ref, dq_ref, token_ref, flipped
):
    ins = mine_ref, sib_ref.at[0], across_ref.at[0], sib_ref.at[1]
    for peer, ref in enumerate(ins):
        flipped[:, place(peer, ref.shape[1])] = ref[...]
    out_ref[...] = dot(flipped[0], weight_ref[...], TN).astype(bf16)
    dq_ref[...] = flipped[1].T
    token_ref[...] = jnp.zeros_like(token_ref)


def key_output_kernel(*refs):
    ins, (dk_ref, dv_ref, token_ref, flipped) = refs[:LAYER], refs[LAYER:]
    for peer, ref in enumerate(ins):
        flipped[:, place(peer, ref.shape[1])] = ref[...]
    dk_ref[...] = flipped[0].T
    dv_ref[...] = flipped[1].T
    token_ref[...] = jnp.zeros_like(token_ref)


def halves(bit, half):
    send = pl.ds(pl.multiple_of((1 - bit) * half, half), half)
    keep = pl.ds(pl.multiple_of(bit * half, half), half)
    return send, keep


def bit_of(stride):
    return lax.rem(lax.axis_index("station") // stride, 2)


def weight_kernel(mixed_ref, mine_ref, sib_ref, send_ref, keep_ref, right):
    for n in range(2):
        right[place(2 * n, mine_ref.shape[1])] = mine_ref[n]
        right[place(2 * n + 1, mine_ref.shape[1])] = sib_ref[n]
    send, keep = halves(lax.rem(lax.axis_index("dp"), 2), send_ref.shape[0])
    send_ref[...] = dot(mixed_ref[send], right[...], NN).astype(bf16)
    keep_ref[...] = dot(mixed_ref[keep], right[...], NN)


def split_kernel(stride, part_ref, got_ref, send_ref, keep_ref):
    send, keep = halves(bit_of(stride), send_ref.shape[0])
    send_ref[...] = (part_ref[send] + got_ref[send].astype(f32)).astype(bf16)
    keep_ref[...] = part_ref[keep] + got_ref[keep].astype(f32)


def round_kernel(part_ref, got_ref, out_ref):
    out_ref[...] = (part_ref[...].astype(f32) + got_ref[...].astype(f32)).astype(bf16)


def join_kernel(stride, scale, mine_ref, got_ref, out_ref):
    other, here = halves(bit_of(stride), mine_ref.shape[0])
    for at, ref in ((here, mine_ref), (other, got_ref)):
        value = ref[...]
        if scale is not None:
            value = value.astype(f32) * scale
        out_ref[at] = value


def cross_kernel(mine_ref, second_ref, first_ref, out_ref):
    window = lax.rem(lax.axis_index("dp"), 2)
    other, here = halves(window, mine_ref.shape[0])
    at_home = bit_of(2) == window
    mine, first, second = mine_ref[...], first_ref[...], second_ref[...]
    out_ref[here] = jnp.where(at_home, mine, first)
    out_ref[other] = jnp.where(at_home, first, second)


def local(
    query_states, key_states, value_states, grad_output, out_weight, partner_ids, partner_count
):
    span, width = query_states.shape[2:]
    stations = lax.axis_size("station")
    windows = lax.axis_size("dp")
    rows = width // LAYER
    dma = pltpu.SemaphoreType.DMA

    def swap(value, stride):
        return lax.ppermute(value, "station", [(s ^ stride, s) for s in range(stations)])

    def in_layer(values):
        return [swap(values[n], n + 1) for n in range(LAYER - 1)]

    def along(up, down):
        low = lax.ppermute(up, "station", [(s, (s + LAYER) % stations) for s in range(stations)])
        high = lax.ppermute(down, "station", [(s, (s - LAYER) % stations) for s in range(stations)])
        return low, high

    def other_window(value):
        return lax.ppermute(value, "dp", [(0, 1), (1, 0)])

    def flat(x):
        return x.reshape(span, width)

    q, k, v, g = flat(query_states), flat(key_states), flat(value_states), flat(grad_output)
    flat_shape = shape_of(span, width)
    part_shape = shape_of(2, rows, span)
    reach_shape = shape_of(2, rows, HOPS * span)
    layer_shape = shape_of(2, rows, LAYER * span)

    def gather(parts, after=()):
        return call(
            gather_kernel, [VMEM] * LAYER, [reach_shape, reach_shape, layer_shape], parts,
            name="gather", after=after,
        )

    g_across = swap(g, 2)
    mine, *parts = call(
        pack_kernel, [HBM] * 2, [part_shape] * LAYER, (k, v),
        [pltpu.VMEM((2, span, width), bf16), pltpu.VMEM((2, width, span), bf16), dma((2,))],
        limit=58, name="pack",
    )
    q, *parts = lax.optimization_barrier((q, *parts))
    parts = in_layer(parts)
    up, down, pair = gather((mine, *parts), (g_across,))
    mine, *query_parts, g_copy = call(
        project_kernel, [VMEM] * 3, [part_shape] * LAYER + [flat_shape],
        (q, g, out_weight), [pltpu.VMEM((2, width, span), bf16)], name="project",
    )
    up, *query_parts = lax.optimization_barrier((up, *query_parts))
    kv_low, kv_high = along(up, down)
    (g_pair,) = call(
        pair_kernel, [VMEM] * 2, [shape_of(2, span, width)], (g_copy, g_across), name="pair",
        after=parts,
    )
    g_pairs = g_pair, swap(g_pair, 1)
    bias, dead = call(
        functools.partial(live_kernel, stations), [SMEM] * 2,
        [shape_of(16, LAYER * span, dtype=f32), shape_of(8, HOPS * span, dtype=f32)],
        (partner_ids, partner_count), name="live",
    )
    up, down, query = gather((mine, *in_layer(query_parts)), (bias, g_pairs[1]))
    qg_low, qg_high = along(up, down)
    stats_shape = shape_of(8, HOPS * span, dtype=f32)
    mixed, stats, up, down, probs, window = call(
        forward_kernel, [VMEM] * 5,
        [
            shape_of(rows, LAYER * span), shape_of(8, LAYER * span, dtype=f32),
            stats_shape, stats_shape,
            shape_of(LOCAL, BLOCKS * span, LAYER * span), shape_of(2, rows, BLOCKS * span),
        ],
        (pair, kv_low, kv_high, query, bias),
        [pltpu.VMEM((BLOCKS * span, LAYER * span), f32)],
        limit=20, name="forward",
    )
    stats_low, stats_high = along(up, down)

    send, part = call(
        weight_kernel, [VMEM] * 3,
        [shape_of(rows // 2, width), shape_of(rows // 2, width, dtype=f32)],
        (mixed, *g_pairs), [pltpu.VMEM((LAYER * span, width), bf16)], name="weight",
    )

    own_return, to_sib, to_across, own_grad, query_token = call(
        query_grad_kernel, [VMEM] * 5,
        [part_shape, part_shape, shape_of(2, 2, rows, span), shape_of(2, rows, LAYER * span, dtype=f32)]
        + [TOKEN],
        (window, probs, query, stats, mixed),
        [pltpu.VMEM((BLOCKS * span, LAYER * span), bf16), pltpu.VMEM((rows, LAYER * span), bf16)],
        limit=20, name="query_grad", after=(send,),
    )
    def first_return(across):
        (relay,) = call(
            relay_kernel, [VMEM] * 2, [shape_of(2, 2, rows, span)], (to_sib, across), name="relay"
        )
        relayed = swap(relay, 1)
        layer_output, grad_query, output_token = call(
            output_kernel, [VMEM] * 4, [flat_shape] * 2 + [TOKEN],
            (own_return, across, relayed, out_weight), [pltpu.VMEM((2, width, span), bf16)], name="output",
        )
        return layer_output, grad_query, output_token

    mine, *parts, key_token = call(
        key_grad_kernel, [VMEM] * 7, [part_shape] * LAYER + [TOKEN],
        (pair, qg_low, qg_high, stats_low, stats_high, dead, own_grad),
        [pltpu.VMEM((2, rows, LAYER * span), bf16)], limit=20, name="key_grad",
    )
    key_parts = in_layer(parts)
    grad_key, grad_value, key_output_token = call(
        key_output_kernel, [VMEM] * LAYER, [flat_shape] * 2 + [TOKEN],
        (mine, *key_parts), [pltpu.VMEM((2, width, span), bf16)], name="key_output",
    )

    scale = 1.0 / math.sqrt(span * windows * stations)
    if windows == 2:
        count = rows // 4
        got = other_window(send)
        send, part = call(
            functools.partial(split_kernel, LAYER), [VMEM] * 2,
            [shape_of(count, width), shape_of(count, width, dtype=f32)],
            (part, got), name="split", after=(query_token, qg_low, qg_high, stats_low, stats_high),
        )

        send, to_across = lax.optimization_barrier((send, to_across))
        across = swap(to_across, 2)
        layer_output, grad_query, output_token = first_return(across)

        def add_round(part, got, after=()):
            out = [shape_of(count, width)]
            return call(round_kernel, [VMEM] * 2, out, (part, got), name="add", after=after)[0]

        total = add_round(part, swap(send, LAYER), (key_token,))
        stride = 2 * LAYER
        while stride < stations:
            total = add_round(total, swap(total, stride), (across,))
            stride *= 2
        (total,) = call(
            functools.partial(join_kernel, LAYER, None), [VMEM] * 2, [shape_of(2 * count, width)],
            (total, swap(total, LAYER)), name="join", after=key_parts,
        )
        first, second = [], []
        for w in range(2):
            for s in range(stations):
                if s // 2 % 2 == w:
                    first.append((w * stations + s, w * stations + (s ^ 2)))
                else:
                    first.append((w * stations + s, (1 - w) * stations + s))
                    second.append((w * stations + s, (1 - w) * stations + (s ^ 2)))
        axes = ("dp", "station")
        (total,) = call(
            cross_kernel, [VMEM] * 3, [shape_of(4 * count, width)],
            (total, lax.ppermute(total, axes, second), lax.ppermute(total, axes, first)),
            name="cross", after=(output_token, key_output_token),
        )
        (grad_weight,) = call(
            functools.partial(join_kernel, 1, scale), [VMEM] * 2,
            [shape_of(8 * count, width, dtype=f32)], (total, swap(total, 1)), name="last",
        )
    else:
        layer_output, grad_query, _ = first_return(swap(to_across, 2))
        start = lax.axis_index("station") % LAYER * rows
        all_grad = jnp.zeros((LAYER * span, width), bf16)
        for peer in range(LAYER):
            value = g_pairs[peer % 2][peer // 2]
            spot = lax.axis_index("station") % LAYER ^ peer
            all_grad = lax.dynamic_update_slice_in_dim(all_grad, value, spot * span, 0)
        mine = dot(mixed, all_grad, NN).astype(bf16)
        whole = lax.dynamic_update_slice_in_dim(jnp.zeros((width, width), bf16), mine, start, 0)
        whole = lax.psum_scatter(whole, "dp", scatter_dimension=0, tiled=True)
        grad_weight = lax.psum(whole.astype(f32), "station") * scale
    shape = query_states.shape
    return (
        layer_output.reshape(shape),
        grad_query.reshape(shape),
        grad_key.reshape(shape),
        grad_value.reshape(shape),
        grad_weight,
    )


def solution(mesh):
    split = P("dp", "station", None, None)
    return jax.shard_map(
        local,
        mesh=mesh,
        in_specs=(split, split, split, split, P(), P(), P()),
        out_specs=(split, split, split, split, P("dp", None)),
        check_vma=False,
    )
```

```python
import functools
import math

import jax
import jax.numpy as jnp
from jax import lax
from jax.experimental import pallas as pl
from jax.experimental.pallas import tpu as pltpu
from jax.sharding import PartitionSpec as P

HEADS = 12
PMAX = 6
HOPS = 3
LAYER = 4
LOCAL = HEADS // LAYER
BLOCKS = LAYER + 2 * HOPS
SLOTS = 2 * HOPS + 1
MIB = 1024 * 1024

neg_big = -1e30
bf16, f32 = jnp.bfloat16, jnp.float32
SMEM = pl.BlockSpec(memory_space=pltpu.SMEM)
VMEM = pl.BlockSpec(memory_space=pltpu.VMEM)
ANY = pl.BlockSpec(memory_space=pl.ANY)
HBM = pl.BlockSpec(memory_space=pltpu.HBM)
NN = (((1,), (0,)), ((), ()))
NT = (((1,), (1,)), ((), ()))
TN = (((0,), (0,)), ((), ()))


def dot(x, y, dims):
    return lax.dot_general(x, y, dims, preferred_element_type=f32)


def shape_of(*dims, dtype=bf16):
    return jax.ShapeDtypeStruct(dims, dtype)


TOKEN = shape_of(8, 128, dtype=f32)


def skip_refs(kernel, first, count, *refs):
    kernel(*refs[:first], *refs[first + count :])


def call(kernel, ins, outs, args, scratch=(), limit=8, name=None, after=()):
    ins, args = [*ins, *[ANY] * len(after)], (*args, *after)
    if after:
        kernel = functools.partial(skip_refs, kernel, len(args) - len(after), len(after))
    return pl.pallas_call(
        kernel,
        in_specs=ins,
        out_specs=[VMEM] * len(outs),
        out_shape=outs,
        scratch_shapes=list(scratch),
        compiler_params=pltpu.CompilerParams(vmem_limit_bytes=limit * MIB),
        cost_estimate=pl.CostEstimate(flops=1, bytes_accessed=1, transcendentals=0),
        name=name,
    )(*args)


def place(peer, size):
    position = jnp.bitwise_xor(lax.rem(lax.axis_index("station"), LAYER), peer)
    return pl.ds(pl.multiple_of(position * size, size), size)


def block(j, span):
    return slice(j * span, (j + 1) * span)


def readers(j):
    return max(0, j - 2 * HOPS), min(LAYER - 1, j)


def pack_kernel(k_ref, v_ref, *refs):
    outs, (natural, flipped, sems) = refs[:LAYER], refs[LAYER:]
    rows = outs[0].shape[1]
    copies = [
        pltpu.make_async_copy(ref, natural.at[n], sems.at[n]) for n, ref in enumerate((k_ref, v_ref))
    ]
    for copy in copies:
        copy.start()
    for n, copy in enumerate(copies):
        copy.wait()
        flipped[n] = natural[n].T
    for peer, out in enumerate(outs):
        out[...] = flipped[:, place(peer, rows)]


def project_kernel(q_ref, g_ref, weight_ref, *refs):
    outs, (copy_ref, flipped) = refs[:LAYER], refs[LAYER:]
    rows = outs[0].shape[1]
    copy_ref[...] = g_ref[...]
    flipped[0] = q_ref[...].T * bf16(1.0 / math.sqrt(flipped.shape[1] // HEADS))
    flipped[1] = dot(weight_ref[...], g_ref[...], NT).astype(bf16)
    for peer, out in enumerate(outs):
        out[...] = flipped[:, place(peer, rows)]


def relay_kernel(sib_ref, across_ref, out_ref):
    out_ref[0] = sib_ref[...]
    out_ref[1] = across_ref[1]


def gather_kernel(*refs):
    ins, (up_ref, down_ref, pair_ref) = refs[:LAYER], refs[LAYER:]
    span = ins[0].shape[2]
    for peer, ref in enumerate(ins):
        pair_ref[:, :, place(peer, span)] = ref[...]
    up_ref[...] = pair_ref[:, :, span:]
    down_ref[...] = pair_ref[:, :, : HOPS * span]


def live_kernel(station_count, ids_ref, count_ref, bias_ref, dead_ref):
    span = bias_ref.shape[1] // LAYER
    first = lax.axis_index("station") // LAYER * LAYER
    ones = jnp.ones((1, span), f32)

    def listed(reader, other):
        hit = jnp.int32(0)
        for j in range(PMAX):
            here = jnp.logical_and(ids_ref[reader, j] == other, j < count_ref[reader])
            hit = jnp.maximum(hit, here.astype(jnp.int32))
        return hit > 0

    for j in range(BLOCKS):
        outer = lax.rem(first + (j - HOPS) + station_count, station_count)
        low, high = readers(j)
        for i in range(low, high + 1):
            inner = first + i
            slot = j - i
            if slot == HOPS:
                bias_ref[j : j + 1, block(i, span)] = 0.0 * ones
            else:
                reads = jnp.where(listed(inner, outer), 0.0, neg_big)
                bias_ref[j : j + 1, block(i, span)] = reads * ones
            if j < HOPS:
                read_by = jnp.where(listed(outer, inner), 0.0, -neg_big)
                dead_ref[i : i + 1, block(slot, span)] = read_by * ones


def clear(ref, span):
    for j in range(BLOCKS):
        low, high = readers(j)
        for i in range(LAYER):
            if not low <= i <= high:
                ref[block(j, span), block(i, span)] = jnp.zeros((span, span), bf16)


def forward_kernel(
    pair_ref, low_ref, high_ref, query_ref, bias_ref,
    mixed_ref, stats_ref, stats_up, probs_ref, window_ref,
    raw,
):
    rows = query_ref.shape[1]
    span = query_ref.shape[2] // LAYER
    head_width = rows // LOCAL
    reach = HOPS * span
    window_ref[:, :, :reach] = low_ref[...]
    window_ref[:, :, reach : reach + LAYER * span] = pair_ref[...]
    window_ref[:, :, reach + LAYER * span :] = high_ref[...]
    for head in range(LOCAL):
        clear(probs_ref.at[head], span)
        at = block(head, head_width)
        query = query_ref[0, at]
        tops = [None] * LAYER
        for j in range(BLOCKS):
            low, high = readers(j)
            cols = slice(low * span, (high + 1) * span)
            scores = dot(window_ref[0, at, block(j, span)], query[:, cols], TN)
            scores = scores + bias_ref[j : j + 1, cols]
            raw[block(j, span), cols] = scores
            here = jnp.max(scores, 0, keepdims=True)
            for i in range(low, high + 1):
                mine = here[:, block(i - low, span)]
                tops[i] = mine if tops[i] is None else jnp.maximum(tops[i], mine)
        top = jnp.concatenate(tops, 1)
        totals = [jnp.zeros((1, span), f32)] * LAYER
        for j in range(BLOCKS):
            low, high = readers(j)
            cols = slice(low * span, (high + 1) * span)
            weight = jnp.exp(raw[block(j, span), cols] - top[:, cols])
            raw[block(j, span), cols] = weight
            here = jnp.sum(weight, 0, keepdims=True)
            for i in range(low, high + 1):
                totals[i] = totals[i] + here[:, block(i - low, span)]
        total = jnp.concatenate(totals, 1)
        inverse = 1.0 / total
        for j in range(BLOCKS):
            low, high = readers(j)
            cols = slice(low * span, (high + 1) * span)
            probs_ref[head, block(j, span), cols] = (
                raw[block(j, span), cols] * inverse[:, cols]
            ).astype(bf16)
        mixed = dot(window_ref[1, at], probs_ref[head], NN).astype(bf16)
        mixed_ref[at] = mixed
        product = query_ref[1, at].astype(f32) * mixed.astype(f32)
        stats_ref[head : head + 1] = top + jnp.log(total)
        stats_ref[LOCAL + head : LOCAL + head + 1] = jnp.sum(product, 0, keepdims=True)
    stats_ref[2 * LOCAL :] = jnp.zeros((8 - 2 * LOCAL, LAYER * span), f32)
    stats_up[...] = stats_ref[:, span:]


def query_grad_kernel(
    window_ref, probs_ref, query_ref, stats_ref, mixed_ref, mine_ref, sib_ref, across_ref, own_ref,
    down_k, down_v, token_ref, grads, flipped
):
    rows = query_ref.shape[1]
    span = query_ref.shape[2] // LAYER
    head_width = rows // LOCAL
    scale = 1.0 / math.sqrt(head_width)
    inside = slice(HOPS * span, (HOPS + LAYER) * span)
    clear(grads, span)
    for head in range(LOCAL):
        at = block(head, head_width)
        grad = query_ref[1, at]
        delta = stats_ref[LOCAL + head : LOCAL + head + 1]
        for j in range(BLOCKS):
            low, high = readers(j)
            cols = slice(low * span, (high + 1) * span)
            back = dot(window_ref[1, at, block(j, span)], grad[:, cols], TN)
            prob = probs_ref[head, block(j, span), cols].astype(f32)
            grads[block(j, span), cols] = (prob * (back - delta[:, cols])).astype(bf16)
        flipped[at] = (dot(window_ref[0, at], grads[...], NN) * scale).astype(bf16)
        own_ref[0, at] = dot(query_ref[0, at], grads[inside], NT)
        own_ref[1, at] = dot(grad, probs_ref[head, inside], NT)
        below = slice(0, HOPS * span)
        down_k[at] = dot(query_ref[0, at, below], grads[below, below], NT).astype(bf16)
        down_v[at] = dot(grad[:, below], probs_ref[head, below, below], NT).astype(bf16)
    for peer, out in enumerate((mine_ref, sib_ref, across_ref.at[0], across_ref.at[1])):
        out[0] = mixed_ref[:, place(peer, span)]
        out[1] = flipped[:, place(peer, span)]
    token_ref[...] = jnp.zeros_like(token_ref)


def key_grad_kernel(pair_ref, low_ref, stats_ref, dead_ref, own_ref, above_k, above_v, *refs):
    outs, (token_ref, flipped) = refs[:LAYER], refs[LAYER:]
    rows = pair_ref.shape[1]
    span = pair_ref.shape[2] // LAYER
    head_width = rows // LOCAL
    for head in range(LOCAL):
        at = block(head, head_width)
        for i in range(LAYER):
            own = block(i, span)
            keys, values = own_ref[0, at, own], own_ref[1, at, own]
            if i:
                keys = keys + above_k[at, block(i - 1, span)].astype(f32)
                values = values + above_v[at, block(i - 1, span)].astype(f32)
            if i < HOPS:
                below = slice(i * span, HOPS * span)
                query, grad = low_ref[0, at, below], low_ref[1, at, below]
                log_sum = stats_ref[head : head + 1, below] + dead_ref[i : i + 1, : (HOPS - i) * span]
                delta = stats_ref[LOCAL + head : LOCAL + head + 1, below]
                prob = jnp.exp(dot(pair_ref[0, at, own], query, TN) - log_sum)
                back = dot(pair_ref[1, at, own], grad, TN)
                grads = (prob * (back - delta)).astype(bf16)
                keys = keys + dot(query, grads, NT)
                values = values + dot(grad, prob.astype(bf16), NT)
            flipped[0, at, own] = keys.astype(bf16)
            flipped[1, at, own] = values.astype(bf16)
    for peer, out in enumerate(outs):
        out[...] = flipped[:, :, place(peer, span)]
    token_ref[...] = jnp.zeros_like(token_ref)


def output_kernel(
    mine_ref, across_ref, sib_ref, weight_ref, out_ref, dq_ref, token_ref, flipped
):
    ins = mine_ref, sib_ref.at[0], across_ref.at[0], sib_ref.at[1]
    for peer, ref in enumerate(ins):
        flipped[:, place(peer, ref.shape[1])] = ref[...]
    out_ref[...] = dot(flipped[0], weight_ref[...], TN).astype(bf16)
    dq_ref[...] = flipped[1].T
    token_ref[...] = jnp.zeros_like(token_ref)


def key_output_kernel(*refs):
    ins, (dk_ref, dv_ref, token_ref, flipped) = refs[:LAYER], refs[LAYER:]
    for peer, ref in enumerate(ins):
        flipped[:, place(peer, ref.shape[1])] = ref[...]
    dk_ref[...] = flipped[0].T
    dv_ref[...] = flipped[1].T
    token_ref[...] = jnp.zeros_like(token_ref)


def halves(bit, half):
    send = pl.ds(pl.multiple_of((1 - bit) * half, half), half)
    keep = pl.ds(pl.multiple_of(bit * half, half), half)
    return send, keep


def bit_of(stride):
    return lax.rem(lax.axis_index("station") // stride, 2)


def weight_kernel(mixed_ref, *refs):
    ins, (send_ref, keep_ref, right) = refs[:LAYER], refs[LAYER:]
    for peer, ref in enumerate(ins):
        right[place(peer, ref.shape[0])] = ref[...]
    send, keep = halves(lax.rem(lax.axis_index("dp"), 2), send_ref.shape[0])
    send_ref[...] = dot(mixed_ref[send], right[...], NN).astype(bf16)
    keep_ref[...] = dot(mixed_ref[keep], right[...], NN)


def split_kernel(stride, part_ref, got_ref, send_ref, keep_ref):
    send, keep = halves(bit_of(stride), send_ref.shape[0])
    send_ref[...] = (part_ref[send] + got_ref[send].astype(f32)).astype(bf16)
    keep_ref[...] = part_ref[keep] + got_ref[keep].astype(f32)


def round_kernel(part_ref, got_ref, out_ref):
    out_ref[...] = (part_ref[...].astype(f32) + got_ref[...].astype(f32)).astype(bf16)


def join_kernel(stride, scale, mine_ref, got_ref, out_ref):
    other, here = halves(bit_of(stride), mine_ref.shape[0])
    for at, ref in ((here, mine_ref), (other, got_ref)):
        value = ref[...]
        if scale is not None:
            value = value.astype(f32) * scale
        out_ref[at] = value


def cross_kernel(mine_ref, second_ref, first_ref, out_ref):
    window = lax.rem(lax.axis_index("dp"), 2)
    other, here = halves(window, mine_ref.shape[0])
    at_home = bit_of(2) == window
    mine, first, second = mine_ref[...], first_ref[...], second_ref[...]
    out_ref[here] = jnp.where(at_home, mine, first)
    out_ref[other] = jnp.where(at_home, first, second)


def local(
    query_states, key_states, value_states, grad_output, out_weight, partner_ids, partner_count
):
    span, width = query_states.shape[2:]
    stations = lax.axis_size("station")
    windows = lax.axis_size("dp")
    rows = width // LAYER
    dma = pltpu.SemaphoreType.DMA

    def swap(value, stride):
        return lax.ppermute(value, "station", [(s ^ stride, s) for s in range(stations)])

    def in_layer(values):
        return [swap(values[n], n + 1) for n in range(LAYER - 1)]

    def from_below(value):
        pairs = [(s, (s + LAYER) % stations) for s in range(stations)]
        return lax.ppermute(value, "station", pairs)

    def from_above(value):
        pairs = [(s, (s - LAYER) % stations) for s in range(stations)]
        return lax.ppermute(value, "station", pairs)

    def other_window(value):
        return lax.ppermute(value, "dp", [(0, 1), (1, 0)])

    def flat(x):
        return x.reshape(span, width)

    q, k, v, g = flat(query_states), flat(key_states), flat(value_states), flat(grad_output)
    flat_shape = shape_of(span, width)
    part_shape = shape_of(2, rows, span)
    reach_shape = shape_of(2, rows, HOPS * span)
    layer_shape = shape_of(2, rows, LAYER * span)

    def gather(parts, after=()):
        return call(
            gather_kernel, [VMEM] * LAYER, [reach_shape, reach_shape, layer_shape], parts,
            name="gather", after=after,
        )

    mine, *parts = call(
        pack_kernel, [HBM] * 2, [part_shape] * LAYER, (k, v),
        [pltpu.VMEM((2, span, width), bf16), pltpu.VMEM((2, width, span), bf16), dma((2,))],
        limit=58, name="pack",
    )
    q, *parts = lax.optimization_barrier((q, *parts))
    parts = in_layer(parts)
    up, down, pair = gather((mine, *parts))
    mine, *query_parts, g_copy = call(
        project_kernel, [VMEM] * 3, [part_shape] * LAYER + [flat_shape],
        (q, g, out_weight), [pltpu.VMEM((2, width, span), bf16)], name="project",
    )
    up, g_later, *query_parts = lax.optimization_barrier((up, g, *query_parts))
    kv_low, kv_high = from_below(up), from_above(down)
    g_across = swap(g_later, 2)
    g_parts = g_copy, swap(g_later, 1), g_across, swap(g_across, 1)
    bias, dead = call(
        functools.partial(live_kernel, stations), [SMEM] * 2,
        [shape_of(16, LAYER * span, dtype=f32), shape_of(8, HOPS * span, dtype=f32)],
        (partner_ids, partner_count), name="live",
    )
    up, _, query = gather((mine, *in_layer(query_parts)), (bias,))
    qg_low = from_below(up)
    stats_shape = shape_of(8, HOPS * span, dtype=f32)
    mixed, stats, up, probs, window = call(
        forward_kernel, [VMEM] * 5,
        [
            shape_of(rows, LAYER * span), shape_of(8, LAYER * span, dtype=f32),
            stats_shape, shape_of(LOCAL, BLOCKS * span, LAYER * span), shape_of(2, rows, BLOCKS * span),
        ],
        (pair, kv_low, kv_high, query, bias),
        [pltpu.VMEM((BLOCKS * span, LAYER * span), f32)],
        limit=20, name="forward",
    )
    stats_low = from_below(up)

    send, part = call(
        weight_kernel, [VMEM] * (LAYER + 1),
        [shape_of(rows // 2, width), shape_of(rows // 2, width, dtype=f32)],
        (mixed, *g_parts), [pltpu.VMEM((LAYER * span, width), bf16)], name="weight",
    )

    own_return, to_sib, to_across, own_grad, down_k, down_v, query_token = call(
        query_grad_kernel, [VMEM] * 5,
        [
            part_shape, part_shape, shape_of(2, 2, rows, span),
            shape_of(2, rows, LAYER * span, dtype=f32),
            shape_of(rows, HOPS * span), shape_of(rows, HOPS * span), TOKEN,
        ],
        (window, probs, query, stats, mixed),
        [pltpu.VMEM((BLOCKS * span, LAYER * span), bf16), pltpu.VMEM((rows, LAYER * span), bf16)],
        limit=20, name="query_grad", after=(send,),
    )
    def first_return(across):
        (relay,) = call(
            relay_kernel, [VMEM] * 2, [shape_of(2, 2, rows, span)], (to_sib, across), name="relay"
        )
        relayed = swap(relay, 1)
        layer_output, grad_query, output_token = call(
            output_kernel, [VMEM] * 4, [flat_shape] * 2 + [TOKEN],
            (own_return, across, relayed, out_weight), [pltpu.VMEM((2, width, span), bf16)], name="output",
        )
        return layer_output, grad_query, output_token

    mine, *parts, key_token = call(
        key_grad_kernel, [VMEM] * 7, [part_shape] * LAYER + [TOKEN],
        (pair, qg_low, stats_low, dead, own_grad, from_above(down_k), from_above(down_v)),
        [pltpu.VMEM((2, rows, LAYER * span), bf16)], limit=20, name="key_grad",
    )
    key_parts = in_layer(parts)
    grad_key, grad_value, key_output_token = call(
        key_output_kernel, [VMEM] * LAYER, [flat_shape] * 2 + [TOKEN],
        (mine, *key_parts), [pltpu.VMEM((2, width, span), bf16)], name="key_output",
    )

    scale = 1.0 / math.sqrt(span * windows * stations)
    if windows == 2:
        count = rows // 4
        got = other_window(send)
        send, part = call(
            functools.partial(split_kernel, LAYER), [VMEM] * 2,
            [shape_of(count, width), shape_of(count, width, dtype=f32)],
            (part, got), name="split", after=(query_token, qg_low, stats_low),
        )

        across = swap(to_across, 2)
        layer_output, grad_query, output_token = first_return(across)

        def add_round(part, got, after=()):
            out = [shape_of(count, width)]
            return call(round_kernel, [VMEM] * 2, out, (part, got), name="add", after=after)[0]

        total = add_round(part, swap(send, LAYER), ())
        stride = 2 * LAYER
        while stride < stations:
            total = add_round(total, swap(total, stride), (across, key_token))
            stride *= 2
        (total,) = call(
            functools.partial(join_kernel, LAYER, None), [VMEM] * 2, [shape_of(2 * count, width)],
            (total, swap(total, LAYER)), name="join", after=key_parts,
        )
        first, second = [], []
        for w in range(2):
            for s in range(stations):
                if s // 2 % 2 == w:
                    first.append((w * stations + s, w * stations + (s ^ 2)))
                else:
                    first.append((w * stations + s, (1 - w) * stations + s))
                    second.append((w * stations + s, (1 - w) * stations + (s ^ 2)))
        axes = ("dp", "station")
        (total,) = call(
            cross_kernel, [VMEM] * 3, [shape_of(4 * count, width)],
            (total, lax.ppermute(total, axes, second), lax.ppermute(total, axes, first)),
            name="cross", after=(output_token, key_output_token),
        )
        (grad_weight,) = call(
            functools.partial(join_kernel, 1, scale), [VMEM] * 2,
            [shape_of(8 * count, width, dtype=f32)], (total, swap(total, 1)), name="last",
        )
    else:
        layer_output, grad_query, _ = first_return(swap(to_across, 2))
        start = lax.axis_index("station") % LAYER * rows
        all_grad = jnp.zeros((LAYER * span, width), bf16)
        for peer in range(LAYER):
            value = g_parts[peer]
            spot = lax.axis_index("station") % LAYER ^ peer
            all_grad = lax.dynamic_update_slice_in_dim(all_grad, value, spot * span, 0)
        mine = dot(mixed, all_grad, NN).astype(bf16)
        whole = lax.dynamic_update_slice_in_dim(jnp.zeros((width, width), bf16), mine, start, 0)
        whole = lax.psum_scatter(whole, "dp", scatter_dimension=0, tiled=True)
        grad_weight = lax.psum(whole.astype(f32), "station") * scale
    shape = query_states.shape
    return (
        layer_output.reshape(shape),
        grad_query.reshape(shape),
        grad_key.reshape(shape),
        grad_value.reshape(shape),
        grad_weight,
    )


def solution(mesh):
    split = P("dp", "station", None, None)
    return jax.shard_map(
        local,
        mesh=mesh,
        in_specs=(split, split, split, split, P(), P(), P()),
        out_specs=(split, split, split, split, P("dp", None)),
        check_vma=False,
    )
```

```python
import functools
import math

import jax
import jax.numpy as jnp
from jax import lax
from jax.experimental import pallas as pl
from jax.experimental.pallas import tpu as pltpu
from jax.sharding import PartitionSpec as P

HEADS = 12
PMAX = 6
HOPS = 3
LAYER = 4
LOCAL = HEADS // LAYER
BLOCKS = LAYER + 2 * HOPS
SLOTS = 2 * HOPS + 1
MIB = 1024 * 1024

neg_big = -1e30
bf16, f32 = jnp.bfloat16, jnp.float32
SMEM = pl.BlockSpec(memory_space=pltpu.SMEM)
VMEM = pl.BlockSpec(memory_space=pltpu.VMEM)
ANY = pl.BlockSpec(memory_space=pl.ANY)
HBM = pl.BlockSpec(memory_space=pltpu.HBM)
NN = (((1,), (0,)), ((), ()))
NT = (((1,), (1,)), ((), ()))
TN = (((0,), (0,)), ((), ()))


def dot(x, y, dims):
    return lax.dot_general(x, y, dims, preferred_element_type=f32)


def shape_of(*dims, dtype=bf16):
    return jax.ShapeDtypeStruct(dims, dtype)


TOKEN = shape_of(8, 128, dtype=f32)


def skip_refs(kernel, first, count, *refs):
    kernel(*refs[:first], *refs[first + count :])


def call(kernel, ins, outs, args, scratch=(), limit=8, name=None, after=()):
    ins, args = [*ins, *[ANY] * len(after)], (*args, *after)
    if after:
        kernel = functools.partial(skip_refs, kernel, len(args) - len(after), len(after))
    return pl.pallas_call(
        kernel,
        in_specs=ins,
        out_specs=[VMEM] * len(outs),
        out_shape=outs,
        scratch_shapes=list(scratch),
        compiler_params=pltpu.CompilerParams(vmem_limit_bytes=limit * MIB),
        cost_estimate=pl.CostEstimate(flops=1, bytes_accessed=1, transcendentals=0),
        name=name,
    )(*args)


def place(peer, size):
    position = jnp.bitwise_xor(lax.rem(lax.axis_index("station"), LAYER), peer)
    return pl.ds(pl.multiple_of(position * size, size), size)


def block(j, span):
    return slice(j * span, (j + 1) * span)


def readers(j):
    return max(0, j - 2 * HOPS), min(LAYER - 1, j)


def pack_kernel(k_ref, v_ref, *refs):
    outs, (natural, flipped, sems) = refs[:LAYER], refs[LAYER:]
    rows = outs[0].shape[1]
    copies = [
        pltpu.make_async_copy(ref, natural.at[n], sems.at[n]) for n, ref in enumerate((k_ref, v_ref))
    ]
    for copy in copies:
        copy.start()
    for n, copy in enumerate(copies):
        copy.wait()
        flipped[n] = natural[n].T
    for peer, out in enumerate(outs):
        out[...] = flipped[:, place(peer, rows)]


def project_kernel(q_ref, g_ref, weight_ref, *refs):
    outs, (copy_ref, flipped) = refs[:LAYER], refs[LAYER:]
    rows = outs[0].shape[1]
    copy_ref[...] = g_ref[...]
    flipped[0] = q_ref[...].T * bf16(1.0 / math.sqrt(flipped.shape[1] // HEADS))
    flipped[1] = dot(weight_ref[...], g_ref[...], NT).astype(bf16)
    for peer, out in enumerate(outs):
        out[...] = flipped[:, place(peer, rows)]


def relay_kernel(sib_ref, across_ref, out_ref):
    out_ref[0] = sib_ref[...]
    out_ref[1] = across_ref[1]


def gather_kernel(*refs):
    ins, (up_ref, down_ref, pair_ref) = refs[:LAYER], refs[LAYER:]
    span = ins[0].shape[2]
    for peer, ref in enumerate(ins):
        pair_ref[:, :, place(peer, span)] = ref[...]
    up_ref[...] = pair_ref[:, :, span:]
    down_ref[...] = pair_ref[:, :, : HOPS * span]


def live_kernel(station_count, ids_ref, count_ref, bias_ref, dead_ref):
    span = bias_ref.shape[1] // LAYER
    first = lax.axis_index("station") // LAYER * LAYER
    ones = jnp.ones((1, span), f32)

    def listed(reader, other):
        hit = jnp.int32(0)
        for j in range(PMAX):
            here = jnp.logical_and(ids_ref[reader, j] == other, j < count_ref[reader])
            hit = jnp.maximum(hit, here.astype(jnp.int32))
        return hit > 0

    for j in range(BLOCKS):
        outer = lax.rem(first + (j - HOPS) + station_count, station_count)
        low, high = readers(j)
        for i in range(low, high + 1):
            inner = first + i
            slot = j - i
            if slot == HOPS:
                bias_ref[j : j + 1, block(i, span)] = 0.0 * ones
            else:
                reads = jnp.where(listed(inner, outer), 0.0, neg_big)
                bias_ref[j : j + 1, block(i, span)] = reads * ones
            if j < HOPS:
                read_by = jnp.where(listed(outer, inner), 0.0, -neg_big)
                dead_ref[i : i + 1, block(slot, span)] = read_by * ones


def clear(ref, span):
    for j in range(BLOCKS):
        low, high = readers(j)
        for i in range(LAYER):
            if not low <= i <= high:
                ref[block(j, span), block(i, span)] = jnp.zeros((span, span), bf16)


def forward_kernel(
    pair_ref, low_ref, high_ref, query_ref, bias_ref,
    mixed_ref, stats_ref, stats_up, probs_ref, window_ref,
    raw,
):
    rows = query_ref.shape[1]
    span = query_ref.shape[2] // LAYER
    head_width = rows // LOCAL
    reach = HOPS * span
    window_ref[:, :, :reach] = low_ref[...]
    window_ref[:, :, reach : reach + LAYER * span] = pair_ref[...]
    window_ref[:, :, reach + LAYER * span :] = high_ref[...]
    for head in range(LOCAL):
        clear(probs_ref.at[head], span)
        at = block(head, head_width)
        query = query_ref[0, at]
        tops = [None] * LAYER
        for j in range(BLOCKS):
            low, high = readers(j)
            cols = slice(low * span, (high + 1) * span)
            scores = dot(window_ref[0, at, block(j, span)], query[:, cols], TN)
            scores = scores + bias_ref[j : j + 1, cols]
            raw[block(j, span), cols] = scores
            here = jnp.max(scores, 0, keepdims=True)
            for i in range(low, high + 1):
                mine = here[:, block(i - low, span)]
                tops[i] = mine if tops[i] is None else jnp.maximum(tops[i], mine)
        top = jnp.concatenate(tops, 1)
        totals = [jnp.zeros((1, span), f32)] * LAYER
        for j in range(BLOCKS):
            low, high = readers(j)
            cols = slice(low * span, (high + 1) * span)
            weight = jnp.exp(raw[block(j, span), cols] - top[:, cols])
            raw[block(j, span), cols] = weight
            here = jnp.sum(weight, 0, keepdims=True)
            for i in range(low, high + 1):
                totals[i] = totals[i] + here[:, block(i - low, span)]
        total = jnp.concatenate(totals, 1)
        inverse = 1.0 / total
        for j in range(BLOCKS):
            low, high = readers(j)
            cols = slice(low * span, (high + 1) * span)
            probs_ref[head, block(j, span), cols] = (
                raw[block(j, span), cols] * inverse[:, cols]
            ).astype(bf16)
        mixed = dot(window_ref[1, at], probs_ref[head], NN).astype(bf16)
        mixed_ref[at] = mixed
        product = query_ref[1, at].astype(f32) * mixed.astype(f32)
        stats_ref[head : head + 1] = top + jnp.log(total)
        stats_ref[LOCAL + head : LOCAL + head + 1] = jnp.sum(product, 0, keepdims=True)
    stats_ref[2 * LOCAL :] = jnp.zeros((8 - 2 * LOCAL, LAYER * span), f32)
    stats_up[...] = stats_ref[:, span:]


def query_grad_kernel(
    window_ref, probs_ref, query_ref, stats_ref, mixed_ref, mine_ref, sib_ref, across_ref, own_ref,
    down_k, down_v, token_ref, grads, flipped
):
    rows = query_ref.shape[1]
    span = query_ref.shape[2] // LAYER
    head_width = rows // LOCAL
    scale = 1.0 / math.sqrt(head_width)
    inside = slice(HOPS * span, (HOPS + LAYER) * span)
    clear(grads, span)
    for head in range(LOCAL):
        at = block(head, head_width)
        grad = query_ref[1, at]
        delta = stats_ref[LOCAL + head : LOCAL + head + 1]
        for j in range(BLOCKS):
            low, high = readers(j)
            cols = slice(low * span, (high + 1) * span)
            back = dot(window_ref[1, at, block(j, span)], grad[:, cols], TN)
            prob = probs_ref[head, block(j, span), cols].astype(f32)
            grads[block(j, span), cols] = (prob * (back - delta[:, cols])).astype(bf16)
        flipped[at] = (dot(window_ref[0, at], grads[...], NN) * scale).astype(bf16)
        own_ref[0, at] = dot(query_ref[0, at], grads[inside], NT)
        own_ref[1, at] = dot(grad, probs_ref[head, inside], NT)
        below = slice(0, HOPS * span)
        down_k[at] = dot(query_ref[0, at, below], grads[below, below], NT).astype(bf16)
        down_v[at] = dot(grad[:, below], probs_ref[head, below, below], NT).astype(bf16)
    for peer, out in enumerate((mine_ref, sib_ref, across_ref.at[0], across_ref.at[1])):
        out[0] = mixed_ref[:, place(peer, span)]
        out[1] = flipped[:, place(peer, span)]
    token_ref[...] = jnp.zeros_like(token_ref)


def key_grad_kernel(pair_ref, low_ref, stats_ref, dead_ref, own_ref, above_k, above_v, *refs):
    outs, (token_ref, flipped) = refs[:LAYER], refs[LAYER:]
    rows = pair_ref.shape[1]
    span = pair_ref.shape[2] // LAYER
    head_width = rows // LOCAL
    for head in range(LOCAL):
        at = block(head, head_width)
        for i in range(LAYER):
            own = block(i, span)
            keys, values = own_ref[0, at, own], own_ref[1, at, own]
            if i:
                keys = keys + above_k[at, block(i - 1, span)].astype(f32)
                values = values + above_v[at, block(i - 1, span)].astype(f32)
            if i < HOPS:
                below = slice(i * span, HOPS * span)
                query, grad = low_ref[0, at, below], low_ref[1, at, below]
                log_sum = stats_ref[head : head + 1, below] + dead_ref[i : i + 1, : (HOPS - i) * span]
                delta = stats_ref[LOCAL + head : LOCAL + head + 1, below]
                prob = jnp.exp(dot(pair_ref[0, at, own], query, TN) - log_sum)
                back = dot(pair_ref[1, at, own], grad, TN)
                grads = (prob * (back - delta)).astype(bf16)
                keys = keys + dot(query, grads, NT)
                values = values + dot(grad, prob.astype(bf16), NT)
            flipped[0, at, own] = keys.astype(bf16)
            flipped[1, at, own] = values.astype(bf16)
    for peer, out in enumerate(outs):
        out[...] = flipped[:, :, place(peer, span)]
    token_ref[...] = jnp.zeros_like(token_ref)


def output_kernel(
    mine_ref, across_ref, sib_ref, weight_ref, out_ref, dq_ref, token_ref, flipped
):
    ins = mine_ref, sib_ref.at[0], across_ref.at[0], sib_ref.at[1]
    for peer, ref in enumerate(ins):
        flipped[:, place(peer, ref.shape[1])] = ref[...]
    out_ref[...] = dot(flipped[0], weight_ref[...], TN).astype(bf16)
    dq_ref[...] = flipped[1].T
    token_ref[...] = jnp.zeros_like(token_ref)


def key_output_kernel(*refs):
    ins, (dk_ref, dv_ref, token_ref, flipped) = refs[:LAYER], refs[LAYER:]
    for peer, ref in enumerate(ins):
        flipped[:, place(peer, ref.shape[1])] = ref[...]
    dk_ref[...] = flipped[0].T
    dv_ref[...] = flipped[1].T
    token_ref[...] = jnp.zeros_like(token_ref)


def halves(bit, half):
    send = pl.ds(pl.multiple_of((1 - bit) * half, half), half)
    keep = pl.ds(pl.multiple_of(bit * half, half), half)
    return send, keep


def bit_of(stride):
    return lax.rem(lax.axis_index("station") // stride, 2)


def weight_kernel(mixed_ref, *refs):
    ins, (send_ref, keep_ref, right) = refs[:LAYER], refs[LAYER:]
    for peer, ref in enumerate(ins):
        right[place(peer, ref.shape[0])] = ref[...]
    send, keep = halves(lax.rem(lax.axis_index("dp"), 2), send_ref.shape[0])
    send_ref[...] = dot(mixed_ref[send], right[...], NN).astype(bf16)
    keep_ref[...] = dot(mixed_ref[keep], right[...], NN)


def split_kernel(stride, part_ref, got_ref, send_ref, keep_ref):
    send, keep = halves(bit_of(stride), send_ref.shape[0])
    send_ref[...] = (part_ref[send] + got_ref[send].astype(f32)).astype(bf16)
    keep_ref[...] = part_ref[keep] + got_ref[keep].astype(f32)


def round_kernel(part_ref, got_ref, out_ref):
    out_ref[...] = (part_ref[...].astype(f32) + got_ref[...].astype(f32)).astype(bf16)


def join_kernel(stride, scale, mine_ref, got_ref, out_ref):
    other, here = halves(bit_of(stride), mine_ref.shape[0])
    for at, ref in ((here, mine_ref), (other, got_ref)):
        value = ref[...]
        if scale is not None:
            value = value.astype(f32) * scale
        out_ref[at] = value


def cross_kernel(mine_ref, second_ref, first_ref, out_ref):
    window = lax.rem(lax.axis_index("dp"), 2)
    other, here = halves(window, mine_ref.shape[0])
    at_home = bit_of(2) == window
    mine, first, second = mine_ref[...], first_ref[...], second_ref[...]
    out_ref[here] = jnp.where(at_home, mine, first)
    out_ref[other] = jnp.where(at_home, first, second)


def local(
    query_states, key_states, value_states, grad_output, out_weight, partner_ids, partner_count
):
    span, width = query_states.shape[2:]
    stations = lax.axis_size("station")
    windows = lax.axis_size("dp")
    rows = width // LAYER
    dma = pltpu.SemaphoreType.DMA

    def swap(value, stride):
        return lax.ppermute(value, "station", [(s ^ stride, s) for s in range(stations)])

    def in_layer(values):
        return [swap(values[n], n + 1) for n in range(LAYER - 1)]

    def from_below(value):
        pairs = [(s, (s + LAYER) % stations) for s in range(stations)]
        return lax.ppermute(value, "station", pairs)

    def from_above(value):
        pairs = [(s, (s - LAYER) % stations) for s in range(stations)]
        return lax.ppermute(value, "station", pairs)

    def other_window(value):
        return lax.ppermute(value, "dp", [(0, 1), (1, 0)])

    def flat(x):
        return x.reshape(span, width)

    q, k, v, g = flat(query_states), flat(key_states), flat(value_states), flat(grad_output)
    flat_shape = shape_of(span, width)
    part_shape = shape_of(2, rows, span)
    reach_shape = shape_of(2, rows, HOPS * span)
    layer_shape = shape_of(2, rows, LAYER * span)

    def gather(parts, after=()):
        return call(
            gather_kernel, [VMEM] * LAYER, [reach_shape, reach_shape, layer_shape], parts,
            name="gather", after=after,
        )

    mine, *parts = call(
        pack_kernel, [HBM] * 2, [part_shape] * LAYER, (k, v),
        [pltpu.VMEM((2, span, width), bf16), pltpu.VMEM((2, width, span), bf16), dma((2,))],
        limit=58, name="pack",
    )
    q, *parts = lax.optimization_barrier((q, *parts))
    parts = in_layer(parts)
    up, down, pair = gather((mine, *parts))
    mine, *query_parts, g_copy = call(
        project_kernel, [VMEM] * 3, [part_shape] * LAYER + [flat_shape],
        (q, g, out_weight), [pltpu.VMEM((2, width, span), bf16)], name="project",
    )
    up, g_later, *query_parts = lax.optimization_barrier((up, g, *query_parts))
    kv_low, kv_high = from_below(up), from_above(down)
    g_across = swap(g_later, 2)
    g_parts = g_copy, swap(g_later, 1), g_across, swap(g_across, 1)
    bias, dead = call(
        functools.partial(live_kernel, stations), [SMEM] * 2,
        [shape_of(16, LAYER * span, dtype=f32), shape_of(8, HOPS * span, dtype=f32)],
        (partner_ids, partner_count), name="live",
    )
    up, _, query = gather((mine, *in_layer(query_parts)), (bias,))
    qg_low = from_below(up)
    stats_shape = shape_of(8, HOPS * span, dtype=f32)
    mixed, stats, up, probs, window = call(
        forward_kernel, [VMEM] * 5,
        [
            shape_of(rows, LAYER * span), shape_of(8, LAYER * span, dtype=f32),
            stats_shape, shape_of(LOCAL, BLOCKS * span, LAYER * span), shape_of(2, rows, BLOCKS * span),
        ],
        (pair, kv_low, kv_high, query, bias),
        [pltpu.VMEM((BLOCKS * span, LAYER * span), f32)],
        limit=20, name="forward",
    )
    stats_low = from_below(up)

    send, part = call(
        weight_kernel, [VMEM] * (LAYER + 1),
        [shape_of(rows // 2, width), shape_of(rows // 2, width, dtype=f32)],
        (mixed, *g_parts), [pltpu.VMEM((LAYER * span, width), bf16)], name="weight",
    )

    own_return, to_sib, to_across, own_grad, down_k, down_v, query_token = call(
        query_grad_kernel, [VMEM] * 5,
        [
            part_shape, part_shape, shape_of(2, 2, rows, span),
            shape_of(2, rows, LAYER * span, dtype=f32),
            shape_of(rows, HOPS * span), shape_of(rows, HOPS * span), TOKEN,
        ],
        (window, probs, query, stats, mixed),
        [pltpu.VMEM((BLOCKS * span, LAYER * span), bf16), pltpu.VMEM((rows, LAYER * span), bf16)],
        limit=20, name="query_grad", after=(send,),
    )
    def first_return(across):
        (relay,) = call(
            relay_kernel, [VMEM] * 2, [shape_of(2, 2, rows, span)], (to_sib, across), name="relay"
        )
        relayed = swap(relay, 1)
        layer_output, grad_query, output_token = call(
            output_kernel, [VMEM] * 4, [flat_shape] * 2 + [TOKEN],
            (own_return, across, relayed, out_weight), [pltpu.VMEM((2, width, span), bf16)], name="output",
        )
        return layer_output, grad_query, output_token

    def key_return(down_k, down_v):
        mine, *parts, key_token = call(
            key_grad_kernel, [VMEM] * 7, [part_shape] * LAYER + [TOKEN],
            (pair, qg_low, stats_low, dead, own_grad, from_above(down_k), from_above(down_v)),
            [pltpu.VMEM((2, rows, LAYER * span), bf16)], limit=20, name="key_grad",
        )
        key_parts = in_layer(parts)
        grad_key, grad_value, key_output_token = call(
            key_output_kernel, [VMEM] * LAYER, [flat_shape] * 2 + [TOKEN],
            (mine, *key_parts), [pltpu.VMEM((2, width, span), bf16)], name="key_output",
        )
        return grad_key, grad_value, key_parts, key_token, key_output_token

    scale = 1.0 / math.sqrt(span * windows * stations)
    if windows == 2:
        count = rows // 4
        got = other_window(send)
        send, part = call(
            functools.partial(split_kernel, LAYER), [VMEM] * 2,
            [shape_of(count, width), shape_of(count, width, dtype=f32)],
            (part, got), name="split", after=(query_token, qg_low),
        )

        across = swap(to_across, 2)
        layer_output, grad_query, output_token = first_return(across)

        def add_round(part, got, after=()):
            out = [shape_of(count, width)]
            return call(round_kernel, [VMEM] * 2, out, (part, got), name="add", after=after)[0]

        total = add_round(part, swap(send, LAYER), (stats_low,))
        total, down_k, down_v = lax.optimization_barrier((total, down_k, down_v))
        grad_key, grad_value, key_parts, key_token, key_output_token = key_return(down_k, down_v)
        stride = 2 * LAYER
        while stride < stations:
            total = add_round(total, swap(total, stride), (across,))
            stride *= 2
        (total,) = call(
            functools.partial(join_kernel, LAYER, None), [VMEM] * 2, [shape_of(2 * count, width)],
            (total, swap(total, LAYER)), name="join", after=key_parts,
        )
        first, second = [], []
        for w in range(2):
            for s in range(stations):
                if s // 2 % 2 == w:
                    first.append((w * stations + s, w * stations + (s ^ 2)))
                else:
                    first.append((w * stations + s, (1 - w) * stations + s))
                    second.append((w * stations + s, (1 - w) * stations + (s ^ 2)))
        axes = ("dp", "station")
        (total,) = call(
            cross_kernel, [VMEM] * 3, [shape_of(4 * count, width)],
            (total, lax.ppermute(total, axes, second), lax.ppermute(total, axes, first)),
            name="cross", after=(output_token, key_output_token),
        )
        (grad_weight,) = call(
            functools.partial(join_kernel, 1, scale), [VMEM] * 2,
            [shape_of(8 * count, width, dtype=f32)], (total, swap(total, 1)), name="last",
        )
    else:
        layer_output, grad_query, _ = first_return(swap(to_across, 2))
        grad_key, grad_value, *_ = key_return(down_k, down_v)
        start = lax.axis_index("station") % LAYER * rows
        all_grad = jnp.zeros((LAYER * span, width), bf16)
        for peer in range(LAYER):
            value = g_parts[peer]
            spot = lax.axis_index("station") % LAYER ^ peer
            all_grad = lax.dynamic_update_slice_in_dim(all_grad, value, spot * span, 0)
        mine = dot(mixed, all_grad, NN).astype(bf16)
        whole = lax.dynamic_update_slice_in_dim(jnp.zeros((width, width), bf16), mine, start, 0)
        whole = lax.psum_scatter(whole, "dp", scatter_dimension=0, tiled=True)
        grad_weight = lax.psum(whole.astype(f32), "station") * scale
    shape = query_states.shape
    return (
        layer_output.reshape(shape),
        grad_query.reshape(shape),
        grad_key.reshape(shape),
        grad_value.reshape(shape),
        grad_weight,
    )


def solution(mesh):
    split = P("dp", "station", None, None)
    return jax.shard_map(
        local,
        mesh=mesh,
        in_specs=(split, split, split, split, P(), P(), P()),
        out_specs=(split, split, split, split, P("dp", None)),
        check_vma=False,
    )
```

```python
import functools
import math

import jax
import jax.numpy as jnp
from jax import lax
from jax.experimental import pallas as pl
from jax.experimental.pallas import tpu as pltpu
from jax.sharding import PartitionSpec as P

HEADS = 12
PMAX = 6
HOPS = 3
LAYER = 4
LOCAL = HEADS // LAYER
BLOCKS = LAYER + 2 * HOPS
SLOTS = 2 * HOPS + 1
MIB = 1024 * 1024

neg_big = -1e30
bf16, f32 = jnp.bfloat16, jnp.float32
SMEM = pl.BlockSpec(memory_space=pltpu.SMEM)
VMEM = pl.BlockSpec(memory_space=pltpu.VMEM)
ANY = pl.BlockSpec(memory_space=pl.ANY)
HBM = pl.BlockSpec(memory_space=pltpu.HBM)
NN = (((1,), (0,)), ((), ()))
NT = (((1,), (1,)), ((), ()))
TN = (((0,), (0,)), ((), ()))


def dot(x, y, dims):
    return lax.dot_general(x, y, dims, preferred_element_type=f32)


def shape_of(*dims, dtype=bf16):
    return jax.ShapeDtypeStruct(dims, dtype)


TOKEN = shape_of(8, 128, dtype=f32)


def skip_refs(kernel, first, count, *refs):
    kernel(*refs[:first], *refs[first + count :])


def call(kernel, ins, outs, args, scratch=(), limit=8, name=None, after=()):
    ins, args = [*ins, *[ANY] * len(after)], (*args, *after)
    if after:
        kernel = functools.partial(skip_refs, kernel, len(args) - len(after), len(after))
    return pl.pallas_call(
        kernel,
        in_specs=ins,
        out_specs=[VMEM] * len(outs),
        out_shape=outs,
        scratch_shapes=list(scratch),
        compiler_params=pltpu.CompilerParams(vmem_limit_bytes=limit * MIB),
        cost_estimate=pl.CostEstimate(flops=1, bytes_accessed=1, transcendentals=0),
        name=name,
    )(*args)


def place(peer, size):
    position = jnp.bitwise_xor(lax.rem(lax.axis_index("station"), LAYER), peer)
    return pl.ds(pl.multiple_of(position * size, size), size)


def block(j, span):
    return slice(j * span, (j + 1) * span)


def readers(j):
    return max(0, j - 2 * HOPS), min(LAYER - 1, j)


def pack_kernel(k_ref, v_ref, *refs):
    outs, (natural, flipped, sems) = refs[:LAYER], refs[LAYER:]
    rows = outs[0].shape[1]
    copies = [
        pltpu.make_async_copy(ref, natural.at[n], sems.at[n]) for n, ref in enumerate((k_ref, v_ref))
    ]
    for copy in copies:
        copy.start()
    for n, copy in enumerate(copies):
        copy.wait()
        flipped[n] = natural[n].T
    for peer, out in enumerate(outs):
        out[...] = flipped[:, place(peer, rows)]


def project_kernel(q_ref, g_ref, weight_ref, *refs):
    outs, (copy_ref, flipped) = refs[:LAYER], refs[LAYER:]
    rows = outs[0].shape[1]
    copy_ref[...] = g_ref[...]
    flipped[0] = q_ref[...].T * bf16(1.0 / math.sqrt(flipped.shape[1] // HEADS))
    flipped[1] = dot(weight_ref[...], g_ref[...], NT).astype(bf16)
    for peer, out in enumerate(outs):
        out[...] = flipped[:, place(peer, rows)]


def gather_kernel(*refs):
    ins, (up_ref, down_ref, pair_ref) = refs[:LAYER], refs[LAYER:]
    span = ins[0].shape[2]
    for peer, ref in enumerate(ins):
        pair_ref[:, :, place(peer, span)] = ref[...]
    up_ref[...] = pair_ref[:, :, span:]
    down_ref[...] = pair_ref[:, :, : HOPS * span]


def live_kernel(station_count, ids_ref, count_ref, bias_ref, dead_ref):
    span = bias_ref.shape[1] // LAYER
    first = lax.axis_index("station") // LAYER * LAYER
    ones = jnp.ones((1, span), f32)

    def listed(reader, other):
        hit = jnp.int32(0)
        for j in range(PMAX):
            here = jnp.logical_and(ids_ref[reader, j] == other, j < count_ref[reader])
            hit = jnp.maximum(hit, here.astype(jnp.int32))
        return hit > 0

    for j in range(BLOCKS):
        outer = lax.rem(first + (j - HOPS) + station_count, station_count)
        low, high = readers(j)
        for i in range(low, high + 1):
            inner = first + i
            slot = j - i
            if slot == HOPS:
                bias_ref[j : j + 1, block(i, span)] = 0.0 * ones
            else:
                reads = jnp.where(listed(inner, outer), 0.0, neg_big)
                bias_ref[j : j + 1, block(i, span)] = reads * ones
            if not HOPS <= j < HOPS + LAYER:
                read_by = jnp.where(listed(outer, inner), 0.0, -neg_big)
                spot = slot if j < HOPS else slot - LAYER
                dead_ref[i : i + 1, block(spot, span)] = read_by * ones


def clear(ref, span):
    for j in range(BLOCKS):
        low, high = readers(j)
        for i in range(LAYER):
            if not low <= i <= high:
                ref[block(j, span), block(i, span)] = jnp.zeros((span, span), bf16)


def forward_kernel(
    pair_ref, low_ref, high_ref, query_ref, bias_ref,
    mixed_ref, stats_ref, stats_up, stats_down, probs_ref, window_ref,
    raw,
):
    rows = query_ref.shape[1]
    span = query_ref.shape[2] // LAYER
    head_width = rows // LOCAL
    reach = HOPS * span
    window_ref[:, :, :reach] = low_ref[...]
    window_ref[:, :, reach : reach + LAYER * span] = pair_ref[...]
    window_ref[:, :, reach + LAYER * span :] = high_ref[...]
    for head in range(LOCAL):
        clear(probs_ref.at[head], span)
        at = block(head, head_width)
        query = query_ref[0, at]
        tops = [None] * LAYER
        for j in range(BLOCKS):
            low, high = readers(j)
            cols = slice(low * span, (high + 1) * span)
            scores = dot(window_ref[0, at, block(j, span)], query[:, cols], TN)
            scores = scores + bias_ref[j : j + 1, cols]
            raw[block(j, span), cols] = scores
            here = jnp.max(scores, 0, keepdims=True)
            for i in range(low, high + 1):
                mine = here[:, block(i - low, span)]
                tops[i] = mine if tops[i] is None else jnp.maximum(tops[i], mine)
        top = jnp.concatenate(tops, 1)
        totals = [jnp.zeros((1, span), f32)] * LAYER
        for j in range(BLOCKS):
            low, high = readers(j)
            cols = slice(low * span, (high + 1) * span)
            weight = jnp.exp(raw[block(j, span), cols] - top[:, cols])
            raw[block(j, span), cols] = weight
            here = jnp.sum(weight, 0, keepdims=True)
            for i in range(low, high + 1):
                totals[i] = totals[i] + here[:, block(i - low, span)]
        total = jnp.concatenate(totals, 1)
        inverse = 1.0 / total
        for j in range(BLOCKS):
            low, high = readers(j)
            cols = slice(low * span, (high + 1) * span)
            probs_ref[head, block(j, span), cols] = (
                raw[block(j, span), cols] * inverse[:, cols]
            ).astype(bf16)
        mixed = dot(window_ref[1, at], probs_ref[head], NN).astype(bf16)
        mixed_ref[at] = mixed
        product = query_ref[1, at].astype(f32) * mixed.astype(f32)
        stats_ref[head : head + 1] = top + jnp.log(total)
        stats_ref[LOCAL + head : LOCAL + head + 1] = jnp.sum(product, 0, keepdims=True)
    stats_ref[2 * LOCAL :] = jnp.zeros((8 - 2 * LOCAL, LAYER * span), f32)
    stats_up[...] = stats_ref[:, span:]
    stats_down[...] = stats_ref[:, :reach]


def query_grad_kernel(
    window_ref, probs_ref, query_ref, stats_ref, dq_ref, own_ref, token_ref, grads
):
    rows = query_ref.shape[1]
    span = query_ref.shape[2] // LAYER
    head_width = rows // LOCAL
    scale = 1.0 / math.sqrt(head_width)
    inside = slice(HOPS * span, (HOPS + LAYER) * span)
    clear(grads, span)
    for head in range(LOCAL):
        at = block(head, head_width)
        grad = query_ref[1, at]
        delta = stats_ref[LOCAL + head : LOCAL + head + 1]
        for j in range(BLOCKS):
            low, high = readers(j)
            cols = slice(low * span, (high + 1) * span)
            back = dot(window_ref[1, at, block(j, span)], grad[:, cols], TN)
            prob = probs_ref[head, block(j, span), cols].astype(f32)
            grads[block(j, span), cols] = (prob * (back - delta[:, cols])).astype(bf16)
        dq_ref[at] = (dot(window_ref[0, at], grads[...], NN) * scale).astype(bf16)
        own_ref[0, at] = dot(query_ref[0, at], grads[inside], NT)
        own_ref[1, at] = dot(grad, probs_ref[head, inside], NT)
    token_ref[...] = jnp.zeros_like(token_ref)


def key_grad_kernel(
    pair_ref, low_ref, high_ref, stats_low, stats_high, dead_ref, own_ref, mixed_ref, dq_ref, *refs
):
    outs, (token_ref, flipped) = refs[:LAYER], refs[LAYER:]
    rows = pair_ref.shape[1]
    span = pair_ref.shape[2] // LAYER
    head_width = rows // LOCAL
    for head in range(LOCAL):
        at = block(head, head_width)
        log_row = slice(head, head + 1)
        delta_row = slice(LOCAL + head, LOCAL + head + 1)
        for i in range(LAYER):
            own = block(i, span)

            def outside(low, high):
                sides = [low[:, i * span :]] if i < HOPS else []
                return jnp.concatenate(sides + ([high[:, : i * span]] if i else []), 1)

            query = outside(low_ref[0, at], high_ref[0, at])
            grad = outside(low_ref[1, at], high_ref[1, at])
            log_sum = outside(stats_low[log_row], stats_high[log_row]) + dead_ref[i : i + 1]
            delta = outside(stats_low[delta_row], stats_high[delta_row])
            prob = jnp.exp(dot(pair_ref[0, at, own], query, TN) - log_sum)
            back = dot(pair_ref[1, at, own], grad, TN)
            grads = (prob * (back - delta)).astype(bf16)
            keys = own_ref[0, at, own] + dot(query, grads, NT)
            values = own_ref[1, at, own] + dot(grad, prob.astype(bf16), NT)
            flipped[0, at, own] = keys.astype(bf16)
            flipped[1, at, own] = values.astype(bf16)
    for peer, out in enumerate(outs):
        at = place(peer, span)
        out[0] = mixed_ref[:, at]
        out[1] = dq_ref[:, at]
        out[2:] = flipped[:, :, at]
    token_ref[...] = jnp.zeros_like(token_ref)


def output_kernel(*refs):
    ins, refs = refs[:LAYER], refs[LAYER:]
    weight_ref, out_ref, dq_ref, dk_ref, dv_ref, token_ref, flipped = refs
    for peer, ref in enumerate(ins):
        flipped[:, place(peer, ref.shape[1])] = ref[...]
    out_ref[...] = dot(flipped[0], weight_ref[...], TN).astype(bf16)
    for n, ref in enumerate((dq_ref, dk_ref, dv_ref)):
        ref[...] = flipped[n + 1].T
    token_ref[...] = jnp.zeros_like(token_ref)


def halves(bit, half):
    send = pl.ds(pl.multiple_of((1 - bit) * half, half), half)
    keep = pl.ds(pl.multiple_of(bit * half, half), half)
    return send, keep


def bit_of(stride):
    return lax.rem(lax.axis_index("station") // stride, 2)


def weight_kernel(mixed_ref, *refs):
    ins, (send_ref, keep_ref, right) = refs[:LAYER], refs[LAYER:]
    for peer, ref in enumerate(ins):
        right[place(peer, ref.shape[0])] = ref[...]
    send, keep = halves(lax.rem(lax.axis_index("dp"), 2), send_ref.shape[0])
    send_ref[...] = dot(mixed_ref[send], right[...], NN).astype(bf16)
    keep_ref[...] = dot(mixed_ref[keep], right[...], NN)


def split_kernel(stride, part_ref, got_ref, send_ref, keep_ref):
    send, keep = halves(bit_of(stride), send_ref.shape[0])
    send_ref[...] = (part_ref[send] + got_ref[send].astype(f32)).astype(bf16)
    keep_ref[...] = part_ref[keep] + got_ref[keep].astype(f32)


def round_kernel(part_ref, got_ref, out_ref):
    out_ref[...] = (part_ref[...].astype(f32) + got_ref[...].astype(f32)).astype(bf16)


def join_kernel(stride, scale, mine_ref, got_ref, out_ref):
    other, here = halves(bit_of(stride), mine_ref.shape[0])
    for at, ref in ((here, mine_ref), (other, got_ref)):
        value = ref[...]
        if scale is not None:
            value = value.astype(f32) * scale
        out_ref[at] = value


def cross_kernel(mine_ref, first_ref, second_ref, out_ref):
    window = lax.rem(lax.axis_index("dp"), 2)
    other, here = halves(window, mine_ref.shape[0])
    at_home = bit_of(2) == window
    mine, first, second = mine_ref[...], first_ref[...], second_ref[...]
    out_ref[here] = jnp.where(at_home, mine, first)
    out_ref[other] = jnp.where(at_home, first, second)


def local(
    query_states, key_states, value_states, grad_output, out_weight, partner_ids, partner_count
):
    span, width = query_states.shape[2:]
    stations = lax.axis_size("station")
    windows = lax.axis_size("dp")
    rows = width // LAYER
    dma = pltpu.SemaphoreType.DMA

    def swap(value, stride):
        return lax.ppermute(value, "station", [(s ^ stride, s) for s in range(stations)])

    def in_layer(values):
        return [swap(values[n], n + 1) for n in range(LAYER - 1)]

    def along(up, down):
        low = lax.ppermute(up, "station", [(s, (s + LAYER) % stations) for s in range(stations)])
        high = lax.ppermute(down, "station", [(s, (s - LAYER) % stations) for s in range(stations)])
        return low, high

    def other_window(value):
        return lax.ppermute(value, "dp", [(0, 1), (1, 0)])

    def flat(x):
        return x.reshape(span, width)

    q, k, v, g = flat(query_states), flat(key_states), flat(value_states), flat(grad_output)
    flat_shape = shape_of(span, width)
    part_shape = shape_of(2, rows, span)
    reach_shape = shape_of(2, rows, HOPS * span)
    layer_shape = shape_of(2, rows, LAYER * span)

    def gather(parts, after=()):
        return call(
            gather_kernel, [VMEM] * LAYER, [reach_shape, reach_shape, layer_shape], parts,
            name="gather", after=after,
        )

    mine, *parts = call(
        pack_kernel, [HBM] * 2, [part_shape] * LAYER, (k, v),
        [pltpu.VMEM((2, span, width), bf16), pltpu.VMEM((2, width, span), bf16), dma((2,))],
        limit=58, name="pack",
    )
    q, *parts = lax.optimization_barrier((q, *parts))
    parts = in_layer(parts)
    up, down, pair = gather((mine, *parts))
    mine, *query_parts, g_copy = call(
        project_kernel, [VMEM] * 3, [part_shape] * LAYER + [flat_shape],
        (q, g, out_weight), [pltpu.VMEM((2, width, span), bf16)], name="project",
    )
    up, g_later, *query_parts = lax.optimization_barrier((up, g, *query_parts))
    kv_low, kv_high = along(up, down)
    g_across = swap(g_later, 2)
    g_parts = g_copy, swap(g_later, 1), g_across, swap(g_across, 1)
    bias, dead = call(
        functools.partial(live_kernel, stations), [SMEM] * 2,
        [shape_of(16, LAYER * span, dtype=f32), shape_of(8, HOPS * span, dtype=f32)],
        (partner_ids, partner_count), name="live",
    )
    up, down, query = gather((mine, *in_layer(query_parts)), (bias,))
    qg_low, qg_high = along(up, down)
    stats_shape = shape_of(8, HOPS * span, dtype=f32)
    mixed, stats, up, down, probs, window = call(
        forward_kernel, [VMEM] * 5,
        [
            shape_of(rows, LAYER * span), shape_of(8, LAYER * span, dtype=f32),
            stats_shape, stats_shape,
            shape_of(LOCAL, BLOCKS * span, LAYER * span), shape_of(2, rows, BLOCKS * span),
        ],
        (pair, kv_low, kv_high, query, bias),
        [pltpu.VMEM((BLOCKS * span, LAYER * span), f32)],
        limit=20, name="forward",
    )
    stats_low, stats_high = along(up, down)

    send, part = call(
        weight_kernel, [VMEM] * (LAYER + 1),
        [shape_of(rows // 2, width), shape_of(rows // 2, width, dtype=f32)],
        (mixed, *g_parts), [pltpu.VMEM((LAYER * span, width), bf16)], name="weight",
    )

    dq, own_grad, query_token = call(
        query_grad_kernel, [VMEM] * 4,
        [shape_of(rows, LAYER * span), shape_of(2, rows, LAYER * span, dtype=f32), TOKEN],
        (window, probs, query, stats), [pltpu.VMEM((BLOCKS * span, LAYER * span), bf16)],
        limit=20, name="query_grad", after=(send,),
    )
    mine, *parts, key_token = call(
        key_grad_kernel, [VMEM] * 9, [shape_of(4, rows, span)] * LAYER + [TOKEN],
        (pair, qg_low, qg_high, stats_low, stats_high, dead, own_grad, mixed, dq),
        [pltpu.VMEM((2, rows, LAYER * span), bf16)], limit=20, name="key_grad",
    )
    parts = in_layer(parts)
    layer_output, grad_query, grad_key, grad_value, output_token = call(
        output_kernel, [VMEM] * (LAYER + 1), [flat_shape] * 4 + [TOKEN],
        (mine, *parts, out_weight), [pltpu.VMEM((4, width, span), bf16)], name="output",
    )

    scale = 1.0 / math.sqrt(span * windows * stations)
    if windows == 2:
        count = rows // 4
        got = other_window(send)
        send, part = call(
            functools.partial(split_kernel, LAYER), [VMEM] * 2,
            [shape_of(count, width), shape_of(count, width, dtype=f32)],
            (part, got), name="split", after=(query_token, qg_low, qg_high, stats_low, stats_high),
        )

        def add_round(part, got, after=()):
            out = [shape_of(count, width)]
            return call(round_kernel, [VMEM] * 2, out, (part, got), name="add", after=after)[0]

        total = add_round(part, swap(send, LAYER), (key_token,))
        stride = 2 * LAYER
        while stride < stations:
            total = add_round(total, swap(total, stride))
            stride *= 2
        (total,) = call(
            functools.partial(join_kernel, LAYER, None), [VMEM] * 2, [shape_of(2 * count, width)],
            (total, swap(total, LAYER)), name="join", after=parts,
        )
        first, second = [], []
        for w in range(2):
            for s in range(stations):
                if s // 2 % 2 == w:
                    first.append((w * stations + s, w * stations + (s ^ 2)))
                else:
                    first.append((w * stations + s, (1 - w) * stations + s))
                    second.append((w * stations + s, (1 - w) * stations + (s ^ 2)))
        axes = ("dp", "station")
        (total,) = call(
            cross_kernel, [VMEM] * 3, [shape_of(4 * count, width)],
            (total, lax.ppermute(total, axes, first), lax.ppermute(total, axes, second)),
            name="cross", after=(output_token,),
        )
        (grad_weight,) = call(
            functools.partial(join_kernel, 1, scale), [VMEM] * 2,
            [shape_of(8 * count, width, dtype=f32)], (total, swap(total, 1)), name="last",
        )
    else:
        start = lax.axis_index("station") % LAYER * rows
        all_grad = jnp.zeros((LAYER * span, width), bf16)
        for peer in range(LAYER):
            value = g_parts[peer]
            spot = lax.axis_index("station") % LAYER ^ peer
            all_grad = lax.dynamic_update_slice_in_dim(all_grad, value, spot * span, 0)
        mine = dot(mixed, all_grad, NN).astype(bf16)
        whole = lax.dynamic_update_slice_in_dim(jnp.zeros((width, width), bf16), mine, start, 0)
        whole = lax.psum_scatter(whole, "dp", scatter_dimension=0, tiled=True)
        grad_weight = lax.psum(whole.astype(f32), "station") * scale
    shape = query_states.shape
    return (
        layer_output.reshape(shape),
        grad_query.reshape(shape),
        grad_key.reshape(shape),
        grad_value.reshape(shape),
        grad_weight,
    )


def solution(mesh):
    split = P("dp", "station", None, None)
    return jax.shard_map(
        local,
        mesh=mesh,
        in_specs=(split, split, split, split, P(), P(), P()),
        out_specs=(split, split, split, split, P("dp", None)),
        check_vma=False,
    )
```

```python
import functools
import math

import jax
import jax.numpy as jnp
from jax import lax
from jax.experimental import pallas as pl
from jax.experimental.pallas import tpu as pltpu
from jax.sharding import PartitionSpec as P

HEADS = 12
PMAX = 6
HOPS = 3
LAYER = 4
LOCAL = HEADS // LAYER
BLOCKS = LAYER + 2 * HOPS
SLOTS = 2 * HOPS + 1
MIB = 1024 * 1024

neg_big = -1e30
bf16, f32 = jnp.bfloat16, jnp.float32
SMEM = pl.BlockSpec(memory_space=pltpu.SMEM)
VMEM = pl.BlockSpec(memory_space=pltpu.VMEM)
ANY = pl.BlockSpec(memory_space=pl.ANY)
HBM = pl.BlockSpec(memory_space=pltpu.HBM)
NN = (((1,), (0,)), ((), ()))
NT = (((1,), (1,)), ((), ()))
TN = (((0,), (0,)), ((), ()))


def dot(x, y, dims):
    return lax.dot_general(x, y, dims, preferred_element_type=f32)


def shape_of(*dims, dtype=bf16):
    return jax.ShapeDtypeStruct(dims, dtype)


TOKEN = shape_of(8, 128, dtype=f32)


def skip_refs(kernel, first, count, *refs):
    kernel(*refs[:first], *refs[first + count :])


def call(kernel, ins, outs, args, scratch=(), limit=8, name=None, after=()):
    ins, args = [*ins, *[ANY] * len(after)], (*args, *after)
    if after:
        kernel = functools.partial(skip_refs, kernel, len(args) - len(after), len(after))
    return pl.pallas_call(
        kernel,
        in_specs=ins,
        out_specs=[VMEM] * len(outs),
        out_shape=outs,
        scratch_shapes=list(scratch),
        compiler_params=pltpu.CompilerParams(vmem_limit_bytes=limit * MIB),
        cost_estimate=pl.CostEstimate(flops=1, bytes_accessed=1, transcendentals=0),
        name=name,
    )(*args)


def place(peer, size):
    position = jnp.bitwise_xor(lax.rem(lax.axis_index("station"), LAYER), peer)
    return pl.ds(pl.multiple_of(position * size, size), size)


def block(j, span):
    return slice(j * span, (j + 1) * span)


def readers(j):
    return max(0, j - 2 * HOPS), min(LAYER - 1, j)


def pack_kernel(k_ref, v_ref, *refs):
    outs, (natural, flipped, sems) = refs[:LAYER], refs[LAYER:]
    rows = outs[0].shape[1]
    copies = [
        pltpu.make_async_copy(ref, natural.at[n], sems.at[n]) for n, ref in enumerate((k_ref, v_ref))
    ]
    for copy in copies:
        copy.start()
    for n, copy in enumerate(copies):
        copy.wait()
        flipped[n] = natural[n].T
    for peer, out in enumerate(outs):
        out[...] = flipped[:, place(peer, rows)]


def project_kernel(q_ref, g_ref, weight_ref, *refs):
    outs, (copy_ref, flipped) = refs[:LAYER], refs[LAYER:]
    rows = outs[0].shape[1]
    copy_ref[...] = g_ref[...]
    flipped[0] = q_ref[...].T * bf16(1.0 / math.sqrt(flipped.shape[1] // HEADS))
    flipped[1] = dot(weight_ref[...], g_ref[...], NT).astype(bf16)
    for peer, out in enumerate(outs):
        out[...] = flipped[:, place(peer, rows)]


def gather_kernel(*refs):
    ins, (up_ref, down_ref, pair_ref) = refs[:LAYER], refs[LAYER:]
    span = ins[0].shape[2]
    for peer, ref in enumerate(ins):
        pair_ref[:, :, place(peer, span)] = ref[...]
    up_ref[...] = pair_ref[:, :, span:]
    down_ref[...] = pair_ref[:, :, : HOPS * span]


def live_kernel(station_count, ids_ref, count_ref, bias_ref, dead_ref):
    span = bias_ref.shape[1] // LAYER
    first = lax.axis_index("station") // LAYER * LAYER
    ones = jnp.ones((1, span), f32)

    def listed(reader, other):
        hit = jnp.int32(0)
        for j in range(PMAX):
            here = jnp.logical_and(ids_ref[reader, j] == other, j < count_ref[reader])
            hit = jnp.maximum(hit, here.astype(jnp.int32))
        return hit > 0

    for j in range(BLOCKS):
        outer = lax.rem(first + (j - HOPS) + station_count, station_count)
        low, high = readers(j)
        for i in range(low, high + 1):
            inner = first + i
            slot = j - i
            if slot == HOPS:
                bias_ref[j : j + 1, block(i, span)] = 0.0 * ones
            else:
                reads = jnp.where(listed(inner, outer), 0.0, neg_big)
                bias_ref[j : j + 1, block(i, span)] = reads * ones
            if not HOPS <= j < HOPS + LAYER:
                read_by = jnp.where(listed(outer, inner), 0.0, -neg_big)
                spot = slot if j < HOPS else slot - LAYER
                dead_ref[i : i + 1, block(spot, span)] = read_by * ones


def clear(ref, span):
    for j in range(BLOCKS):
        low, high = readers(j)
        for i in range(LAYER):
            if not low <= i <= high:
                ref[block(j, span), block(i, span)] = jnp.zeros((span, span), bf16)


def forward_kernel(
    pair_ref, low_ref, high_ref, query_ref, bias_ref,
    mixed_ref, stats_ref, stats_up, stats_down, probs_ref, window_ref,
    raw,
):
    rows = query_ref.shape[1]
    span = query_ref.shape[2] // LAYER
    head_width = rows // LOCAL
    reach = HOPS * span
    window_ref[:, :, :reach] = low_ref[...]
    window_ref[:, :, reach : reach + LAYER * span] = pair_ref[...]
    window_ref[:, :, reach + LAYER * span :] = high_ref[...]
    for head in range(LOCAL):
        clear(probs_ref.at[head], span)
        at = block(head, head_width)
        query = query_ref[0, at]
        tops = [None] * LAYER
        for j in range(BLOCKS):
            low, high = readers(j)
            cols = slice(low * span, (high + 1) * span)
            scores = dot(window_ref[0, at, block(j, span)], query[:, cols], TN)
            scores = scores + bias_ref[j : j + 1, cols]
            raw[block(j, span), cols] = scores
            here = jnp.max(scores, 0, keepdims=True)
            for i in range(low, high + 1):
                mine = here[:, block(i - low, span)]
                tops[i] = mine if tops[i] is None else jnp.maximum(tops[i], mine)
        top = jnp.concatenate(tops, 1)
        totals = [jnp.zeros((1, span), f32)] * LAYER
        for j in range(BLOCKS):
            low, high = readers(j)
            cols = slice(low * span, (high + 1) * span)
            weight = jnp.exp(raw[block(j, span), cols] - top[:, cols])
            raw[block(j, span), cols] = weight
            here = jnp.sum(weight, 0, keepdims=True)
            for i in range(low, high + 1):
                totals[i] = totals[i] + here[:, block(i - low, span)]
        total = jnp.concatenate(totals, 1)
        inverse = 1.0 / total
        for j in range(BLOCKS):
            low, high = readers(j)
            cols = slice(low * span, (high + 1) * span)
            probs_ref[head, block(j, span), cols] = (
                raw[block(j, span), cols] * inverse[:, cols]
            ).astype(bf16)
        mixed = dot(window_ref[1, at], probs_ref[head], NN).astype(bf16)
        mixed_ref[at] = mixed
        product = query_ref[1, at].astype(f32) * mixed.astype(f32)
        stats_ref[head : head + 1] = top + jnp.log(total)
        stats_ref[LOCAL + head : LOCAL + head + 1] = jnp.sum(product, 0, keepdims=True)
    stats_ref[2 * LOCAL :] = jnp.zeros((8 - 2 * LOCAL, LAYER * span), f32)
    stats_up[...] = stats_ref[:, span:]
    stats_down[...] = stats_ref[:, :reach]


def query_grad_kernel(
    window_ref, probs_ref, query_ref, stats_ref, dq_ref, own_ref, token_ref, grads
):
    rows = query_ref.shape[1]
    span = query_ref.shape[2] // LAYER
    head_width = rows // LOCAL
    scale = 1.0 / math.sqrt(head_width)
    inside = slice(HOPS * span, (HOPS + LAYER) * span)
    clear(grads, span)
    for head in range(LOCAL):
        at = block(head, head_width)
        grad = query_ref[1, at]
        delta = stats_ref[LOCAL + head : LOCAL + head + 1]
        for j in range(BLOCKS):
            low, high = readers(j)
            cols = slice(low * span, (high + 1) * span)
            back = dot(window_ref[1, at, block(j, span)], grad[:, cols], TN)
            prob = probs_ref[head, block(j, span), cols].astype(f32)
            grads[block(j, span), cols] = (prob * (back - delta[:, cols])).astype(bf16)
        dq_ref[at] = (dot(window_ref[0, at], grads[...], NN) * scale).astype(bf16)
        own_ref[0, at] = dot(query_ref[0, at], grads[inside], NT)
        own_ref[1, at] = dot(grad, probs_ref[head, inside], NT)
    token_ref[...] = jnp.zeros_like(token_ref)


def key_grad_kernel(
    pair_ref, low_ref, high_ref, stats_low, stats_high, dead_ref, own_ref, mixed_ref, dq_ref, *refs
):
    outs, (token_ref, flipped) = refs[:LAYER], refs[LAYER:]
    rows = pair_ref.shape[1]
    span = pair_ref.shape[2] // LAYER
    head_width = rows // LOCAL
    for head in range(LOCAL):
        at = block(head, head_width)
        log_row = slice(head, head + 1)
        delta_row = slice(LOCAL + head, LOCAL + head + 1)
        for i in range(LAYER):
            own = block(i, span)

            def outside(low, high):
                sides = [low[:, i * span :]] if i < HOPS else []
                return jnp.concatenate(sides + ([high[:, : i * span]] if i else []), 1)

            query = outside(low_ref[0, at], high_ref[0, at])
            grad = outside(low_ref[1, at], high_ref[1, at])
            log_sum = outside(stats_low[log_row], stats_high[log_row]) + dead_ref[i : i + 1]
            delta = outside(stats_low[delta_row], stats_high[delta_row])
            prob = jnp.exp(dot(pair_ref[0, at, own], query, TN) - log_sum)
            back = dot(pair_ref[1, at, own], grad, TN)
            grads = (prob * (back - delta)).astype(bf16)
            keys = own_ref[0, at, own] + dot(query, grads, NT)
            values = own_ref[1, at, own] + dot(grad, prob.astype(bf16), NT)
            flipped[0, at, own] = keys.astype(bf16)
            flipped[1, at, own] = values.astype(bf16)
    for peer, out in enumerate(outs):
        at = place(peer, span)
        out[0] = mixed_ref[:, at]
        out[1] = dq_ref[:, at]
        out[2:] = flipped[:, :, at]
    token_ref[...] = jnp.zeros_like(token_ref)


def output_kernel(*refs):
    ins, refs = refs[:LAYER], refs[LAYER:]
    weight_ref, out_ref, dq_ref, dk_ref, dv_ref, token_ref, flipped = refs
    for peer, ref in enumerate(ins):
        flipped[:, place(peer, ref.shape[1])] = ref[...]
    out_ref[...] = dot(flipped[0], weight_ref[...], TN).astype(bf16)
    for n, ref in enumerate((dq_ref, dk_ref, dv_ref)):
        ref[...] = flipped[n + 1].T
    token_ref[...] = jnp.zeros_like(token_ref)


def halves(bit, half):
    send = pl.ds(pl.multiple_of((1 - bit) * half, half), half)
    keep = pl.ds(pl.multiple_of(bit * half, half), half)
    return send, keep


def bit_of(stride):
    return lax.rem(lax.axis_index("station") // stride, 2)


def weight_kernel(mixed_ref, *refs):
    ins, (send_ref, keep_ref, right) = refs[:LAYER], refs[LAYER:]
    for peer, ref in enumerate(ins):
        right[place(peer, ref.shape[0])] = ref[...]
    send, keep = halves(lax.rem(lax.axis_index("dp"), 2), send_ref.shape[0])
    send_ref[...] = dot(mixed_ref[send], right[...], NN).astype(bf16)
    keep_ref[...] = dot(mixed_ref[keep], right[...], NN)


def split_kernel(stride, part_ref, got_ref, send_ref, keep_ref):
    send, keep = halves(bit_of(stride), send_ref.shape[0])
    send_ref[...] = (part_ref[send] + got_ref[send].astype(f32)).astype(bf16)
    keep_ref[...] = part_ref[keep] + got_ref[keep].astype(f32)


def round_kernel(part_ref, got_ref, out_ref):
    out_ref[...] = (part_ref[...].astype(f32) + got_ref[...].astype(f32)).astype(bf16)


def join_kernel(stride, scale, mine_ref, got_ref, out_ref):
    other, here = halves(bit_of(stride), mine_ref.shape[0])
    for at, ref in ((here, mine_ref), (other, got_ref)):
        value = ref[...]
        if scale is not None:
            value = value.astype(f32) * scale
        out_ref[at] = value


def cross_kernel(mine_ref, first_ref, second_ref, out_ref):
    window = lax.rem(lax.axis_index("dp"), 2)
    other, here = halves(window, mine_ref.shape[0])
    at_home = bit_of(2) == window
    mine, first, second = mine_ref[...], first_ref[...], second_ref[...]
    out_ref[here] = jnp.where(at_home, mine, first)
    out_ref[other] = jnp.where(at_home, first, second)


def local(
    query_states, key_states, value_states, grad_output, out_weight, partner_ids, partner_count
):
    span, width = query_states.shape[2:]
    stations = lax.axis_size("station")
    windows = lax.axis_size("dp")
    rows = width // LAYER
    dma = pltpu.SemaphoreType.DMA

    def swap(value, stride):
        return lax.ppermute(value, "station", [(s ^ stride, s) for s in range(stations)])

    def in_layer(values):
        return [swap(values[n], n + 1) for n in range(LAYER - 1)]

    def along(up, down):
        low = lax.ppermute(up, "station", [(s, (s + LAYER) % stations) for s in range(stations)])
        high = lax.ppermute(down, "station", [(s, (s - LAYER) % stations) for s in range(stations)])
        return low, high

    def other_window(value):
        return lax.ppermute(value, "dp", [(0, 1), (1, 0)])

    def flat(x):
        return x.reshape(span, width)

    q, k, v, g = flat(query_states), flat(key_states), flat(value_states), flat(grad_output)
    flat_shape = shape_of(span, width)
    part_shape = shape_of(2, rows, span)
    reach_shape = shape_of(2, rows, HOPS * span)
    layer_shape = shape_of(2, rows, LAYER * span)

    def gather(parts, after=()):
        return call(
            gather_kernel, [VMEM] * LAYER, [reach_shape, reach_shape, layer_shape], parts,
            name="gather", after=after,
        )

    mine, *parts = call(
        pack_kernel, [HBM] * 2, [part_shape] * LAYER, (k, v),
        [pltpu.VMEM((2, span, width), bf16), pltpu.VMEM((2, width, span), bf16), dma((2,))],
        limit=58, name="pack",
    )
    q, *parts = lax.optimization_barrier((q, *parts))
    parts = in_layer(parts)
    up, down, pair = gather((mine, *parts))
    mine, *query_parts, g_copy = call(
        project_kernel, [VMEM] * 3, [part_shape] * LAYER + [flat_shape],
        (q, g, out_weight), [pltpu.VMEM((2, width, span), bf16)], name="project",
    )
    up, g_later, *query_parts = lax.optimization_barrier((up, g, *query_parts))
    kv_low, kv_high = along(up, down)
    g_across = swap(g_later, 2)
    g_parts = g_copy, swap(g_later, 1), g_across, swap(g_across, 1)
    bias, dead = call(
        functools.partial(live_kernel, stations), [SMEM] * 2,
        [shape_of(16, LAYER * span, dtype=f32), shape_of(8, HOPS * span, dtype=f32)],
        (partner_ids, partner_count), name="live",
    )
    up, down, query = gather((mine, *in_layer(query_parts)), (bias,))
    qg_low, qg_high = along(up, down)
    stats_shape = shape_of(8, HOPS * span, dtype=f32)
    mixed, stats, up, down, probs, window = call(
        forward_kernel, [VMEM] * 5,
        [
            shape_of(rows, LAYER * span), shape_of(8, LAYER * span, dtype=f32),
            stats_shape, stats_shape,
            shape_of(LOCAL, BLOCKS * span, LAYER * span), shape_of(2, rows, BLOCKS * span),
        ],
        (pair, kv_low, kv_high, query, bias),
        [pltpu.VMEM((BLOCKS * span, LAYER * span), f32)],
        limit=20, name="forward",
    )
    stats_low, stats_high = along(up, down)

    send, part = call(
        weight_kernel, [VMEM] * (LAYER + 1),
        [shape_of(rows // 2, width), shape_of(rows // 2, width, dtype=f32)],
        (mixed, *g_parts), [pltpu.VMEM((LAYER * span, width), bf16)], name="weight",
    )

    dq, own_grad, query_token = call(
        query_grad_kernel, [VMEM] * 4,
        [shape_of(rows, LAYER * span), shape_of(2, rows, LAYER * span, dtype=f32), TOKEN],
        (window, probs, query, stats), [pltpu.VMEM((BLOCKS * span, LAYER * span), bf16)],
        limit=20, name="query_grad", after=(send,),
    )
    mine, *parts, key_token = call(
        key_grad_kernel, [VMEM] * 9, [shape_of(4, rows, span)] * LAYER + [TOKEN],
        (pair, qg_low, qg_high, stats_low, stats_high, dead, own_grad, mixed, dq),
        [pltpu.VMEM((2, rows, LAYER * span), bf16)], limit=20, name="key_grad",
    )
    parts = in_layer(parts)
    layer_output, grad_query, grad_key, grad_value, output_token = call(
        output_kernel, [VMEM] * (LAYER + 1), [flat_shape] * 4 + [TOKEN],
        (mine, *parts, out_weight), [pltpu.VMEM((4, width, span), bf16)], name="output",
    )

    scale = 1.0 / math.sqrt(span * windows * stations)
    if windows == 2:
        count = rows // 4
        got = other_window(send)
        send, part = call(
            functools.partial(split_kernel, LAYER), [VMEM] * 2,
            [shape_of(count, width), shape_of(count, width, dtype=f32)],
            (part, got), name="split", after=(query_token,),
        )

        def add_round(part, got, after=()):
            out = [shape_of(count, width)]
            return call(round_kernel, [VMEM] * 2, out, (part, got), name="add", after=after)[0]

        total = add_round(part, swap(send, LAYER), (key_token,))
        stride = 2 * LAYER
        while stride < stations:
            total = add_round(total, swap(total, stride))
            stride *= 2
        (total,) = call(
            functools.partial(join_kernel, LAYER, None), [VMEM] * 2, [shape_of(2 * count, width)],
            (total, swap(total, LAYER)), name="join", after=parts,
        )
        first, second = [], []
        for w in range(2):
            for s in range(stations):
                if s // 2 % 2 == w:
                    first.append((w * stations + s, w * stations + (s ^ 2)))
                else:
                    first.append((w * stations + s, (1 - w) * stations + s))
                    second.append((w * stations + s, (1 - w) * stations + (s ^ 2)))
        axes = ("dp", "station")
        (total,) = call(
            cross_kernel, [VMEM] * 3, [shape_of(4 * count, width)],
            (total, lax.ppermute(total, axes, first), lax.ppermute(total, axes, second)),
            name="cross", after=(output_token,),
        )
        (grad_weight,) = call(
            functools.partial(join_kernel, 1, scale), [VMEM] * 2,
            [shape_of(8 * count, width, dtype=f32)], (total, swap(total, 1)), name="last",
        )
    else:
        start = lax.axis_index("station") % LAYER * rows
        all_grad = jnp.zeros((LAYER * span, width), bf16)
        for peer in range(LAYER):
            value = g_parts[peer]
            spot = lax.axis_index("station") % LAYER ^ peer
            all_grad = lax.dynamic_update_slice_in_dim(all_grad, value, spot * span, 0)
        mine = dot(mixed, all_grad, NN).astype(bf16)
        whole = lax.dynamic_update_slice_in_dim(jnp.zeros((width, width), bf16), mine, start, 0)
        whole = lax.psum_scatter(whole, "dp", scatter_dimension=0, tiled=True)
        grad_weight = lax.psum(whole.astype(f32), "station") * scale
    shape = query_states.shape
    return (
        layer_output.reshape(shape),
        grad_query.reshape(shape),
        grad_key.reshape(shape),
        grad_value.reshape(shape),
        grad_weight,
    )


def solution(mesh):
    split = P("dp", "station", None, None)
    return jax.shard_map(
        local,
        mesh=mesh,
        in_specs=(split, split, split, split, P(), P(), P()),
        out_specs=(split, split, split, split, P("dp", None)),
        check_vma=False,
    )
```

```python
import functools
import math

import jax
import jax.numpy as jnp
from jax import lax
from jax.experimental import pallas as pl
from jax.experimental.pallas import tpu as pltpu
from jax.sharding import PartitionSpec as P

HEADS = 12
PMAX = 6
HOPS = 3
LAYER = 4
LOCAL = HEADS // LAYER
BLOCKS = LAYER + 2 * HOPS
SLOTS = 2 * HOPS + 1
MIB = 1024 * 1024

neg_big = -1e30
bf16, f32 = jnp.bfloat16, jnp.float32
SMEM = pl.BlockSpec(memory_space=pltpu.SMEM)
VMEM = pl.BlockSpec(memory_space=pltpu.VMEM)
ANY = pl.BlockSpec(memory_space=pl.ANY)
HBM = pl.BlockSpec(memory_space=pltpu.HBM)
NN = (((1,), (0,)), ((), ()))
NT = (((1,), (1,)), ((), ()))
TN = (((0,), (0,)), ((), ()))


def dot(x, y, dims):
    return lax.dot_general(x, y, dims, preferred_element_type=f32)


def shape_of(*dims, dtype=bf16):
    return jax.ShapeDtypeStruct(dims, dtype)


TOKEN = shape_of(8, 128, dtype=f32)


def skip_refs(kernel, first, count, *refs):
    kernel(*refs[:first], *refs[first + count :])


def call(kernel, ins, outs, args, scratch=(), limit=8, name=None, after=()):
    ins, args = [*ins, *[ANY] * len(after)], (*args, *after)
    if after:
        kernel = functools.partial(skip_refs, kernel, len(args) - len(after), len(after))
    return pl.pallas_call(
        kernel,
        in_specs=ins,
        out_specs=[VMEM] * len(outs),
        out_shape=outs,
        scratch_shapes=list(scratch),
        compiler_params=pltpu.CompilerParams(vmem_limit_bytes=limit * MIB),
        cost_estimate=pl.CostEstimate(flops=1, bytes_accessed=1, transcendentals=0),
        name=name,
    )(*args)


def place(peer, size):
    position = jnp.bitwise_xor(lax.rem(lax.axis_index("station"), LAYER), peer)
    return pl.ds(pl.multiple_of(position * size, size), size)


def block(j, span):
    return slice(j * span, (j + 1) * span)


def readers(j):
    return max(0, j - 2 * HOPS), min(LAYER - 1, j)


def pack_kernel(k_ref, v_ref, *refs):
    outs, (natural, flipped, sems) = refs[:LAYER], refs[LAYER:]
    rows = outs[0].shape[1]
    copies = [
        pltpu.make_async_copy(ref, natural.at[n], sems.at[n]) for n, ref in enumerate((k_ref, v_ref))
    ]
    for copy in copies:
        copy.start()
    for n, copy in enumerate(copies):
        copy.wait()
        flipped[n] = natural[n].T
    for peer, out in enumerate(outs):
        out[...] = flipped[:, place(peer, rows)]


def project_kernel(q_ref, g_ref, weight_ref, *refs):
    outs, (copy_ref, flipped) = refs[:LAYER], refs[LAYER:]
    rows = outs[0].shape[1]
    copy_ref[...] = g_ref[...]
    flipped[0] = q_ref[...].T * bf16(1.0 / math.sqrt(flipped.shape[1] // HEADS))
    flipped[1] = dot(weight_ref[...], g_ref[...], NT).astype(bf16)
    for peer, out in enumerate(outs):
        out[...] = flipped[:, place(peer, rows)]


def relay_kernel(sib_ref, across_ref, out_ref):
    out_ref[0] = sib_ref[...]
    out_ref[1] = across_ref[1]


def gather_kernel(*refs):
    ins, (up_ref, down_ref, pair_ref) = refs[:LAYER], refs[LAYER:]
    span = ins[0].shape[2]
    for peer, ref in enumerate(ins):
        pair_ref[:, :, place(peer, span)] = ref[...]
    up_ref[...] = pair_ref[:, :, span:]
    down_ref[...] = pair_ref[:, :, : HOPS * span]


def live_kernel(station_count, ids_ref, count_ref, bias_ref, dead_ref):
    span = bias_ref.shape[1] // LAYER
    first = lax.axis_index("station") // LAYER * LAYER
    ones = jnp.ones((1, span), f32)

    def listed(reader, other):
        hit = jnp.int32(0)
        for j in range(PMAX):
            here = jnp.logical_and(ids_ref[reader, j] == other, j < count_ref[reader])
            hit = jnp.maximum(hit, here.astype(jnp.int32))
        return hit > 0

    for j in range(BLOCKS):
        outer = lax.rem(first + (j - HOPS) + station_count, station_count)
        low, high = readers(j)
        for i in range(low, high + 1):
            inner = first + i
            slot = j - i
            if slot == HOPS:
                bias_ref[j : j + 1, block(i, span)] = 0.0 * ones
            else:
                reads = jnp.where(listed(inner, outer), 0.0, neg_big)
                bias_ref[j : j + 1, block(i, span)] = reads * ones
            if not HOPS <= j < HOPS + LAYER:
                read_by = jnp.where(listed(outer, inner), 0.0, -neg_big)
                spot = slot if j < HOPS else slot - LAYER
                dead_ref[i : i + 1, block(spot, span)] = read_by * ones


def clear(ref, span):
    for j in range(BLOCKS):
        low, high = readers(j)
        for i in range(LAYER):
            if not low <= i <= high:
                ref[block(j, span), block(i, span)] = jnp.zeros((span, span), bf16)


def forward_kernel(
    pair_ref, low_ref, high_ref, query_ref, bias_ref,
    mixed_ref, stats_ref, stats_up, stats_down, probs_ref, window_ref,
    raw,
):
    rows = query_ref.shape[1]
    span = query_ref.shape[2] // LAYER
    head_width = rows // LOCAL
    reach = HOPS * span
    window_ref[:, :, :reach] = low_ref[...]
    window_ref[:, :, reach : reach + LAYER * span] = pair_ref[...]
    window_ref[:, :, reach + LAYER * span :] = high_ref[...]
    for head in range(LOCAL):
        clear(probs_ref.at[head], span)
        at = block(head, head_width)
        query = query_ref[0, at]
        tops = [None] * LAYER
        for j in range(BLOCKS):
            low, high = readers(j)
            cols = slice(low * span, (high + 1) * span)
            scores = dot(window_ref[0, at, block(j, span)], query[:, cols], TN)
            scores = scores + bias_ref[j : j + 1, cols]
            raw[block(j, span), cols] = scores
            here = jnp.max(scores, 0, keepdims=True)
            for i in range(low, high + 1):
                mine = here[:, block(i - low, span)]
                tops[i] = mine if tops[i] is None else jnp.maximum(tops[i], mine)
        top = jnp.concatenate(tops, 1)
        totals = [jnp.zeros((1, span), f32)] * LAYER
        for j in range(BLOCKS):
            low, high = readers(j)
            cols = slice(low * span, (high + 1) * span)
            weight = jnp.exp(raw[block(j, span), cols] - top[:, cols])
            raw[block(j, span), cols] = weight
            here = jnp.sum(weight, 0, keepdims=True)
            for i in range(low, high + 1):
                totals[i] = totals[i] + here[:, block(i - low, span)]
        total = jnp.concatenate(totals, 1)
        inverse = 1.0 / total
        for j in range(BLOCKS):
            low, high = readers(j)
            cols = slice(low * span, (high + 1) * span)
            probs_ref[head, block(j, span), cols] = (
                raw[block(j, span), cols] * inverse[:, cols]
            ).astype(bf16)
        mixed = dot(window_ref[1, at], probs_ref[head], NN).astype(bf16)
        mixed_ref[at] = mixed
        product = query_ref[1, at].astype(f32) * mixed.astype(f32)
        stats_ref[head : head + 1] = top + jnp.log(total)
        stats_ref[LOCAL + head : LOCAL + head + 1] = jnp.sum(product, 0, keepdims=True)
    stats_ref[2 * LOCAL :] = jnp.zeros((8 - 2 * LOCAL, LAYER * span), f32)
    stats_up[...] = stats_ref[:, span:]
    stats_down[...] = stats_ref[:, :reach]


def query_grad_kernel(
    window_ref, probs_ref, query_ref, stats_ref, mixed_ref, mine_ref, sib_ref, across_ref, own_ref,
    token_ref, grads, flipped
):
    rows = query_ref.shape[1]
    span = query_ref.shape[2] // LAYER
    head_width = rows // LOCAL
    scale = 1.0 / math.sqrt(head_width)
    inside = slice(HOPS * span, (HOPS + LAYER) * span)
    clear(grads, span)
    for head in range(LOCAL):
        at = block(head, head_width)
        grad = query_ref[1, at]
        delta = stats_ref[LOCAL + head : LOCAL + head + 1]
        for j in range(BLOCKS):
            low, high = readers(j)
            cols = slice(low * span, (high + 1) * span)
            back = dot(window_ref[1, at, block(j, span)], grad[:, cols], TN)
            prob = probs_ref[head, block(j, span), cols].astype(f32)
            grads[block(j, span), cols] = (prob * (back - delta[:, cols])).astype(bf16)
        flipped[at] = (dot(window_ref[0, at], grads[...], NN) * scale).astype(bf16)
        own_ref[0, at] = dot(query_ref[0, at], grads[inside], NT)
        own_ref[1, at] = dot(grad, probs_ref[head, inside], NT)
    for peer, out in enumerate((mine_ref, sib_ref, across_ref.at[0], across_ref.at[1])):
        out[0] = mixed_ref[:, place(peer, span)]
        out[1] = flipped[:, place(peer, span)]
    token_ref[...] = jnp.zeros_like(token_ref)


def key_grad_kernel(
    pair_ref, low_ref, high_ref, stats_low, stats_high, dead_ref, own_ref, *refs
):
    outs, (token_ref, flipped) = refs[:LAYER], refs[LAYER:]
    rows = pair_ref.shape[1]
    span = pair_ref.shape[2] // LAYER
    head_width = rows // LOCAL
    for head in range(LOCAL):
        at = block(head, head_width)
        log_row = slice(head, head + 1)
        delta_row = slice(LOCAL + head, LOCAL + head + 1)
        for i in range(LAYER):
            own = block(i, span)

            def outside(low, high):
                sides = [low[:, i * span :]] if i < HOPS else []
                return jnp.concatenate(sides + ([high[:, : i * span]] if i else []), 1)

            query = outside(low_ref[0, at], high_ref[0, at])
            grad = outside(low_ref[1, at], high_ref[1, at])
            log_sum = outside(stats_low[log_row], stats_high[log_row]) + dead_ref[i : i + 1]
            delta = outside(stats_low[delta_row], stats_high[delta_row])
            prob = jnp.exp(dot(pair_ref[0, at, own], query, TN) - log_sum)
            back = dot(pair_ref[1, at, own], grad, TN)
            grads = (prob * (back - delta)).astype(bf16)
            keys = own_ref[0, at, own] + dot(query, grads, NT)
            values = own_ref[1, at, own] + dot(grad, prob.astype(bf16), NT)
            flipped[0, at, own] = keys.astype(bf16)
            flipped[1, at, own] = values.astype(bf16)
    for peer, out in enumerate(outs):
        out[...] = flipped[:, :, place(peer, span)]
    token_ref[...] = jnp.zeros_like(token_ref)


def output_kernel(
    mine_ref, across_ref, sib_ref, weight_ref, out_ref, dq_ref, token_ref, flipped
):
    ins = mine_ref, sib_ref.at[0], across_ref.at[0], sib_ref.at[1]
    for peer, ref in enumerate(ins):
        flipped[:, place(peer, ref.shape[1])] = ref[...]
    out_ref[...] = dot(flipped[0], weight_ref[...], TN).astype(bf16)
    dq_ref[...] = flipped[1].T
    token_ref[...] = jnp.zeros_like(token_ref)


def key_output_kernel(*refs):
    ins, (dk_ref, dv_ref, token_ref, flipped) = refs[:LAYER], refs[LAYER:]
    for peer, ref in enumerate(ins):
        flipped[:, place(peer, ref.shape[1])] = ref[...]
    dk_ref[...] = flipped[0].T
    dv_ref[...] = flipped[1].T
    token_ref[...] = jnp.zeros_like(token_ref)


def halves(bit, half):
    send = pl.ds(pl.multiple_of((1 - bit) * half, half), half)
    keep = pl.ds(pl.multiple_of(bit * half, half), half)
    return send, keep


def bit_of(stride):
    return lax.rem(lax.axis_index("station") // stride, 2)


def weight_kernel(mixed_ref, *refs):
    ins, (send_ref, keep_ref, right) = refs[:LAYER], refs[LAYER:]
    for peer, ref in enumerate(ins):
        right[place(peer, ref.shape[0])] = ref[...]
    send, keep = halves(lax.rem(lax.axis_index("dp"), 2), send_ref.shape[0])
    send_ref[...] = dot(mixed_ref[send], right[...], NN).astype(bf16)
    keep_ref[...] = dot(mixed_ref[keep], right[...], NN)


def split_kernel(stride, part_ref, got_ref, send_ref, keep_ref):
    send, keep = halves(bit_of(stride), send_ref.shape[0])
    send_ref[...] = (part_ref[send] + got_ref[send].astype(f32)).astype(bf16)
    keep_ref[...] = part_ref[keep] + got_ref[keep].astype(f32)


def round_kernel(part_ref, got_ref, out_ref):
    out_ref[...] = (part_ref[...].astype(f32) + got_ref[...].astype(f32)).astype(bf16)


def join_kernel(stride, scale, mine_ref, got_ref, out_ref):
    other, here = halves(bit_of(stride), mine_ref.shape[0])
    for at, ref in ((here, mine_ref), (other, got_ref)):
        value = ref[...]
        if scale is not None:
            value = value.astype(f32) * scale
        out_ref[at] = value


def cross_kernel(mine_ref, second_ref, first_ref, out_ref):
    window = lax.rem(lax.axis_index("dp"), 2)
    other, here = halves(window, mine_ref.shape[0])
    at_home = bit_of(2) == window
    mine, first, second = mine_ref[...], first_ref[...], second_ref[...]
    out_ref[here] = jnp.where(at_home, mine, first)
    out_ref[other] = jnp.where(at_home, first, second)


def local(
    query_states, key_states, value_states, grad_output, out_weight, partner_ids, partner_count
):
    span, width = query_states.shape[2:]
    stations = lax.axis_size("station")
    windows = lax.axis_size("dp")
    rows = width // LAYER
    dma = pltpu.SemaphoreType.DMA

    def swap(value, stride):
        return lax.ppermute(value, "station", [(s ^ stride, s) for s in range(stations)])

    def in_layer(values):
        return [swap(values[n], n + 1) for n in range(LAYER - 1)]

    def along(up, down):
        low = lax.ppermute(up, "station", [(s, (s + LAYER) % stations) for s in range(stations)])
        high = lax.ppermute(down, "station", [(s, (s - LAYER) % stations) for s in range(stations)])
        return low, high

    def other_window(value):
        return lax.ppermute(value, "dp", [(0, 1), (1, 0)])

    def flat(x):
        return x.reshape(span, width)

    q, k, v, g = flat(query_states), flat(key_states), flat(value_states), flat(grad_output)
    flat_shape = shape_of(span, width)
    part_shape = shape_of(2, rows, span)
    reach_shape = shape_of(2, rows, HOPS * span)
    layer_shape = shape_of(2, rows, LAYER * span)

    def gather(parts, after=()):
        return call(
            gather_kernel, [VMEM] * LAYER, [reach_shape, reach_shape, layer_shape], parts,
            name="gather", after=after,
        )

    mine, *parts = call(
        pack_kernel, [HBM] * 2, [part_shape] * LAYER, (k, v),
        [pltpu.VMEM((2, span, width), bf16), pltpu.VMEM((2, width, span), bf16), dma((2,))],
        limit=58, name="pack",
    )
    q, *parts = lax.optimization_barrier((q, *parts))
    parts = in_layer(parts)
    up, down, pair = gather((mine, *parts))
    mine, *query_parts, g_copy = call(
        project_kernel, [VMEM] * 3, [part_shape] * LAYER + [flat_shape],
        (q, g, out_weight), [pltpu.VMEM((2, width, span), bf16)], name="project",
    )
    up, g_later, *query_parts = lax.optimization_barrier((up, g, *query_parts))
    kv_low, kv_high = along(up, down)
    g_across = swap(g_later, 2)
    g_parts = g_copy, swap(g_later, 1), g_across, swap(g_across, 1)
    bias, dead = call(
        functools.partial(live_kernel, stations), [SMEM] * 2,
        [shape_of(16, LAYER * span, dtype=f32), shape_of(8, HOPS * span, dtype=f32)],
        (partner_ids, partner_count), name="live",
    )
    up, down, query = gather((mine, *in_layer(query_parts)), (bias,))
    qg_low, qg_high = along(up, down)
    stats_shape = shape_of(8, HOPS * span, dtype=f32)
    mixed, stats, up, down, probs, window = call(
        forward_kernel, [VMEM] * 5,
        [
            shape_of(rows, LAYER * span), shape_of(8, LAYER * span, dtype=f32),
            stats_shape, stats_shape,
            shape_of(LOCAL, BLOCKS * span, LAYER * span), shape_of(2, rows, BLOCKS * span),
        ],
        (pair, kv_low, kv_high, query, bias),
        [pltpu.VMEM((BLOCKS * span, LAYER * span), f32)],
        limit=20, name="forward",
    )

    send, part = call(
        weight_kernel, [VMEM] * (LAYER + 1),
        [shape_of(rows // 2, width), shape_of(rows // 2, width, dtype=f32)],
        (mixed, *g_parts), [pltpu.VMEM((LAYER * span, width), bf16)], name="weight",
    )

    if windows == 2:
        got = other_window(send)
        up, down, got = lax.optimization_barrier((up, down, got))
    stats_low, stats_high = along(up, down)
    own_return, to_sib, to_across, own_grad, query_token = call(
        query_grad_kernel, [VMEM] * 5,
        [part_shape, part_shape, shape_of(2, 2, rows, span), shape_of(2, rows, LAYER * span, dtype=f32)]
        + [TOKEN],
        (window, probs, query, stats, mixed),
        [pltpu.VMEM((BLOCKS * span, LAYER * span), bf16), pltpu.VMEM((rows, LAYER * span), bf16)],
        limit=20, name="query_grad", after=(send,),
    )
    def first_return(across):
        (relay,) = call(
            relay_kernel, [VMEM] * 2, [shape_of(2, 2, rows, span)], (to_sib, across), name="relay"
        )
        relayed = swap(relay, 1)
        layer_output, grad_query, output_token = call(
            output_kernel, [VMEM] * 4, [flat_shape] * 2 + [TOKEN],
            (own_return, across, relayed, out_weight), [pltpu.VMEM((2, width, span), bf16)], name="output",
        )
        return layer_output, grad_query, output_token

    mine, *parts, key_token = call(
        key_grad_kernel, [VMEM] * 7, [part_shape] * LAYER + [TOKEN],
        (pair, qg_low, qg_high, stats_low, stats_high, dead, own_grad),
        [pltpu.VMEM((2, rows, LAYER * span), bf16)], limit=20, name="key_grad",
    )
    key_parts = in_layer(parts)
    grad_key, grad_value, key_output_token = call(
        key_output_kernel, [VMEM] * LAYER, [flat_shape] * 2 + [TOKEN],
        (mine, *key_parts), [pltpu.VMEM((2, width, span), bf16)], name="key_output",
    )

    scale = 1.0 / math.sqrt(span * windows * stations)
    if windows == 2:
        count = rows // 4
        across = swap(to_across, 2)
        send, part = call(
            functools.partial(split_kernel, LAYER), [VMEM] * 2,
            [shape_of(count, width), shape_of(count, width, dtype=f32)],
            (part, got), name="split", after=(query_token, qg_low, qg_high, stats_low, stats_high),
        )

        layer_output, grad_query, output_token = first_return(across)

        def add_round(part, got, after=()):
            out = [shape_of(count, width)]
            return call(round_kernel, [VMEM] * 2, out, (part, got), name="add", after=after)[0]

        total = add_round(part, swap(send, LAYER), (key_token, across))
        stride = 2 * LAYER
        while stride < stations:
            total = add_round(total, swap(total, stride))
            stride *= 2
        (total,) = call(
            functools.partial(join_kernel, LAYER, None), [VMEM] * 2, [shape_of(2 * count, width)],
            (total, swap(total, LAYER)), name="join", after=key_parts,
        )
        first, second = [], []
        for w in range(2):
            for s in range(stations):
                if s // 2 % 2 == w:
                    first.append((w * stations + s, w * stations + (s ^ 2)))
                else:
                    first.append((w * stations + s, (1 - w) * stations + s))
                    second.append((w * stations + s, (1 - w) * stations + (s ^ 2)))
        axes = ("dp", "station")
        (total,) = call(
            cross_kernel, [VMEM] * 3, [shape_of(4 * count, width)],
            (total, lax.ppermute(total, axes, second), lax.ppermute(total, axes, first)),
            name="cross", after=(output_token, key_output_token),
        )
        (grad_weight,) = call(
            functools.partial(join_kernel, 1, scale), [VMEM] * 2,
            [shape_of(8 * count, width, dtype=f32)], (total, swap(total, 1)), name="last",
        )
    else:
        layer_output, grad_query, _ = first_return(swap(to_across, 2))
        start = lax.axis_index("station") % LAYER * rows
        all_grad = jnp.zeros((LAYER * span, width), bf16)
        for peer in range(LAYER):
            value = g_parts[peer]
            spot = lax.axis_index("station") % LAYER ^ peer
            all_grad = lax.dynamic_update_slice_in_dim(all_grad, value, spot * span, 0)
        mine = dot(mixed, all_grad, NN).astype(bf16)
        whole = lax.dynamic_update_slice_in_dim(jnp.zeros((width, width), bf16), mine, start, 0)
        whole = lax.psum_scatter(whole, "dp", scatter_dimension=0, tiled=True)
        grad_weight = lax.psum(whole.astype(f32), "station") * scale
    shape = query_states.shape
    return (
        layer_output.reshape(shape),
        grad_query.reshape(shape),
        grad_key.reshape(shape),
        grad_value.reshape(shape),
        grad_weight,
    )


def solution(mesh):
    split = P("dp", "station", None, None)
    return jax.shard_map(
        local,
        mesh=mesh,
        in_specs=(split, split, split, split, P(), P(), P()),
        out_specs=(split, split, split, split, P("dp", None)),
        check_vma=False,
    )
```

```python
import functools
import math

import jax
import jax.numpy as jnp
from jax import lax
from jax.experimental import pallas as pl
from jax.experimental.pallas import tpu as pltpu
from jax.sharding import PartitionSpec as P

HEADS = 12
PMAX = 6
HOPS = 3
LAYER = 4
LOCAL = HEADS // LAYER
BLOCKS = LAYER + 2 * HOPS
SLOTS = 2 * HOPS + 1
MIB = 1024 * 1024

neg_big = -1e30
bf16, f32 = jnp.bfloat16, jnp.float32
SMEM = pl.BlockSpec(memory_space=pltpu.SMEM)
VMEM = pl.BlockSpec(memory_space=pltpu.VMEM)
ANY = pl.BlockSpec(memory_space=pl.ANY)
HBM = pl.BlockSpec(memory_space=pltpu.HBM)
NN = (((1,), (0,)), ((), ()))
NT = (((1,), (1,)), ((), ()))
TN = (((0,), (0,)), ((), ()))


def dot(x, y, dims):
    return lax.dot_general(x, y, dims, preferred_element_type=f32)


def shape_of(*dims, dtype=bf16):
    return jax.ShapeDtypeStruct(dims, dtype)


TOKEN = shape_of(8, 128, dtype=f32)


def skip_refs(kernel, first, count, *refs):
    kernel(*refs[:first], *refs[first + count :])


def call(kernel, ins, outs, args, scratch=(), limit=8, name=None, after=()):
    ins, args = [*ins, *[ANY] * len(after)], (*args, *after)
    if after:
        kernel = functools.partial(skip_refs, kernel, len(args) - len(after), len(after))
    return pl.pallas_call(
        kernel,
        in_specs=ins,
        out_specs=[VMEM] * len(outs),
        out_shape=outs,
        scratch_shapes=list(scratch),
        compiler_params=pltpu.CompilerParams(vmem_limit_bytes=limit * MIB),
        cost_estimate=pl.CostEstimate(flops=1, bytes_accessed=1, transcendentals=0),
        name=name,
    )(*args)


def place(peer, size):
    position = jnp.bitwise_xor(lax.rem(lax.axis_index("station"), LAYER), peer)
    return pl.ds(pl.multiple_of(position * size, size), size)


def block(j, span):
    return slice(j * span, (j + 1) * span)


def readers(j):
    return max(0, j - 2 * HOPS), min(LAYER - 1, j)


def pack_kernel(k_ref, v_ref, *refs):
    outs, (natural, flipped, sems) = refs[:LAYER], refs[LAYER:]
    rows = outs[0].shape[1]
    copies = [
        pltpu.make_async_copy(ref, natural.at[n], sems.at[n]) for n, ref in enumerate((k_ref, v_ref))
    ]
    for copy in copies:
        copy.start()
    for n, copy in enumerate(copies):
        copy.wait()
        flipped[n] = natural[n].T
    for peer, out in enumerate(outs):
        out[...] = flipped[:, place(peer, rows)]


def project_kernel(q_ref, g_ref, weight_ref, *refs):
    outs, (copy_ref, flipped) = refs[:LAYER], refs[LAYER:]
    rows = outs[0].shape[1]
    copy_ref[...] = g_ref[...]
    flipped[0] = q_ref[...].T * bf16(1.0 / math.sqrt(flipped.shape[1] // HEADS))
    flipped[1] = dot(weight_ref[...], g_ref[...], NT).astype(bf16)
    for peer, out in enumerate(outs):
        out[...] = flipped[:, place(peer, rows)]


def gather_kernel(*refs):
    ins, (up_ref, down_ref, pair_ref) = refs[:LAYER], refs[LAYER:]
    span = ins[0].shape[2]
    for peer, ref in enumerate(ins):
        pair_ref[:, :, place(peer, span)] = ref[...]
    up_ref[...] = pair_ref[:, :, span:]
    down_ref[...] = pair_ref[:, :, : HOPS * span]


def live_kernel(station_count, ids_ref, count_ref, bias_ref, dead_ref):
    span = bias_ref.shape[1] // LAYER
    first = lax.axis_index("station") // LAYER * LAYER
    ones = jnp.ones((1, span), f32)

    def listed(reader, other):
        hit = jnp.int32(0)
        for j in range(PMAX):
            here = jnp.logical_and(ids_ref[reader, j] == other, j < count_ref[reader])
            hit = jnp.maximum(hit, here.astype(jnp.int32))
        return hit > 0

    for j in range(BLOCKS):
        outer = lax.rem(first + (j - HOPS) + station_count, station_count)
        low, high = readers(j)
        for i in range(low, high + 1):
            inner = first + i
            slot = j - i
            if slot == HOPS:
                bias_ref[j : j + 1, block(i, span)] = 0.0 * ones
            else:
                reads = jnp.where(listed(inner, outer), 0.0, neg_big)
                bias_ref[j : j + 1, block(i, span)] = reads * ones
            if not HOPS <= j < HOPS + LAYER:
                read_by = jnp.where(listed(outer, inner), 0.0, -neg_big)
                spot = slot if j < HOPS else slot - LAYER
                dead_ref[i : i + 1, block(spot, span)] = read_by * ones


def clear(ref, span):
    for j in range(BLOCKS):
        low, high = readers(j)
        for i in range(LAYER):
            if not low <= i <= high:
                ref[block(j, span), block(i, span)] = jnp.zeros((span, span), bf16)


def forward_kernel(
    pair_ref, low_ref, high_ref, query_ref, bias_ref,
    mixed_ref, stats_ref, stats_up, stats_down, probs_ref, window_ref,
    raw,
):
    rows = query_ref.shape[1]
    span = query_ref.shape[2] // LAYER
    head_width = rows // LOCAL
    reach = HOPS * span
    window_ref[:, :, :reach] = low_ref[...]
    window_ref[:, :, reach : reach + LAYER * span] = pair_ref[...]
    window_ref[:, :, reach + LAYER * span :] = high_ref[...]
    for head in range(LOCAL):
        clear(probs_ref.at[head], span)
        at = block(head, head_width)
        query = query_ref[0, at]
        tops = [None] * LAYER
        for j in range(BLOCKS):
            low, high = readers(j)
            cols = slice(low * span, (high + 1) * span)
            scores = dot(window_ref[0, at, block(j, span)], query[:, cols], TN)
            scores = scores + bias_ref[j : j + 1, cols]
            raw[block(j, span), cols] = scores
            here = jnp.max(scores, 0, keepdims=True)
            for i in range(low, high + 1):
                mine = here[:, block(i - low, span)]
                tops[i] = mine if tops[i] is None else jnp.maximum(tops[i], mine)
        top = jnp.concatenate(tops, 1)
        totals = [jnp.zeros((1, span), f32)] * LAYER
        for j in range(BLOCKS):
            low, high = readers(j)
            cols = slice(low * span, (high + 1) * span)
            weight = jnp.exp(raw[block(j, span), cols] - top[:, cols])
            raw[block(j, span), cols] = weight
            here = jnp.sum(weight, 0, keepdims=True)
            for i in range(low, high + 1):
                totals[i] = totals[i] + here[:, block(i - low, span)]
        total = jnp.concatenate(totals, 1)
        inverse = 1.0 / total
        for j in range(BLOCKS):
            low, high = readers(j)
            cols = slice(low * span, (high + 1) * span)
            probs_ref[head, block(j, span), cols] = (
                raw[block(j, span), cols] * inverse[:, cols]
            ).astype(bf16)
        mixed = dot(window_ref[1, at], probs_ref[head], NN).astype(bf16)
        mixed_ref[at] = mixed
        product = query_ref[1, at].astype(f32) * mixed.astype(f32)
        stats_ref[head : head + 1] = top + jnp.log(total)
        stats_ref[LOCAL + head : LOCAL + head + 1] = jnp.sum(product, 0, keepdims=True)
    stats_ref[2 * LOCAL :] = jnp.zeros((8 - 2 * LOCAL, LAYER * span), f32)
    stats_up[...] = stats_ref[:, span:]
    stats_down[...] = stats_ref[:, :reach]


def query_grad_kernel(
    window_ref, probs_ref, query_ref, stats_ref, dq_ref, own_ref, token_ref, grads
):
    rows = query_ref.shape[1]
    span = query_ref.shape[2] // LAYER
    head_width = rows // LOCAL
    scale = 1.0 / math.sqrt(head_width)
    inside = slice(HOPS * span, (HOPS + LAYER) * span)
    clear(grads, span)
    for head in range(LOCAL):
        at = block(head, head_width)
        grad = query_ref[1, at]
        delta = stats_ref[LOCAL + head : LOCAL + head + 1]
        for j in range(BLOCKS):
            low, high = readers(j)
            cols = slice(low * span, (high + 1) * span)
            back = dot(window_ref[1, at, block(j, span)], grad[:, cols], TN)
            prob = probs_ref[head, block(j, span), cols].astype(f32)
            grads[block(j, span), cols] = (prob * (back - delta[:, cols])).astype(bf16)
        dq_ref[at] = (dot(window_ref[0, at], grads[...], NN) * scale).astype(bf16)
        own_ref[0, at] = dot(query_ref[0, at], grads[inside], NT)
        own_ref[1, at] = dot(grad, probs_ref[head, inside], NT)
    token_ref[...] = jnp.zeros_like(token_ref)


def key_grad_kernel(
    pair_ref, low_ref, high_ref, stats_low, stats_high, dead_ref, own_ref, mixed_ref, dq_ref, *refs
):
    outs, (token_ref, flipped, scores, backs, probs, grads) = refs[:LAYER], refs[LAYER:]
    rows = pair_ref.shape[1]
    span = pair_ref.shape[2] // LAYER
    head_width = rows // LOCAL
    pairs = [(head, i) for head in range(LOCAL) for i in range(LAYER)]

    def outside(low, high, i):
        sides = [low[:, i * span :]] if i < HOPS else []
        return jnp.concatenate(sides + ([high[:, : i * span]] if i else []), 1)

    def both(part, head, i):
        at = block(head, head_width)
        return outside(low_ref[part, at], high_ref[part, at], i)

    for n, (head, i) in enumerate(pairs):
        at, own = block(head, head_width), block(i, span)
        scores[n] = dot(pair_ref[0, at, own], both(0, head, i), TN)
        backs[n] = dot(pair_ref[1, at, own], both(1, head, i), TN)
    for n, (head, i) in enumerate(pairs):
        row = slice(head, head + 1)
        log_sum = outside(stats_low[row], stats_high[row], i) + dead_ref[i : i + 1]
        row = slice(LOCAL + head, LOCAL + head + 1)
        delta = outside(stats_low[row], stats_high[row], i)
        prob = jnp.exp(scores[n] - log_sum)
        probs[n] = prob.astype(bf16)
        grads[n] = (prob * (backs[n] - delta)).astype(bf16)
    for n, (head, i) in enumerate(pairs):
        at, own = block(head, head_width), block(i, span)
        keys = own_ref[0, at, own] + dot(both(0, head, i), grads[n], NT)
        values = own_ref[1, at, own] + dot(both(1, head, i), probs[n], NT)
        flipped[0, at, own] = keys.astype(bf16)
        flipped[1, at, own] = values.astype(bf16)
    for peer, out in enumerate(outs):
        at = place(peer, span)
        out[0] = mixed_ref[:, at]
        out[1] = dq_ref[:, at]
        out[2:] = flipped[:, :, at]
    token_ref[...] = jnp.zeros_like(token_ref)


def output_kernel(*refs):
    ins, refs = refs[:LAYER], refs[LAYER:]
    weight_ref, out_ref, dq_ref, dk_ref, dv_ref, token_ref, flipped = refs
    for peer, ref in enumerate(ins):
        flipped[:, place(peer, ref.shape[1])] = ref[...]
    out_ref[...] = dot(flipped[0], weight_ref[...], TN).astype(bf16)
    for n, ref in enumerate((dq_ref, dk_ref, dv_ref)):
        ref[...] = flipped[n + 1].T
    token_ref[...] = jnp.zeros_like(token_ref)


def halves(bit, half):
    send = pl.ds(pl.multiple_of((1 - bit) * half, half), half)
    keep = pl.ds(pl.multiple_of(bit * half, half), half)
    return send, keep


def bit_of(stride):
    return lax.rem(lax.axis_index("station") // stride, 2)


def weight_kernel(mixed_ref, *refs):
    ins, (send_ref, keep_ref, right) = refs[:LAYER], refs[LAYER:]
    for peer, ref in enumerate(ins):
        right[place(peer, ref.shape[0])] = ref[...]
    send, keep = halves(lax.rem(lax.axis_index("dp"), 2), send_ref.shape[0])
    send_ref[...] = dot(mixed_ref[send], right[...], NN).astype(bf16)
    keep_ref[...] = dot(mixed_ref[keep], right[...], NN)


def split_kernel(stride, part_ref, got_ref, send_ref, keep_ref):
    send, keep = halves(bit_of(stride), send_ref.shape[0])
    send_ref[...] = (part_ref[send] + got_ref[send].astype(f32)).astype(bf16)
    keep_ref[...] = part_ref[keep] + got_ref[keep].astype(f32)


def round_kernel(part_ref, got_ref, out_ref):
    out_ref[...] = (part_ref[...].astype(f32) + got_ref[...].astype(f32)).astype(bf16)


def join_kernel(stride, mine_ref, got_ref, out_ref):
    other, here = halves(bit_of(stride), mine_ref.shape[0])
    out_ref[here] = mine_ref[...]
    out_ref[other] = got_ref[...]


def write_kernel(own, scale, value_ref, *refs):
    out_ref, wide, sem = refs[-3:]
    half = value_ref.shape[0]
    other, here = halves(bit_of(1), half)
    wide[...] = value_ref[...].astype(f32) * scale
    copy = pltpu.make_async_copy(wide, out_ref.at[here if own else other], sem)
    copy.start()
    copy.wait()


def cross_kernel(mine_ref, first_ref, second_ref, out_ref):
    window = lax.rem(lax.axis_index("dp"), 2)
    other, here = halves(window, mine_ref.shape[0])
    at_home = bit_of(2) == window
    mine, first, second = mine_ref[...], first_ref[...], second_ref[...]
    out_ref[here] = jnp.where(at_home, mine, first)
    out_ref[other] = jnp.where(at_home, first, second)


def local(
    query_states, key_states, value_states, grad_output, out_weight, partner_ids, partner_count
):
    span, width = query_states.shape[2:]
    stations = lax.axis_size("station")
    windows = lax.axis_size("dp")
    rows = width // LAYER
    dma = pltpu.SemaphoreType.DMA

    def swap(value, stride):
        return lax.ppermute(value, "station", [(s ^ stride, s) for s in range(stations)])

    def in_layer(values):
        return [swap(values[n], n + 1) for n in range(LAYER - 1)]

    def along(up, down):
        low = lax.ppermute(up, "station", [(s, (s + LAYER) % stations) for s in range(stations)])
        high = lax.ppermute(down, "station", [(s, (s - LAYER) % stations) for s in range(stations)])
        return low, high

    def other_window(value):
        return lax.ppermute(value, "dp", [(0, 1), (1, 0)])

    def flat(x):
        return x.reshape(span, width)

    q, k, v, g = flat(query_states), flat(key_states), flat(value_states), flat(grad_output)
    flat_shape = shape_of(span, width)
    part_shape = shape_of(2, rows, span)
    reach_shape = shape_of(2, rows, HOPS * span)
    layer_shape = shape_of(2, rows, LAYER * span)

    def gather(parts, after=()):
        return call(
            gather_kernel, [VMEM] * LAYER, [reach_shape, reach_shape, layer_shape], parts,
            name="gather", after=after,
        )

    mine, *parts = call(
        pack_kernel, [HBM] * 2, [part_shape] * LAYER, (k, v),
        [pltpu.VMEM((2, span, width), bf16), pltpu.VMEM((2, width, span), bf16), dma((2,))],
        limit=58, name="pack",
    )
    q, *parts = lax.optimization_barrier((q, *parts))
    parts = in_layer(parts)
    up, down, pair = gather((mine, *parts))
    mine, *query_parts, g_copy = call(
        project_kernel, [VMEM] * 3, [part_shape] * LAYER + [flat_shape],
        (q, g, out_weight), [pltpu.VMEM((2, width, span), bf16)], name="project",
    )
    up, g_later, *query_parts = lax.optimization_barrier((up, g, *query_parts))
    kv_low, kv_high = along(up, down)
    g_across = swap(g_later, 2)
    g_parts = g_copy, swap(g_later, 1), g_across, swap(g_across, 1)
    bias, dead = call(
        functools.partial(live_kernel, stations), [SMEM] * 2,
        [shape_of(16, LAYER * span, dtype=f32), shape_of(8, HOPS * span, dtype=f32)],
        (partner_ids, partner_count), name="live",
    )
    up, down, query = gather((mine, *in_layer(query_parts)), (bias,))
    qg_low, qg_high = along(up, down)
    stats_shape = shape_of(8, HOPS * span, dtype=f32)
    mixed, stats, up, down, probs, window = call(
        forward_kernel, [VMEM] * 5,
        [
            shape_of(rows, LAYER * span), shape_of(8, LAYER * span, dtype=f32),
            stats_shape, stats_shape,
            shape_of(LOCAL, BLOCKS * span, LAYER * span), shape_of(2, rows, BLOCKS * span),
        ],
        (pair, kv_low, kv_high, query, bias),
        [pltpu.VMEM((BLOCKS * span, LAYER * span), f32)],
        limit=20, name="forward",
    )
    stats_low, stats_high = along(up, down)

    send, part = call(
        weight_kernel, [VMEM] * (LAYER + 1),
        [shape_of(rows // 2, width), shape_of(rows // 2, width, dtype=f32)],
        (mixed, *g_parts), [pltpu.VMEM((LAYER * span, width), bf16)], name="weight",
    )

    dq, own_grad, query_token = call(
        query_grad_kernel, [VMEM] * 4,
        [shape_of(rows, LAYER * span), shape_of(2, rows, LAYER * span, dtype=f32), TOKEN],
        (window, probs, query, stats), [pltpu.VMEM((BLOCKS * span, LAYER * span), bf16)],
        limit=20, name="query_grad", after=(send,),
    )
    mine, *parts, key_token = call(
        key_grad_kernel, [VMEM] * 9, [shape_of(4, rows, span)] * LAYER + [TOKEN],
        (pair, qg_low, qg_high, stats_low, stats_high, dead, own_grad, mixed, dq),
        [
            pltpu.VMEM((2, rows, LAYER * span), bf16),
            pltpu.VMEM((HEADS, span, HOPS * span), f32),
            pltpu.VMEM((HEADS, span, HOPS * span), f32),
            pltpu.VMEM((HEADS, span, HOPS * span), bf16),
            pltpu.VMEM((HEADS, span, HOPS * span), bf16),
        ],
        limit=24, name="key_grad",
    )
    parts = in_layer(parts)
    layer_output, grad_query, grad_key, grad_value, output_token = call(
        output_kernel, [VMEM] * (LAYER + 1), [flat_shape] * 4 + [TOKEN],
        (mine, *parts, out_weight), [pltpu.VMEM((4, width, span), bf16)], name="output",
    )

    scale = 1.0 / math.sqrt(span * windows * stations)
    if windows == 2:
        count = rows // 4
        got = other_window(send)
        send, part = call(
            functools.partial(split_kernel, LAYER), [VMEM] * 2,
            [shape_of(count, width), shape_of(count, width, dtype=f32)],
            (part, got), name="split", after=(query_token, qg_low, qg_high, stats_low, stats_high),
        )

        def add_round(part, got, after=()):
            out = [shape_of(count, width)]
            return call(round_kernel, [VMEM] * 2, out, (part, got), name="add", after=after)[0]

        total = add_round(part, swap(send, LAYER), (key_token,))
        stride = 2 * LAYER
        while stride < stations:
            total = add_round(total, swap(total, stride))
            stride *= 2
        (total,) = call(
            functools.partial(join_kernel, LAYER), [VMEM] * 2, [shape_of(2 * count, width)],
            (total, swap(total, LAYER)), name="join", after=parts,
        )
        first, second = [], []
        for w in range(2):
            for s in range(stations):
                if s // 2 % 2 == w:
                    first.append((w * stations + s, w * stations + (s ^ 2)))
                else:
                    first.append((w * stations + s, (1 - w) * stations + s))
                    second.append((w * stations + s, (1 - w) * stations + (s ^ 2)))
        axes = ("dp", "station")
        (total,) = call(
            cross_kernel, [VMEM] * 3, [shape_of(4 * count, width)],
            (total, lax.ppermute(total, axes, first), lax.ppermute(total, axes, second)),
            name="cross", after=(output_token,),
        )
        grad_weight = ()
        for own, value in ((True, total), (False, swap(total, 1))):
            grad_weight = (pl.pallas_call(
                functools.partial(write_kernel, own, scale),
                in_specs=[VMEM] + [ANY] * len(grad_weight),
                out_specs=ANY,
                out_shape=shape_of(8 * count, width, dtype=f32),
                scratch_shapes=[pltpu.VMEM((4 * count, width), f32), dma],
                input_output_aliases={1: 0} if grad_weight else {},
                compiler_params=pltpu.CompilerParams(vmem_limit_bytes=8 * MIB),
                cost_estimate=pl.CostEstimate(flops=1, bytes_accessed=1, transcendentals=0),
                name="write",
            )(value, *grad_weight),)
        (grad_weight,) = grad_weight
    else:
        start = lax.axis_index("station") % LAYER * rows
        all_grad = jnp.zeros((LAYER * span, width), bf16)
        for peer in range(LAYER):
            value = g_parts[peer]
            spot = lax.axis_index("station") % LAYER ^ peer
            all_grad = lax.dynamic_update_slice_in_dim(all_grad, value, spot * span, 0)
        mine = dot(mixed, all_grad, NN).astype(bf16)
        whole = lax.dynamic_update_slice_in_dim(jnp.zeros((width, width), bf16), mine, start, 0)
        whole = lax.psum_scatter(whole, "dp", scatter_dimension=0, tiled=True)
        grad_weight = lax.psum(whole.astype(f32), "station") * scale
    shape = query_states.shape
    return (
        layer_output.reshape(shape),
        grad_query.reshape(shape),
        grad_key.reshape(shape),
        grad_value.reshape(shape),
        grad_weight,
    )


def solution(mesh):
    split = P("dp", "station", None, None)
    return jax.shard_map(
        local,
        mesh=mesh,
        in_specs=(split, split, split, split, P(), P(), P()),
        out_specs=(split, split, split, split, P("dp", None)),
        check_vma=False,
    )
```

```python
import functools
import math

import jax
import jax.numpy as jnp
from jax import lax
from jax.experimental import pallas as pl
from jax.experimental.pallas import tpu as pltpu
from jax.sharding import PartitionSpec as P

HEADS = 12
PMAX = 6
HOPS = 3
LAYER = 4
LOCAL = HEADS // LAYER
BLOCKS = LAYER + 2 * HOPS
SLOTS = 2 * HOPS + 1
MIB = 1024 * 1024

neg_big = -1e30
bf16, f32 = jnp.bfloat16, jnp.float32
SMEM = pl.BlockSpec(memory_space=pltpu.SMEM)
VMEM = pl.BlockSpec(memory_space=pltpu.VMEM)
ANY = pl.BlockSpec(memory_space=pl.ANY)
HBM = pl.BlockSpec(memory_space=pltpu.HBM)
NN = (((1,), (0,)), ((), ()))
NT = (((1,), (1,)), ((), ()))
TN = (((0,), (0,)), ((), ()))


def dot(x, y, dims):
    return lax.dot_general(x, y, dims, preferred_element_type=f32)


def shape_of(*dims, dtype=bf16):
    return jax.ShapeDtypeStruct(dims, dtype)


TOKEN = shape_of(8, 128, dtype=f32)


def skip_refs(kernel, first, count, *refs):
    kernel(*refs[:first], *refs[first + count :])


def call(kernel, ins, outs, args, scratch=(), limit=8, name=None, after=()):
    ins, args = [*ins, *[ANY] * len(after)], (*args, *after)
    if after:
        kernel = functools.partial(skip_refs, kernel, len(args) - len(after), len(after))
    return pl.pallas_call(
        kernel,
        in_specs=ins,
        out_specs=[VMEM] * len(outs),
        out_shape=outs,
        scratch_shapes=list(scratch),
        compiler_params=pltpu.CompilerParams(vmem_limit_bytes=int(limit * MIB)),
        cost_estimate=pl.CostEstimate(flops=1, bytes_accessed=1, transcendentals=0),
        name=name,
    )(*args)


def place(peer, size):
    position = jnp.bitwise_xor(lax.rem(lax.axis_index("station"), LAYER), peer)
    return pl.ds(pl.multiple_of(position * size, size), size)


def block(j, span):
    return slice(j * span, (j + 1) * span)


def readers(j):
    return max(0, j - 2 * HOPS), min(LAYER - 1, j)


def pack_kernel(k_ref, v_ref, *refs):
    outs, (natural, flipped, sems) = refs[:LAYER], refs[LAYER:]
    rows = outs[0].shape[1]
    copies = [
        pltpu.make_async_copy(ref, natural.at[n], sems.at[n]) for n, ref in enumerate((k_ref, v_ref))
    ]
    for copy in copies:
        copy.start()
    for n, copy in enumerate(copies):
        copy.wait()
        flipped[n] = natural[n].T
    for peer, out in enumerate(outs):
        out[...] = flipped[:, place(peer, rows)]


def project_kernel(q_ref, g_ref, weight_ref, *refs):
    outs, (copy_ref, flipped) = refs[:LAYER], refs[LAYER:]
    rows = outs[0].shape[1]
    copy_ref[...] = g_ref[...]
    flipped[0] = q_ref[...].T * bf16(1.0 / math.sqrt(flipped.shape[1] // HEADS))
    flipped[1] = dot(weight_ref[...], g_ref[...], NT).astype(bf16)
    for peer, out in enumerate(outs):
        out[...] = flipped[:, place(peer, rows)]


def gather_kernel(*refs):
    ins, (up_ref, down_ref, pair_ref) = refs[:LAYER], refs[LAYER:]
    span = ins[0].shape[2]
    for peer, ref in enumerate(ins):
        pair_ref[:, :, place(peer, span)] = ref[...]
    up_ref[...] = pair_ref[:, :, span:]
    down_ref[...] = pair_ref[:, :, : HOPS * span]


def live_kernel(station_count, ids_ref, count_ref, bias_ref, dead_ref):
    span = bias_ref.shape[1] // LAYER
    first = lax.axis_index("station") // LAYER * LAYER
    ones = jnp.ones((1, span), f32)

    def listed(reader, other):
        hit = jnp.int32(0)
        for j in range(PMAX):
            here = jnp.logical_and(ids_ref[reader, j] == other, j < count_ref[reader])
            hit = jnp.maximum(hit, here.astype(jnp.int32))
        return hit > 0

    for j in range(BLOCKS):
        outer = lax.rem(first + (j - HOPS) + station_count, station_count)
        low, high = readers(j)
        for i in range(low, high + 1):
            inner = first + i
            slot = j - i
            if slot == HOPS:
                bias_ref[j : j + 1, block(i, span)] = 0.0 * ones
            else:
                reads = jnp.where(listed(inner, outer), 0.0, neg_big)
                bias_ref[j : j + 1, block(i, span)] = reads * ones
            if not HOPS <= j < HOPS + LAYER:
                read_by = jnp.where(listed(outer, inner), 0.0, -neg_big)
                spot = slot if j < HOPS else slot - LAYER
                dead_ref[i : i + 1, block(spot, span)] = read_by * ones


def clear(ref, span):
    for j in range(BLOCKS):
        low, high = readers(j)
        for i in range(LAYER):
            if not low <= i <= high:
                ref[block(j, span), block(i, span)] = jnp.zeros((span, span), bf16)


def forward_kernel(
    pair_ref, low_ref, high_ref, query_ref, bias_ref,
    mixed_ref, stats_ref, stats_up, stats_down, probs_ref, window_ref,
    raw,
):
    rows = query_ref.shape[1]
    span = query_ref.shape[2] // LAYER
    head_width = rows // LOCAL
    reach = HOPS * span
    window_ref[:, :, :reach] = low_ref[...]
    window_ref[:, :, reach : reach + LAYER * span] = pair_ref[...]
    window_ref[:, :, reach + LAYER * span :] = high_ref[...]
    for head in range(LOCAL):
        clear(probs_ref.at[head], span)
        at = block(head, head_width)
        query = query_ref[0, at]
        tops = [None] * LAYER
        for j in range(BLOCKS):
            low, high = readers(j)
            cols = slice(low * span, (high + 1) * span)
            scores = dot(window_ref[0, at, block(j, span)], query[:, cols], TN)
            scores = scores + bias_ref[j : j + 1, cols]
            raw[block(j, span), cols] = scores
            here = jnp.max(scores, 0, keepdims=True)
            for i in range(low, high + 1):
                mine = here[:, block(i - low, span)]
                tops[i] = mine if tops[i] is None else jnp.maximum(tops[i], mine)
        top = jnp.concatenate(tops, 1)
        totals = [jnp.zeros((1, span), f32)] * LAYER
        for j in range(BLOCKS):
            low, high = readers(j)
            cols = slice(low * span, (high + 1) * span)
            weight = jnp.exp(raw[block(j, span), cols] - top[:, cols])
            raw[block(j, span), cols] = weight
            here = jnp.sum(weight, 0, keepdims=True)
            for i in range(low, high + 1):
                totals[i] = totals[i] + here[:, block(i - low, span)]
        total = jnp.concatenate(totals, 1)
        inverse = 1.0 / total
        for j in range(BLOCKS):
            low, high = readers(j)
            cols = slice(low * span, (high + 1) * span)
            probs_ref[head, block(j, span), cols] = (
                raw[block(j, span), cols] * inverse[:, cols]
            ).astype(bf16)
        mixed = dot(window_ref[1, at], probs_ref[head], NN).astype(bf16)
        mixed_ref[at] = mixed
        product = query_ref[1, at].astype(f32) * mixed.astype(f32)
        stats_ref[head : head + 1] = top + jnp.log(total)
        stats_ref[LOCAL + head : LOCAL + head + 1] = jnp.sum(product, 0, keepdims=True)
    stats_ref[2 * LOCAL :] = jnp.zeros((8 - 2 * LOCAL, LAYER * span), f32)
    for ref, at in ((stats_up, slice(span, None)), (stats_down, slice(0, reach))):
        ref[...] = jnp.zeros_like(ref)
        ref[:8] = stats_ref[:, at]


def query_grad_kernel(
    window_ref, probs_ref, query_ref, stats_ref, dq_ref, own_ref, token_ref, grads
):
    rows = query_ref.shape[1]
    span = query_ref.shape[2] // LAYER
    head_width = rows // LOCAL
    scale = 1.0 / math.sqrt(head_width)
    inside = slice(HOPS * span, (HOPS + LAYER) * span)
    clear(grads, span)
    for head in range(LOCAL):
        at = block(head, head_width)
        grad = query_ref[1, at]
        delta = stats_ref[LOCAL + head : LOCAL + head + 1]
        for j in range(BLOCKS):
            low, high = readers(j)
            cols = slice(low * span, (high + 1) * span)
            back = dot(window_ref[1, at, block(j, span)], grad[:, cols], TN)
            prob = probs_ref[head, block(j, span), cols].astype(f32)
            grads[block(j, span), cols] = (prob * (back - delta[:, cols])).astype(bf16)
        dq_ref[at] = (dot(window_ref[0, at], grads[...], NN) * scale).astype(bf16)
        own_ref[0, at] = dot(query_ref[0, at], grads[inside], NT)
        own_ref[1, at] = dot(grad, probs_ref[head, inside], NT)
    token_ref[...] = jnp.zeros_like(token_ref)


def key_grad_kernel(
    pair_ref, low_ref, high_ref, stats_low, stats_high, dead_ref, own_ref, mixed_ref, dq_ref, *refs
):
    outs, (token_ref, flipped, scores, backs, probs, grads) = refs[:LAYER], refs[LAYER:]
    rows = pair_ref.shape[1]
    span = pair_ref.shape[2] // LAYER
    head_width = rows // LOCAL
    pairs = [(head, i) for head in range(LOCAL) for i in range(LAYER)]

    def outside(low, high, i):
        sides = [low[:, i * span :]] if i < HOPS else []
        return jnp.concatenate(sides + ([high[:, : i * span]] if i else []), 1)

    def both(part, head, i):
        at = block(head, head_width)
        return outside(low_ref[part, at], high_ref[part, at], i)

    for n, (head, i) in enumerate(pairs):
        at, own = block(head, head_width), block(i, span)
        scores[n] = dot(pair_ref[0, at, own], both(0, head, i), TN)
        backs[n] = dot(pair_ref[1, at, own], both(1, head, i), TN)
    for n, (head, i) in enumerate(pairs):
        row = slice(head, head + 1)
        log_sum = outside(stats_low[row], stats_high[row], i) + dead_ref[i : i + 1]
        row = slice(LOCAL + head, LOCAL + head + 1)
        delta = outside(stats_low[row], stats_high[row], i)
        prob = jnp.exp(scores[n] - log_sum)
        probs[n] = prob.astype(bf16)
        grads[n] = (prob * (backs[n] - delta)).astype(bf16)
    for n, (head, i) in enumerate(pairs):
        at, own = block(head, head_width), block(i, span)
        keys = own_ref[0, at, own] + dot(both(0, head, i), grads[n], NT)
        values = own_ref[1, at, own] + dot(both(1, head, i), probs[n], NT)
        flipped[0, at, own] = keys.astype(bf16)
        flipped[1, at, own] = values.astype(bf16)
    for peer, out in enumerate(outs):
        at = place(peer, span)
        out[0] = mixed_ref[:, at]
        out[1] = dq_ref[:, at]
        out[2:] = flipped[:, :, at]
    token_ref[...] = jnp.zeros_like(token_ref)


def output_kernel(*refs):
    ins, refs = refs[:LAYER], refs[LAYER:]
    weight_ref, out_ref, dq_ref, dk_ref, dv_ref, token_ref, flipped = refs
    for peer, ref in enumerate(ins):
        flipped[:, place(peer, ref.shape[1])] = ref[...]
    out_ref[...] = dot(flipped[0], weight_ref[...], TN).astype(bf16)
    for n, ref in enumerate((dq_ref, dk_ref, dv_ref)):
        ref[...] = flipped[n + 1].T
    token_ref[...] = jnp.zeros_like(token_ref)


def halves(bit, half):
    send = pl.ds(pl.multiple_of((1 - bit) * half, half), half)
    keep = pl.ds(pl.multiple_of(bit * half, half), half)
    return send, keep


def bit_of(stride):
    return lax.rem(lax.axis_index("station") // stride, 2)


def weight_kernel(mixed_ref, *refs):
    ins, (send_ref, keep_ref, right) = refs[:LAYER], refs[LAYER:]
    for peer, ref in enumerate(ins):
        right[place(peer, ref.shape[0])] = ref[...]
    send, keep = halves(lax.rem(lax.axis_index("dp"), 2), send_ref.shape[0])
    send_ref[...] = dot(mixed_ref[send], right[...], NN).astype(bf16)
    keep_ref[...] = dot(mixed_ref[keep], right[...], NN)


def split_kernel(stride, part_ref, got_ref, send_ref, keep_ref):
    send, keep = halves(bit_of(stride), send_ref.shape[0])
    send_ref[...] = (part_ref[send] + got_ref[send].astype(f32)).astype(bf16)
    keep_ref[...] = part_ref[keep] + got_ref[keep].astype(f32)


def round_kernel(part_ref, got_ref, out_ref):
    out_ref[...] = (part_ref[...].astype(f32) + got_ref[...].astype(f32)).astype(bf16)


def join_kernel(stride, mine_ref, got_ref, out_ref):
    other, here = halves(bit_of(stride), mine_ref.shape[0])
    out_ref[here] = mine_ref[...]
    out_ref[other] = got_ref[...]


def write_kernel(own, scale, value_ref, *refs):
    out_ref, wide, sem = refs[-3:]
    half = value_ref.shape[0]
    other, here = halves(bit_of(1), half)
    wide[...] = value_ref[...].astype(f32) * scale
    copy = pltpu.make_async_copy(wide, out_ref.at[here if own else other], sem)
    copy.start()
    copy.wait()


def cross_kernel(mine_ref, first_ref, second_ref, out_ref):
    window = lax.rem(lax.axis_index("dp"), 2)
    other, here = halves(window, mine_ref.shape[0])
    at_home = bit_of(2) == window
    mine, first, second = mine_ref[...], first_ref[...], second_ref[...]
    out_ref[here] = jnp.where(at_home, mine, first)
    out_ref[other] = jnp.where(at_home, first, second)


def local(
    query_states, key_states, value_states, grad_output, out_weight, partner_ids, partner_count
):
    span, width = query_states.shape[2:]
    stations = lax.axis_size("station")
    windows = lax.axis_size("dp")
    rows = width // LAYER
    dma = pltpu.SemaphoreType.DMA

    def swap(value, stride):
        return lax.ppermute(value, "station", [(s ^ stride, s) for s in range(stations)])

    def in_layer(values):
        return [swap(values[n], n + 1) for n in range(LAYER - 1)]

    def along(up, down):
        low = lax.ppermute(up, "station", [(s, (s + LAYER) % stations) for s in range(stations)])
        high = lax.ppermute(down, "station", [(s, (s - LAYER) % stations) for s in range(stations)])
        return low, high

    def other_window(value):
        return lax.ppermute(value, "dp", [(0, 1), (1, 0)])

    def flat(x):
        return x.reshape(span, width)

    q, k, v, g = flat(query_states), flat(key_states), flat(value_states), flat(grad_output)
    flat_shape = shape_of(span, width)
    part_shape = shape_of(2, rows, span)
    reach_shape = shape_of(2, rows, HOPS * span)
    layer_shape = shape_of(2, rows, LAYER * span)

    def gather(parts, after=()):
        return call(
            gather_kernel, [VMEM] * LAYER, [reach_shape, reach_shape, layer_shape], parts,
            name="gather", after=after,
        )

    mine, *parts = call(
        pack_kernel, [HBM] * 2, [part_shape] * LAYER, (k, v),
        [pltpu.VMEM((2, span, width), bf16), pltpu.VMEM((2, width, span), bf16), dma((2,))],
        limit=53.5, name="pack",
    )
    q, *parts = lax.optimization_barrier((q, *parts))
    parts = in_layer(parts)
    up, down, pair = gather((mine, *parts))
    mine, *query_parts, g_copy = call(
        project_kernel, [VMEM] * 3, [part_shape] * LAYER + [flat_shape],
        (q, g, out_weight), [pltpu.VMEM((2, width, span), bf16)], name="project",
    )
    up, g_later, *query_parts = lax.optimization_barrier((up, g, *query_parts))
    kv_low, kv_high = along(up, down)
    g_across = swap(g_later, 2)
    g_parts = g_copy, swap(g_later, 1), g_across, swap(g_across, 1)
    bias, dead = call(
        functools.partial(live_kernel, stations), [SMEM] * 2,
        [shape_of(16, LAYER * span, dtype=f32), shape_of(8, HOPS * span, dtype=f32)],
        (partner_ids, partner_count), name="live",
    )
    up, down, query = gather((mine, *in_layer(query_parts)), (bias,))
    qg_low, qg_high = along(up, down)
    stats_shape = shape_of(16, HOPS * span, dtype=f32)
    mixed, stats, up, down, probs, window = call(
        forward_kernel, [VMEM] * 5,
        [
            shape_of(rows, LAYER * span), shape_of(8, LAYER * span, dtype=f32),
            stats_shape, stats_shape,
            shape_of(LOCAL, BLOCKS * span, LAYER * span), shape_of(2, rows, BLOCKS * span),
        ],
        (pair, kv_low, kv_high, query, bias),
        [pltpu.VMEM((BLOCKS * span, LAYER * span), f32)],
        limit=20, name="forward",
    )
    stats_low, stats_high = along(up, down)

    send, part = call(
        weight_kernel, [VMEM] * (LAYER + 1),
        [shape_of(rows // 2, width), shape_of(rows // 2, width, dtype=f32)],
        (mixed, *g_parts), [pltpu.VMEM((LAYER * span, width), bf16)], name="weight",
    )

    dq, own_grad, query_token = call(
        query_grad_kernel, [VMEM] * 4,
        [shape_of(rows, LAYER * span), shape_of(2, rows, LAYER * span, dtype=f32), TOKEN],
        (window, probs, query, stats), [pltpu.VMEM((BLOCKS * span, LAYER * span), bf16)],
        limit=20, name="query_grad", after=(send,),
    )
    mine, *parts, key_token = call(
        key_grad_kernel, [VMEM] * 9, [shape_of(4, rows, span)] * LAYER + [TOKEN],
        (pair, qg_low, qg_high, stats_low, stats_high, dead, own_grad, mixed, dq),
        [
            pltpu.VMEM((2, rows, LAYER * span), bf16),
            pltpu.VMEM((HEADS, span, HOPS * span), f32),
            pltpu.VMEM((HEADS, span, HOPS * span), f32),
            pltpu.VMEM((HEADS, span, HOPS * span), bf16),
            pltpu.VMEM((HEADS, span, HOPS * span), bf16),
        ],
        limit=24, name="key_grad",
    )
    parts = in_layer(parts)
    layer_output, grad_query, grad_key, grad_value, output_token = call(
        output_kernel, [VMEM] * (LAYER + 1), [flat_shape] * 4 + [TOKEN],
        (mine, *parts, out_weight), [pltpu.VMEM((4, width, span), bf16)], name="output",
    )

    scale = 1.0 / math.sqrt(span * windows * stations)
    if windows == 2:
        count = rows // 4
        got = other_window(send)
        send, part = call(
            functools.partial(split_kernel, LAYER), [VMEM] * 2,
            [shape_of(count, width), shape_of(count, width, dtype=f32)],
            (part, got), name="split", after=(query_token,),
        )

        def add_round(part, got, after=()):
            out = [shape_of(count, width)]
            return call(round_kernel, [VMEM] * 2, out, (part, got), name="add", after=after)[0]

        total = add_round(part, swap(send, LAYER), (key_token,))
        stride = 2 * LAYER
        while stride < stations:
            total = add_round(total, swap(total, stride))
            stride *= 2
        (total,) = call(
            functools.partial(join_kernel, LAYER), [VMEM] * 2, [shape_of(2 * count, width)],
            (total, swap(total, LAYER)), name="join", after=parts,
        )
        first, second = [], []
        for w in range(2):
            for s in range(stations):
                if s // 2 % 2 == w:
                    first.append((w * stations + s, w * stations + (s ^ 2)))
                else:
                    first.append((w * stations + s, (1 - w) * stations + s))
                    second.append((w * stations + s, (1 - w) * stations + (s ^ 2)))
        axes = ("dp", "station")
        (total,) = call(
            cross_kernel, [VMEM] * 3, [shape_of(4 * count, width)],
            (total, lax.ppermute(total, axes, first), lax.ppermute(total, axes, second)),
            name="cross", after=(output_token,),
        )
        grad_weight = ()
        for own, value in ((True, total), (False, swap(total, 1))):
            grad_weight = (pl.pallas_call(
                functools.partial(write_kernel, own, scale),
                in_specs=[VMEM] + [ANY] * len(grad_weight),
                out_specs=ANY,
                out_shape=shape_of(8 * count, width, dtype=f32),
                scratch_shapes=[pltpu.VMEM((4 * count, width), f32), dma],
                input_output_aliases={1: 0} if grad_weight else {},
                compiler_params=pltpu.CompilerParams(vmem_limit_bytes=8 * MIB),
                cost_estimate=pl.CostEstimate(flops=1, bytes_accessed=1, transcendentals=0),
                name="write",
            )(value, *grad_weight),)
        (grad_weight,) = grad_weight
    else:
        start = lax.axis_index("station") % LAYER * rows
        all_grad = jnp.zeros((LAYER * span, width), bf16)
        for peer in range(LAYER):
            value = g_parts[peer]
            spot = lax.axis_index("station") % LAYER ^ peer
            all_grad = lax.dynamic_update_slice_in_dim(all_grad, value, spot * span, 0)
        mine = dot(mixed, all_grad, NN).astype(bf16)
        whole = lax.dynamic_update_slice_in_dim(jnp.zeros((width, width), bf16), mine, start, 0)
        whole = lax.psum_scatter(whole, "dp", scatter_dimension=0, tiled=True)
        grad_weight = lax.psum(whole.astype(f32), "station") * scale
    shape = query_states.shape
    return (
        layer_output.reshape(shape),
        grad_query.reshape(shape),
        grad_key.reshape(shape),
        grad_value.reshape(shape),
        grad_weight,
    )


def solution(mesh):
    split = P("dp", "station", None, None)
    return jax.shard_map(
        local,
        mesh=mesh,
        in_specs=(split, split, split, split, P(), P(), P()),
        out_specs=(split, split, split, split, P("dp", None)),
        check_vma=False,
    )
```

```python
import functools
import math

import jax
import jax.numpy as jnp
from jax import lax
from jax.experimental import pallas as pl
from jax.experimental.pallas import tpu as pltpu
from jax.sharding import PartitionSpec as P

HEADS = 12
PMAX = 6
HOPS = 3
LAYER = 4
LOCAL = HEADS // LAYER
BLOCKS = LAYER + 2 * HOPS
SLOTS = 2 * HOPS + 1
MIB = 1024 * 1024

neg_big = -1e30
bf16, f32 = jnp.bfloat16, jnp.float32
SMEM = pl.BlockSpec(memory_space=pltpu.SMEM)
VMEM = pl.BlockSpec(memory_space=pltpu.VMEM)
ANY = pl.BlockSpec(memory_space=pl.ANY)
HBM = pl.BlockSpec(memory_space=pltpu.HBM)
NN = (((1,), (0,)), ((), ()))
NT = (((1,), (1,)), ((), ()))
TN = (((0,), (0,)), ((), ()))


def dot(x, y, dims):
    return lax.dot_general(x, y, dims, preferred_element_type=f32)


def shape_of(*dims, dtype=bf16):
    return jax.ShapeDtypeStruct(dims, dtype)


TOKEN = shape_of(8, 128, dtype=f32)


def skip_refs(kernel, first, count, *refs):
    kernel(*refs[:first], *refs[first + count :])


def call(kernel, ins, outs, args, scratch=(), limit=8, name=None, after=()):
    ins, args = [*ins, *[ANY] * len(after)], (*args, *after)
    if after:
        kernel = functools.partial(skip_refs, kernel, len(args) - len(after), len(after))
    return pl.pallas_call(
        kernel,
        in_specs=ins,
        out_specs=[VMEM] * len(outs),
        out_shape=outs,
        scratch_shapes=list(scratch),
        compiler_params=pltpu.CompilerParams(vmem_limit_bytes=int(limit * MIB)),
        cost_estimate=pl.CostEstimate(flops=1, bytes_accessed=1, transcendentals=0),
        name=name,
    )(*args)


def place(peer, size):
    position = jnp.bitwise_xor(lax.rem(lax.axis_index("station"), LAYER), peer)
    return pl.ds(pl.multiple_of(position * size, size), size)


def block(j, span):
    return slice(j * span, (j + 1) * span)


def readers(j):
    return max(0, j - 2 * HOPS), min(LAYER - 1, j)


def pack_kernel(k_ref, v_ref, *refs):
    outs, (natural, flipped, sems) = refs[:LAYER], refs[LAYER:]
    rows = outs[0].shape[1]
    copies = [
        pltpu.make_async_copy(ref, natural.at[n], sems.at[n]) for n, ref in enumerate((k_ref, v_ref))
    ]
    for copy in copies:
        copy.start()
    for n, copy in enumerate(copies):
        copy.wait()
        flipped[n] = natural[n].T
    for peer, out in enumerate(outs):
        out[...] = flipped[:, place(peer, rows)]


def project_kernel(q_ref, g_ref, weight_ref, *refs):
    outs, (copy_ref, flipped) = refs[:LAYER], refs[LAYER:]
    rows = outs[0].shape[1]
    copy_ref[...] = g_ref[...]
    flipped[0] = q_ref[...].T * bf16(1.0 / math.sqrt(flipped.shape[1] // HEADS))
    flipped[1] = dot(weight_ref[...], g_ref[...], NT).astype(bf16)
    for peer, out in enumerate(outs):
        out[...] = flipped[:, place(peer, rows)]


def gather_kernel(*refs):
    ins, (up_ref, down_ref, pair_ref) = refs[:LAYER], refs[LAYER:]
    span = ins[0].shape[2]
    for peer, ref in enumerate(ins):
        pair_ref[:, :, place(peer, span)] = ref[...]
    up_ref[...] = pair_ref[:, :, span:]
    down_ref[...] = pair_ref[:, :, : HOPS * span]


def live_kernel(station_count, ids_ref, count_ref, bias_ref, dead_ref):
    span = bias_ref.shape[1] // LAYER
    first = lax.axis_index("station") // LAYER * LAYER
    ones = jnp.ones((1, span), f32)

    def listed(reader, other):
        hit = jnp.int32(0)
        for j in range(PMAX):
            here = jnp.logical_and(ids_ref[reader, j] == other, j < count_ref[reader])
            hit = jnp.maximum(hit, here.astype(jnp.int32))
        return hit > 0

    for j in range(BLOCKS):
        outer = lax.rem(first + (j - HOPS) + station_count, station_count)
        low, high = readers(j)
        for i in range(low, high + 1):
            inner = first + i
            slot = j - i
            if slot == HOPS:
                bias_ref[j : j + 1, block(i, span)] = 0.0 * ones
            else:
                reads = jnp.where(listed(inner, outer), 0.0, neg_big)
                bias_ref[j : j + 1, block(i, span)] = reads * ones
            if not HOPS <= j < HOPS + LAYER:
                read_by = jnp.where(listed(outer, inner), 0.0, -neg_big)
                spot = slot if j < HOPS else slot - LAYER
                dead_ref[i : i + 1, block(spot, span)] = read_by * ones


def clear(ref, span):
    for j in range(BLOCKS):
        low, high = readers(j)
        for i in range(LAYER):
            if not low <= i <= high:
                ref[block(j, span), block(i, span)] = jnp.zeros((span, span), bf16)


def forward_kernel(
    pair_ref, low_ref, high_ref, query_ref, bias_ref,
    mixed_ref, stats_ref, stats_up, stats_down, probs_ref, window_ref,
    raw,
):
    rows = query_ref.shape[1]
    span = query_ref.shape[2] // LAYER
    head_width = rows // LOCAL
    reach = HOPS * span
    window_ref[:, :, :reach] = low_ref[...]
    window_ref[:, :, reach : reach + LAYER * span] = pair_ref[...]
    window_ref[:, :, reach + LAYER * span :] = high_ref[...]
    for head in range(LOCAL):
        clear(probs_ref.at[head], span)
        at = block(head, head_width)
        query = query_ref[0, at]
        tops = [None] * LAYER
        for j in range(BLOCKS):
            low, high = readers(j)
            cols = slice(low * span, (high + 1) * span)
            scores = dot(window_ref[0, at, block(j, span)], query[:, cols], TN)
            scores = scores + bias_ref[j : j + 1, cols]
            raw[block(j, span), cols] = scores
            here = jnp.max(scores, 0, keepdims=True)
            for i in range(low, high + 1):
                mine = here[:, block(i - low, span)]
                tops[i] = mine if tops[i] is None else jnp.maximum(tops[i], mine)
        top = jnp.concatenate(tops, 1)
        totals = [jnp.zeros((1, span), f32)] * LAYER
        for j in range(BLOCKS):
            low, high = readers(j)
            cols = slice(low * span, (high + 1) * span)
            weight = jnp.exp(raw[block(j, span), cols] - top[:, cols])
            raw[block(j, span), cols] = weight
            here = jnp.sum(weight, 0, keepdims=True)
            for i in range(low, high + 1):
                totals[i] = totals[i] + here[:, block(i - low, span)]
        total = jnp.concatenate(totals, 1)
        inverse = 1.0 / total
        for j in range(BLOCKS):
            low, high = readers(j)
            cols = slice(low * span, (high + 1) * span)
            probs_ref[head, block(j, span), cols] = (
                raw[block(j, span), cols] * inverse[:, cols]
            ).astype(bf16)
        mixed = dot(window_ref[1, at], probs_ref[head], NN).astype(bf16)
        mixed_ref[at] = mixed
        product = query_ref[1, at].astype(f32) * mixed.astype(f32)
        stats_ref[head : head + 1] = top + jnp.log(total)
        stats_ref[LOCAL + head : LOCAL + head + 1] = jnp.sum(product, 0, keepdims=True)
    stats_ref[2 * LOCAL :] = jnp.zeros((8 - 2 * LOCAL, LAYER * span), f32)
    for ref, at in ((stats_up, slice(span, None)), (stats_down, slice(0, reach))):
        ref[...] = jnp.zeros_like(ref)
        ref[:8] = stats_ref[:, at]


def query_grad_kernel(
    window_ref, probs_ref, query_ref, stats_ref, dq_ref, own_ref, token_ref, grads
):
    rows = query_ref.shape[1]
    span = query_ref.shape[2] // LAYER
    head_width = rows // LOCAL
    scale = 1.0 / math.sqrt(head_width)
    inside = slice(HOPS * span, (HOPS + LAYER) * span)
    clear(grads, span)
    for head in range(LOCAL):
        at = block(head, head_width)
        grad = query_ref[1, at]
        delta = stats_ref[LOCAL + head : LOCAL + head + 1]
        for j in range(BLOCKS):
            low, high = readers(j)
            cols = slice(low * span, (high + 1) * span)
            back = dot(window_ref[1, at, block(j, span)], grad[:, cols], TN)
            prob = probs_ref[head, block(j, span), cols].astype(f32)
            grads[block(j, span), cols] = (prob * (back - delta[:, cols])).astype(bf16)
        dq_ref[at] = (dot(window_ref[0, at], grads[...], NN) * scale).astype(bf16)
        own_ref[0, at] = dot(query_ref[0, at], grads[inside], NT)
        own_ref[1, at] = dot(grad, probs_ref[head, inside], NT)
    token_ref[...] = jnp.zeros_like(token_ref)


def key_grad_kernel(
    pair_ref, low_ref, high_ref, stats_low, stats_high, dead_ref, own_ref, mixed_ref, dq_ref, *refs
):
    outs, (token_ref, flipped, scores, backs, probs, grads) = refs[:LAYER], refs[LAYER:]
    rows = pair_ref.shape[1]
    span = pair_ref.shape[2] // LAYER
    head_width = rows // LOCAL
    pairs = [(head, i) for head in range(LOCAL) for i in range(LAYER)]

    def outside(low, high, i):
        sides = [low[:, i * span :]] if i < HOPS else []
        return jnp.concatenate(sides + ([high[:, : i * span]] if i else []), 1)

    def both(part, head, i):
        at = block(head, head_width)
        return outside(low_ref[part, at], high_ref[part, at], i)

    for n, (head, i) in enumerate(pairs):
        at, own = block(head, head_width), block(i, span)
        scores[n] = dot(pair_ref[0, at, own], both(0, head, i), TN)
        backs[n] = dot(pair_ref[1, at, own], both(1, head, i), TN)
    for n, (head, i) in enumerate(pairs):
        row = slice(head, head + 1)
        log_sum = outside(stats_low[row], stats_high[row], i) + dead_ref[i : i + 1]
        row = slice(LOCAL + head, LOCAL + head + 1)
        delta = outside(stats_low[row], stats_high[row], i)
        prob = jnp.exp(scores[n] - log_sum)
        probs[n] = prob.astype(bf16)
        grads[n] = (prob * (backs[n] - delta)).astype(bf16)
    for n, (head, i) in enumerate(pairs):
        at, own = block(head, head_width), block(i, span)
        keys = own_ref[0, at, own] + dot(both(0, head, i), grads[n], NT)
        values = own_ref[1, at, own] + dot(both(1, head, i), probs[n], NT)
        flipped[0, at, own] = keys.astype(bf16)
        flipped[1, at, own] = values.astype(bf16)
    for peer, out in enumerate(outs):
        at = place(peer, span)
        out[0] = mixed_ref[:, at]
        out[1] = dq_ref[:, at]
        out[2:] = flipped[:, :, at]
    token_ref[...] = jnp.zeros_like(token_ref)


def output_kernel(*refs):
    ins, refs = refs[:LAYER], refs[LAYER:]
    weight_ref, out_ref, dq_ref, dk_ref, dv_ref, token_ref, flipped = refs
    for peer, ref in enumerate(ins):
        flipped[:, place(peer, ref.shape[1])] = ref[...]
    out_ref[...] = dot(flipped[0], weight_ref[...], TN).astype(bf16)
    for n, ref in enumerate((dq_ref, dk_ref, dv_ref)):
        ref[...] = flipped[n + 1].T
    token_ref[...] = jnp.zeros_like(token_ref)


def halves(bit, half):
    send = pl.ds(pl.multiple_of((1 - bit) * half, half), half)
    keep = pl.ds(pl.multiple_of(bit * half, half), half)
    return send, keep


def bit_of(stride):
    return lax.rem(lax.axis_index("station") // stride, 2)


def weight_kernel(mixed_ref, *refs):
    ins, (send_ref, keep_ref, right) = refs[:LAYER], refs[LAYER:]
    for peer, ref in enumerate(ins):
        right[place(peer, ref.shape[0])] = ref[...]
    send, keep = halves(lax.rem(lax.axis_index("dp"), 2), send_ref.shape[0])
    send_ref[...] = dot(mixed_ref[send], right[...], NN).astype(bf16)
    keep_ref[...] = dot(mixed_ref[keep], right[...], NN)


def split_kernel(part_ref, got_ref, top_ref, bottom_ref):
    half = top_ref.shape[0]
    for out, at in ((top_ref, slice(0, half)), (bottom_ref, slice(half, 2 * half))):
        out[...] = (part_ref[at] + got_ref[at].astype(f32)).astype(bf16)


def meet_kernel(top_ref, bottom_ref, got_top, got_bottom, out_ref):
    half = top_ref.shape[0]
    for n, (mine, got) in enumerate(((top_ref, got_top), (bottom_ref, got_bottom))):
        out_ref[n * half : (n + 1) * half] = (mine[...].astype(f32) + got[...].astype(f32)).astype(bf16)


def round_kernel(part_ref, got_ref, out_ref):
    out_ref[...] = (part_ref[...].astype(f32) + got_ref[...].astype(f32)).astype(bf16)


def write_kernel(own, scale, value_ref, *refs):
    out_ref, wide, sem = refs[-3:]
    half = value_ref.shape[0]
    other, here = halves(bit_of(1), half)
    wide[...] = value_ref[...].astype(f32) * scale
    copy = pltpu.make_async_copy(wide, out_ref.at[here if own else other], sem)
    copy.start()
    copy.wait()


def cross_kernel(mine_ref, first_ref, second_ref, out_ref):
    window = lax.rem(lax.axis_index("dp"), 2)
    other, here = halves(window, mine_ref.shape[0])
    at_home = bit_of(2) == window
    mine, first, second = mine_ref[...], first_ref[...], second_ref[...]
    out_ref[here] = jnp.where(at_home, mine, first)
    out_ref[other] = jnp.where(at_home, first, second)


def local(
    query_states, key_states, value_states, grad_output, out_weight, partner_ids, partner_count
):
    span, width = query_states.shape[2:]
    stations = lax.axis_size("station")
    windows = lax.axis_size("dp")
    rows = width // LAYER
    dma = pltpu.SemaphoreType.DMA

    def swap(value, stride):
        return lax.ppermute(value, "station", [(s ^ stride, s) for s in range(stations)])

    def in_layer(values):
        return [swap(values[n], n + 1) for n in range(LAYER - 1)]

    def along(up, down):
        low = lax.ppermute(up, "station", [(s, (s + LAYER) % stations) for s in range(stations)])
        high = lax.ppermute(down, "station", [(s, (s - LAYER) % stations) for s in range(stations)])
        return low, high

    def other_window(value):
        return lax.ppermute(value, "dp", [(0, 1), (1, 0)])

    def flat(x):
        return x.reshape(span, width)

    q, k, v, g = flat(query_states), flat(key_states), flat(value_states), flat(grad_output)
    flat_shape = shape_of(span, width)
    part_shape = shape_of(2, rows, span)
    reach_shape = shape_of(2, rows, HOPS * span)
    layer_shape = shape_of(2, rows, LAYER * span)

    def gather(parts, after=()):
        return call(
            gather_kernel, [VMEM] * LAYER, [reach_shape, reach_shape, layer_shape], parts,
            name="gather", after=after,
        )

    mine, *parts = call(
        pack_kernel, [HBM] * 2, [part_shape] * LAYER, (k, v),
        [pltpu.VMEM((2, span, width), bf16), pltpu.VMEM((2, width, span), bf16), dma((2,))],
        limit=53.5, name="pack",
    )
    q, *parts = lax.optimization_barrier((q, *parts))
    parts = in_layer(parts)
    up, down, pair = gather((mine, *parts))
    mine, *query_parts, g_copy = call(
        project_kernel, [VMEM] * 3, [part_shape] * LAYER + [flat_shape],
        (q, g, out_weight), [pltpu.VMEM((2, width, span), bf16)], name="project",
    )
    up, g_later, *query_parts = lax.optimization_barrier((up, g, *query_parts))
    kv_low, kv_high = along(up, down)
    g_across = swap(g_later, 2)
    g_parts = g_copy, swap(g_later, 1), g_across, swap(g_across, 1)
    bias, dead = call(
        functools.partial(live_kernel, stations), [SMEM] * 2,
        [shape_of(16, LAYER * span, dtype=f32), shape_of(8, HOPS * span, dtype=f32)],
        (partner_ids, partner_count), name="live",
    )
    up, down, query = gather((mine, *in_layer(query_parts)), (bias,))
    qg_low, qg_high = along(up, down)
    stats_shape = shape_of(16, HOPS * span, dtype=f32)
    mixed, stats, up, down, probs, window = call(
        forward_kernel, [VMEM] * 5,
        [
            shape_of(rows, LAYER * span), shape_of(8, LAYER * span, dtype=f32),
            stats_shape, stats_shape,
            shape_of(LOCAL, BLOCKS * span, LAYER * span), shape_of(2, rows, BLOCKS * span),
        ],
        (pair, kv_low, kv_high, query, bias),
        [pltpu.VMEM((BLOCKS * span, LAYER * span), f32)],
        limit=20, name="forward",
    )
    stats_low, stats_high = along(up, down)

    send, part = call(
        weight_kernel, [VMEM] * (LAYER + 1),
        [shape_of(rows // 2, width), shape_of(rows // 2, width, dtype=f32)],
        (mixed, *g_parts), [pltpu.VMEM((LAYER * span, width), bf16)], name="weight",
    )

    dq, own_grad, query_token = call(
        query_grad_kernel, [VMEM] * 4,
        [shape_of(rows, LAYER * span), shape_of(2, rows, LAYER * span, dtype=f32), TOKEN],
        (window, probs, query, stats), [pltpu.VMEM((BLOCKS * span, LAYER * span), bf16)],
        limit=20, name="query_grad", after=(send,),
    )
    mine, *parts, key_token = call(
        key_grad_kernel, [VMEM] * 9, [shape_of(4, rows, span)] * LAYER + [TOKEN],
        (pair, qg_low, qg_high, stats_low, stats_high, dead, own_grad, mixed, dq),
        [
            pltpu.VMEM((2, rows, LAYER * span), bf16),
            pltpu.VMEM((HEADS, span, HOPS * span), f32),
            pltpu.VMEM((HEADS, span, HOPS * span), f32),
            pltpu.VMEM((HEADS, span, HOPS * span), bf16),
            pltpu.VMEM((HEADS, span, HOPS * span), bf16),
        ],
        limit=24, name="key_grad",
    )
    parts = in_layer(parts)
    layer_output, grad_query, grad_key, grad_value, output_token = call(
        output_kernel, [VMEM] * (LAYER + 1), [flat_shape] * 4 + [TOKEN],
        (mine, *parts, out_weight), [pltpu.VMEM((4, width, span), bf16)], name="output",
    )

    scale = 1.0 / math.sqrt(span * windows * stations)
    if windows == 2:
        count = rows // 2
        got = other_window(send)
        top, bottom = call(
            split_kernel, [VMEM] * 2, [shape_of(count // 2, width)] * 2, (part, got), name="split",
            after=(query_token,),
        )
        (total,) = call(
            meet_kernel, [VMEM] * 4, [shape_of(count, width)],
            (top, bottom, swap(top, LAYER), swap(bottom, LAYER)), name="meet", after=(key_token,),
        )
        stride = 2 * LAYER
        while stride < stations:
            (total,) = call(
                round_kernel, [VMEM] * 2, [shape_of(count, width)], (total, swap(total, stride)),
                name="add", after=parts if 2 * stride >= stations else (),
            )
            stride *= 2
        first, second = [], []
        for w in range(2):
            for s in range(stations):
                if s // 2 % 2 == w:
                    first.append((w * stations + s, w * stations + (s ^ 2)))
                else:
                    first.append((w * stations + s, (1 - w) * stations + s))
                    second.append((w * stations + s, (1 - w) * stations + (s ^ 2)))
        axes = ("dp", "station")
        (total,) = call(
            cross_kernel, [VMEM] * 3, [shape_of(2 * count, width)],
            (total, lax.ppermute(total, axes, first), lax.ppermute(total, axes, second)),
            name="cross", after=(output_token,),
        )
        grad_weight = ()
        for own, value in ((True, total), (False, swap(total, 1))):
            grad_weight = (pl.pallas_call(
                functools.partial(write_kernel, own, scale),
                in_specs=[VMEM] + [ANY] * len(grad_weight),
                out_specs=ANY,
                out_shape=shape_of(4 * count, width, dtype=f32),
                scratch_shapes=[pltpu.VMEM((2 * count, width), f32), dma],
                input_output_aliases={1: 0} if grad_weight else {},
                compiler_params=pltpu.CompilerParams(vmem_limit_bytes=8 * MIB),
                cost_estimate=pl.CostEstimate(flops=1, bytes_accessed=1, transcendentals=0),
                name="write",
            )(value, *grad_weight),)
        (grad_weight,) = grad_weight
    else:
        start = lax.axis_index("station") % LAYER * rows
        all_grad = jnp.zeros((LAYER * span, width), bf16)
        for peer in range(LAYER):
            value = g_parts[peer]
            spot = lax.axis_index("station") % LAYER ^ peer
            all_grad = lax.dynamic_update_slice_in_dim(all_grad, value, spot * span, 0)
        mine = dot(mixed, all_grad, NN).astype(bf16)
        whole = lax.dynamic_update_slice_in_dim(jnp.zeros((width, width), bf16), mine, start, 0)
        whole = lax.psum_scatter(whole, "dp", scatter_dimension=0, tiled=True)
        grad_weight = lax.psum(whole.astype(f32), "station") * scale
    shape = query_states.shape
    return (
        layer_output.reshape(shape),
        grad_query.reshape(shape),
        grad_key.reshape(shape),
        grad_value.reshape(shape),
        grad_weight,
    )


def solution(mesh):
    split = P("dp", "station", None, None)
    return jax.shard_map(
        local,
        mesh=mesh,
        in_specs=(split, split, split, split, P(), P(), P()),
        out_specs=(split, split, split, split, P("dp", None)),
        check_vma=False,
    )
```

```python
import functools
import math

import jax
import jax.numpy as jnp
from jax import lax
from jax.experimental import pallas as pl
from jax.experimental.pallas import tpu as pltpu
from jax.sharding import PartitionSpec as P

HEADS = 12
PMAX = 6
HOPS = 3
LAYER = 4
LOCAL = HEADS // LAYER
BLOCKS = LAYER + 2 * HOPS
SLOTS = 2 * HOPS + 1
MIB = 1024 * 1024

neg_big = -1e30
bf16, f32 = jnp.bfloat16, jnp.float32
SMEM = pl.BlockSpec(memory_space=pltpu.SMEM)
VMEM = pl.BlockSpec(memory_space=pltpu.VMEM)
ANY = pl.BlockSpec(memory_space=pl.ANY)
HBM = pl.BlockSpec(memory_space=pltpu.HBM)
NN = (((1,), (0,)), ((), ()))
NT = (((1,), (1,)), ((), ()))
TN = (((0,), (0,)), ((), ()))


def dot(x, y, dims):
    return lax.dot_general(x, y, dims, preferred_element_type=f32)


def shape_of(*dims, dtype=bf16):
    return jax.ShapeDtypeStruct(dims, dtype)


TOKEN = shape_of(8, 128, dtype=f32)


def skip_refs(kernel, first, count, *refs):
    kernel(*refs[:first], *refs[first + count :])


def call(kernel, ins, outs, args, scratch=(), limit=8, name=None, after=()):
    ins, args = [*ins, *[ANY] * len(after)], (*args, *after)
    if after:
        kernel = functools.partial(skip_refs, kernel, len(args) - len(after), len(after))
    return pl.pallas_call(
        kernel,
        in_specs=ins,
        out_specs=[VMEM] * len(outs),
        out_shape=outs,
        scratch_shapes=list(scratch),
        compiler_params=pltpu.CompilerParams(vmem_limit_bytes=int(limit * MIB)),
        cost_estimate=pl.CostEstimate(flops=1, bytes_accessed=1, transcendentals=0),
        name=name,
    )(*args)


def place(peer, size):
    position = jnp.bitwise_xor(lax.rem(lax.axis_index("station"), LAYER), peer)
    return pl.ds(pl.multiple_of(position * size, size), size)


def block(j, span):
    return slice(j * span, (j + 1) * span)


def readers(j):
    return max(0, j - 2 * HOPS), min(LAYER - 1, j)


def pack_kernel(k_ref, v_ref, *refs):
    outs, (natural, flipped, sems) = refs[:LAYER], refs[LAYER:]
    rows = outs[0].shape[1]
    copies = [
        pltpu.make_async_copy(ref, natural.at[n], sems.at[n]) for n, ref in enumerate((k_ref, v_ref))
    ]
    for copy in copies:
        copy.start()
    for n, copy in enumerate(copies):
        copy.wait()
        flipped[n] = natural[n].T
    for peer, out in enumerate(outs):
        out[...] = flipped[:, place(peer, rows)]


def project_kernel(q_ref, g_ref, weight_ref, *refs):
    outs, (copy_ref, flipped) = refs[:LAYER], refs[LAYER:]
    rows = outs[0].shape[1]
    copy_ref[...] = g_ref[...]
    flipped[0] = q_ref[...].T * bf16(1.0 / math.sqrt(flipped.shape[1] // HEADS))
    flipped[1] = dot(weight_ref[...], g_ref[...], NT).astype(bf16)
    for peer, out in enumerate(outs):
        out[...] = flipped[:, place(peer, rows)]


def gather_kernel(*refs):
    ins, (up_ref, down_ref, pair_ref) = refs[:LAYER], refs[LAYER:]
    span = ins[0].shape[2]
    for peer, ref in enumerate(ins):
        pair_ref[:, :, place(peer, span)] = ref[...]
    up_ref[...] = pair_ref[:, :, span:]
    down_ref[...] = pair_ref[:, :, : HOPS * span]


def live_kernel(station_count, ids_ref, count_ref, bias_ref, dead_ref):
    span = bias_ref.shape[1] // LAYER
    first = lax.axis_index("station") // LAYER * LAYER
    ones = jnp.ones((1, span), f32)

    def listed(reader, other):
        hit = jnp.int32(0)
        for j in range(PMAX):
            here = jnp.logical_and(ids_ref[reader, j] == other, j < count_ref[reader])
            hit = jnp.maximum(hit, here.astype(jnp.int32))
        return hit > 0

    for j in range(BLOCKS):
        outer = lax.rem(first + (j - HOPS) + station_count, station_count)
        low, high = readers(j)
        for i in range(low, high + 1):
            inner = first + i
            slot = j - i
            if slot == HOPS:
                bias_ref[j : j + 1, block(i, span)] = 0.0 * ones
            else:
                reads = jnp.where(listed(inner, outer), 0.0, neg_big)
                bias_ref[j : j + 1, block(i, span)] = reads * ones
            if not HOPS <= j < HOPS + LAYER:
                read_by = jnp.where(listed(outer, inner), 0.0, -neg_big)
                spot = slot if j < HOPS else slot - LAYER
                dead_ref[i : i + 1, block(spot, span)] = read_by * ones


def clear(ref, span):
    for j in range(BLOCKS):
        low, high = readers(j)
        for i in range(LAYER):
            if not low <= i <= high:
                ref[block(j, span), block(i, span)] = jnp.zeros((span, span), bf16)


def forward_kernel(
    pair_ref, low_ref, high_ref, query_ref, bias_ref,
    mixed_ref, stats_ref, stats_up, stats_down, probs_ref, window_ref,
    raw,
):
    rows = query_ref.shape[1]
    span = query_ref.shape[2] // LAYER
    head_width = rows // LOCAL
    reach = HOPS * span
    window_ref[:, :, :reach] = low_ref[...]
    window_ref[:, :, reach : reach + LAYER * span] = pair_ref[...]
    window_ref[:, :, reach + LAYER * span :] = high_ref[...]
    for head in range(LOCAL):
        clear(probs_ref.at[head], span)
        at = block(head, head_width)
        query = query_ref[0, at]
        tops = [None] * LAYER
        for j in range(BLOCKS):
            low, high = readers(j)
            cols = slice(low * span, (high + 1) * span)
            scores = dot(window_ref[0, at, block(j, span)], query[:, cols], TN)
            scores = scores + bias_ref[j : j + 1, cols]
            raw[block(j, span), cols] = scores
            here = jnp.max(scores, 0, keepdims=True)
            for i in range(low, high + 1):
                mine = here[:, block(i - low, span)]
                tops[i] = mine if tops[i] is None else jnp.maximum(tops[i], mine)
        top = jnp.concatenate(tops, 1)
        totals = [jnp.zeros((1, span), f32)] * LAYER
        for j in range(BLOCKS):
            low, high = readers(j)
            cols = slice(low * span, (high + 1) * span)
            weight = jnp.exp(raw[block(j, span), cols] - top[:, cols])
            raw[block(j, span), cols] = weight
            here = jnp.sum(weight, 0, keepdims=True)
            for i in range(low, high + 1):
                totals[i] = totals[i] + here[:, block(i - low, span)]
        total = jnp.concatenate(totals, 1)
        inverse = 1.0 / total
        for j in range(BLOCKS):
            low, high = readers(j)
            cols = slice(low * span, (high + 1) * span)
            probs_ref[head, block(j, span), cols] = (
                raw[block(j, span), cols] * inverse[:, cols]
            ).astype(bf16)
        mixed = dot(window_ref[1, at], probs_ref[head], NN).astype(bf16)
        mixed_ref[at] = mixed
        product = query_ref[1, at].astype(f32) * mixed.astype(f32)
        stats_ref[head : head + 1] = top + jnp.log(total)
        stats_ref[LOCAL + head : LOCAL + head + 1] = jnp.sum(product, 0, keepdims=True)
    stats_ref[2 * LOCAL :] = jnp.zeros((8 - 2 * LOCAL, LAYER * span), f32)
    for ref, at in ((stats_up, slice(span, None)), (stats_down, slice(0, reach))):
        ref[...] = jnp.zeros_like(ref)
        ref[:8] = stats_ref[:, at]


def query_grad_kernel(
    window_ref, probs_ref, query_ref, stats_ref, dq_ref, own_ref, token_ref, grads
):
    rows = query_ref.shape[1]
    span = query_ref.shape[2] // LAYER
    head_width = rows // LOCAL
    scale = 1.0 / math.sqrt(head_width)
    inside = slice(HOPS * span, (HOPS + LAYER) * span)
    clear(grads, span)
    for head in range(LOCAL):
        at = block(head, head_width)
        grad = query_ref[1, at]
        delta = stats_ref[LOCAL + head : LOCAL + head + 1]
        for j in range(BLOCKS):
            low, high = readers(j)
            cols = slice(low * span, (high + 1) * span)
            back = dot(window_ref[1, at, block(j, span)], grad[:, cols], TN)
            prob = probs_ref[head, block(j, span), cols].astype(f32)
            grads[block(j, span), cols] = (prob * (back - delta[:, cols])).astype(bf16)
        dq_ref[at] = (dot(window_ref[0, at], grads[...], NN) * scale).astype(bf16)
        own_ref[0, at] = dot(query_ref[0, at], grads[inside], NT)
        own_ref[1, at] = dot(grad, probs_ref[head, inside], NT)
    token_ref[...] = jnp.zeros_like(token_ref)


def key_grad_kernel(
    pair_ref, low_ref, high_ref, stats_low, stats_high, dead_ref, own_ref, mixed_ref, dq_ref, *refs
):
    outs, (token_ref, flipped, scores, backs, probs, grads) = refs[:LAYER], refs[LAYER:]
    rows = pair_ref.shape[1]
    span = pair_ref.shape[2] // LAYER
    head_width = rows // LOCAL
    pairs = [(head, i) for head in range(LOCAL) for i in range(LAYER)]

    def outside(low, high, i):
        sides = [low[:, i * span :]] if i < HOPS else []
        return jnp.concatenate(sides + ([high[:, : i * span]] if i else []), 1)

    def both(part, head, i):
        at = block(head, head_width)
        return outside(low_ref[part, at], high_ref[part, at], i)

    for n, (head, i) in enumerate(pairs):
        at, own = block(head, head_width), block(i, span)
        scores[n] = dot(pair_ref[0, at, own], both(0, head, i), TN)
        backs[n] = dot(pair_ref[1, at, own], both(1, head, i), TN)
    for n, (head, i) in enumerate(pairs):
        row = slice(head, head + 1)
        log_sum = outside(stats_low[row], stats_high[row], i) + dead_ref[i : i + 1]
        row = slice(LOCAL + head, LOCAL + head + 1)
        delta = outside(stats_low[row], stats_high[row], i)
        prob = jnp.exp(scores[n] - log_sum)
        probs[n] = prob.astype(bf16)
        grads[n] = (prob * (backs[n] - delta)).astype(bf16)
    for n, (head, i) in enumerate(pairs):
        at, own = block(head, head_width), block(i, span)
        keys = own_ref[0, at, own] + dot(both(0, head, i), grads[n], NT)
        values = own_ref[1, at, own] + dot(both(1, head, i), probs[n], NT)
        flipped[0, at, own] = keys.astype(bf16)
        flipped[1, at, own] = values.astype(bf16)
    for peer, out in enumerate(outs):
        at = place(peer, span)
        out[0] = mixed_ref[:, at]
        out[1] = dq_ref[:, at]
        out[2:] = flipped[:, :, at]
    token_ref[...] = jnp.zeros_like(token_ref)


def output_kernel(*refs):
    ins, refs = refs[:LAYER], refs[LAYER:]
    weight_ref, out_ref, dq_ref, dk_ref, dv_ref, token_ref, flipped = refs
    for peer, ref in enumerate(ins):
        flipped[:, place(peer, ref.shape[1])] = ref[...]
    out_ref[...] = dot(flipped[0], weight_ref[...], TN).astype(bf16)
    for n, ref in enumerate((dq_ref, dk_ref, dv_ref)):
        ref[...] = flipped[n + 1].T
    token_ref[...] = jnp.zeros_like(token_ref)


def halves(bit, half):
    send = pl.ds(pl.multiple_of((1 - bit) * half, half), half)
    keep = pl.ds(pl.multiple_of(bit * half, half), half)
    return send, keep


def bit_of(stride):
    return lax.rem(lax.axis_index("station") // stride, 2)


def weight_kernel(mixed_ref, *refs):
    ins, (send_ref, keep_ref, right) = refs[:LAYER], refs[LAYER:]
    for peer, ref in enumerate(ins):
        right[place(peer, ref.shape[0])] = ref[...]
    send, keep = halves(lax.rem(lax.axis_index("dp"), 2), send_ref.shape[0])
    send_ref[...] = dot(mixed_ref[send], right[...], NN).astype(bf16)
    keep_ref[...] = dot(mixed_ref[keep], right[...], NN)


def split_kernel(part_ref, got_ref, top_ref, bottom_ref):
    half = top_ref.shape[0]
    for out, at in ((top_ref, slice(0, half)), (bottom_ref, slice(half, 2 * half))):
        out[...] = (part_ref[at] + got_ref[at].astype(f32)).astype(bf16)


def meet_kernel(top_ref, bottom_ref, got_top, got_bottom, out_ref):
    half = top_ref.shape[0]
    for n, (mine, got) in enumerate(((top_ref, got_top), (bottom_ref, got_bottom))):
        out_ref[n * half : (n + 1) * half] = (mine[...].astype(f32) + got[...].astype(f32)).astype(bf16)


def round_kernel(part_ref, got_ref, out_ref):
    out_ref[...] = (part_ref[...].astype(f32) + got_ref[...].astype(f32)).astype(bf16)


def write_kernel(own, scale, value_ref, *refs):
    out_ref, wide, sem = refs[-3:]
    half = value_ref.shape[0]
    other, here = halves(bit_of(1), half)
    wide[...] = value_ref[...].astype(f32) * scale
    copy = pltpu.make_async_copy(wide, out_ref.at[here if own else other], sem)
    copy.start()
    copy.wait()


def cross_kernel(mine_ref, first_ref, second_ref, out_ref):
    window = lax.rem(lax.axis_index("dp"), 2)
    other, here = halves(window, mine_ref.shape[0])
    at_home = bit_of(2) == window
    mine, first, second = mine_ref[...], first_ref[...], second_ref[...]
    out_ref[here] = jnp.where(at_home, mine, first)
    out_ref[other] = jnp.where(at_home, first, second)


def local(
    query_states, key_states, value_states, grad_output, out_weight, partner_ids, partner_count
):
    span, width = query_states.shape[2:]
    stations = lax.axis_size("station")
    windows = lax.axis_size("dp")
    rows = width // LAYER
    dma = pltpu.SemaphoreType.DMA

    def swap(value, stride):
        return lax.ppermute(value, "station", [(s ^ stride, s) for s in range(stations)])

    def in_layer(values):
        return [swap(values[n], n + 1) for n in range(LAYER - 1)]

    def along(up, down):
        low = lax.ppermute(up, "station", [(s, (s + LAYER) % stations) for s in range(stations)])
        high = lax.ppermute(down, "station", [(s, (s - LAYER) % stations) for s in range(stations)])
        return low, high

    def other_window(value):
        return lax.ppermute(value, "dp", [(0, 1), (1, 0)])

    def flat(x):
        return x.reshape(span, width)

    q, k, v, g = flat(query_states), flat(key_states), flat(value_states), flat(grad_output)
    flat_shape = shape_of(span, width)
    part_shape = shape_of(2, rows, span)
    reach_shape = shape_of(2, rows, HOPS * span)
    layer_shape = shape_of(2, rows, LAYER * span)

    def gather(parts, after=()):
        return call(
            gather_kernel, [VMEM] * LAYER, [reach_shape, reach_shape, layer_shape], parts,
            name="gather", after=after,
        )

    mine, *parts = call(
        pack_kernel, [HBM] * 2, [part_shape] * LAYER, (k, v),
        [pltpu.VMEM((2, span, width), bf16), pltpu.VMEM((2, width, span), bf16), dma((2,))],
        limit=53.5, name="pack",
    )
    q, *parts = lax.optimization_barrier((q, *parts))
    parts = in_layer(parts)
    up, down, pair = gather((mine, *parts))
    mine, *query_parts, g_copy = call(
        project_kernel, [VMEM] * 3, [part_shape] * LAYER + [flat_shape],
        (q, g, out_weight), [pltpu.VMEM((2, width, span), bf16)], name="project",
    )
    up, g_later, *query_parts = lax.optimization_barrier((up, g, *query_parts))
    kv_low, kv_high = along(up, down)
    g_across = swap(g_later, 2)
    g_parts = g_copy, swap(g_later, 1), g_across, swap(g_across, 1)
    bias, dead = call(
        functools.partial(live_kernel, stations), [SMEM] * 2,
        [shape_of(16, LAYER * span, dtype=f32), shape_of(8, HOPS * span, dtype=f32)],
        (partner_ids, partner_count), name="live",
    )
    up, down, query = gather((mine, *in_layer(query_parts)), (bias,))
    qg_low, qg_high = along(up, down)
    stats_shape = shape_of(16, HOPS * span, dtype=f32)
    mixed, stats, up, down, probs, window = call(
        forward_kernel, [VMEM] * 5,
        [
            shape_of(rows, LAYER * span), shape_of(8, LAYER * span, dtype=f32),
            stats_shape, stats_shape,
            shape_of(LOCAL, BLOCKS * span, LAYER * span), shape_of(2, rows, BLOCKS * span),
        ],
        (pair, kv_low, kv_high, query, bias),
        [pltpu.VMEM((BLOCKS * span, LAYER * span), f32)],
        limit=20, name="forward",
    )
    stats_low, stats_high = along(up, down)

    send, part = call(
        weight_kernel, [VMEM] * (LAYER + 1),
        [shape_of(rows // 2, width), shape_of(rows // 2, width, dtype=f32)],
        (mixed, *g_parts), [pltpu.VMEM((LAYER * span, width), bf16)], name="weight",
    )

    dq, own_grad, query_token = call(
        query_grad_kernel, [VMEM] * 4,
        [shape_of(rows, LAYER * span), shape_of(2, rows, LAYER * span, dtype=f32), TOKEN],
        (window, probs, query, stats), [pltpu.VMEM((BLOCKS * span, LAYER * span), bf16)],
        limit=20, name="query_grad", after=(send,),
    )
    mine, *parts, key_token = call(
        key_grad_kernel, [VMEM] * 9, [shape_of(4, rows, span)] * LAYER + [TOKEN],
        (pair, qg_low, qg_high, stats_low, stats_high, dead, own_grad, mixed, dq),
        [
            pltpu.VMEM((2, rows, LAYER * span), bf16),
            pltpu.VMEM((HEADS, span, HOPS * span), f32),
            pltpu.VMEM((HEADS, span, HOPS * span), f32),
            pltpu.VMEM((HEADS, span, HOPS * span), bf16),
            pltpu.VMEM((HEADS, span, HOPS * span), bf16),
        ],
        limit=24, name="key_grad",
    )
    parts = in_layer(parts)
    layer_output, grad_query, grad_key, grad_value, output_token = call(
        output_kernel, [VMEM] * (LAYER + 1), [flat_shape] * 4 + [TOKEN],
        (mine, *parts, out_weight), [pltpu.VMEM((4, width, span), bf16)], name="output",
    )

    scale = 1.0 / math.sqrt(span * windows * stations)
    if windows == 2:
        count = rows // 2
        got = other_window(send)
        top, bottom = call(
            split_kernel, [VMEM] * 2, [shape_of(count // 2, width)] * 2, (part, got), name="split",
            after=(query_token,),
        )
        (total,) = call(
            meet_kernel, [VMEM] * 4, [shape_of(count, width)],
            (top, bottom, swap(top, LAYER), swap(bottom, LAYER)), name="meet", after=(key_token,),
        )
        stride = 2 * LAYER
        while stride < stations:
            (total,) = call(
                round_kernel, [VMEM] * 2, [shape_of(count, width)], (total, swap(total, stride)),
                name="add", after=parts[:1] if 2 * stride >= stations else (),
            )
            stride *= 2
        first, second = [], []
        for w in range(2):
            for s in range(stations):
                if s // 2 % 2 == w:
                    first.append((w * stations + s, w * stations + (s ^ 2)))
                else:
                    first.append((w * stations + s, (1 - w) * stations + s))
                    second.append((w * stations + s, (1 - w) * stations + (s ^ 2)))
        axes = ("dp", "station")
        (total,) = call(
            cross_kernel, [VMEM] * 3, [shape_of(2 * count, width)],
            (total, lax.ppermute(total, axes, first), lax.ppermute(total, axes, second)),
            name="cross", after=(output_token,),
        )
        grad_weight = ()
        for own, value in ((True, total), (False, swap(total, 1))):
            grad_weight = (pl.pallas_call(
                functools.partial(write_kernel, own, scale),
                in_specs=[VMEM] + [ANY] * len(grad_weight),
                out_specs=ANY,
                out_shape=shape_of(4 * count, width, dtype=f32),
                scratch_shapes=[pltpu.VMEM((2 * count, width), f32), dma],
                input_output_aliases={1: 0} if grad_weight else {},
                compiler_params=pltpu.CompilerParams(vmem_limit_bytes=8 * MIB),
                cost_estimate=pl.CostEstimate(flops=1, bytes_accessed=1, transcendentals=0),
                name="write",
            )(value, *grad_weight),)
        (grad_weight,) = grad_weight
    else:
        start = lax.axis_index("station") % LAYER * rows
        all_grad = jnp.zeros((LAYER * span, width), bf16)
        for peer in range(LAYER):
            value = g_parts[peer]
            spot = lax.axis_index("station") % LAYER ^ peer
            all_grad = lax.dynamic_update_slice_in_dim(all_grad, value, spot * span, 0)
        mine = dot(mixed, all_grad, NN).astype(bf16)
        whole = lax.dynamic_update_slice_in_dim(jnp.zeros((width, width), bf16), mine, start, 0)
        whole = lax.psum_scatter(whole, "dp", scatter_dimension=0, tiled=True)
        grad_weight = lax.psum(whole.astype(f32), "station") * scale
    shape = query_states.shape
    return (
        layer_output.reshape(shape),
        grad_query.reshape(shape),
        grad_key.reshape(shape),
        grad_value.reshape(shape),
        grad_weight,
    )


def solution(mesh):
    split = P("dp", "station", None, None)
    return jax.shard_map(
        local,
        mesh=mesh,
        in_specs=(split, split, split, split, P(), P(), P()),
        out_specs=(split, split, split, split, P("dp", None)),
        check_vma=False,
    )
```

```python
import functools
import math

import jax
import jax.numpy as jnp
from jax import lax
from jax.experimental import pallas as pl
from jax.experimental.pallas import tpu as pltpu
from jax.sharding import PartitionSpec as P

HEADS = 12
PMAX = 6
HOPS = 3
LAYER = 4
LOCAL = HEADS // LAYER
BLOCKS = LAYER + 2 * HOPS
SLOTS = 2 * HOPS + 1
MIB = 1024 * 1024

neg_big = -1e30
bf16, f32 = jnp.bfloat16, jnp.float32
SMEM = pl.BlockSpec(memory_space=pltpu.SMEM)
VMEM = pl.BlockSpec(memory_space=pltpu.VMEM)
ANY = pl.BlockSpec(memory_space=pl.ANY)
HBM = pl.BlockSpec(memory_space=pltpu.HBM)
NN = (((1,), (0,)), ((), ()))
NT = (((1,), (1,)), ((), ()))
TN = (((0,), (0,)), ((), ()))


def dot(x, y, dims):
    return lax.dot_general(x, y, dims, preferred_element_type=f32)


def shape_of(*dims, dtype=bf16):
    return jax.ShapeDtypeStruct(dims, dtype)


TOKEN = shape_of(8, 128, dtype=f32)


def skip_refs(kernel, first, count, *refs):
    kernel(*refs[:first], *refs[first + count :])


def call(kernel, ins, outs, args, scratch=(), limit=8, name=None, after=()):
    ins, args = [*ins, *[ANY] * len(after)], (*args, *after)
    if after:
        kernel = functools.partial(skip_refs, kernel, len(args) - len(after), len(after))
    return pl.pallas_call(
        kernel,
        in_specs=ins,
        out_specs=[VMEM] * len(outs),
        out_shape=outs,
        scratch_shapes=list(scratch),
        compiler_params=pltpu.CompilerParams(vmem_limit_bytes=int(limit * MIB)),
        cost_estimate=pl.CostEstimate(flops=1, bytes_accessed=1, transcendentals=0),
        name=name,
    )(*args)


def place(peer, size):
    position = jnp.bitwise_xor(lax.rem(lax.axis_index("station"), LAYER), peer)
    return pl.ds(pl.multiple_of(position * size, size), size)


def block(j, span):
    return slice(j * span, (j + 1) * span)


def readers(j):
    return max(0, j - 2 * HOPS), min(LAYER - 1, j)


def pack_kernel(k_ref, v_ref, *refs):
    outs, (natural, flipped, sems) = refs[:LAYER], refs[LAYER:]
    rows = outs[0].shape[1]
    copies = [
        pltpu.make_async_copy(ref, natural.at[n], sems.at[n]) for n, ref in enumerate((k_ref, v_ref))
    ]
    for copy in copies:
        copy.start()
    for n, copy in enumerate(copies):
        copy.wait()
        flipped[n] = natural[n].T
    for peer, out in enumerate(outs):
        out[...] = flipped[:, place(peer, rows)]


def project_kernel(q_ref, g_ref, weight_ref, *refs):
    outs, (copy_ref, flipped) = refs[:LAYER], refs[LAYER:]
    rows = outs[0].shape[1]
    copy_ref[...] = g_ref[...]
    flipped[0] = q_ref[...].T * bf16(1.0 / math.sqrt(flipped.shape[1] // HEADS))
    flipped[1] = dot(weight_ref[...], g_ref[...], NT).astype(bf16)
    for peer, out in enumerate(outs):
        out[...] = flipped[:, place(peer, rows)]


def gather_kernel(*refs):
    ins, (up_ref, down_ref, pair_ref) = refs[:LAYER], refs[LAYER:]
    span = ins[0].shape[2]
    for peer, ref in enumerate(ins):
        pair_ref[:, :, place(peer, span)] = ref[...]
    up_ref[...] = pair_ref[:, :, span:]
    down_ref[...] = pair_ref[:, :, : HOPS * span]


def live_kernel(station_count, ids_ref, count_ref, bias_ref, dead_ref):
    span = bias_ref.shape[1] // LAYER
    first = lax.axis_index("station") // LAYER * LAYER
    ones = jnp.ones((1, span), f32)

    def listed(reader, other):
        hit = jnp.int32(0)
        for j in range(PMAX):
            here = jnp.logical_and(ids_ref[reader, j] == other, j < count_ref[reader])
            hit = jnp.maximum(hit, here.astype(jnp.int32))
        return hit > 0

    for j in range(BLOCKS):
        outer = lax.rem(first + (j - HOPS) + station_count, station_count)
        low, high = readers(j)
        for i in range(low, high + 1):
            inner = first + i
            slot = j - i
            if slot == HOPS:
                bias_ref[j : j + 1, block(i, span)] = 0.0 * ones
            else:
                reads = jnp.where(listed(inner, outer), 0.0, neg_big)
                bias_ref[j : j + 1, block(i, span)] = reads * ones
            if not HOPS <= j < HOPS + LAYER:
                read_by = jnp.where(listed(outer, inner), 0.0, -neg_big)
                spot = slot if j < HOPS else slot - LAYER
                dead_ref[i : i + 1, block(spot, span)] = read_by * ones


def clear(ref, span):
    for j in range(BLOCKS):
        low, high = readers(j)
        for i in range(LAYER):
            if not low <= i <= high:
                ref[block(j, span), block(i, span)] = jnp.zeros((span, span), bf16)


def forward_kernel(
    pair_ref, low_ref, high_ref, query_ref, bias_ref,
    mixed_ref, stats_ref, stats_up, stats_down, probs_ref, window_ref,
    raw,
):
    rows = query_ref.shape[1]
    span = query_ref.shape[2] // LAYER
    head_width = rows // LOCAL
    reach = HOPS * span
    window_ref[:, :, :reach] = low_ref[...]
    window_ref[:, :, reach : reach + LAYER * span] = pair_ref[...]
    window_ref[:, :, reach + LAYER * span :] = high_ref[...]
    for head in range(LOCAL):
        clear(probs_ref.at[head], span)
        at = block(head, head_width)
        query = query_ref[0, at]
        tops = [None] * LAYER
        for j in range(BLOCKS):
            low, high = readers(j)
            cols = slice(low * span, (high + 1) * span)
            scores = dot(window_ref[0, at, block(j, span)], query[:, cols], TN)
            scores = scores + bias_ref[j : j + 1, cols]
            raw[block(j, span), cols] = scores
            here = jnp.max(scores, 0, keepdims=True)
            for i in range(low, high + 1):
                mine = here[:, block(i - low, span)]
                tops[i] = mine if tops[i] is None else jnp.maximum(tops[i], mine)
        top = jnp.concatenate(tops, 1)
        totals = [jnp.zeros((1, span), f32)] * LAYER
        for j in range(BLOCKS):
            low, high = readers(j)
            cols = slice(low * span, (high + 1) * span)
            weight = jnp.exp(raw[block(j, span), cols] - top[:, cols])
            raw[block(j, span), cols] = weight
            here = jnp.sum(weight, 0, keepdims=True)
            for i in range(low, high + 1):
                totals[i] = totals[i] + here[:, block(i - low, span)]
        total = jnp.concatenate(totals, 1)
        inverse = 1.0 / total
        for j in range(BLOCKS):
            low, high = readers(j)
            cols = slice(low * span, (high + 1) * span)
            probs_ref[head, block(j, span), cols] = (
                raw[block(j, span), cols] * inverse[:, cols]
            ).astype(bf16)
        mixed = dot(window_ref[1, at], probs_ref[head], NN).astype(bf16)
        mixed_ref[at] = mixed
        product = query_ref[1, at].astype(f32) * mixed.astype(f32)
        stats_ref[head : head + 1] = top + jnp.log(total)
        stats_ref[LOCAL + head : LOCAL + head + 1] = jnp.sum(product, 0, keepdims=True)
    stats_ref[2 * LOCAL :] = jnp.zeros((8 - 2 * LOCAL, LAYER * span), f32)
    for ref, at in ((stats_up, slice(span, None)), (stats_down, slice(0, reach))):
        ref[...] = jnp.zeros_like(ref)
        ref[:8] = stats_ref[:, at]


def query_grad_kernel(
    window_ref, probs_ref, query_ref, stats_ref, dq_ref, own_ref, token_ref, grads
):
    rows = query_ref.shape[1]
    span = query_ref.shape[2] // LAYER
    head_width = rows // LOCAL
    scale = 1.0 / math.sqrt(head_width)
    inside = slice(HOPS * span, (HOPS + LAYER) * span)
    clear(grads, span)
    for head in range(LOCAL):
        at = block(head, head_width)
        grad = query_ref[1, at]
        delta = stats_ref[LOCAL + head : LOCAL + head + 1]
        for j in range(BLOCKS):
            low, high = readers(j)
            cols = slice(low * span, (high + 1) * span)
            back = dot(window_ref[1, at, block(j, span)], grad[:, cols], TN)
            prob = probs_ref[head, block(j, span), cols].astype(f32)
            grads[block(j, span), cols] = (prob * (back - delta[:, cols])).astype(bf16)
        dq_ref[at] = (dot(window_ref[0, at], grads[...], NN) * scale).astype(bf16)
        own_ref[0, at] = dot(query_ref[0, at], grads[inside], NT)
        own_ref[1, at] = dot(grad, probs_ref[head, inside], NT)
    token_ref[...] = jnp.zeros_like(token_ref)


def key_grad_kernel(
    pair_ref, low_ref, high_ref, stats_low, stats_high, dead_ref, own_ref, mixed_ref, dq_ref, *refs
):
    outs, (token_ref, flipped, scores, backs, probs, grads) = refs[:LAYER], refs[LAYER:]
    rows = pair_ref.shape[1]
    span = pair_ref.shape[2] // LAYER
    head_width = rows // LOCAL
    pairs = [(head, i) for head in range(LOCAL) for i in range(LAYER)]

    def outside(low, high, i):
        sides = [low[:, i * span :]] if i < HOPS else []
        return jnp.concatenate(sides + ([high[:, : i * span]] if i else []), 1)

    def both(part, head, i):
        at = block(head, head_width)
        return outside(low_ref[part, at], high_ref[part, at], i)

    for n, (head, i) in enumerate(pairs):
        at, own = block(head, head_width), block(i, span)
        scores[n] = dot(pair_ref[0, at, own], both(0, head, i), TN)
        backs[n] = dot(pair_ref[1, at, own], both(1, head, i), TN)
    for n, (head, i) in enumerate(pairs):
        row = slice(head, head + 1)
        log_sum = outside(stats_low[row], stats_high[row], i) + dead_ref[i : i + 1]
        row = slice(LOCAL + head, LOCAL + head + 1)
        delta = outside(stats_low[row], stats_high[row], i)
        prob = jnp.exp(scores[n] - log_sum)
        probs[n] = prob.astype(bf16)
        grads[n] = (prob * (backs[n] - delta)).astype(bf16)
    for n, (head, i) in enumerate(pairs):
        at, own = block(head, head_width), block(i, span)
        keys = own_ref[0, at, own] + dot(both(0, head, i), grads[n], NT)
        values = own_ref[1, at, own] + dot(both(1, head, i), probs[n], NT)
        flipped[0, at, own] = keys.astype(bf16)
        flipped[1, at, own] = values.astype(bf16)
    for peer, out in enumerate(outs):
        at = place(peer, span)
        out[0] = mixed_ref[:, at]
        out[1] = dq_ref[:, at]
        out[2:] = flipped[:, :, at]
    token_ref[...] = jnp.zeros_like(token_ref)


def output_kernel(*refs):
    ins, refs = refs[:LAYER], refs[LAYER:]
    weight_ref, out_ref, dq_ref, dk_ref, dv_ref, token_ref, flipped = refs
    for peer, ref in enumerate(ins):
        flipped[:, place(peer, ref.shape[1])] = ref[...]
    out_ref[...] = dot(flipped[0], weight_ref[...], TN).astype(bf16)
    for n, ref in enumerate((dq_ref, dk_ref, dv_ref)):
        ref[...] = flipped[n + 1].T
    token_ref[...] = jnp.zeros_like(token_ref)


def halves(bit, half):
    send = pl.ds(pl.multiple_of((1 - bit) * half, half), half)
    keep = pl.ds(pl.multiple_of(bit * half, half), half)
    return send, keep


def bit_of(stride):
    return lax.rem(lax.axis_index("station") // stride, 2)


def weight_kernel(mixed_ref, *refs):
    ins, (send_ref, keep_ref, right) = refs[:LAYER], refs[LAYER:]
    for peer, ref in enumerate(ins):
        right[place(peer, ref.shape[0])] = ref[...]
    send, keep = halves(lax.rem(lax.axis_index("dp"), 2), send_ref.shape[0])
    send_ref[...] = dot(mixed_ref[send], right[...], NN).astype(bf16)
    keep_ref[...] = dot(mixed_ref[keep], right[...], NN)


def split_kernel(part_ref, got_ref, top_ref, bottom_ref):
    half = top_ref.shape[0]
    for out, at in ((top_ref, slice(0, half)), (bottom_ref, slice(half, 2 * half))):
        out[...] = (part_ref[at] + got_ref[at].astype(f32)).astype(bf16)


def meet_kernel(top_ref, bottom_ref, got_top, got_bottom, out_ref):
    half = top_ref.shape[0]
    for n, (mine, got) in enumerate(((top_ref, got_top), (bottom_ref, got_bottom))):
        out_ref[n * half : (n + 1) * half] = (mine[...].astype(f32) + got[...].astype(f32)).astype(bf16)


def round_kernel(part_ref, got_ref, out_ref):
    out_ref[...] = (part_ref[...].astype(f32) + got_ref[...].astype(f32)).astype(bf16)


def write_kernel(own, scale, value_ref, *refs):
    out_ref, wide, sem = refs[-3:]
    half = value_ref.shape[0]
    other, here = halves(bit_of(1), half)
    wide[...] = value_ref[...].astype(f32) * scale
    copy = pltpu.make_async_copy(wide, out_ref.at[here if own else other], sem)
    copy.start()
    copy.wait()


def cross_kernel(mine_ref, first_ref, second_ref, out_ref):
    window = lax.rem(lax.axis_index("dp"), 2)
    other, here = halves(window, mine_ref.shape[0])
    at_home = bit_of(2) == window
    mine, first, second = mine_ref[...], first_ref[...], second_ref[...]
    out_ref[here] = jnp.where(at_home, mine, first)
    out_ref[other] = jnp.where(at_home, first, second)


def local(
    query_states, key_states, value_states, grad_output, out_weight, partner_ids, partner_count
):
    span, width = query_states.shape[2:]
    stations = lax.axis_size("station")
    windows = lax.axis_size("dp")
    rows = width // LAYER
    dma = pltpu.SemaphoreType.DMA

    def swap(value, stride):
        return lax.ppermute(value, "station", [(s ^ stride, s) for s in range(stations)])

    def in_layer(values):
        return [swap(values[n], n + 1) for n in range(LAYER - 1)]

    def along(up, down):
        low = lax.ppermute(up, "station", [(s, (s + LAYER) % stations) for s in range(stations)])
        high = lax.ppermute(down, "station", [(s, (s - LAYER) % stations) for s in range(stations)])
        return low, high

    def other_window(value):
        return lax.ppermute(value, "dp", [(0, 1), (1, 0)])

    def flat(x):
        return x.reshape(span, width)

    q, k, v, g = flat(query_states), flat(key_states), flat(value_states), flat(grad_output)
    flat_shape = shape_of(span, width)
    part_shape = shape_of(2, rows, span)
    reach_shape = shape_of(2, rows, HOPS * span)
    layer_shape = shape_of(2, rows, LAYER * span)

    def gather(parts, after=()):
        return call(
            gather_kernel, [VMEM] * LAYER, [reach_shape, reach_shape, layer_shape], parts,
            name="gather", after=after,
        )

    mine, *parts = call(
        pack_kernel, [HBM] * 2, [part_shape] * LAYER, (k, v),
        [pltpu.VMEM((2, span, width), bf16), pltpu.VMEM((2, width, span), bf16), dma((2,))],
        limit=53.5, name="pack",
    )
    q, *parts = lax.optimization_barrier((q, *parts))
    parts = in_layer(parts)
    up, down, pair = gather((mine, *parts))
    mine, *query_parts, g_copy = call(
        project_kernel, [VMEM] * 3, [part_shape] * LAYER + [flat_shape],
        (q, g, out_weight), [pltpu.VMEM((2, width, span), bf16)], name="project",
    )
    up, g_later, *query_parts = lax.optimization_barrier((up, g, *query_parts))
    kv_low, kv_high = along(up, down)
    g_across = swap(g_later, 2)
    g_parts = g_copy, swap(g_later, 1), g_across, swap(g_across, 1)
    bias, dead = call(
        functools.partial(live_kernel, stations), [SMEM] * 2,
        [shape_of(16, LAYER * span, dtype=f32), shape_of(8, HOPS * span, dtype=f32)],
        (partner_ids, partner_count), name="live",
    )
    up, down, query = gather((mine, *in_layer(query_parts)), (bias,))
    qg_low, qg_high = along(up, down)
    stats_shape = shape_of(16, HOPS * span, dtype=f32)
    mixed, stats, up, down, probs, window = call(
        forward_kernel, [VMEM] * 5,
        [
            shape_of(rows, LAYER * span), shape_of(8, LAYER * span, dtype=f32),
            stats_shape, stats_shape,
            shape_of(LOCAL, BLOCKS * span, LAYER * span), shape_of(2, rows, BLOCKS * span),
        ],
        (pair, kv_low, kv_high, query, bias),
        [pltpu.VMEM((BLOCKS * span, LAYER * span), f32)],
        limit=20, name="forward",
    )

    send, part = call(
        weight_kernel, [VMEM] * (LAYER + 1),
        [shape_of(rows // 2, width), shape_of(rows // 2, width, dtype=f32)],
        (mixed, *g_parts), [pltpu.VMEM((LAYER * span, width), bf16)], name="weight",
    )

    dq, own_grad, query_token = call(
        query_grad_kernel, [VMEM] * 4,
        [shape_of(rows, LAYER * span), shape_of(2, rows, LAYER * span, dtype=f32), TOKEN],
        (window, probs, query, stats), [pltpu.VMEM((BLOCKS * span, LAYER * span), bf16)],
        limit=20, name="query_grad", after=(send,),
    )
    up, down, query_token = lax.optimization_barrier((up, down, query_token))
    stats_low, stats_high = along(up, down)
    mine, *parts, key_token = call(
        key_grad_kernel, [VMEM] * 9, [shape_of(4, rows, span)] * LAYER + [TOKEN],
        (pair, qg_low, qg_high, stats_low, stats_high, dead, own_grad, mixed, dq),
        [
            pltpu.VMEM((2, rows, LAYER * span), bf16),
            pltpu.VMEM((HEADS, span, HOPS * span), f32),
            pltpu.VMEM((HEADS, span, HOPS * span), f32),
            pltpu.VMEM((HEADS, span, HOPS * span), bf16),
            pltpu.VMEM((HEADS, span, HOPS * span), bf16),
        ],
        limit=24, name="key_grad",
    )
    parts = in_layer(parts)
    layer_output, grad_query, grad_key, grad_value, output_token = call(
        output_kernel, [VMEM] * (LAYER + 1), [flat_shape] * 4 + [TOKEN],
        (mine, *parts, out_weight), [pltpu.VMEM((4, width, span), bf16)], name="output",
    )

    scale = 1.0 / math.sqrt(span * windows * stations)
    if windows == 2:
        count = rows // 2
        got = other_window(send)
        top, bottom = call(
            split_kernel, [VMEM] * 2, [shape_of(count // 2, width)] * 2, (part, got), name="split",
            after=(query_token,),
        )
        (total,) = call(
            meet_kernel, [VMEM] * 4, [shape_of(count, width)],
            (top, bottom, swap(top, LAYER), swap(bottom, LAYER)), name="meet", after=(key_token,),
        )
        stride = 2 * LAYER
        while stride < stations:
            (total,) = call(
                round_kernel, [VMEM] * 2, [shape_of(count, width)], (total, swap(total, stride)),
                name="add", after=parts[:1] if 2 * stride >= stations else (),
            )
            stride *= 2
        first, second = [], []
        for w in range(2):
            for s in range(stations):
                if s // 2 % 2 == w:
                    first.append((w * stations + s, w * stations + (s ^ 2)))
                else:
                    first.append((w * stations + s, (1 - w) * stations + s))
                    second.append((w * stations + s, (1 - w) * stations + (s ^ 2)))
        axes = ("dp", "station")
        (total,) = call(
            cross_kernel, [VMEM] * 3, [shape_of(2 * count, width)],
            (total, lax.ppermute(total, axes, first), lax.ppermute(total, axes, second)),
            name="cross", after=(output_token,),
        )
        grad_weight = ()
        for own, value in ((True, total), (False, swap(total, 1))):
            grad_weight = (pl.pallas_call(
                functools.partial(write_kernel, own, scale),
                in_specs=[VMEM] + [ANY] * len(grad_weight),
                out_specs=ANY,
                out_shape=shape_of(4 * count, width, dtype=f32),
                scratch_shapes=[pltpu.VMEM((2 * count, width), f32), dma],
                input_output_aliases={1: 0} if grad_weight else {},
                compiler_params=pltpu.CompilerParams(vmem_limit_bytes=8 * MIB),
                cost_estimate=pl.CostEstimate(flops=1, bytes_accessed=1, transcendentals=0),
                name="write",
            )(value, *grad_weight),)
        (grad_weight,) = grad_weight
    else:
        start = lax.axis_index("station") % LAYER * rows
        all_grad = jnp.zeros((LAYER * span, width), bf16)
        for peer in range(LAYER):
            value = g_parts[peer]
            spot = lax.axis_index("station") % LAYER ^ peer
            all_grad = lax.dynamic_update_slice_in_dim(all_grad, value, spot * span, 0)
        mine = dot(mixed, all_grad, NN).astype(bf16)
        whole = lax.dynamic_update_slice_in_dim(jnp.zeros((width, width), bf16), mine, start, 0)
        whole = lax.psum_scatter(whole, "dp", scatter_dimension=0, tiled=True)
        grad_weight = lax.psum(whole.astype(f32), "station") * scale
    shape = query_states.shape
    return (
        layer_output.reshape(shape),
        grad_query.reshape(shape),
        grad_key.reshape(shape),
        grad_value.reshape(shape),
        grad_weight,
    )


def solution(mesh):
    split = P("dp", "station", None, None)
    return jax.shard_map(
        local,
        mesh=mesh,
        in_specs=(split, split, split, split, P(), P(), P()),
        out_specs=(split, split, split, split, P("dp", None)),
        check_vma=False,
    )
```

```python
import functools
import math

import jax
import jax.numpy as jnp
from jax import lax
from jax.experimental import pallas as pl
from jax.experimental.pallas import tpu as pltpu
from jax.sharding import PartitionSpec as P

HEADS = 12
PMAX = 6
HOPS = 3
LAYER = 4
LOCAL = HEADS // LAYER
BLOCKS = LAYER + 2 * HOPS
SLOTS = 2 * HOPS + 1
MIB = 1024 * 1024

neg_big = -1e30
bf16, f32 = jnp.bfloat16, jnp.float32
SMEM = pl.BlockSpec(memory_space=pltpu.SMEM)
VMEM = pl.BlockSpec(memory_space=pltpu.VMEM)
ANY = pl.BlockSpec(memory_space=pl.ANY)
HBM = pl.BlockSpec(memory_space=pltpu.HBM)
NN = (((1,), (0,)), ((), ()))
NT = (((1,), (1,)), ((), ()))
TN = (((0,), (0,)), ((), ()))


def dot(x, y, dims):
    return lax.dot_general(x, y, dims, preferred_element_type=f32)


def shape_of(*dims, dtype=bf16):
    return jax.ShapeDtypeStruct(dims, dtype)


TOKEN = shape_of(8, 128, dtype=f32)


def skip_refs(kernel, first, count, *refs):
    kernel(*refs[:first], *refs[first + count :])


def call(kernel, ins, outs, args, scratch=(), limit=8, name=None, after=()):
    ins, args = [*ins, *[ANY] * len(after)], (*args, *after)
    if after:
        kernel = functools.partial(skip_refs, kernel, len(args) - len(after), len(after))
    return pl.pallas_call(
        kernel,
        in_specs=ins,
        out_specs=[VMEM] * len(outs),
        out_shape=outs,
        scratch_shapes=list(scratch),
        compiler_params=pltpu.CompilerParams(vmem_limit_bytes=int(limit * MIB)),
        cost_estimate=pl.CostEstimate(flops=1, bytes_accessed=1, transcendentals=0),
        name=name,
    )(*args)


def place(peer, size):
    position = jnp.bitwise_xor(lax.rem(lax.axis_index("station"), LAYER), peer)
    return pl.ds(pl.multiple_of(position * size, size), size)


def block(j, span):
    return slice(j * span, (j + 1) * span)


def readers(j):
    return max(0, j - 2 * HOPS), min(LAYER - 1, j)


def pack_kernel(k_ref, v_ref, *refs):
    outs, (natural, flipped, sems) = refs[:LAYER], refs[LAYER:]
    rows = outs[0].shape[1]
    copies = [
        pltpu.make_async_copy(ref, natural.at[n], sems.at[n]) for n, ref in enumerate((k_ref, v_ref))
    ]
    for copy in copies:
        copy.start()
    for n, copy in enumerate(copies):
        copy.wait()
        flipped[n] = natural[n].T
    for peer, out in enumerate(outs):
        out[...] = flipped[:, place(peer, rows)]


def project_kernel(q_ref, g_ref, weight_ref, *refs):
    outs, (copy_ref, flipped) = refs[:LAYER], refs[LAYER:]
    rows = outs[0].shape[1]
    copy_ref[...] = g_ref[...]
    flipped[0] = q_ref[...].T * bf16(1.0 / math.sqrt(flipped.shape[1] // HEADS))
    flipped[1] = dot(weight_ref[...], g_ref[...], NT).astype(bf16)
    for peer, out in enumerate(outs):
        out[...] = flipped[:, place(peer, rows)]


def gather_kernel(*refs):
    ins, (up_ref, down_ref, pair_ref) = refs[:LAYER], refs[LAYER:]
    span = ins[0].shape[2]
    for peer, ref in enumerate(ins):
        pair_ref[:, :, place(peer, span)] = ref[...]
    up_ref[...] = pair_ref[:, :, span:]
    down_ref[...] = pair_ref[:, :, : HOPS * span]


def live_kernel(station_count, ids_ref, count_ref, bias_ref, dead_ref):
    span = bias_ref.shape[1] // LAYER
    first = lax.axis_index("station") // LAYER * LAYER
    ones = jnp.ones((1, span), f32)

    def listed(reader, other):
        hit = jnp.int32(0)
        for j in range(PMAX):
            here = jnp.logical_and(ids_ref[reader, j] == other, j < count_ref[reader])
            hit = jnp.maximum(hit, here.astype(jnp.int32))
        return hit > 0

    for j in range(BLOCKS):
        outer = lax.rem(first + (j - HOPS) + station_count, station_count)
        low, high = readers(j)
        for i in range(low, high + 1):
            inner = first + i
            slot = j - i
            if slot == HOPS:
                bias_ref[j : j + 1, block(i, span)] = 0.0 * ones
            else:
                reads = jnp.where(listed(inner, outer), 0.0, neg_big)
                bias_ref[j : j + 1, block(i, span)] = reads * ones
            if not HOPS <= j < HOPS + LAYER:
                read_by = jnp.where(listed(outer, inner), 0.0, -neg_big)
                spot = slot if j < HOPS else slot - LAYER
                dead_ref[i : i + 1, block(spot, span)] = read_by * ones


def clear(ref, span):
    for j in range(BLOCKS):
        low, high = readers(j)
        for i in range(LAYER):
            if not low <= i <= high:
                ref[block(j, span), block(i, span)] = jnp.zeros((span, span), bf16)


def forward_kernel(
    pair_ref, low_ref, high_ref, query_ref, bias_ref,
    mixed_ref, stats_ref, stats_up, stats_down, probs_ref, window_ref,
    raw,
):
    rows = query_ref.shape[1]
    span = query_ref.shape[2] // LAYER
    head_width = rows // LOCAL
    reach = HOPS * span
    window_ref[:, :, :reach] = low_ref[...]
    window_ref[:, :, reach : reach + LAYER * span] = pair_ref[...]
    window_ref[:, :, reach + LAYER * span :] = high_ref[...]
    for head in range(LOCAL):
        clear(probs_ref.at[head], span)
        at = block(head, head_width)
        query = query_ref[0, at]
        tops = [None] * LAYER
        for j in range(BLOCKS):
            low, high = readers(j)
            cols = slice(low * span, (high + 1) * span)
            scores = dot(window_ref[0, at, block(j, span)], query[:, cols], TN)
            scores = scores + bias_ref[j : j + 1, cols]
            raw[block(j, span), cols] = scores
            here = jnp.max(scores, 0, keepdims=True)
            for i in range(low, high + 1):
                mine = here[:, block(i - low, span)]
                tops[i] = mine if tops[i] is None else jnp.maximum(tops[i], mine)
        top = jnp.concatenate(tops, 1)
        totals = [jnp.zeros((1, span), f32)] * LAYER
        for j in range(BLOCKS):
            low, high = readers(j)
            cols = slice(low * span, (high + 1) * span)
            weight = jnp.exp(raw[block(j, span), cols] - top[:, cols])
            raw[block(j, span), cols] = weight
            here = jnp.sum(weight, 0, keepdims=True)
            for i in range(low, high + 1):
                totals[i] = totals[i] + here[:, block(i - low, span)]
        total = jnp.concatenate(totals, 1)
        inverse = 1.0 / total
        for j in range(BLOCKS):
            low, high = readers(j)
            cols = slice(low * span, (high + 1) * span)
            probs_ref[head, block(j, span), cols] = (
                raw[block(j, span), cols] * inverse[:, cols]
            ).astype(bf16)
        mixed = dot(window_ref[1, at], probs_ref[head], NN).astype(bf16)
        mixed_ref[at] = mixed
        product = query_ref[1, at].astype(f32) * mixed.astype(f32)
        stats_ref[head : head + 1] = top + jnp.log(total)
        stats_ref[LOCAL + head : LOCAL + head + 1] = jnp.sum(product, 0, keepdims=True)
    stats_ref[2 * LOCAL :] = jnp.zeros((8 - 2 * LOCAL, LAYER * span), f32)
    for ref, at in ((stats_up, slice(span, None)), (stats_down, slice(0, reach))):
        ref[...] = jnp.zeros_like(ref)
        ref[:8] = stats_ref[:, at]


def query_grad_kernel(
    window_ref, probs_ref, query_ref, stats_ref, dq_ref, own_ref, token_ref, grads
):
    rows = query_ref.shape[1]
    span = query_ref.shape[2] // LAYER
    head_width = rows // LOCAL
    scale = 1.0 / math.sqrt(head_width)
    inside = slice(HOPS * span, (HOPS + LAYER) * span)
    clear(grads, span)
    for head in range(LOCAL):
        at = block(head, head_width)
        grad = query_ref[1, at]
        delta = stats_ref[LOCAL + head : LOCAL + head + 1]
        for j in range(BLOCKS):
            low, high = readers(j)
            cols = slice(low * span, (high + 1) * span)
            back = dot(window_ref[1, at, block(j, span)], grad[:, cols], TN)
            prob = probs_ref[head, block(j, span), cols].astype(f32)
            grads[block(j, span), cols] = (prob * (back - delta[:, cols])).astype(bf16)
        dq_ref[at] = (dot(window_ref[0, at], grads[...], NN) * scale).astype(bf16)
        own_ref[0, at] = dot(query_ref[0, at], grads[inside], NT)
        own_ref[1, at] = dot(grad, probs_ref[head, inside], NT)
    token_ref[...] = jnp.zeros_like(token_ref)


def key_grad_kernel(
    pair_ref, low_ref, high_ref, stats_low, stats_high, dead_ref, own_ref, mixed_ref, dq_ref, *refs
):
    outs, (token_ref, flipped, scores, backs, probs, grads) = refs[:LAYER], refs[LAYER:]
    rows = pair_ref.shape[1]
    span = pair_ref.shape[2] // LAYER
    head_width = rows // LOCAL
    pairs = [(head, i) for head in range(LOCAL) for i in range(LAYER)]

    def outside(low, high, i):
        sides = [low[:, i * span :]] if i < HOPS else []
        return jnp.concatenate(sides + ([high[:, : i * span]] if i else []), 1)

    def both(part, head, i):
        at = block(head, head_width)
        return outside(low_ref[part, at], high_ref[part, at], i)

    for n, (head, i) in enumerate(pairs):
        at, own = block(head, head_width), block(i, span)
        scores[n] = dot(pair_ref[0, at, own], both(0, head, i), TN)
        backs[n] = dot(pair_ref[1, at, own], both(1, head, i), TN)
    for n, (head, i) in enumerate(pairs):
        row = slice(head, head + 1)
        log_sum = outside(stats_low[row], stats_high[row], i) + dead_ref[i : i + 1]
        row = slice(LOCAL + head, LOCAL + head + 1)
        delta = outside(stats_low[row], stats_high[row], i)
        prob = jnp.exp(scores[n] - log_sum)
        probs[n] = prob.astype(bf16)
        grads[n] = (prob * (backs[n] - delta)).astype(bf16)
    for n, (head, i) in enumerate(pairs):
        at, own = block(head, head_width), block(i, span)
        keys = own_ref[0, at, own] + dot(both(0, head, i), grads[n], NT)
        values = own_ref[1, at, own] + dot(both(1, head, i), probs[n], NT)
        flipped[0, at, own] = keys.astype(bf16)
        flipped[1, at, own] = values.astype(bf16)
    for peer, out in enumerate(outs):
        at = place(peer, span)
        out[0] = mixed_ref[:, at]
        out[1] = dq_ref[:, at]
        out[2:] = flipped[:, :, at]
    token_ref[...] = jnp.zeros_like(token_ref)


def output_kernel(*refs):
    ins, refs = refs[:LAYER], refs[LAYER:]
    weight_ref, out_ref, dq_ref, dk_ref, dv_ref, token_ref, flipped = refs
    for peer, ref in enumerate(ins):
        flipped[:, place(peer, ref.shape[1])] = ref[...]
    out_ref[...] = dot(flipped[0], weight_ref[...], TN).astype(bf16)
    for n, ref in enumerate((dq_ref, dk_ref, dv_ref)):
        ref[...] = flipped[n + 1].T
    token_ref[...] = jnp.zeros_like(token_ref)


def halves(bit, half):
    send = pl.ds(pl.multiple_of((1 - bit) * half, half), half)
    keep = pl.ds(pl.multiple_of(bit * half, half), half)
    return send, keep


def bit_of(stride):
    return lax.rem(lax.axis_index("station") // stride, 2)


def weight_kernel(mixed_ref, *refs):
    ins, (send_ref, keep_ref, right) = refs[:LAYER], refs[LAYER:]
    for peer, ref in enumerate(ins):
        right[place(peer, ref.shape[0])] = ref[...]
    send, keep = halves(lax.rem(lax.axis_index("dp"), 2), send_ref.shape[0])
    send_ref[...] = dot(mixed_ref[send], right[...], NN).astype(bf16)
    keep_ref[...] = dot(mixed_ref[keep], right[...], NN)


def split_kernel(part_ref, got_ref, top_ref, bottom_ref):
    half = top_ref.shape[0]
    for out, at in ((top_ref, slice(0, half)), (bottom_ref, slice(half, 2 * half))):
        out[...] = (part_ref[at] + got_ref[at].astype(f32)).astype(bf16)


def meet_kernel(top_ref, bottom_ref, got_top, got_bottom, out_ref):
    half = top_ref.shape[0]
    for n, (mine, got) in enumerate(((top_ref, got_top), (bottom_ref, got_bottom))):
        out_ref[n * half : (n + 1) * half] = (mine[...].astype(f32) + got[...].astype(f32)).astype(bf16)


def round_kernel(part_ref, got_ref, out_ref):
    out_ref[...] = (part_ref[...].astype(f32) + got_ref[...].astype(f32)).astype(bf16)


def write_kernel(own, scale, value_ref, *refs):
    out_ref, wide, sem = refs[-3:]
    half = value_ref.shape[0]
    other, here = halves(bit_of(1), half)
    wide[...] = value_ref[...].astype(f32) * scale
    copy = pltpu.make_async_copy(wide, out_ref.at[here if own else other], sem)
    copy.start()
    copy.wait()


def cross_kernel(mine_ref, first_ref, second_ref, out_ref):
    window = lax.rem(lax.axis_index("dp"), 2)
    other, here = halves(window, mine_ref.shape[0])
    at_home = bit_of(2) == window
    mine, first, second = mine_ref[...], first_ref[...], second_ref[...]
    out_ref[here] = jnp.where(at_home, mine, first)
    out_ref[other] = jnp.where(at_home, first, second)


def local(
    query_states, key_states, value_states, grad_output, out_weight, partner_ids, partner_count
):
    span, width = query_states.shape[2:]
    stations = lax.axis_size("station")
    windows = lax.axis_size("dp")
    rows = width // LAYER
    dma = pltpu.SemaphoreType.DMA

    def swap(value, stride):
        return lax.ppermute(value, "station", [(s ^ stride, s) for s in range(stations)])

    def in_layer(values):
        return [swap(values[n], n + 1) for n in range(LAYER - 1)]

    def along(up, down):
        low = lax.ppermute(up, "station", [(s, (s + LAYER) % stations) for s in range(stations)])
        high = lax.ppermute(down, "station", [(s, (s - LAYER) % stations) for s in range(stations)])
        return low, high

    def other_window(value):
        return lax.ppermute(value, "dp", [(0, 1), (1, 0)])

    def flat(x):
        return x.reshape(span, width)

    q, k, v, g = flat(query_states), flat(key_states), flat(value_states), flat(grad_output)
    flat_shape = shape_of(span, width)
    part_shape = shape_of(2, rows, span)
    reach_shape = shape_of(2, rows, HOPS * span)
    layer_shape = shape_of(2, rows, LAYER * span)

    def gather(parts, after=()):
        return call(
            gather_kernel, [VMEM] * LAYER, [reach_shape, reach_shape, layer_shape], parts,
            name="gather", after=after,
        )

    mine, *parts = call(
        pack_kernel, [HBM] * 2, [part_shape] * LAYER, (k, v),
        [pltpu.VMEM((2, span, width), bf16), pltpu.VMEM((2, width, span), bf16), dma((2,))],
        limit=53.5, name="pack",
    )
    q, *parts = lax.optimization_barrier((q, *parts))
    parts = in_layer(parts)
    up, down, pair = gather((mine, *parts))
    mine, *query_parts, g_copy = call(
        project_kernel, [VMEM] * 3, [part_shape] * LAYER + [flat_shape],
        (q, g, out_weight), [pltpu.VMEM((2, width, span), bf16)], name="project",
    )
    up, g_later, *query_parts = lax.optimization_barrier((up, g, *query_parts))
    kv_low, kv_high = along(up, down)
    g_across = swap(g_later, 2)
    g_parts = g_copy, swap(g_later, 1), g_across, swap(g_across, 1)
    bias, dead = call(
        functools.partial(live_kernel, stations), [SMEM] * 2,
        [shape_of(16, LAYER * span, dtype=f32), shape_of(8, HOPS * span, dtype=f32)],
        (partner_ids, partner_count), name="live",
    )
    up, down, query = gather((mine, *in_layer(query_parts)), (bias,))
    qg_low, qg_high = along(up, down)
    stats_shape = shape_of(16, HOPS * span, dtype=f32)
    mixed, stats, up, down, probs, window = call(
        forward_kernel, [VMEM] * 5,
        [
            shape_of(rows, LAYER * span), shape_of(8, LAYER * span, dtype=f32),
            stats_shape, stats_shape,
            shape_of(LOCAL, BLOCKS * span, LAYER * span), shape_of(2, rows, BLOCKS * span),
        ],
        (pair, kv_low, kv_high, query, bias),
        [pltpu.VMEM((BLOCKS * span, LAYER * span), f32)],
        limit=20, name="forward",
    )

    send, part = call(
        weight_kernel, [VMEM] * (LAYER + 1),
        [shape_of(rows // 2, width), shape_of(rows // 2, width, dtype=f32)],
        (mixed, *g_parts), [pltpu.VMEM((LAYER * span, width), bf16)], name="weight",
    )

    dq, own_grad, query_token = call(
        query_grad_kernel, [VMEM] * 4,
        [shape_of(rows, LAYER * span), shape_of(2, rows, LAYER * span, dtype=f32), TOKEN],
        (window, probs, query, stats), [pltpu.VMEM((BLOCKS * span, LAYER * span), bf16)],
        limit=20, name="query_grad", after=(send,),
    )
    up, down, query_token = lax.optimization_barrier((up, down, query_token))
    stats_low, stats_high = along(up, down)
    mine, *parts, key_token = call(
        key_grad_kernel, [VMEM] * 9, [shape_of(4, rows, span)] * LAYER + [TOKEN],
        (pair, qg_low, qg_high, stats_low, stats_high, dead, own_grad, mixed, dq),
        [
            pltpu.VMEM((2, rows, LAYER * span), bf16),
            pltpu.VMEM((HEADS, span, HOPS * span), f32),
            pltpu.VMEM((HEADS, span, HOPS * span), f32),
            pltpu.VMEM((HEADS, span, HOPS * span), bf16),
            pltpu.VMEM((HEADS, span, HOPS * span), bf16),
        ],
        limit=24, name="key_grad",
    )
    parts = in_layer(parts)
    layer_output, grad_query, grad_key, grad_value, output_token = call(
        output_kernel, [VMEM] * (LAYER + 1), [flat_shape] * 4 + [TOKEN],
        (mine, *parts, out_weight), [pltpu.VMEM((4, width, span), bf16)], name="output",
    )

    scale = 1.0 / math.sqrt(span * windows * stations)
    if windows == 2:
        count = rows // 2
        got = other_window(send)
        top, bottom = call(
            split_kernel, [VMEM] * 2, [shape_of(count // 2, width)] * 2, (part, got), name="split",
            after=(query_token,),
        )
        (total,) = call(
            meet_kernel, [VMEM] * 4, [shape_of(count, width)],
            (top, bottom, swap(top, stations // 2), swap(bottom, stations // 2)), name="meet", after=(key_token,),
        )
        stride = stations // 4
        while stride >= LAYER:
            (total,) = call(
                round_kernel, [VMEM] * 2, [shape_of(count, width)], (total, swap(total, stride)),
                name="add", after=parts[:1] if stride == LAYER else (),
            )
            stride //= 2
        first, second = [], []
        for w in range(2):
            for s in range(stations):
                if s // 2 % 2 == w:
                    first.append((w * stations + s, w * stations + (s ^ 2)))
                else:
                    first.append((w * stations + s, (1 - w) * stations + s))
                    second.append((w * stations + s, (1 - w) * stations + (s ^ 2)))
        axes = ("dp", "station")
        (total,) = call(
            cross_kernel, [VMEM] * 3, [shape_of(2 * count, width)],
            (total, lax.ppermute(total, axes, first), lax.ppermute(total, axes, second)),
            name="cross", after=(output_token,),
        )
        grad_weight = ()
        for own, value in ((True, total), (False, swap(total, 1))):
            grad_weight = (pl.pallas_call(
                functools.partial(write_kernel, own, scale),
                in_specs=[VMEM] + [ANY] * len(grad_weight),
                out_specs=ANY,
                out_shape=shape_of(4 * count, width, dtype=f32),
                scratch_shapes=[pltpu.VMEM((2 * count, width), f32), dma],
                input_output_aliases={1: 0} if grad_weight else {},
                compiler_params=pltpu.CompilerParams(vmem_limit_bytes=8 * MIB),
                cost_estimate=pl.CostEstimate(flops=1, bytes_accessed=1, transcendentals=0),
                name="write",
            )(value, *grad_weight),)
        (grad_weight,) = grad_weight
    else:
        start = lax.axis_index("station") % LAYER * rows
        all_grad = jnp.zeros((LAYER * span, width), bf16)
        for peer in range(LAYER):
            value = g_parts[peer]
            spot = lax.axis_index("station") % LAYER ^ peer
            all_grad = lax.dynamic_update_slice_in_dim(all_grad, value, spot * span, 0)
        mine = dot(mixed, all_grad, NN).astype(bf16)
        whole = lax.dynamic_update_slice_in_dim(jnp.zeros((width, width), bf16), mine, start, 0)
        whole = lax.psum_scatter(whole, "dp", scatter_dimension=0, tiled=True)
        grad_weight = lax.psum(whole.astype(f32), "station") * scale
    shape = query_states.shape
    return (
        layer_output.reshape(shape),
        grad_query.reshape(shape),
        grad_key.reshape(shape),
        grad_value.reshape(shape),
        grad_weight,
    )


def solution(mesh):
    split = P("dp", "station", None, None)
    return jax.shard_map(
        local,
        mesh=mesh,
        in_specs=(split, split, split, split, P(), P(), P()),
        out_specs=(split, split, split, split, P("dp", None)),
        check_vma=False,
    )
```

```python
import functools
import math

import jax
import jax.numpy as jnp
from jax import lax
from jax.experimental import pallas as pl
from jax.experimental.pallas import tpu as pltpu
from jax.sharding import PartitionSpec as P

HEADS = 12
PMAX = 6
HOPS = 3
LAYER = 4
LOCAL = HEADS // LAYER
BLOCKS = LAYER + 2 * HOPS
SLOTS = 2 * HOPS + 1
MIB = 1024 * 1024

neg_big = -1e30
bf16, f32 = jnp.bfloat16, jnp.float32
SMEM = pl.BlockSpec(memory_space=pltpu.SMEM)
VMEM = pl.BlockSpec(memory_space=pltpu.VMEM)
ANY = pl.BlockSpec(memory_space=pl.ANY)
HBM = pl.BlockSpec(memory_space=pltpu.HBM)
NN = (((1,), (0,)), ((), ()))
NT = (((1,), (1,)), ((), ()))
TN = (((0,), (0,)), ((), ()))


def dot(x, y, dims):
    return lax.dot_general(x, y, dims, preferred_element_type=f32)


def shape_of(*dims, dtype=bf16):
    return jax.ShapeDtypeStruct(dims, dtype)


TOKEN = shape_of(8, 128, dtype=f32)


def skip_refs(kernel, first, count, *refs):
    kernel(*refs[:first], *refs[first + count :])


def call(kernel, ins, outs, args, scratch=(), limit=8, name=None, after=()):
    ins, args = [*ins, *[ANY] * len(after)], (*args, *after)
    if after:
        kernel = functools.partial(skip_refs, kernel, len(args) - len(after), len(after))
    return pl.pallas_call(
        kernel,
        in_specs=ins,
        out_specs=[VMEM] * len(outs),
        out_shape=outs,
        scratch_shapes=list(scratch),
        compiler_params=pltpu.CompilerParams(vmem_limit_bytes=int(limit * MIB)),
        cost_estimate=pl.CostEstimate(flops=1, bytes_accessed=1, transcendentals=0),
        name=name,
    )(*args)


def place(peer, size):
    position = jnp.bitwise_xor(lax.rem(lax.axis_index("station"), LAYER), peer)
    return pl.ds(pl.multiple_of(position * size, size), size)


def block(j, span):
    return slice(j * span, (j + 1) * span)


def readers(j):
    return max(0, j - 2 * HOPS), min(LAYER - 1, j)


def pack_kernel(k_ref, v_ref, *refs):
    outs, (natural, flipped, sems) = refs[:LAYER], refs[LAYER:]
    rows = outs[0].shape[1]
    copies = [
        pltpu.make_async_copy(ref, natural.at[n], sems.at[n]) for n, ref in enumerate((k_ref, v_ref))
    ]
    for copy in copies:
        copy.start()
    for n, copy in enumerate(copies):
        copy.wait()
        flipped[n] = natural[n].T
    for peer, out in enumerate(outs):
        out[...] = flipped[:, place(peer, rows)]


def project_kernel(q_ref, g_ref, weight_ref, *refs):
    outs, (copy_ref, flipped) = refs[:LAYER], refs[LAYER:]
    rows = outs[0].shape[1]
    copy_ref[...] = g_ref[...]
    flipped[0] = q_ref[...].T * bf16(1.0 / math.sqrt(flipped.shape[1] // HEADS))
    flipped[1] = dot(weight_ref[...], g_ref[...], NT).astype(bf16)
    for peer, out in enumerate(outs):
        out[...] = flipped[:, place(peer, rows)]


def gather_kernel(*refs):
    ins, (up_ref, down_ref, pair_ref) = refs[:LAYER], refs[LAYER:]
    span = ins[0].shape[2]
    for peer, ref in enumerate(ins):
        pair_ref[:, :, place(peer, span)] = ref[...]
    up_ref[...] = pair_ref[:, :, span:]
    down_ref[...] = pair_ref[:, :, : HOPS * span]


def live_kernel(station_count, ids_ref, count_ref, bias_ref, dead_ref):
    span = bias_ref.shape[1] // LAYER
    first = lax.axis_index("station") // LAYER * LAYER
    ones = jnp.ones((1, span), f32)

    def listed(reader, other):
        hit = jnp.int32(0)
        for j in range(PMAX):
            here = jnp.logical_and(ids_ref[reader, j] == other, j < count_ref[reader])
            hit = jnp.maximum(hit, here.astype(jnp.int32))
        return hit > 0

    for j in range(BLOCKS):
        outer = lax.rem(first + (j - HOPS) + station_count, station_count)
        low, high = readers(j)
        for i in range(low, high + 1):
            inner = first + i
            slot = j - i
            if slot == HOPS:
                bias_ref[j : j + 1, block(i, span)] = 0.0 * ones
            else:
                reads = jnp.where(listed(inner, outer), 0.0, neg_big)
                bias_ref[j : j + 1, block(i, span)] = reads * ones
            if not HOPS <= j < HOPS + LAYER:
                read_by = jnp.where(listed(outer, inner), 0.0, -neg_big)
                spot = slot if j < HOPS else slot - LAYER
                dead_ref[i : i + 1, block(spot, span)] = read_by * ones


def clear(ref, span):
    for j in range(BLOCKS):
        low, high = readers(j)
        for i in range(LAYER):
            if not low <= i <= high:
                ref[block(j, span), block(i, span)] = jnp.zeros((span, span), bf16)


def forward_kernel(
    pair_ref, low_ref, high_ref, query_ref, bias_ref,
    mixed_ref, stats_ref, stats_up, stats_down, probs_ref, window_ref,
    raw,
):
    rows = query_ref.shape[1]
    span = query_ref.shape[2] // LAYER
    head_width = rows // LOCAL
    reach = HOPS * span
    window_ref[:, :, :reach] = low_ref[...]
    window_ref[:, :, reach : reach + LAYER * span] = pair_ref[...]
    window_ref[:, :, reach + LAYER * span :] = high_ref[...]
    for head in range(LOCAL):
        clear(probs_ref.at[head], span)
        at = block(head, head_width)
        query = query_ref[0, at]
        tops = [None] * LAYER
        for j in range(BLOCKS):
            low, high = readers(j)
            cols = slice(low * span, (high + 1) * span)
            scores = dot(window_ref[0, at, block(j, span)], query[:, cols], TN)
            scores = scores + bias_ref[j : j + 1, cols]
            raw[block(j, span), cols] = scores
            here = jnp.max(scores, 0, keepdims=True)
            for i in range(low, high + 1):
                mine = here[:, block(i - low, span)]
                tops[i] = mine if tops[i] is None else jnp.maximum(tops[i], mine)
        top = jnp.concatenate(tops, 1)
        totals = [jnp.zeros((1, span), f32)] * LAYER
        for j in range(BLOCKS):
            low, high = readers(j)
            cols = slice(low * span, (high + 1) * span)
            weight = jnp.exp(raw[block(j, span), cols] - top[:, cols])
            raw[block(j, span), cols] = weight
            here = jnp.sum(weight, 0, keepdims=True)
            for i in range(low, high + 1):
                totals[i] = totals[i] + here[:, block(i - low, span)]
        total = jnp.concatenate(totals, 1)
        inverse = 1.0 / total
        for j in range(BLOCKS):
            low, high = readers(j)
            cols = slice(low * span, (high + 1) * span)
            probs_ref[head, block(j, span), cols] = (
                raw[block(j, span), cols] * inverse[:, cols]
            ).astype(bf16)
        mixed = dot(window_ref[1, at], probs_ref[head], NN).astype(bf16)
        mixed_ref[at] = mixed
        product = query_ref[1, at].astype(f32) * mixed.astype(f32)
        stats_ref[head : head + 1] = top + jnp.log(total)
        stats_ref[LOCAL + head : LOCAL + head + 1] = jnp.sum(product, 0, keepdims=True)
    stats_ref[2 * LOCAL :] = jnp.zeros((8 - 2 * LOCAL, LAYER * span), f32)
    for ref, at in ((stats_up, slice(span, None)), (stats_down, slice(0, reach))):
        ref[...] = jnp.zeros_like(ref)
        ref[:8] = stats_ref[:, at]


def query_grad_kernel(
    window_ref, probs_ref, query_ref, stats_ref, dq_ref, own_ref, token_ref, grads
):
    rows = query_ref.shape[1]
    span = query_ref.shape[2] // LAYER
    head_width = rows // LOCAL
    scale = 1.0 / math.sqrt(head_width)
    inside = slice(HOPS * span, (HOPS + LAYER) * span)
    clear(grads, span)
    for head in range(LOCAL):
        at = block(head, head_width)
        grad = query_ref[1, at]
        delta = stats_ref[LOCAL + head : LOCAL + head + 1]
        for j in range(BLOCKS):
            low, high = readers(j)
            cols = slice(low * span, (high + 1) * span)
            back = dot(window_ref[1, at, block(j, span)], grad[:, cols], TN)
            prob = probs_ref[head, block(j, span), cols].astype(f32)
            grads[block(j, span), cols] = (prob * (back - delta[:, cols])).astype(bf16)
        dq_ref[at] = (dot(window_ref[0, at], grads[...], NN) * scale).astype(bf16)
        own_ref[0, at] = dot(query_ref[0, at], grads[inside], NT)
        own_ref[1, at] = dot(grad, probs_ref[head, inside], NT)
    token_ref[...] = jnp.zeros_like(token_ref)


def key_grad_kernel(
    pair_ref, low_ref, high_ref, stats_low, stats_high, dead_ref, own_ref, mixed_ref, dq_ref, *refs
):
    outs, (token_ref, flipped, scores, backs, probs, grads) = refs[:LAYER], refs[LAYER:]
    rows = pair_ref.shape[1]
    span = pair_ref.shape[2] // LAYER
    head_width = rows // LOCAL
    pairs = [(head, i) for head in range(LOCAL) for i in range(LAYER)]

    def outside(low, high, i):
        sides = [low[:, i * span :]] if i < HOPS else []
        return jnp.concatenate(sides + ([high[:, : i * span]] if i else []), 1)

    def both(part, head, i):
        at = block(head, head_width)
        return outside(low_ref[part, at], high_ref[part, at], i)

    for n, (head, i) in enumerate(pairs):
        at, own = block(head, head_width), block(i, span)
        scores[n] = dot(pair_ref[0, at, own], both(0, head, i), TN)
        backs[n] = dot(pair_ref[1, at, own], both(1, head, i), TN)
    for n, (head, i) in enumerate(pairs):
        row = slice(head, head + 1)
        log_sum = outside(stats_low[row], stats_high[row], i) + dead_ref[i : i + 1]
        row = slice(LOCAL + head, LOCAL + head + 1)
        delta = outside(stats_low[row], stats_high[row], i)
        prob = jnp.exp(scores[n] - log_sum)
        probs[n] = prob.astype(bf16)
        grads[n] = (prob * (backs[n] - delta)).astype(bf16)
    for n, (head, i) in enumerate(pairs):
        at, own = block(head, head_width), block(i, span)
        keys = own_ref[0, at, own] + dot(both(0, head, i), grads[n], NT)
        values = own_ref[1, at, own] + dot(both(1, head, i), probs[n], NT)
        flipped[0, at, own] = keys.astype(bf16)
        flipped[1, at, own] = values.astype(bf16)
    for peer, out in enumerate(outs):
        at = place(peer, span)
        out[0] = mixed_ref[:, at]
        out[1] = dq_ref[:, at]
        out[2:] = flipped[:, :, at]
    token_ref[...] = jnp.zeros_like(token_ref)


def output_kernel(*refs):
    ins, refs = refs[:LAYER], refs[LAYER:]
    weight_ref, out_ref, dq_ref, dk_ref, dv_ref, token_ref, flipped = refs
    for peer, ref in enumerate(ins):
        flipped[:, place(peer, ref.shape[1])] = ref[...]
    out_ref[...] = dot(flipped[0], weight_ref[...], TN).astype(bf16)
    for n, ref in enumerate((dq_ref, dk_ref, dv_ref)):
        ref[...] = flipped[n + 1].T
    token_ref[...] = jnp.zeros_like(token_ref)


def halves(bit, half):
    send = pl.ds(pl.multiple_of((1 - bit) * half, half), half)
    keep = pl.ds(pl.multiple_of(bit * half, half), half)
    return send, keep


def bit_of(stride):
    return lax.rem(lax.axis_index("station") // stride, 2)


def weight_kernel(mixed_ref, *refs):
    ins, (send_ref, keep_ref, right) = refs[:LAYER], refs[LAYER:]
    for peer, ref in enumerate(ins):
        right[place(peer, ref.shape[0])] = ref[...]
    send, keep = halves(lax.rem(lax.axis_index("dp"), 2), send_ref.shape[0])
    send_ref[...] = dot(mixed_ref[send], right[...], NN).astype(bf16)
    keep_ref[...] = dot(mixed_ref[keep], right[...], NN)


def split_kernel(part_ref, got_ref, top_ref, bottom_ref):
    half = top_ref.shape[0]
    for out, at in ((top_ref, slice(0, half)), (bottom_ref, slice(half, 2 * half))):
        out[...] = (part_ref[at] + got_ref[at].astype(f32)).astype(bf16)


def meet_kernel(top_ref, bottom_ref, got_top, got_bottom, out_ref):
    half = top_ref.shape[0]
    for n, (mine, got) in enumerate(((top_ref, got_top), (bottom_ref, got_bottom))):
        out_ref[n * half : (n + 1) * half] = (mine[...].astype(f32) + got[...].astype(f32)).astype(bf16)


def round_kernel(part_ref, got_ref, out_ref):
    out_ref[...] = (part_ref[...].astype(f32) + got_ref[...].astype(f32)).astype(bf16)


def write_kernel(own, scale, value_ref, *refs):
    out_ref, wide, sem = refs[-3:]
    half = value_ref.shape[0]
    other, here = halves(bit_of(1), half)
    wide[...] = value_ref[...].astype(f32) * scale
    copy = pltpu.make_async_copy(wide, out_ref.at[here if own else other], sem)
    copy.start()
    copy.wait()


def cross_kernel(mine_ref, first_ref, second_ref, out_ref):
    window = lax.rem(lax.axis_index("dp"), 2)
    other, here = halves(window, mine_ref.shape[0])
    at_home = bit_of(2) == window
    mine, first, second = mine_ref[...], first_ref[...], second_ref[...]
    out_ref[here] = jnp.where(at_home, mine, first)
    out_ref[other] = jnp.where(at_home, first, second)


def local(
    query_states, key_states, value_states, grad_output, out_weight, partner_ids, partner_count
):
    span, width = query_states.shape[2:]
    stations = lax.axis_size("station")
    windows = lax.axis_size("dp")
    rows = width // LAYER
    dma = pltpu.SemaphoreType.DMA

    def swap(value, stride):
        return lax.ppermute(value, "station", [(s ^ stride, s) for s in range(stations)])

    def in_layer(values):
        return [swap(values[n], n + 1) for n in range(LAYER - 1)]

    def along(up, down):
        low = lax.ppermute(up, "station", [(s, (s + LAYER) % stations) for s in range(stations)])
        high = lax.ppermute(down, "station", [(s, (s - LAYER) % stations) for s in range(stations)])
        return low, high

    def other_window(value):
        return lax.ppermute(value, "dp", [(0, 1), (1, 0)])

    def flat(x):
        return x.reshape(span, width)

    q, k, v, g = flat(query_states), flat(key_states), flat(value_states), flat(grad_output)
    flat_shape = shape_of(span, width)
    part_shape = shape_of(2, rows, span)
    reach_shape = shape_of(2, rows, HOPS * span)
    layer_shape = shape_of(2, rows, LAYER * span)

    def gather(parts, after=()):
        return call(
            gather_kernel, [VMEM] * LAYER, [reach_shape, reach_shape, layer_shape], parts,
            name="gather", after=after,
        )

    mine, *parts = call(
        pack_kernel, [HBM] * 2, [part_shape] * LAYER, (k, v),
        [pltpu.VMEM((2, span, width), bf16), pltpu.VMEM((2, width, span), bf16), dma((2,))],
        limit=53.5, name="pack",
    )
    q, *parts = lax.optimization_barrier((q, *parts))
    parts = in_layer(parts)
    up, down, pair = gather((mine, *parts))
    mine, *query_parts, g_copy = call(
        project_kernel, [VMEM] * 3, [part_shape] * LAYER + [flat_shape],
        (q, g, out_weight), [pltpu.VMEM((2, width, span), bf16)], name="project",
    )
    up, g_later, *query_parts = lax.optimization_barrier((up, g, *query_parts))
    kv_low, kv_high = along(up, down)
    g_across = swap(g_later, 2)
    g_parts = g_copy, swap(g_later, 1), g_across, swap(g_across, 1)
    bias, dead = call(
        functools.partial(live_kernel, stations), [SMEM] * 2,
        [shape_of(16, LAYER * span, dtype=f32), shape_of(8, HOPS * span, dtype=f32)],
        (partner_ids, partner_count), name="live",
    )
    up, down, query = gather((mine, *in_layer(query_parts)), (bias,))
    qg_low, qg_high = along(up, down)
    stats_shape = shape_of(16, HOPS * span, dtype=f32)
    mixed, stats, up, down, probs, window = call(
        forward_kernel, [VMEM] * 5,
        [
            shape_of(rows, LAYER * span), shape_of(8, LAYER * span, dtype=f32),
            stats_shape, stats_shape,
            shape_of(LOCAL, BLOCKS * span, LAYER * span), shape_of(2, rows, BLOCKS * span),
        ],
        (pair, kv_low, kv_high, query, bias),
        [pltpu.VMEM((BLOCKS * span, LAYER * span), f32)],
        limit=20, name="forward",
    )

    send, part = call(
        weight_kernel, [VMEM] * (LAYER + 1),
        [shape_of(rows // 2, width), shape_of(rows // 2, width, dtype=f32)],
        (mixed, *g_parts), [pltpu.VMEM((LAYER * span, width), bf16)], name="weight",
    )

    dq, own_grad, query_token = call(
        query_grad_kernel, [VMEM] * 4,
        [shape_of(rows, LAYER * span), shape_of(2, rows, LAYER * span, dtype=f32), TOKEN],
        (window, probs, query, stats), [pltpu.VMEM((BLOCKS * span, LAYER * span), bf16)],
        limit=20, name="query_grad", after=(send,),
    )
    up, down, query_token = lax.optimization_barrier((up, down, query_token))
    stats_low, stats_high = along(up, down)
    mine, *parts, key_token = call(
        key_grad_kernel, [VMEM] * 9, [shape_of(4, rows, span)] * LAYER + [TOKEN],
        (pair, qg_low, qg_high, stats_low, stats_high, dead, own_grad, mixed, dq),
        [
            pltpu.VMEM((2, rows, LAYER * span), bf16),
            pltpu.VMEM((HEADS, span, HOPS * span), f32),
            pltpu.VMEM((HEADS, span, HOPS * span), f32),
            pltpu.VMEM((HEADS, span, HOPS * span), bf16),
            pltpu.VMEM((HEADS, span, HOPS * span), bf16),
        ],
        limit=24, name="key_grad",
    )
    parts = in_layer(parts)
    layer_output, grad_query, grad_key, grad_value, output_token = call(
        output_kernel, [VMEM] * (LAYER + 1), [flat_shape] * 4 + [TOKEN],
        (mine, *parts, out_weight), [pltpu.VMEM((4, width, span), bf16)], name="output",
    )

    scale = 1.0 / math.sqrt(span * windows * stations)
    if windows == 2:
        count = rows // 2
        got = other_window(send)
        top, bottom = call(
            split_kernel, [VMEM] * 2, [shape_of(count // 2, width)] * 2, (part, got), name="split",
            after=(query_token,),
        )
        (total,) = call(
            meet_kernel, [VMEM] * 4, [shape_of(count, width)],
            (top, bottom, swap(top, stations // 2), swap(bottom, stations // 2)), name="meet", after=(key_token,),
        )
        stride = stations // 4
        while stride >= LAYER:
            (total,) = call(
                round_kernel, [VMEM] * 2, [shape_of(count, width)], (total, swap(total, stride)),
                name="add", after=parts[:1] if stride == LAYER else (),
            )
            stride //= 2
        first, second = [], []
        for w in range(2):
            for s in range(stations):
                if s // 2 % 2 == w:
                    first.append((w * stations + s, w * stations + (s ^ 2)))
                else:
                    first.append((w * stations + s, (1 - w) * stations + s))
                    second.append((w * stations + s, (1 - w) * stations + (s ^ 2)))
        axes = ("dp", "station")
        (total,) = call(
            cross_kernel, [VMEM] * 3, [shape_of(2 * count, width)],
            (total, lax.ppermute(total, axes, first), lax.ppermute(total, axes, second)),
            name="cross", after=parts[1:],
        )
        grad_weight = ()
        for own, value in ((True, total), (False, swap(total, 1))):
            grad_weight = (pl.pallas_call(
                functools.partial(write_kernel, own, scale),
                in_specs=[VMEM] + [ANY] * len(grad_weight),
                out_specs=ANY,
                out_shape=shape_of(4 * count, width, dtype=f32),
                scratch_shapes=[pltpu.VMEM((2 * count, width), f32), dma],
                input_output_aliases={1: 0} if grad_weight else {},
                compiler_params=pltpu.CompilerParams(vmem_limit_bytes=8 * MIB),
                cost_estimate=pl.CostEstimate(flops=1, bytes_accessed=1, transcendentals=0),
                name="write",
            )(value, *grad_weight),)
        (grad_weight,) = grad_weight
    else:
        start = lax.axis_index("station") % LAYER * rows
        all_grad = jnp.zeros((LAYER * span, width), bf16)
        for peer in range(LAYER):
            value = g_parts[peer]
            spot = lax.axis_index("station") % LAYER ^ peer
            all_grad = lax.dynamic_update_slice_in_dim(all_grad, value, spot * span, 0)
        mine = dot(mixed, all_grad, NN).astype(bf16)
        whole = lax.dynamic_update_slice_in_dim(jnp.zeros((width, width), bf16), mine, start, 0)
        whole = lax.psum_scatter(whole, "dp", scatter_dimension=0, tiled=True)
        grad_weight = lax.psum(whole.astype(f32), "station") * scale
    shape = query_states.shape
    return (
        layer_output.reshape(shape),
        grad_query.reshape(shape),
        grad_key.reshape(shape),
        grad_value.reshape(shape),
        grad_weight,
    )


def solution(mesh):
    split = P("dp", "station", None, None)
    return jax.shard_map(
        local,
        mesh=mesh,
        in_specs=(split, split, split, split, P(), P(), P()),
        out_specs=(split, split, split, split, P("dp", None)),
        check_vma=False,
    )
```
